32 devices in a mesh: seq: 4 (over y, core), tp: 8 (over z, x).
Axes of the slice: x: 2, y: 2, z: 4, core: 2. Of those that a mesh axis runs over, the one named last changes fastest.
Arguments:
- layer_input: bfloat16 [16384, 2048], P(('seq', 'tp')), may hold values from -6 to 6
- cotangent: bfloat16 [16384, 2048], P(('seq', 'tp')), may hold values from -6 to 6
- counts: int32 [4], P('seq'), may hold values from 100 to 320
- positions: int32 [16384], P('seq'), may hold values from 0 to 4095, as said below
- qkv_master: float32 [2048, 6144], P('seq', 'tp'), may hold values from -0.125 to 0.125
- qkv_moment: float32 [2048, 6144], P('seq', 'tp'), may hold values from -1536 to 1536
- qkv_average: float32 [2048, 6144], P('seq', 'tp'), may hold values from -0.125 to 0.125
- out_master: float32 [2048, 2048], P('tp', 'seq'), may hold values from -2 to 2
- out_moment: float32 [2048, 2048], P('tp', 'seq'), may hold values from -40 to 40
- out_average: float32 [2048, 2048], P('tp', 'seq'), may hold values from -2 to 2
- gate_up_master: float32 [2, 2048, 8192], P(None, 'seq', 'tp'), may hold values from -0.125 to 0.125
- gate_up_moment: float32 [2, 2048, 8192], P(None, 'seq', 'tp'), may hold values from -224 to 224
- gate_up_average: float32 [2, 2048, 8192], P(None, 'seq', 'tp'), may hold values from -0.125 to 0.125
- down_master: float32 [8192, 2048], P('tp', 'seq'), may hold values from -0.0625 to 0.0625
- down_moment: float32 [8192, 2048], P('tp', 'seq'), may hold values from -384 to 384
- down_average: float32 [8192, 2048], P('tp', 'seq'), may hold values from -0.0625 to 0.0625
- gains_master: float32 [2, 2048], P(None, 'seq'), may hold values from 0.5 to 1.5
- gains_moment: float32 [2, 2048], P(None, 'seq'), may hold values from -1536 to 1536
- gains_average: float32 [2, 2048], P(None, 'seq'), may hold values from 0.5 to 1.5
Outputs:
- layer_output: bfloat16 [16384, 2048], P(('seq', 'tp'))
- input_grad: float32 [16384, 2048], P(('seq', 'tp'))
- qkv_moment_new: float32 [2048, 6144], P('seq', 'tp')
- qkv_average_new: float32 [2048, 6144], P('seq', 'tp')
- qkv_master_new: float32 [2048, 6144], P('seq', 'tp')
- qkv_copy_new: bfloat16 [2048, 6144], P('seq', 'tp')
- out_moment_new: float32 [2048, 2048], P('tp', 'seq')
- out_average_new: float32 [2048, 2048], P('tp', 'seq')
- out_master_new: float32 [2048, 2048], P('tp', 'seq')
- out_copy_new: bfloat16 [2048, 2048], P('tp', 'seq')
- gate_up_moment_new: float32 [2, 2048, 8192], P(None, 'seq', 'tp')
- gate_up_average_new: float32 [2, 2048, 8192], P(None, 'seq', 'tp')
- gate_up_master_new: float32 [2, 2048, 8192], P(None, 'seq', 'tp')
- gate_up_copy_new: bfloat16 [2, 2048, 8192], P(None, 'seq', 'tp')
- down_moment_new: float32 [8192, 2048], P('tp', 'seq')
- down_average_new: float32 [8192, 2048], P('tp', 'seq')
- down_master_new: float32 [8192, 2048], P('tp', 'seq')
- down_copy_new: bfloat16 [8192, 2048], P('tp', 'seq')
- gains_moment_new: float32 [2, 2048], P(None, 'seq')
- gains_average_new: float32 [2, 2048], P(None, 'seq')
- gains_master_new: float32 [2, 2048], P(None, 'seq')
- gains_copy_new: bfloat16 [2, 2048], P(None, 'seq')
The draws below stay inside these ranges and needn't reach their ends.
Inputs may be any that keep to these rules, and one draw needn't show every extreme that they name: `positions`: in each sequence of 4096 tokens the position is 0 at the first token and at up to 3 document starts, and rises by one from token to token elsewhere; the first sequence holds a single document.
All inputs are finite; a program needn't handle non-finite values.
Results may differ from the reference program's by a relative error of at most 0.02.
Values may be sent and summed in bfloat16 or wider, within the bound.
A program may use at most 640 MiB of HBM per device.

```python
import jax
import jax.numpy as jnp
from jax import lax

D = 2048
H = 32
HD = 64
FF = 8192
LEN = 4096
DOCS = 4
SEQS = 4
TOKENS = 16384


def draw_counts(key, part):
    seq_index = jnp.arange(SEQS, dtype=jnp.int32)
    base_count = 100 + 200 * seq_index // max(SEQS - 1, 1)
    extra_count = jax.random.randint(key, (SEQS,), 0, 21, dtype=jnp.int32)
    return (base_count + extra_count).astype(jnp.int32)


def draw_positions(key, part):
    cut_points = jax.random.randint(key, (SEQS, DOCS - 1), 1, LEN, dtype=jnp.int32)
    seq_index = jnp.arange(SEQS, dtype=jnp.int32)
    cut_points = jnp.where(seq_index[:, None] == 0, LEN, cut_points).astype(jnp.int32)
    token_index = jnp.arange(LEN, dtype=jnp.int32)
    passed = cut_points[:, None, :] <= token_index[None, :, None]
    doc_starts = jnp.max(jnp.where(passed, cut_points[:, None, :], 0), axis=-1)
    return (token_index[None, :] - doc_starts).reshape(SEQS * LEN).astype(jnp.int32)


def block_levels(rng, shape, cuts, low, top_value):
    def one(position, parts):
        heights = jax.random.uniform(jax.random.fold_in(jax.random.fold_in(rng, 6), position), (parts,), jnp.float32, low / len(cuts), top_value / len(cuts))
        return jnp.repeat(jnp.exp(heights), shape[position] // parts).reshape((-1,) + (1,) * (len(shape) - position - 1))

    gain = one(*cuts[0])
    for cut in cuts[1:]:
        gain = gain * one(*cut)
    return gain


def centred(key, shape, width, most, shards=(), kind=jnp.bfloat16):
    drawn = jax.random.normal(key, shape, jnp.float32) * width
    if len(shards) > 0:
        drawn = block_levels(key, shape, shards, -0.22, 0.18) * drawn
    return jnp.clip(drawn, min=-most, max=most).astype(kind)


def setup_inputs(seed: int = 0) -> dict:
    streams_of = jax.random.split(jax.random.key(seed), 20)
    return {
        "layer_input": centred(streams_of[0], (TOKENS, D), 1.0, 6.0, ((0, 32),)),
        "cotangent": centred(streams_of[1], (TOKENS, D), 1.0, 6.0, ((0, 32),)),
        "counts": draw_counts(jax.random.fold_in(streams_of[19], 71), 0),
        "positions": draw_positions(jax.random.fold_in(streams_of[19], 71), 0),
        "qkv_master": centred(streams_of[4], (D, H * 3 * HD), D ** -0.5, 0.125, ((0, 4), (1, 8)), jnp.float32),
        "qkv_moment": centred(streams_of[5], (D, H * 3 * HD), (2.0 * (LEN * SEQS) ** 0.5), 1536.0, ((0, 4), (1, 8)), jnp.float32),
        "qkv_average": centred(streams_of[6], (D, H * 3 * HD), D ** -0.5, 0.125, ((0, 4), (1, 8)), jnp.float32),
        "out_master": centred(streams_of[7], (H * HD, D), (max(H * HD * 16 // LEN, 1)) ** -0.5, 2.0, ((0, 8), (1, 4)), jnp.float32),
        "out_moment": centred(streams_of[8], (H * HD, D), (0.05 * (LEN * SEQS) ** 0.5), 40.0, ((0, 8), (1, 4)), jnp.float32),
        "out_average": centred(streams_of[9], (H * HD, D), (max(H * HD * 16 // LEN, 1)) ** -0.5, 2.0, ((0, 8), (1, 4)), jnp.float32),
        "gate_up_master": centred(streams_of[10], (2, D, FF), D ** -0.5, 0.125, ((1, 4), (2, 8)), jnp.float32),
        "gate_up_moment": centred(streams_of[11], (2, D, FF), (0.3 * (LEN * SEQS) ** 0.5), 224.0, ((1, 4), (2, 8)), jnp.float32),
        "gate_up_average": centred(streams_of[12], (2, D, FF), D ** -0.5, 0.125, ((1, 4), (2, 8)), jnp.float32),
        "down_master": centred(streams_of[13], (FF, D), FF ** -0.5, 0.0625, ((0, 8), (1, 4)), jnp.float32),
        "down_moment": centred(streams_of[14], (FF, D), (0.5 * (LEN * SEQS) ** 0.5), 384.0, ((0, 8), (1, 4)), jnp.float32),
        "down_average": centred(streams_of[15], (FF, D), FF ** -0.5, 0.0625, ((0, 8), (1, 4)), jnp.float32),
        "gains_master": jnp.clip(1.0 + 0.1 * jax.random.normal(streams_of[16], (2, D), jnp.float32), 0.5, 1.5),
        "gains_moment": centred(streams_of[17], (2, D), (2.0 * (LEN * SEQS) ** 0.5), 1536.0, ((1, 4),), jnp.float32),
        "gains_average": jnp.clip(0.5 + 1.0 * jax.random.uniform(streams_of[18], (2, D), jnp.float32) ** block_levels(streams_of[18], (2, D), ((1, 4),), -0.2, 0.2), 0.5, 1.5),
    }


norm_epsilon = 1e-05
rope_theta = 130000.0
momentum_coef = 0.9
average_coef = 0.5
masked_score = -1e+30
rate_qkv = 0.004
rate_out = 2.0
rate_gate_up = 0.03
rate_down = 0.009
rate_gains = 0.1
highest = lax.Precision.HIGHEST

@jax.custom_vjp
def low(v):
    return lax.optimization_barrier(v.astype(jnp.bfloat16)).astype(jnp.float32)

@jax.custom_vjp
def low_back(v):
    return v

def low_keep(v):
    return (low(v), None)

def low_pass(kept, grad):
    return (grad,)

def back_keep(v):
    return (v, None)

def back_low(kept, grad):
    return (low(grad),)
low.defvjp(low_keep, low_pass)
low_back.defvjp(back_keep, back_low)

def rms_scale(values):
    return lax.rsqrt(lax.optimization_barrier(jnp.mean(values * values, axis=-1, keepdims=True)) + norm_epsilon)

def rope_tables(positions):
    frequency = rope_theta ** (-(jnp.arange(HD // 2, dtype=jnp.float32) * 2.0) / HD)
    angles = positions.astype(jnp.float32)[:, None] * frequency[None, :]
    return (jnp.cos(angles)[:, None, :], jnp.sin(angles)[:, None, :])

def rotate(vectors, cosine_table, sine_table):
    half_width = vectors.shape[-1] // 2
    lower_half = vectors[..., :half_width]
    upper_half = vectors[..., half_width:]
    return jnp.concatenate([lower_half * cosine_table - upper_half * sine_table, upper_half * cosine_table + lower_half * sine_table], axis=-1)

def decoder_layer(inputs, params, cosine_table, sine_table):
    qkv_weight, out_weight, gate_up_weight, down_weight, gain_weight = params
    normed = low(inputs * rms_scale(inputs) * gain_weight[0])
    mixture = low_back(jnp.dot(normed, qkv_weight, precision=highest)).reshape(LEN, H, 3, HD)
    queries = low(rotate(mixture[:, :, 0], cosine_table, sine_table))
    key_rows = low(rotate(mixture[:, :, 1], cosine_table, sine_table))
    value_rows = low(mixture[:, :, 2])
    block_rows = min(512, LEN)
    score_scale = HD ** (-0.5)

    def attend(block_index):
        query_block = lax.dynamic_slice_in_dim(queries, block_index * block_rows, block_rows, 0)
        scores = low_back(score_scale * jnp.einsum('qhd,khd->hqk', query_block, key_rows, precision=highest))
        row_index = block_index * block_rows + jnp.arange(block_rows)
        allowed = jnp.arange(LEN)[None, :] <= row_index[:, None]
        scores = jnp.where(allowed[None], scores, masked_score)
        shifted = scores - lax.optimization_barrier(jnp.max(scores, axis=-1, keepdims=True))
        exp_scores = jnp.exp(shifted)
        soft_scores = low(exp_scores / lax.optimization_barrier(jnp.sum(exp_scores, axis=-1, keepdims=True)))
        return jnp.einsum('hqk,khd->qhd', soft_scores, value_rows, precision=highest)
    blocks = lax.map(jax.checkpoint(attend), jnp.arange(LEN // block_rows))
    attended = low(low_back(blocks.reshape(LEN, H * HD)))
    residual = inputs + low_back(jnp.dot(attended, out_weight, precision=highest))
    normed_second = low(residual * rms_scale(residual) * gain_weight[1])
    gate_pre = low_back(jnp.dot(normed_second, gate_up_weight[0], precision=highest))
    up_pre = low_back(jnp.dot(normed_second, gate_up_weight[1], precision=highest))
    activation = low(gate_pre * jax.nn.sigmoid(gate_pre) * up_pre)
    return residual + low_back(jnp.dot(activation, down_weight, precision=highest))

def apply_update(master, grad, moment, average, rate):
    moment_new = momentum_coef * moment + grad
    master_new = master - rate * (grad + momentum_coef * moment_new)
    average_new = average_coef * average + (1.0 - average_coef) * master_new
    return (moment_new, average_new, master_new, master_new.astype(jnp.bfloat16))

def round_copy(master):
    return lax.optimization_barrier(master.astype(jnp.bfloat16)).astype(jnp.float32)

def reference(layer_input, cotangent, counts, positions, qkv_master, qkv_moment, qkv_average, out_master, out_moment, out_average, gate_up_master, gate_up_moment, gate_up_average, down_master, down_moment, down_average, gains_master, gains_moment, gains_average):
    params = (round_copy(qkv_master), round_copy(out_master), round_copy(gate_up_master), round_copy(down_master), round_copy(gains_master))
    count_values = counts.astype(jnp.float32)
    seq_weights = SEQS * count_values / jnp.sum(count_values)
    inputs = layer_input.astype(jnp.float32).reshape(SEQS, LEN, D)
    cot_rows = cotangent.astype(jnp.float32).reshape(SEQS, LEN, D)
    seq_positions = positions.reshape(SEQS, LEN)

    def one_sequence(running, seq_item):
        input_rows, cot_item, position_rows, weight_item = seq_item
        cosine_table, sine_table = rope_tables(position_rows)

        def forward(input_arg, param_arg):
            return decoder_layer(input_arg, param_arg, cosine_table, sine_table)
        seq_output, pull_back = jax.vjp(forward, input_rows, params)
        grad_input, grad_params = pull_back(weight_item * cot_item)
        running = jax.tree.map(jnp.add, running, grad_params)
        return (running, (seq_output.astype(jnp.bfloat16), grad_input))
    zero_grads = jax.tree.map(jnp.zeros_like, params)
    grads, (seq_outputs, grad_inputs) = lax.scan(one_sequence, zero_grads, (inputs, cot_rows, seq_positions, seq_weights))
    rate_unit = float(TOKENS) ** (-0.5)
    qkv_new = apply_update(qkv_master, grads[0], qkv_moment, qkv_average, rate_qkv * rate_unit)
    out_new = apply_update(out_master, grads[1], out_moment, out_average, rate_out * rate_unit)
    gate_up_new = apply_update(gate_up_master, grads[2], gate_up_moment, gate_up_average, rate_gate_up * rate_unit)
    down_new = apply_update(down_master, grads[3], down_moment, down_average, rate_down * rate_unit)
    gains_new = apply_update(gains_master, grads[4], gains_moment, gains_average, rate_gains * rate_unit)
    layer_output = seq_outputs.reshape(TOKENS, D)
    input_grad = grad_inputs.reshape(TOKENS, D)
    return (layer_output, input_grad, qkv_new[0], qkv_new[1], qkv_new[2], qkv_new[3], out_new[0], out_new[1], out_new[2], out_new[3], gate_up_new[0], gate_up_new[1], gate_up_new[2], gate_up_new[3], down_new[0], down_new[1], down_new[2], down_new[3], gains_new[0], gains_new[1], gains_new[2], gains_new[3])
```

```python
import jax
import jax.numpy as jnp
from jax import lax
from jax.experimental import pallas as pl
from jax.experimental.pallas import tpu as pltpu
from jax.sharding import PartitionSpec as P

HD = 64


norm_epsilon = 1e-05
rope_theta = 130000.0
momentum_coef = 0.9
average_coef = 0.5
masked_score = -1e30
rate_qkv = 0.004
rate_out = 2.0
rate_gate_up = 0.03
rate_down = 0.009
rate_gains = 0.1


def rms_scale(values):
    return lax.rsqrt(jnp.mean(values * values, axis=-1, keepdims=True) + norm_epsilon)


def rope_tables(positions, head_size):
    frequency = rope_theta ** (-(jnp.arange(head_size // 2, dtype=jnp.float32) * 2.0) / head_size)
    angles = positions.astype(jnp.float32)[:, None] * frequency[None, :]
    return (jnp.cos(angles)[:, None, :], jnp.sin(angles)[:, None, :])


def rotate(vectors, cosine_table, sine_table):
    half_width = vectors.shape[-1] // 2
    lower_half = vectors[..., :half_width]
    upper_half = vectors[..., half_width:]
    return jnp.concatenate(
        [
            lower_half * cosine_table - upper_half * sine_table,
            upper_half * cosine_table + lower_half * sine_table,
        ],
        axis=-1,
    )


def unrotate(grads, cosine_table, sine_table):
    half_width = grads.shape[-1] // 2
    lower_half = grads[..., :half_width]
    upper_half = grads[..., half_width:]
    return jnp.concatenate(
        [
            lower_half * cosine_table + upper_half * sine_table,
            upper_half * cosine_table - lower_half * sine_table,
        ],
        axis=-1,
    )


def norm_back(values, gain, grad):
    scale_rows = rms_scale(values)
    scaled = grad * gain
    back = scale_rows * (
        scaled
        - values * scale_rows * scale_rows * jnp.mean(scaled * values, axis=-1, keepdims=True)
    )
    return (back, jnp.sum(grad * values * scale_rows, axis=0))


def apply_update(master, grad, moment, average, rate):
    moment_new = momentum_coef * moment + grad
    master_new = master - rate * (grad + momentum_coef * moment_new)
    average_new = average_coef * average + (1.0 - average_coef) * master_new
    return (moment_new, average_new, master_new, master_new.astype(jnp.bfloat16))


def shards(
    layer_input,
    cotangent,
    counts,
    positions,
    qkv_master,
    qkv_moment,
    qkv_average,
    out_master,
    out_moment,
    out_average,
    gate_up_master,
    gate_up_moment,
    gate_up_average,
    down_master,
    down_moment,
    down_average,
    gains_master,
    gains_moment,
    gains_average,
):
    tp_size = lax.axis_size("tp")
    seq_size = lax.axis_size("seq")
    own_rows = layer_input.shape[0]
    length = own_rows * tp_size
    qkv_weight, out_weight, gate_up_weight, down_weight, gain_weight = (
        lax.all_gather(qkv_master.astype(jnp.bfloat16), "seq", axis=0, tiled=True),
        lax.all_gather(out_master.astype(jnp.bfloat16), "seq", axis=1, tiled=True),
        lax.all_gather(gate_up_master.astype(jnp.bfloat16), "seq", axis=1, tiled=True),
        lax.all_gather(down_master.astype(jnp.bfloat16), "seq", axis=1, tiled=True),
        lax.all_gather(gains_master.astype(jnp.bfloat16), "seq", axis=1, tiled=True),
    )
    heads_local = qkv_weight.shape[1] // (3 * HD)
    count_total = lax.psum(counts.astype(jnp.float32), "seq")
    seq_weight = seq_size * counts.astype(jnp.float32)[0] / count_total[0]
    gain_first = gain_weight[0].astype(jnp.float32)
    gain_second = gain_weight[1].astype(jnp.float32)
    gathered = lax.all_gather(layer_input, "tp", axis=0, tiled=True)
    inputs = gathered.astype(jnp.float32)
    normed = (inputs * rms_scale(inputs) * gain_first).astype(jnp.bfloat16)
    mixture = jnp.dot(normed, qkv_weight, preferred_element_type=jnp.float32).reshape(
        length, heads_local, 3, HD
    )
    cosine_table, sine_table = rope_tables(positions, HD)
    queries = rotate(mixture[:, :, 0], cosine_table, sine_table).astype(jnp.bfloat16)
    key_rows = rotate(mixture[:, :, 1], cosine_table, sine_table).astype(jnp.bfloat16)
    value_rows = mixture[:, :, 2].astype(jnp.bfloat16)
    block_rows = min(512, length)
    block_count = length // block_rows
    score_scale = HD ** (-0.5)

    def block_scores(block_index):
        key_end = (block_index + 1) * block_rows
        query_block = queries[block_index * block_rows : key_end]
        row_index = block_index * block_rows + jnp.arange(block_rows)
        allowed = jnp.arange(key_end)[None, :] <= row_index[:, None]
        scores = score_scale * jnp.einsum(
            "qhd,khd->hqk", query_block, key_rows[:key_end], preferred_element_type=jnp.float32
        )
        return (query_block, jnp.where(allowed[None], scores, masked_score))

    attended_list = []
    log_totals = []
    for block_index in range(block_count):
        query_block, scores = block_scores(block_index)
        key_end = (block_index + 1) * block_rows
        row_max = jnp.max(scores, axis=-1, keepdims=True)
        exp_scores = jnp.exp(scores - row_max)
        row_total = jnp.sum(exp_scores, axis=-1, keepdims=True)
        soft_scores = (exp_scores / row_total).astype(jnp.bfloat16)
        attended_block = jnp.einsum(
            "hqk,khd->qhd", soft_scores, value_rows[:key_end], preferred_element_type=jnp.float32
        )
        attended_list.append(attended_block.astype(jnp.bfloat16))
        log_totals.append(row_max + jnp.log(row_total))
    attended = jnp.concatenate(attended_list, axis=0).reshape(length, heads_local * HD)
    own_start = lax.axis_index("tp") * own_rows
    input_own = layer_input.astype(jnp.float32)
    branch = lax.psum(
        jnp.dot(attended, out_weight, preferred_element_type=jnp.float32).astype(jnp.bfloat16), "tp"
    ).astype(jnp.float32)
    residual = inputs + branch
    normed_second = (residual * rms_scale(residual) * gain_second).astype(jnp.bfloat16)
    resid_own = lax.dynamic_slice_in_dim(residual, own_start, own_rows, 0)
    gate_pre = jnp.dot(normed_second, gate_up_weight[0], preferred_element_type=jnp.float32)
    up_pre = jnp.dot(normed_second, gate_up_weight[1], preferred_element_type=jnp.float32)
    gate_sigmoid = jax.nn.sigmoid(gate_pre)
    activation = (gate_pre * gate_sigmoid * up_pre).astype(jnp.bfloat16)
    layer_output = (
        resid_own
        + lax.psum_scatter(
            jnp.dot(activation, down_weight, preferred_element_type=jnp.float32).astype(
                jnp.bfloat16
            ),
            "tp",
            scatter_dimension=0,
            tiled=True,
        ).astype(jnp.float32)
    ).astype(jnp.bfloat16)
    cot_all = lax.all_gather(cotangent, "tp", axis=0, tiled=True)
    grad_out = (seq_weight * cot_all.astype(jnp.float32)).astype(jnp.bfloat16)
    grad_down = jnp.einsum("tf,td->fd", activation, grad_out, preferred_element_type=jnp.float32)
    grad_act = jnp.einsum("td,fd->tf", grad_out, down_weight, preferred_element_type=jnp.float32)
    grad_gate = (grad_act * up_pre * gate_sigmoid * (1.0 + gate_pre * (1.0 - gate_sigmoid))).astype(
        jnp.bfloat16
    )
    grad_up = (grad_act * gate_pre * gate_sigmoid).astype(jnp.bfloat16)
    grad_gate_up = jnp.stack(
        [
            jnp.einsum("td,tf->df", normed_second, grad_gate, preferred_element_type=jnp.float32),
            jnp.einsum("td,tf->df", normed_second, grad_up, preferred_element_type=jnp.float32),
        ]
    )
    grad_normed_second = lax.psum_scatter(
        (
            jnp.einsum(
                "tf,df->td", grad_gate, gate_up_weight[0], preferred_element_type=jnp.float32
            )
            + jnp.einsum(
                "tf,df->td", grad_up, gate_up_weight[1], preferred_element_type=jnp.float32
            )
        ).astype(jnp.bfloat16),
        "tp",
        scatter_dimension=0,
        tiled=True,
    ).astype(jnp.float32)
    grad_resid_own, gain_second_part = norm_back(resid_own, gain_second, grad_normed_second)
    grad_resid_own = grad_resid_own + seq_weight * cotangent.astype(jnp.float32)
    resid_grad_rows = lax.all_gather(grad_resid_own.astype(jnp.bfloat16), "tp", axis=0, tiled=True)
    grad_out_proj = jnp.einsum(
        "tc,td->cd", attended, resid_grad_rows, preferred_element_type=jnp.float32
    )
    grad_attended = (
        jnp.einsum("td,cd->tc", resid_grad_rows, out_weight, preferred_element_type=jnp.float32)
        .astype(jnp.bfloat16)
        .reshape(length, heads_local, HD)
    )
    grad_keys = jnp.zeros((length, heads_local, HD), jnp.float32)
    grad_values = jnp.zeros((length, heads_local, HD), jnp.float32)
    query_grads = []
    for block_index in range(block_count):
        key_end = (block_index + 1) * block_rows
        query_block, scores = block_scores(block_index)
        soft_scores = jnp.exp(scores - log_totals[block_index])
        grad_block = grad_attended[block_index * block_rows : key_end]
        grad_soft = jnp.einsum(
            "qhd,khd->hqk", grad_block, value_rows[:key_end], preferred_element_type=jnp.float32
        )
        row_delta = jnp.sum(soft_scores * grad_soft, axis=-1, keepdims=True)
        grad_scores = (soft_scores * (grad_soft - row_delta)).astype(jnp.bfloat16)
        query_grads.append(
            score_scale
            * jnp.einsum(
                "hqk,khd->qhd", grad_scores, key_rows[:key_end], preferred_element_type=jnp.float32
            )
        )
        grad_keys = grad_keys.at[:key_end].add(
            score_scale
            * jnp.einsum(
                "hqk,qhd->khd", grad_scores, query_block, preferred_element_type=jnp.float32
            )
        )
        grad_values = grad_values.at[:key_end].add(
            jnp.einsum(
                "hqk,qhd->khd",
                soft_scores.astype(jnp.bfloat16),
                grad_block,
                preferred_element_type=jnp.float32,
            )
        )
    grad_queries = jnp.concatenate(query_grads, axis=0)
    grad_mixture = (
        jnp.stack(
            [
                unrotate(grad_queries, cosine_table, sine_table),
                unrotate(grad_keys, cosine_table, sine_table),
                grad_values,
            ],
            axis=2,
        )
        .astype(jnp.bfloat16)
        .reshape(length, heads_local * 3 * HD)
    )
    grad_qkv = jnp.einsum("td,tc->dc", normed, grad_mixture, preferred_element_type=jnp.float32)
    grad_normed_first = lax.psum_scatter(
        jnp.einsum(
            "tc,dc->td", grad_mixture, qkv_weight, preferred_element_type=jnp.float32
        ).astype(jnp.bfloat16),
        "tp",
        scatter_dimension=0,
        tiled=True,
    ).astype(jnp.float32)
    grad_input_own, gain_first_part = norm_back(input_own, gain_first, grad_normed_first)
    input_grad = grad_resid_own + grad_input_own
    gain_grads = lax.psum(jnp.stack([gain_first_part, gain_second_part]), ("seq", "tp"))
    gain_grad_own = lax.dynamic_slice_in_dim(
        gain_grads, lax.axis_index("seq") * gains_master.shape[1], gains_master.shape[1], 1
    )
    qkv_grad_own, out_grad_own, gate_up_grad_own, down_grad_own = (
        lax.psum_scatter(
            grad_qkv.astype(jnp.bfloat16), "seq", scatter_dimension=0, tiled=True
        ).astype(jnp.float32),
        lax.psum_scatter(
            grad_out_proj.astype(jnp.bfloat16), "seq", scatter_dimension=1, tiled=True
        ).astype(jnp.float32),
        lax.psum_scatter(
            grad_gate_up.astype(jnp.bfloat16), "seq", scatter_dimension=1, tiled=True
        ).astype(jnp.float32),
        lax.psum_scatter(
            grad_down.astype(jnp.bfloat16), "seq", scatter_dimension=1, tiled=True
        ).astype(jnp.float32),
    )
    rate_unit = float(length * seq_size) ** (-0.5)
    qkv_new = apply_update(qkv_master, qkv_grad_own, qkv_moment, qkv_average, rate_qkv * rate_unit)
    out_new = apply_update(out_master, out_grad_own, out_moment, out_average, rate_out * rate_unit)
    gate_up_new = apply_update(
        gate_up_master, gate_up_grad_own, gate_up_moment, gate_up_average, rate_gate_up * rate_unit
    )
    down_new = apply_update(
        down_master, down_grad_own, down_moment, down_average, rate_down * rate_unit
    )
    gains_new = apply_update(
        gains_master, gain_grad_own, gains_moment, gains_average, rate_gains * rate_unit
    )
    return (
        layer_output,
        input_grad,
        qkv_new[0],
        qkv_new[1],
        qkv_new[2],
        qkv_new[3],
        out_new[0],
        out_new[1],
        out_new[2],
        out_new[3],
        gate_up_new[0],
        gate_up_new[1],
        gate_up_new[2],
        gate_up_new[3],
        down_new[0],
        down_new[1],
        down_new[2],
        down_new[3],
        gains_new[0],
        gains_new[1],
        gains_new[2],
        gains_new[3],
    )


ROW = 512
BF = jnp.bfloat16
F32 = jnp.float32
LOG2E = 1.4426950408889634
STORED = (0, 4, 1, 5, 2, 6, 3, 7)
NT = (((1,), (1,)), ((), ()))
NN = (((1,), (0,)), ((), ()))
TN = (((0,), (0,)), ((), ()))


def ring_plan_fits(mesh):
    return mesh.shape["seq"] == 4 and mesh.shape["tp"] == 8


def device_pairs(target):
    pairs = []
    for index in range(32):
        y, c, h, l, x = (index >> 4) & 1, (index >> 3) & 1, (index >> 2) & 1, (index >> 1) & 1, index & 1
        goal = target(y, c, h, l, x)
        if goal is not None:
            y, c, h, l, x = goal
            pairs.append((index, 16 * y + 8 * c + 4 * h + 2 * l + x))
    return pairs


def move(values, target):
    return lax.ppermute(values, ("seq", "tp"), device_pairs(target))


def flip(values, bits):
    return move(
        values,
        lambda y, c, h, l, x: (
            y ^ ("y" in bits),
            c ^ ("c" in bits),
            h ^ ("h" in bits),
            l ^ ("l" in bits),
            x ^ ("x" in bits),
        ),
    )


def swap_ch(values):
    return move(values, lambda y, c, h, l, x: (y, h, c, l, x))


def flip_slot(values, slot):
    return flip(values, ("c" if slot & 4 else "") + ("l" if slot & 2 else "") + ("x" if slot & 1 else ""))


def ring_gather(own):
    half = own.shape[0] // 2
    s1 = flip(own, "x")
    s2 = flip(own, "l")
    s4 = flip(own, "c")
    s3a = flip(s1[:half], "l")
    s3b = flip(s2[half:], "x")
    s5 = flip(s1, "c")
    s6 = flip(s2, "c")
    s7a = flip(s3a, "c")
    s7b = flip(s3b, "c")
    return (
        jnp.concatenate([own, s4]),
        jnp.concatenate([s1, s5]),
        jnp.concatenate([s2, s6]),
        jnp.concatenate([s3a, s3b, s7a, s7b]),
    )


def ring_scatter(part):
    def rounded(values):
        return values.astype(BF)

    q3 = rounded(part(3) + flip(rounded(part(7)), "c").astype(F32))
    half = q3.shape[0] // 2
    ra = flip(q3[:half], "x").astype(F32)
    rb = flip(q3[half:], "l").astype(F32)
    q1 = part(1) + flip(rounded(part(5)), "c").astype(F32)
    q2 = part(2) + flip(rounded(part(6)), "c").astype(F32)
    r1a = flip(rounded(q1[:half]), "x").astype(F32)
    r2b = flip(rounded(q2[half:]), "l").astype(F32)
    r1b = flip(rounded(q1[half:] + rb), "x").astype(F32)
    r2a = flip(rounded(q2[:half] + ra), "l").astype(F32)
    q0 = part(0) + flip(rounded(part(4)), "c").astype(F32)
    return q0 + jnp.concatenate([r1a + r2a, r1b + r2b])


def heads_to_rows(blocks):
    got = []
    for place, slot in enumerate(STORED):
        block = blocks[place * ROW : (place + 1) * ROW]
        got.append(block if slot == 0 else flip_slot(block, slot))
    return jnp.concatenate(got, axis=1)


def rows_to_heads(rows):
    width = rows.shape[1] // 8
    got = []
    for place, slot in enumerate(STORED):
        block = rows[:, place * width : (place + 1) * width]
        got.append(block if slot == 0 else flip_slot(block, slot))
    return jnp.concatenate(got, axis=0)


def column_order():
    column = lax.broadcasted_iota(jnp.int32, (768, 768), 1)
    row = lax.broadcasted_iota(jnp.int32, (768, 768), 0)
    part, within = column // 256, column % 256
    turned = ((within % 128) // 32) * 192 + part * 64 + (within // 128) * 32 + within % 32
    plain = (within // 64) * 192 + 128 + within % 64
    return (row == jnp.where(part == 2, plain, turned)).astype(BF)


def head_lanes_turned(head):
    lane = lax.broadcasted_iota(jnp.int32, (1, 256), 1)
    return (lane % 128) // 32 == head


def head_lanes_plain(head):
    lane = lax.broadcasted_iota(jnp.int32, (1, 256), 1)
    return lane // 64 == head


def stored_place(block, me):
    slot = block ^ me
    return (slot & 3) * 2 + (slot >> 2)


def picked_block(step, split, splits):
    half = 4 // splits
    return jnp.where(step < half, split * half + step, 7 - (split * half + step - half))


def attend_kernel(split, splits, me_ref, q_ref, k_ref, v_ref, *refs):
    o_ref, l_ref, s_scr, m_scr, acc_scr, o_scr = refs[-6:]
    heads = 4
    block = picked_block(pl.program_id(0), split, splits)
    me = me_ref[0]
    q = q_ref[...]
    row = lax.broadcasted_iota(jnp.int32, (ROW, ROW), 0)
    col = lax.broadcasted_iota(jnp.int32, (ROW, ROW), 1)

    def lane_max(s):
        return jnp.maximum(
            jnp.maximum(s[:, :128], s[:, 128:256]), jnp.maximum(s[:, 256:384], s[:, 384:])
        )

    def lane_sum(s):
        return (s[:, :128] + s[:, 128:256]) + (s[:, 256:384] + s[:, 384:])

    def start_of(key_block):
        return pl.multiple_of(stored_place(key_block, me) * ROW, ROW)

    for head in range(heads):
        qh = jnp.where(head_lanes_turned(head), q, jnp.zeros_like(q))

        def scores(key_block):
            return lax.dot_general(
                qh, k_ref[pl.ds(start_of(key_block), ROW), :], NT, preferred_element_type=F32
            )

        s = jnp.where(col <= row, scores(block), masked_score)
        s_scr[block] = s
        m_scr[...] = lane_max(s)

        def first_pass(key_block, carry):
            s = scores(key_block)
            s_scr[key_block] = s
            m_scr[...] = jnp.maximum(m_scr[...], lane_max(s))
            return carry

        lax.fori_loop(0, block, first_pass, 0)
        top = jnp.max(m_scr[...], axis=1, keepdims=True)
        m_scr[...] = jnp.zeros_like(m_scr)
        acc_scr[...] = jnp.zeros_like(acc_scr)

        def second_pass(key_block, carry):
            e = jnp.exp2(s_scr[key_block] - top)
            m_scr[...] += lane_sum(e)
            acc_scr[...] += lax.dot_general(
                e.astype(BF), v_ref[pl.ds(start_of(key_block), ROW), :], NN, preferred_element_type=F32
            )
            return carry

        lax.fori_loop(0, block + 1, second_pass, 0)
        total = jnp.sum(m_scr[...], axis=1, keepdims=True)
        part = acc_scr[...] * (1.0 / total)
        if head == 0:
            o_scr[...] = part
        else:
            o_scr[...] = jnp.where(head_lanes_plain(head), part, o_scr[...])
        level = jnp.broadcast_to(top + jnp.log2(total), (ROW, 128))
        l_ref[0, head : head + 1, :] = jnp.transpose(level)[0:1, :]
    o_ref[...] = o_scr[...].astype(BF)


def attend(me, q, k, v, split, splits, earlier):
    length = q.shape[0]
    blocks = length // ROW

    def place(step, me):
        return stored_place(picked_block(step, split, splits), me[0])

    whole = pl.BlockSpec((length, 256), lambda step, me: (0, 0))
    grid = pltpu.PrefetchScalarGridSpec(
        num_scalar_prefetch=1,
        grid=(blocks // splits,),
        in_specs=[pl.BlockSpec((ROW, 256), lambda step, me: (place(step, me), 0)), whole, whole]
        + [pl.BlockSpec(memory_space=pl.ANY)] * len(earlier),
        out_specs=[
            pl.BlockSpec((ROW, 256), lambda step, me: (place(step, me), 0)),
            pl.BlockSpec((1, 4, ROW), lambda step, me: (place(step, me), 0, 0)),
        ],
        scratch_shapes=[
            pltpu.VMEM((blocks, ROW, ROW), F32),
            pltpu.VMEM((ROW, 128), F32),
            pltpu.VMEM((ROW, 256), F32),
            pltpu.VMEM((ROW, 256), F32),
        ],
    )
    return pl.pallas_call(
        lambda *refs: attend_kernel(split, splits, *refs),
        grid_spec=grid,
        out_shape=[
            jax.ShapeDtypeStruct((length, 256), BF),
            jax.ShapeDtypeStruct((blocks, 4, ROW), F32),
        ],
        input_output_aliases={4: 0, 5: 1} if earlier else {},
        compiler_params=pltpu.CompilerParams(vmem_limit_bytes=48 * 2**20),
        cost_estimate=pl.CostEstimate(
            flops=10**11 // splits, bytes_accessed=10 * 2**20, transcendentals=0
        ),
    )(me, q, k, v, *earlier)


KEYS = 256


def attend_back_kernel(split, splits, me_ref, q_ref, k_ref, v_ref, do_ref, o_ref, l_ref, cos_ref, sin_ref, *refs):
    if split == 0:
        dq_in = None
    else:
        dq_in = refs[0]
    dkv_ref, dq_out, qm, dom, delta, dq, dk, dv, km, pt, dst = refs[-11:]
    heads = 4
    me = me_ref[0]
    step = pl.program_id(0)
    blocks = q_ref.shape[0] // ROW

    @pl.when(step == 0)
    def _():
        def prepare(place, carry):
            start = pl.multiple_of(place * ROW, ROW)
            q = q_ref[pl.ds(start, ROW), :]
            do = do_ref[pl.ds(start, ROW), :]
            for head in range(heads):
                rows = slice(head * ROW, (head + 1) * ROW)
                qm[place, rows, :] = jnp.where(head_lanes_turned(head), q, jnp.zeros_like(q))
                dom[place, rows, :] = jnp.where(head_lanes_plain(head), do, jnp.zeros_like(do))
            product = do.astype(F32) * o_ref[pl.ds(start, ROW), :].astype(F32)
            high = product.astype(BF)
            low = (product - high.astype(F32)).astype(BF)
            head_row = lax.broadcasted_iota(jnp.int32, (8, 256), 0)
            lane = lax.broadcasted_iota(jnp.int32, (8, 256), 1)
            pick = jnp.where(lane // 64 == head_row, 1.0, 0.0).astype(BF)
            sums = lax.dot_general(pick, high, NT, preferred_element_type=F32)
            sums += lax.dot_general(pick, low, NT, preferred_element_type=F32)
            delta[place] = sums[:heads, :]
            if split == 0:
                dq[pl.ds(start, ROW), :] = jnp.zeros((ROW, 256), F32)
            else:
                dq[pl.ds(start, ROW), :] = dq_in[pl.ds(start, ROW), :]
            return carry

        lax.fori_loop(0, blocks, prepare, 0)

    key_row = lax.broadcasted_iota(jnp.int32, (KEYS, ROW), 0)
    query_col = lax.broadcasted_iota(jnp.int32, (KEYS, ROW), 1)
    block = picked_block(step, split, splits)
    key_place = stored_place(block, me)

    def key_part(sub, carry):
        inner = pl.multiple_of(sub * KEYS, KEYS)
        table = pl.ds(pl.multiple_of(key_place * ROW + sub * KEYS, KEYS), KEYS)
        k = k_ref[pl.ds(inner, KEYS), :]
        v = v_ref[pl.ds(inner, KEYS), :]
        for head in range(heads):
            km[head] = jnp.where(head_lanes_turned(head), k, jnp.zeros_like(k))
        dk[...] = jnp.zeros_like(dk)
        dv[...] = jnp.zeros_like(dv)

        def query_part(query_block, diagonal):
            place = stored_place(query_block, me)
            rows = pl.ds(pl.multiple_of(place * ROW, ROW), ROW)
            for head in range(heads):
                part = slice(head * ROW, (head + 1) * ROW)
                st = lax.dot_general(k, qm[place, part, :], NT, preferred_element_type=F32)
                dp = lax.dot_general(v, dom[place, part, :], NT, preferred_element_type=F32)
                p = jnp.exp2(st - l_ref[place, head : head + 1, :])
                if diagonal:
                    p = jnp.where(key_row + inner <= query_col, p, 0.0)
                ds = p * (dp - delta[place, head : head + 1, :])
                pt[:, part] = p.astype(BF)
                dst[:, part] = ds.astype(BF)
            dv[...] += lax.dot_general(pt[...], dom[place], NN, preferred_element_type=F32)
            dk[...] += lax.dot_general(dst[...], qm[place], NN, preferred_element_type=F32)
            total = lax.dot_general(dst[:, 0:ROW], km[0], TN, preferred_element_type=F32)
            for head in range(1, heads):
                part = slice(head * ROW, (head + 1) * ROW)
                total += lax.dot_general(dst[:, part], km[head], TN, preferred_element_type=F32)
            dq[rows, :] += total

        query_part(block, True)

        def later(query_block, carry):
            query_part(query_block, False)
            return carry

        lax.fori_loop(block + 1, blocks, later, 0)
        cs = cos_ref[table, :]
        sn = sin_ref[table, :]
        d = dk[...] * (1.0 / LOG2E)
        d1, d2 = d[:, :128], d[:, 128:]
        dkv_ref[pl.ds(inner, KEYS), 0:128] = (d1 * cs + d2 * sn).astype(BF)
        dkv_ref[pl.ds(inner, KEYS), 128:256] = (d2 * cs - d1 * sn).astype(BF)
        dkv_ref[pl.ds(inner, KEYS), 256:512] = dv[...].astype(BF)
        return carry

    lax.fori_loop(0, ROW // KEYS, key_part, 0)

    @pl.when(step == pl.num_programs(0) - 1)
    def _():
        def finish(place, carry):
            rows = pl.ds(pl.multiple_of(place * ROW, ROW), ROW)
            if split < splits - 1:
                dq_out[rows, :] = dq[rows, :]
            else:
                cs = cos_ref[rows, :]
                sn = sin_ref[rows, :]
                d = dq[rows, :] * 0.125
                d1, d2 = d[:, :128], d[:, 128:]
                dq_out[rows, 0:128] = (d1 * cs + d2 * sn).astype(BF)
                dq_out[rows, 128:256] = (d2 * cs - d1 * sn).astype(BF)
            return carry

        lax.fori_loop(0, blocks, finish, 0)


def attend_back(me, q, k, v, do, o, level, cos, sin, split, splits, earlier):
    length = q.shape[0]
    blocks = length // ROW

    def place(step, me):
        return stored_place(picked_block(step, split, splits), me[0])

    def whole(width):
        return pl.BlockSpec((length, width), lambda step, me: (0, 0))

    key_spec = pl.BlockSpec((ROW, 256), lambda step, me: (place(step, me), 0))
    more = []
    if earlier:
        more = [whole(256), pl.BlockSpec(memory_space=pl.ANY)]
    grid = pltpu.PrefetchScalarGridSpec(
        num_scalar_prefetch=1,
        grid=(blocks // splits,),
        in_specs=[
            whole(256),
            key_spec,
            key_spec,
            whole(256),
            whole(256),
            pl.BlockSpec((blocks, 4, ROW), lambda step, me: (0, 0, 0)),
            whole(128),
            whole(128),
        ]
        + more,
        out_specs=[pl.BlockSpec((ROW, 512), lambda step, me: (place(step, me), 0)), whole(256)],
        scratch_shapes=[
            pltpu.VMEM((blocks, 4 * ROW, 256), BF),
            pltpu.VMEM((blocks, 4 * ROW, 256), BF),
            pltpu.VMEM((blocks, 4, ROW), F32),
            pltpu.VMEM((length, 256), F32),
            pltpu.VMEM((KEYS, 256), F32),
            pltpu.VMEM((KEYS, 256), F32),
            pltpu.VMEM((4, KEYS, 256), BF),
            pltpu.VMEM((KEYS, 4 * ROW), BF),
            pltpu.VMEM((KEYS, 4 * ROW), BF),
        ],
    )
    last = split == splits - 1
    return pl.pallas_call(
        lambda *refs: attend_back_kernel(split, splits, *refs),
        grid_spec=grid,
        out_shape=[
            jax.ShapeDtypeStruct((length, 512), BF),
            jax.ShapeDtypeStruct((length, 256), BF if last else F32),
        ],
        input_output_aliases={10: 0} if earlier else {},
        compiler_params=pltpu.CompilerParams(vmem_limit_bytes=62 * 2**20),
        cost_estimate=pl.CostEstimate(
            flops=14 * 10**10 // splits, bytes_accessed=20 * 2**20, transcendentals=0
        ),
    )(me, q, k, v, do, o, level, cos, sin, *earlier)


def ring_shards(
    layer_input,
    cotangent,
    counts,
    positions,
    qkv_master,
    qkv_moment,
    qkv_average,
    out_master,
    out_moment,
    out_average,
    gate_up_master,
    gate_up_moment,
    gate_up_average,
    down_master,
    down_moment,
    down_average,
    gains_master,
    gains_moment,
    gains_average,
):
    seq, tp = lax.axis_index("seq"), lax.axis_index("tp")
    y, c, h = seq >> 1, seq & 1, tp >> 2
    own = c * 4 + (tp & 3)
    me = own.astype(jnp.int32).reshape(1)
    plain_y, plain_c, straight = y == 0, c == 0, c == h

    def features(values):
        half = values.shape[-1] // 2
        return jnp.where(
            plain_y, values, jnp.concatenate([values[..., half:], values[..., :half]], axis=-1)
        )

    def both_cores(mine, other):
        return jnp.where(plain_c, mine, other), jnp.where(plain_c, other, mine)

    def gather_weight(shard):
        r1 = move(shard, lambda y, c, h, l, x: (y, c, 1 - h, l, x) if c == h else None)
        r2a = move(shard, lambda y, c, h, l, x: (y, 1 - c, h, l, x) if c != h else None)
        r2b = move(shard, lambda y, c, h, l, x: (y, h, c, l, x) if c != h else None)
        near = jnp.stack(both_cores(jnp.where(straight, shard, r1), jnp.where(straight, r2a, r2b)))
        far = flip(near, "y")
        return near[0], near[1], far[0], far[1]

    def scatter_grad(near, far):
        total = (near.astype(F32) + flip(far, "y").astype(F32)).astype(BF)
        kept, other = both_cores(total[0], total[1])
        r1 = move(kept, lambda y, c, h, l, x: (y, c, 1 - h, l, x) if c != h else None)
        r2a = move(other, lambda y, c, h, l, x: (y, 1 - c, h, l, x) if c == h else None)
        r2b = move(other, lambda y, c, h, l, x: (y, h, c, l, x) if c != h else None)
        return jnp.where(
            straight,
            kept.astype(F32) + r1.astype(F32),
            r2a.astype(F32) + r2b.astype(F32),
        )

    turn = column_order()
    qkv_shard = jnp.dot(qkv_master.astype(BF), turn, preferred_element_type=F32).astype(BF)
    rows_in = features(swap_ch(layer_input)).astype(F32)
    gains_here = gains_master.astype(BF)
    gains_near = jnp.concatenate(both_cores(gains_here, flip(gains_here, "c")), axis=1)
    gains_all = jnp.concatenate([gains_near, flip(gains_near, "y")], axis=1).astype(F32)
    gain_first, gain_second = gains_all[0], gains_all[1]
    count_here = counts.astype(F32)
    count_pair = both_cores(count_here, flip(count_here, "c"))
    pair_total = count_pair[0] + count_pair[1]
    count_total = pair_total + flip(pair_total, "y")
    seq_weight = 4.0 * jnp.where(h == 0, count_pair[0], count_pair[1])[0] / count_total[0]

    scale_first = rms_scale(rows_in)
    normed_groups = ring_gather((rows_in * scale_first * gain_first).astype(BF))
    qkv_weight = jnp.concatenate(gather_weight(qkv_shard), axis=0)

    place_order = jnp.stack([own ^ slot for slot in STORED])
    positions_here = swap_ch(positions).reshape(8, ROW)[place_order].reshape(8 * ROW)
    frequency = rope_theta ** (
        -((jnp.arange(128, dtype=jnp.int32) % 32).astype(F32) * 2.0) / HD
    )
    angles = positions_here.astype(F32)[:, None] * frequency[None, :]
    cosine, sine = jnp.cos(angles), jnp.sin(angles)

    queries, keys, values = [], [], []
    for place, group in enumerate(normed_groups):
        mixed = jnp.dot(group, qkv_weight, preferred_element_type=F32)
        rows = slice(place * 2 * ROW, (place + 1) * 2 * ROW)
        cs, sn = cosine[rows], sine[rows]

        def turned(u1, u2):
            return jnp.concatenate([u1 * cs - u2 * sn, u2 * cs + u1 * sn], axis=1)

        queries.append((turned(mixed[:, :128], mixed[:, 128:256]) * (0.125 * LOG2E)).astype(BF))
        keys.append(turned(mixed[:, 256:384], mixed[:, 384:512]).astype(BF))
        values.append(mixed[:, 512:].astype(BF))
    queries, keys, values = (jnp.concatenate(v, axis=0) for v in (queries, keys, values))

    gate_up_shard = jnp.concatenate(
        [gate_up_master[m, :, k * 512 : (k + 1) * 512] for m in range(2) for k in range(2)]
        + [out_master],
        axis=0,
    ).astype(BF)
    gate_up_blocks = gather_weight(gate_up_shard)
    gate_up_weight = jnp.concatenate(
        [
            jnp.concatenate([block[k * 512 : (k + 1) * 512] for k in range(4)], axis=1)
            for block in gate_up_blocks
        ],
        axis=0,
    )
    out_heads = jnp.concatenate([block[2048:] for block in gate_up_blocks], axis=1)
    out_weight = jnp.concatenate(ring_gather(out_heads), axis=0)
    down_weight = jnp.concatenate(gather_weight(down_master.astype(BF)), axis=1)

    grad_rows = seq_weight * features(swap_ch(cotangent)).astype(F32)
    grad_out = jnp.concatenate(ring_gather(grad_rows.astype(BF)), axis=0)

    splits = 4
    done = ()
    for split in range(splits):
        done = tuple(attend(me, queries, keys, values, split, splits, done))
    attended, level = done
    attended_own = heads_to_rows(attended)
    residual = rows_in + jnp.dot(attended_own, out_weight, preferred_element_type=F32)
    scale_second = rms_scale(residual)
    second_groups = ring_gather((residual * scale_second * gain_second).astype(BF))
    gate, up, activation = [], [], []
    for group in second_groups:
        g = jnp.dot(group, gate_up_weight[:, :1024], preferred_element_type=F32)
        u = jnp.dot(group, gate_up_weight[:, 1024:], preferred_element_type=F32)
        gate.append(g.astype(BF))
        up.append(u.astype(BF))
        activation.append((g * jax.nn.sigmoid(g) * u).astype(BF))
    gate, up, activation = (jnp.concatenate(v, axis=0) for v in (gate, up, activation))
    normed_second = jnp.concatenate(second_groups, axis=0)

    def rows_of(slot):
        place = STORED.index(slot)
        return slice(place * ROW, (place + 1) * ROW)

    grad_act = lax.dot_general(grad_out, down_weight, NT, preferred_element_type=F32)
    g = gate.astype(F32)
    sigmoid = jax.nn.sigmoid(g)
    grad_gate = (grad_act * up.astype(F32) * sigmoid * (1.0 + g * (1.0 - sigmoid))).astype(BF)
    grad_up = (grad_act * g * sigmoid).astype(BF)
    grad_gate_up = jnp.concatenate([grad_gate, grad_up], axis=1)

    grad_normed_second = ring_scatter(
        lambda slot: lax.dot_general(
            grad_gate_up[rows_of(slot)], gate_up_weight, NT, preferred_element_type=F32
        )
    )
    layer_own = residual + ring_scatter(
        lambda slot: jnp.dot(activation[rows_of(slot)], down_weight, preferred_element_type=F32)
    )
    layer_output = swap_ch(features(layer_own.astype(BF)))

    down_grad = lax.dot_general(activation, grad_out, TN, preferred_element_type=F32).astype(BF)
    down_grad = down_grad.reshape(1024, 4, 512).transpose(1, 0, 2)
    down_grad_own = scatter_grad(down_grad[:2], down_grad[2:])
    gate_up_grad = lax.dot_general(
        normed_second, grad_gate_up, TN, preferred_element_type=F32
    ).astype(BF)
    gate_up_grad = gate_up_grad.reshape(4, 512, 2048)
    gate_up_grad_own = scatter_grad(gate_up_grad[:2], gate_up_grad[2:])

    def norm_grad(values, scale, gain, grad):
        scaled = grad * gain
        back = scale * (
            scaled - values * scale * scale * jnp.mean(scaled * values, axis=-1, keepdims=True)
        )
        return back, jnp.sum(grad * values * scale, axis=0)

    residual_grad, gain_second_part = norm_grad(
        residual, scale_second, gain_second, grad_normed_second
    )
    residual_grad = residual_grad + grad_rows
    residual_low = residual_grad.astype(BF)
    grad_attended = rows_to_heads(
        lax.dot_general(residual_low, out_weight, NT, preferred_element_type=F32).astype(BF)
    )
    out_grad = lax.dot_general(attended_own, residual_low, TN, preferred_element_type=F32).astype(BF)
    out_grad = ring_scatter(
        lambda slot: out_grad[STORED.index(slot) * 256 : (STORED.index(slot) + 1) * 256].astype(F32)
    ).astype(BF)
    out_grad = out_grad.reshape(256, 4, 512).transpose(1, 0, 2)
    out_grad_own = scatter_grad(out_grad[:2], out_grad[2:])

    splits = 2
    earlier = ()
    for split in range(splits):
        grad_kv, grad_q = attend_back(
            me, queries, keys, values, grad_attended, attended, level, cosine, sine, split, splits, earlier
        )
        earlier = (grad_q, grad_kv)
    grad_mixture = jnp.concatenate([grad_q, grad_kv], axis=1)
    grad_normed_first = ring_scatter(
        lambda slot: lax.dot_general(
            grad_mixture[rows_of(slot)], qkv_weight, NT, preferred_element_type=F32
        )
    )
    qkv_grad = lax.dot_general(
        jnp.concatenate(normed_groups, axis=0), grad_mixture, TN, preferred_element_type=F32
    ).astype(BF)
    qkv_grad = lax.dot_general(qkv_grad, turn, NT, preferred_element_type=F32).astype(BF)
    qkv_grad = qkv_grad.reshape(4, 512, 768)
    qkv_grad_own = scatter_grad(qkv_grad[:2], qkv_grad[2:])

    input_back, gain_first_part = norm_grad(rows_in, scale_first, gain_first, grad_normed_first)
    input_grad = swap_ch(features(residual_grad + input_back).astype(BF)).astype(F32)

    gain_grads = jnp.stack([gain_first_part, gain_second_part])
    for bit in "xlch":
        gain_grads = gain_grads + flip(gain_grads, bit)
    gain_grads = gain_grads[:, :1024] + flip(gain_grads[:, 1024:], "y")
    gain_grad_own = jnp.where(plain_c, gain_grads[:, :512], gain_grads[:, 512:])

    rate_unit = float(4 * 8 * ROW) ** (-0.5)
    qkv_new = apply_update(qkv_master, qkv_grad_own, qkv_moment, qkv_average, rate_qkv * rate_unit)
    out_new = apply_update(out_master, out_grad_own, out_moment, out_average, rate_out * rate_unit)
    gate_up_grad_own = jnp.stack([gate_up_grad_own[:, :1024], gate_up_grad_own[:, 1024:]])
    gate_up_new = apply_update(
        gate_up_master, gate_up_grad_own, gate_up_moment, gate_up_average, rate_gate_up * rate_unit
    )
    down_new = apply_update(
        down_master, down_grad_own, down_moment, down_average, rate_down * rate_unit
    )
    gains_new = apply_update(
        gains_master, gain_grad_own, gains_moment, gains_average, rate_gains * rate_unit
    )
    return (layer_output, input_grad) + qkv_new + out_new + gate_up_new + down_new + gains_new


def solution(mesh):
    in_specs = (
        P(("seq", "tp"), None),
        P(("seq", "tp"), None),
        P("seq"),
        P("seq"),
        P("seq", "tp"),
        P("seq", "tp"),
        P("seq", "tp"),
        P("tp", "seq"),
        P("tp", "seq"),
        P("tp", "seq"),
        P(None, "seq", "tp"),
        P(None, "seq", "tp"),
        P(None, "seq", "tp"),
        P("tp", "seq"),
        P("tp", "seq"),
        P("tp", "seq"),
        P(None, "seq"),
        P(None, "seq"),
        P(None, "seq"),
    )
    out_specs = (
        P(("seq", "tp"), None),
        P(("seq", "tp"), None),
        P("seq", "tp"),
        P("seq", "tp"),
        P("seq", "tp"),
        P("seq", "tp"),
        P("tp", "seq"),
        P("tp", "seq"),
        P("tp", "seq"),
        P("tp", "seq"),
        P(None, "seq", "tp"),
        P(None, "seq", "tp"),
        P(None, "seq", "tp"),
        P(None, "seq", "tp"),
        P("tp", "seq"),
        P("tp", "seq"),
        P("tp", "seq"),
        P("tp", "seq"),
        P(None, "seq"),
        P(None, "seq"),
        P(None, "seq"),
        P(None, "seq"),
    )
    body = ring_shards if ring_plan_fits(mesh) else shards
    return jax.shard_map(body, mesh=mesh, in_specs=in_specs, out_specs=out_specs, check_vma=False)
```

```python
import jax
import jax.numpy as jnp
from jax import lax
from jax.experimental import pallas as pl
from jax.experimental.pallas import tpu as pltpu
from jax.sharding import PartitionSpec as P

HD = 64


norm_epsilon = 1e-05
rope_theta = 130000.0
momentum_coef = 0.9
average_coef = 0.5
masked_score = -1e30
rate_qkv = 0.004
rate_out = 2.0
rate_gate_up = 0.03
rate_down = 0.009
rate_gains = 0.1


def rms_scale(values):
    return lax.rsqrt(jnp.mean(values * values, axis=-1, keepdims=True) + norm_epsilon)


def rope_tables(positions, head_size):
    frequency = rope_theta ** (-(jnp.arange(head_size // 2, dtype=jnp.float32) * 2.0) / head_size)
    angles = positions.astype(jnp.float32)[:, None] * frequency[None, :]
    return (jnp.cos(angles)[:, None, :], jnp.sin(angles)[:, None, :])


def rotate(vectors, cosine_table, sine_table):
    half_width = vectors.shape[-1] // 2
    lower_half = vectors[..., :half_width]
    upper_half = vectors[..., half_width:]
    return jnp.concatenate(
        [
            lower_half * cosine_table - upper_half * sine_table,
            upper_half * cosine_table + lower_half * sine_table,
        ],
        axis=-1,
    )


def unrotate(grads, cosine_table, sine_table):
    half_width = grads.shape[-1] // 2
    lower_half = grads[..., :half_width]
    upper_half = grads[..., half_width:]
    return jnp.concatenate(
        [
            lower_half * cosine_table + upper_half * sine_table,
            upper_half * cosine_table - lower_half * sine_table,
        ],
        axis=-1,
    )


def norm_back(values, gain, grad):
    scale_rows = rms_scale(values)
    scaled = grad * gain
    back = scale_rows * (
        scaled
        - values * scale_rows * scale_rows * jnp.mean(scaled * values, axis=-1, keepdims=True)
    )
    return (back, jnp.sum(grad * values * scale_rows, axis=0))


def apply_update(master, grad, moment, average, rate):
    moment_new = momentum_coef * moment + grad
    master_new = master - rate * (grad + momentum_coef * moment_new)
    average_new = average_coef * average + (1.0 - average_coef) * master_new
    return (moment_new, average_new, master_new, master_new.astype(jnp.bfloat16))


def shards(
    layer_input,
    cotangent,
    counts,
    positions,
    qkv_master,
    qkv_moment,
    qkv_average,
    out_master,
    out_moment,
    out_average,
    gate_up_master,
    gate_up_moment,
    gate_up_average,
    down_master,
    down_moment,
    down_average,
    gains_master,
    gains_moment,
    gains_average,
):
    tp_size = lax.axis_size("tp")
    seq_size = lax.axis_size("seq")
    own_rows = layer_input.shape[0]
    length = own_rows * tp_size
    qkv_weight, out_weight, gate_up_weight, down_weight, gain_weight = (
        lax.all_gather(qkv_master.astype(jnp.bfloat16), "seq", axis=0, tiled=True),
        lax.all_gather(out_master.astype(jnp.bfloat16), "seq", axis=1, tiled=True),
        lax.all_gather(gate_up_master.astype(jnp.bfloat16), "seq", axis=1, tiled=True),
        lax.all_gather(down_master.astype(jnp.bfloat16), "seq", axis=1, tiled=True),
        lax.all_gather(gains_master.astype(jnp.bfloat16), "seq", axis=1, tiled=True),
    )
    heads_local = qkv_weight.shape[1] // (3 * HD)
    count_total = lax.psum(counts.astype(jnp.float32), "seq")
    seq_weight = seq_size * counts.astype(jnp.float32)[0] / count_total[0]
    gain_first = gain_weight[0].astype(jnp.float32)
    gain_second = gain_weight[1].astype(jnp.float32)
    gathered = lax.all_gather(layer_input, "tp", axis=0, tiled=True)
    inputs = gathered.astype(jnp.float32)
    normed = (inputs * rms_scale(inputs) * gain_first).astype(jnp.bfloat16)
    mixture = jnp.dot(normed, qkv_weight, preferred_element_type=jnp.float32).reshape(
        length, heads_local, 3, HD
    )
    cosine_table, sine_table = rope_tables(positions, HD)
    queries = rotate(mixture[:, :, 0], cosine_table, sine_table).astype(jnp.bfloat16)
    key_rows = rotate(mixture[:, :, 1], cosine_table, sine_table).astype(jnp.bfloat16)
    value_rows = mixture[:, :, 2].astype(jnp.bfloat16)
    block_rows = min(512, length)
    block_count = length // block_rows
    score_scale = HD ** (-0.5)

    def block_scores(block_index):
        key_end = (block_index + 1) * block_rows
        query_block = queries[block_index * block_rows : key_end]
        row_index = block_index * block_rows + jnp.arange(block_rows)
        allowed = jnp.arange(key_end)[None, :] <= row_index[:, None]
        scores = score_scale * jnp.einsum(
            "qhd,khd->hqk", query_block, key_rows[:key_end], preferred_element_type=jnp.float32
        )
        return (query_block, jnp.where(allowed[None], scores, masked_score))

    attended_list = []
    log_totals = []
    for block_index in range(block_count):
        query_block, scores = block_scores(block_index)
        key_end = (block_index + 1) * block_rows
        row_max = jnp.max(scores, axis=-1, keepdims=True)
        exp_scores = jnp.exp(scores - row_max)
        row_total = jnp.sum(exp_scores, axis=-1, keepdims=True)
        soft_scores = (exp_scores / row_total).astype(jnp.bfloat16)
        attended_block = jnp.einsum(
            "hqk,khd->qhd", soft_scores, value_rows[:key_end], preferred_element_type=jnp.float32
        )
        attended_list.append(attended_block.astype(jnp.bfloat16))
        log_totals.append(row_max + jnp.log(row_total))
    attended = jnp.concatenate(attended_list, axis=0).reshape(length, heads_local * HD)
    own_start = lax.axis_index("tp") * own_rows
    input_own = layer_input.astype(jnp.float32)
    branch = lax.psum(
        jnp.dot(attended, out_weight, preferred_element_type=jnp.float32).astype(jnp.bfloat16), "tp"
    ).astype(jnp.float32)
    residual = inputs + branch
    normed_second = (residual * rms_scale(residual) * gain_second).astype(jnp.bfloat16)
    resid_own = lax.dynamic_slice_in_dim(residual, own_start, own_rows, 0)
    gate_pre = jnp.dot(normed_second, gate_up_weight[0], preferred_element_type=jnp.float32)
    up_pre = jnp.dot(normed_second, gate_up_weight[1], preferred_element_type=jnp.float32)
    gate_sigmoid = jax.nn.sigmoid(gate_pre)
    activation = (gate_pre * gate_sigmoid * up_pre).astype(jnp.bfloat16)
    layer_output = (
        resid_own
        + lax.psum_scatter(
            jnp.dot(activation, down_weight, preferred_element_type=jnp.float32).astype(
                jnp.bfloat16
            ),
            "tp",
            scatter_dimension=0,
            tiled=True,
        ).astype(jnp.float32)
    ).astype(jnp.bfloat16)
    cot_all = lax.all_gather(cotangent, "tp", axis=0, tiled=True)
    grad_out = (seq_weight * cot_all.astype(jnp.float32)).astype(jnp.bfloat16)
    grad_down = jnp.einsum("tf,td->fd", activation, grad_out, preferred_element_type=jnp.float32)
    grad_act = jnp.einsum("td,fd->tf", grad_out, down_weight, preferred_element_type=jnp.float32)
    grad_gate = (grad_act * up_pre * gate_sigmoid * (1.0 + gate_pre * (1.0 - gate_sigmoid))).astype(
        jnp.bfloat16
    )
    grad_up = (grad_act * gate_pre * gate_sigmoid).astype(jnp.bfloat16)
    grad_gate_up = jnp.stack(
        [
            jnp.einsum("td,tf->df", normed_second, grad_gate, preferred_element_type=jnp.float32),
            jnp.einsum("td,tf->df", normed_second, grad_up, preferred_element_type=jnp.float32),
        ]
    )
    grad_normed_second = lax.psum_scatter(
        (
            jnp.einsum(
                "tf,df->td", grad_gate, gate_up_weight[0], preferred_element_type=jnp.float32
            )
            + jnp.einsum(
                "tf,df->td", grad_up, gate_up_weight[1], preferred_element_type=jnp.float32
            )
        ).astype(jnp.bfloat16),
        "tp",
        scatter_dimension=0,
        tiled=True,
    ).astype(jnp.float32)
    grad_resid_own, gain_second_part = norm_back(resid_own, gain_second, grad_normed_second)
    grad_resid_own = grad_resid_own + seq_weight * cotangent.astype(jnp.float32)
    resid_grad_rows = lax.all_gather(grad_resid_own.astype(jnp.bfloat16), "tp", axis=0, tiled=True)
    grad_out_proj = jnp.einsum(
        "tc,td->cd", attended, resid_grad_rows, preferred_element_type=jnp.float32
    )
    grad_attended = (
        jnp.einsum("td,cd->tc", resid_grad_rows, out_weight, preferred_element_type=jnp.float32)
        .astype(jnp.bfloat16)
        .reshape(length, heads_local, HD)
    )
    grad_keys = jnp.zeros((length, heads_local, HD), jnp.float32)
    grad_values = jnp.zeros((length, heads_local, HD), jnp.float32)
    query_grads = []
    for block_index in range(block_count):
        key_end = (block_index + 1) * block_rows
        query_block, scores = block_scores(block_index)
        soft_scores = jnp.exp(scores - log_totals[block_index])
        grad_block = grad_attended[block_index * block_rows : key_end]
        grad_soft = jnp.einsum(
            "qhd,khd->hqk", grad_block, value_rows[:key_end], preferred_element_type=jnp.float32
        )
        row_delta = jnp.sum(soft_scores * grad_soft, axis=-1, keepdims=True)
        grad_scores = (soft_scores * (grad_soft - row_delta)).astype(jnp.bfloat16)
        query_grads.append(
            score_scale
            * jnp.einsum(
                "hqk,khd->qhd", grad_scores, key_rows[:key_end], preferred_element_type=jnp.float32
            )
        )
        grad_keys = grad_keys.at[:key_end].add(
            score_scale
            * jnp.einsum(
                "hqk,qhd->khd", grad_scores, query_block, preferred_element_type=jnp.float32
            )
        )
        grad_values = grad_values.at[:key_end].add(
            jnp.einsum(
                "hqk,qhd->khd",
                soft_scores.astype(jnp.bfloat16),
                grad_block,
                preferred_element_type=jnp.float32,
            )
        )
    grad_queries = jnp.concatenate(query_grads, axis=0)
    grad_mixture = (
        jnp.stack(
            [
                unrotate(grad_queries, cosine_table, sine_table),
                unrotate(grad_keys, cosine_table, sine_table),
                grad_values,
            ],
            axis=2,
        )
        .astype(jnp.bfloat16)
        .reshape(length, heads_local * 3 * HD)
    )
    grad_qkv = jnp.einsum("td,tc->dc", normed, grad_mixture, preferred_element_type=jnp.float32)
    grad_normed_first = lax.psum_scatter(
        jnp.einsum(
            "tc,dc->td", grad_mixture, qkv_weight, preferred_element_type=jnp.float32
        ).astype(jnp.bfloat16),
        "tp",
        scatter_dimension=0,
        tiled=True,
    ).astype(jnp.float32)
    grad_input_own, gain_first_part = norm_back(input_own, gain_first, grad_normed_first)
    input_grad = grad_resid_own + grad_input_own
    gain_grads = lax.psum(jnp.stack([gain_first_part, gain_second_part]), ("seq", "tp"))
    gain_grad_own = lax.dynamic_slice_in_dim(
        gain_grads, lax.axis_index("seq") * gains_master.shape[1], gains_master.shape[1], 1
    )
    qkv_grad_own, out_grad_own, gate_up_grad_own, down_grad_own = (
        lax.psum_scatter(
            grad_qkv.astype(jnp.bfloat16), "seq", scatter_dimension=0, tiled=True
        ).astype(jnp.float32),
        lax.psum_scatter(
            grad_out_proj.astype(jnp.bfloat16), "seq", scatter_dimension=1, tiled=True
        ).astype(jnp.float32),
        lax.psum_scatter(
            grad_gate_up.astype(jnp.bfloat16), "seq", scatter_dimension=1, tiled=True
        ).astype(jnp.float32),
        lax.psum_scatter(
            grad_down.astype(jnp.bfloat16), "seq", scatter_dimension=1, tiled=True
        ).astype(jnp.float32),
    )
    rate_unit = float(length * seq_size) ** (-0.5)
    qkv_new = apply_update(qkv_master, qkv_grad_own, qkv_moment, qkv_average, rate_qkv * rate_unit)
    out_new = apply_update(out_master, out_grad_own, out_moment, out_average, rate_out * rate_unit)
    gate_up_new = apply_update(
        gate_up_master, gate_up_grad_own, gate_up_moment, gate_up_average, rate_gate_up * rate_unit
    )
    down_new = apply_update(
        down_master, down_grad_own, down_moment, down_average, rate_down * rate_unit
    )
    gains_new = apply_update(
        gains_master, gain_grad_own, gains_moment, gains_average, rate_gains * rate_unit
    )
    return (
        layer_output,
        input_grad,
        qkv_new[0],
        qkv_new[1],
        qkv_new[2],
        qkv_new[3],
        out_new[0],
        out_new[1],
        out_new[2],
        out_new[3],
        gate_up_new[0],
        gate_up_new[1],
        gate_up_new[2],
        gate_up_new[3],
        down_new[0],
        down_new[1],
        down_new[2],
        down_new[3],
        gains_new[0],
        gains_new[1],
        gains_new[2],
        gains_new[3],
    )


AXES = ("y", "c", "h", "l", "x")
RING = ("c", "l", "x")
MESH = pl.DeviceIdType.MESH
ROW = 512
BF = jnp.bfloat16
F32 = jnp.float32
LOG2E = 1.4426950408889634
NT = (((1,), (1,)), ((), ()))
NN = (((1,), (0,)), ((), ()))
TN = (((0,), (0,)), ((), ()))


def ring_plan_fits(mesh):
    return mesh.shape["seq"] == 4 and mesh.shape["tp"] == 8


def device_pairs(target):
    pairs = []
    for index in range(32):
        y, c, h, l, x = (index >> 4) & 1, (index >> 3) & 1, (index >> 2) & 1, (index >> 1) & 1, index & 1
        goal = target(y, c, h, l, x)
        if goal is not None:
            y, c, h, l, x = goal
            pairs.append((index, 16 * y + 8 * c + 4 * h + 2 * l + x))
    return pairs


def move(values, target):
    return lax.ppermute(values, AXES, device_pairs(target))


def flip(values, bits):
    return move(
        values,
        lambda y, c, h, l, x: (
            y ^ ("y" in bits),
            c ^ ("c" in bits),
            h ^ ("h" in bits),
            l ^ ("l" in bits),
            x ^ ("x" in bits),
        ),
    )


def swap_ch(values):
    return move(values, lambda y, c, h, l, x: (y, h, c, l, x))


def rounded(values):
    return values.astype(BF)


def ring_position():
    c, l, x = (lax.axis_index(name) for name in RING)
    partners = ({"x": 1 - x}, {"l": 1 - l}, {"c": 1 - c})
    return 4 * c + 2 * l + x, partners


def enter_ring(partners):
    barrier = pltpu.get_barrier_semaphore()
    for partner in partners:
        pl.semaphore_signal(barrier, inc=1, device_id=partner, device_id_type=MESH)
    pl.semaphore_wait(barrier, len(partners))


def rows_at(block, part=None):
    if part is None:
        return pl.ds(pl.multiple_of(block * ROW, ROW), ROW)
    half = ROW // 2
    return pl.ds(pl.multiple_of(block * ROW + part * half, half), half)


def gather_kernel(finish, width, tables, own_ref, w_ref, *refs):
    cs_ref, sn_ref = refs[:2] if tables else (None, None)
    full_ref, *outs = refs[2 if tables else 0 :][:4]
    buf, res, send, recv, own_sem, full_sem, out_sem = refs[-7:]
    me, partners = ring_position()
    to_x, to_l, to_c = partners
    load = pltpu.make_async_copy(own_ref, buf.at[rows_at(me)], own_sem)
    load.start()
    enter_ring(partners)
    load.wait()

    def copy(index, block, part, partner):
        place = buf.at[rows_at(block, part)]
        return pltpu.make_async_remote_copy(
            src_ref=place,
            dst_ref=place,
            send_sem=send.at[index],
            recv_sem=recv.at[index],
            device_id=partner,
            device_id_type=MESH,
        )

    plan = (
        (me, 0, to_x, me ^ 1),
        (me, 1, to_l, me ^ 2),
        (me, None, to_c, me ^ 4),
        (me, 1, to_x, me ^ 1),
        (me, 0, to_l, me ^ 2),
        (me ^ 1, 0, to_l, me ^ 3),
        (me ^ 2, 1, to_x, me ^ 3),
        (me ^ 1, None, to_c, me ^ 5),
        (me ^ 2, None, to_c, me ^ 6),
        (me ^ 3, None, to_c, me ^ 7),
    )

    def start(index):
        block, part, partner, _ = plan[index]
        copy(index, block, part, partner).start()

    def arrived(index):
        _, part, partner, block = plan[index]
        copy(index, block, part, partner).wait_recv()

    for index in range(5):
        start(index)

    def step_body(step, carry):
        block = me ^ ((step >> 1) | ((step & 1) << 2))
        rows = rows_at(block)

        @pl.when(step == 1)
        def _():
            arrived(2)

        @pl.when(step == 2)
        def _():
            arrived(0)
            start(5)
            arrived(1)
            start(6)
            arrived(3)
            start(7)
            arrived(4)
            start(8)

        @pl.when(step == 3)
        def _():
            arrived(7)

        @pl.when(step == 5)
        def _():
            arrived(8)

        @pl.when(step == 6)
        def _():
            arrived(5)
            arrived(6)
            start(9)

        @pl.when(step == 7)
        def _():
            arrived(9)

        pltpu.make_async_copy(buf.at[rows], full_ref.at[rows], full_sem.at[step]).start()
        turn = step & 1

        def out_copy(which, rows):
            return pltpu.make_async_copy(
                res.at[turn, which], outs[which].at[rows], out_sem.at[turn, which]
            )

        @pl.when(step >= 2)
        def _():
            for which in range(3):
                out_copy(which, rows).wait()

        finish(buf, rows, w_ref, cs_ref, sn_ref, res, turn)
        for which in range(3):
            out_copy(which, rows).start()
        return carry

    lax.fori_loop(0, 8, step_body, 0)
    for index in range(10):
        block, part, partner, _ = plan[index]
        copy(index, block, part, partner).wait_send()

    def drain(step, carry):
        rows = rows_at(step)
        pltpu.make_async_copy(buf.at[rows], full_ref.at[rows], full_sem.at[step]).wait()
        return carry

    lax.fori_loop(0, 8, drain, 0)
    for turn in range(2):
        for which in range(3):
            pltpu.make_async_copy(
                res.at[turn, which], outs[which].at[rows_at(0)], out_sem.at[turn, which]
            ).wait()


def feed_forward_finish(buf, rows, w_ref, cs_ref, sn_ref, res, turn):
    def columns(chunk, carry):
        here = pl.multiple_of(chunk * 256, 256)
        block = buf[rows, :]
        g = jnp.dot(block, w_ref[:, pl.ds(here, 256)], preferred_element_type=F32)
        u = jnp.dot(block, w_ref[:, pl.ds(here + 1024, 256)], preferred_element_type=F32)
        res[turn, 0, :, pl.ds(here, 256)] = rounded(g)
        res[turn, 1, :, pl.ds(here, 256)] = rounded(u)
        res[turn, 2, :, pl.ds(here, 256)] = rounded(g * (1.0 / (1.0 + jnp.exp(-g))) * u)
        return carry

    lax.fori_loop(0, 4, columns, 0)


def attention_finish(buf, rows, w_ref, cs_ref, sn_ref, res, turn):
    block = buf[rows, :]
    cs, sn = cs_ref[rows, :], sn_ref[rows, :]
    for which in range(2):
        m = jnp.dot(block, w_ref[:, which * 256 : which * 256 + 256], preferred_element_type=F32)
        if which == 0:
            m = m * (0.125 * LOG2E)
        m1, m2 = m[:, :128], m[:, 128:]
        res[turn, which, :, 0:128] = rounded(m1 * cs - m2 * sn)
        res[turn, which, :, 128:256] = rounded(m2 * cs + m1 * sn)
    res[turn, 2] = rounded(jnp.dot(block, w_ref[:, 512:768], preferred_element_type=F32))


def gather_product(own, weight, width, finish, number, tables=()):
    anywhere = pl.BlockSpec(memory_space=pl.ANY)
    vmem = pl.BlockSpec(memory_space=pltpu.VMEM)
    length, depth = 8 * ROW, own.shape[1]
    return pl.pallas_call(
        lambda *refs: gather_kernel(finish, width, bool(tables), *refs),
        in_specs=[anywhere, vmem] + [vmem] * len(tables),
        out_specs=[anywhere] * 4,
        out_shape=[jax.ShapeDtypeStruct((length, depth), BF)]
        + [jax.ShapeDtypeStruct((length, width), BF)] * 3,
        scratch_shapes=[
            pltpu.VMEM((length, depth), BF),
            pltpu.VMEM((2, 3, ROW, width), BF),
            pltpu.SemaphoreType.DMA((10,)),
            pltpu.SemaphoreType.DMA((10,)),
            pltpu.SemaphoreType.DMA,
            pltpu.SemaphoreType.DMA((8,)),
            pltpu.SemaphoreType.DMA((2, 3)),
        ],
        compiler_params=pltpu.CompilerParams(
            collective_id=number, has_side_effects=True, vmem_limit_bytes=56 * 2**20
        ),
        cost_estimate=pl.CostEstimate(
            flops=80 * 10**9, bytes_accessed=30 * 2**20, transcendentals=0
        ),
    )(own, weight, *tables)


def scatter_kernel(dims, a_ref, w_ref, out_ref, abuf, mine, other, sums, ra, rb, near_x, near_l, send, recv, a_sem):
    me, partners = ring_position()
    to_x, to_l, to_c = partners
    order = (7, 3, 5, 6, 1, 2, 4, 0)

    def load(index):
        return pltpu.make_async_copy(
            a_ref.at[rows_at(me ^ order[index])], abuf.at[index % 2], a_sem.at[index % 2]
        )

    load(0).start()
    enter_ring(partners)

    def copy(index, source, target, partner):
        return pltpu.make_async_remote_copy(
            src_ref=source,
            dst_ref=target,
            send_sem=send.at[index],
            recv_sem=recv.at[index],
            device_id=partner,
            device_id_type=MESH,
        )

    half = ROW // 2
    top, bottom = pl.ds(0, half), pl.ds(half, half)
    copies = [copy(slot, mine.at[slot], other.at[slot], to_c) for slot in range(4)] + [
        copy(4, sums.at[2, top], ra, to_x),
        copy(5, sums.at[2, bottom], rb, to_l),
        copy(6, sums.at[0, top], near_x.at[top], to_x),
        copy(7, sums.at[1, bottom], near_l.at[bottom], to_l),
        copy(8, sums.at[0, bottom], near_x.at[bottom], to_x),
        copy(9, sums.at[1, top], near_l.at[top], to_l),
    ]

    def product(index, store):
        def columns(chunk, carry):
            here = pl.ds(pl.multiple_of(chunk * 256, 256), 256)
            w = w_ref[here, :] if dims == NT else w_ref[:, here]
            store(
                here, lax.dot_general(abuf[index % 2], w, dims, preferred_element_type=F32)
            )
            return carry

        lax.fori_loop(0, 8, columns, 0)

    for index, slot in enumerate(order):
        load(index).wait()
        if index + 1 < 8:
            load(index + 1).start()
        if slot >= 4:

            def store(here, value, slot=slot):
                mine[slot - 4, :, here] = rounded(value)

            product(index, store)
            copies[slot - 4].start()
        elif slot > 0:
            copies[slot].wait_recv()

            def store(here, value, slot=slot):
                sums[slot - 1, :, here] = rounded(value + other[slot, :, here].astype(F32))

            product(index, store)
            if slot == 3:
                copies[4].start()
                copies[5].start()
            if slot == 1:
                copies[6].start()
            if slot == 2:
                copies[7].start()
                copies[5].wait_recv()
                sums[0, bottom, :] = rounded(
                    sums[0, bottom, :].astype(F32) + rb[...].astype(F32)
                )
                copies[8].start()
                copies[4].wait_recv()
                sums[1, top, :] = rounded(sums[1, top, :].astype(F32) + ra[...].astype(F32))
                copies[9].start()
        else:
            copies[0].wait_recv()

            def store(here, value):
                out_ref[:, here] = value + other[0, :, here].astype(F32)

            product(index, store)
    for part, first, second in ((top, 6, 9), (bottom, 8, 7)):
        copies[first].wait_recv()
        copies[second].wait_recv()
        out_ref[part, :] = out_ref[part, :] + (
            near_x[part, :].astype(F32) + near_l[part, :].astype(F32)
        )
    for each in copies:
        each.wait_send()


def product_scatter(a, weight, dims, number):
    anywhere = pl.BlockSpec(memory_space=pl.ANY)
    vmem = pl.BlockSpec(memory_space=pltpu.VMEM)
    depth = a.shape[1]
    width = weight.shape[0] if dims == NT else weight.shape[1]
    return pl.pallas_call(
        lambda *refs: scatter_kernel(dims, *refs),
        in_specs=[anywhere, vmem],
        out_specs=vmem,
        out_shape=jax.ShapeDtypeStruct((ROW, width), F32),
        scratch_shapes=[
            pltpu.VMEM((2, ROW, depth), BF),
            pltpu.VMEM((4, ROW, width), BF),
            pltpu.VMEM((4, ROW, width), BF),
            pltpu.VMEM((3, ROW, width), BF),
            pltpu.VMEM((ROW // 2, width), BF),
            pltpu.VMEM((ROW // 2, width), BF),
            pltpu.VMEM((ROW, width), BF),
            pltpu.VMEM((ROW, width), BF),
            pltpu.SemaphoreType.DMA((10,)),
            pltpu.SemaphoreType.DMA((10,)),
            pltpu.SemaphoreType.DMA((2,)),
        ],
        compiler_params=pltpu.CompilerParams(
            collective_id=number, has_side_effects=True, vmem_limit_bytes=58 * 2**20
        ),
        cost_estimate=pl.CostEstimate(
            flops=80 * 10**9, bytes_accessed=30 * 2**20, transcendentals=0
        ),
    )(a, weight)


def column_order():
    column = lax.broadcasted_iota(jnp.int32, (768, 768), 1)
    row = lax.broadcasted_iota(jnp.int32, (768, 768), 0)
    part, within = column // 256, column % 256
    turned = ((within % 128) // 32) * 192 + part * 64 + (within // 128) * 32 + within % 32
    plain = (within // 64) * 192 + 128 + within % 64
    return (row == jnp.where(part == 2, plain, turned)).astype(BF)


def head_lanes_turned(head):
    lane = lax.broadcasted_iota(jnp.int32, (1, 256), 1)
    return (lane % 128) // 32 == head


def head_lanes_plain(head):
    lane = lax.broadcasted_iota(jnp.int32, (1, 256), 1)
    return lane // 64 == head


def picked_block(step, blocks):
    block = jnp.int32(blocks[0])
    for index in range(1, len(blocks)):
        block = jnp.where(step == index, blocks[index], block)
    return block


def mark(*values):
    return sum(value[(0,) * value.ndim].astype(F32) for value in values) * 0.0


def after(values, zero):
    return values + zero.astype(values.dtype)


def held(values, zero):
    if zero is None:
        return values
    return after(lax.optimization_barrier(values), zero)


def attend_kernel(chosen, me_ref, q_ref, k_ref, v_ref, *refs):
    o_ref, l_ref, s_scr, m_scr, acc_scr, o_scr = refs[-6:]
    heads = 4
    block = picked_block(pl.program_id(0), chosen)
    q = q_ref[...]
    row = lax.broadcasted_iota(jnp.int32, (ROW, ROW), 0)
    col = lax.broadcasted_iota(jnp.int32, (ROW, ROW), 1)

    def lane_max(s):
        return jnp.maximum(
            jnp.maximum(s[:, :128], s[:, 128:256]), jnp.maximum(s[:, 256:384], s[:, 384:])
        )

    def lane_sum(s):
        return (s[:, :128] + s[:, 128:256]) + (s[:, 256:384] + s[:, 384:])

    def start_of(key_block):
        return pl.multiple_of(key_block * ROW, ROW)

    for head in range(heads):
        qh = jnp.where(head_lanes_turned(head), q, jnp.zeros_like(q))

        def scores(key_block):
            return lax.dot_general(
                qh, k_ref[pl.ds(start_of(key_block), ROW), :], NT, preferred_element_type=F32
            )

        s = jnp.where(col <= row, scores(block), masked_score)
        s_scr[block] = s
        m_scr[...] = lane_max(s)

        def first_pass(key_block, carry):
            s = scores(key_block)
            s_scr[key_block] = s
            m_scr[...] = jnp.maximum(m_scr[...], lane_max(s))
            return carry

        lax.fori_loop(0, block, first_pass, 0)
        top = jnp.max(m_scr[...], axis=1, keepdims=True)
        m_scr[...] = jnp.zeros_like(m_scr)
        acc_scr[...] = jnp.zeros_like(acc_scr)

        def second_pass(key_block, carry):
            e = jnp.exp2(s_scr[key_block] - top)
            m_scr[...] += lane_sum(e)
            acc_scr[...] += lax.dot_general(
                e.astype(BF), v_ref[pl.ds(start_of(key_block), ROW), :], NN, preferred_element_type=F32
            )
            return carry

        lax.fori_loop(0, block + 1, second_pass, 0)
        total = jnp.sum(m_scr[...], axis=1, keepdims=True)
        part = acc_scr[...] * (1.0 / total)
        if head == 0:
            o_scr[...] = part
        else:
            o_scr[...] = jnp.where(head_lanes_plain(head), part, o_scr[...])
        level = jnp.broadcast_to(top + jnp.log2(total), (ROW, 128))
        l_ref[0, head : head + 1, :] = jnp.transpose(level)[0:1, :]
    o_ref[...] = o_scr[...].astype(BF)


def attend(me, q, k, v, chosen, earlier):
    length = q.shape[0]
    blocks = length // ROW

    def place(step, me):
        return picked_block(step, chosen)

    whole = pl.BlockSpec((length, 256), lambda step, me: (0, 0))
    grid = pltpu.PrefetchScalarGridSpec(
        num_scalar_prefetch=1,
        grid=(len(chosen),),
        in_specs=[pl.BlockSpec((ROW, 256), lambda step, me: (place(step, me), 0)), whole, whole]
        + [pl.BlockSpec(memory_space=pl.ANY)] * len(earlier),
        out_specs=[
            pl.BlockSpec((ROW, 256), lambda step, me: (place(step, me), 0)),
            pl.BlockSpec((1, 4, ROW), lambda step, me: (place(step, me), 0, 0)),
        ],
        scratch_shapes=[
            pltpu.VMEM((blocks, ROW, ROW), F32),
            pltpu.VMEM((ROW, 128), F32),
            pltpu.VMEM((ROW, 256), F32),
            pltpu.VMEM((ROW, 256), F32),
        ],
    )
    return pl.pallas_call(
        lambda *refs: attend_kernel(chosen, *refs),
        grid_spec=grid,
        out_shape=[
            jax.ShapeDtypeStruct((length, 256), BF),
            jax.ShapeDtypeStruct((blocks, 4, ROW), F32),
        ],
        input_output_aliases={4: 0, 5: 1} if earlier else {},
        compiler_params=pltpu.CompilerParams(vmem_limit_bytes=48 * 2**20),
        cost_estimate=pl.CostEstimate(
            flops=14 * 10**9 * len(chosen), bytes_accessed=10 * 2**20, transcendentals=0
        ),
    )(me, q, k, v, *earlier)


KEYS = 256


def attend_back_kernel(chosen, first, last, me_ref, q_ref, k_ref, v_ref, do_ref, l_ref, cos_ref, sin_ref, *refs):
    if first:
        o_ref, dkv_ref, dq_out, delta = refs[:4]
        rest = refs[4:]
    else:
        if last:
            all_cos, all_sin = refs[:2]
            refs = refs[2:]
        delta, dq_in, _, dkv_ref, dq_out = refs[:5]
        rest = refs[5:]
    qm, dom, dq, dk, dv, km, pt, dst = rest
    heads = 4
    step = pl.program_id(0)
    blocks = q_ref.shape[0] // ROW

    @pl.when(step == 0)
    def _():
        def prepare(place, carry):
            start = pl.multiple_of(place * ROW, ROW)
            q = q_ref[pl.ds(start, ROW), :]
            do = do_ref[pl.ds(start, ROW), :]
            for head in range(heads):
                rows = slice(head * ROW, (head + 1) * ROW)
                qm[place, rows, :] = jnp.where(head_lanes_turned(head), q, jnp.zeros_like(q))
                dom[place, rows, :] = jnp.where(head_lanes_plain(head), do, jnp.zeros_like(do))
            if first:
                product = do.astype(F32) * o_ref[pl.ds(start, ROW), :].astype(F32)
                high = product.astype(BF)
                low = (product - high.astype(F32)).astype(BF)
                head_row = lax.broadcasted_iota(jnp.int32, (8, 256), 0)
                lane = lax.broadcasted_iota(jnp.int32, (8, 256), 1)
                pick = jnp.where(lane // 64 == head_row, 1.0, 0.0).astype(BF)
                sums = lax.dot_general(pick, high, NT, preferred_element_type=F32)
                sums += lax.dot_general(pick, low, NT, preferred_element_type=F32)
                delta[place] = sums[:heads, :]
                dq[pl.ds(start, ROW), :] = jnp.zeros((ROW, 256), F32)
            else:
                dq[pl.ds(start, ROW), :] = dq_in[pl.ds(start, ROW), :]
            return carry

        lax.fori_loop(0, blocks, prepare, 0)

    key_row = lax.broadcasted_iota(jnp.int32, (KEYS, ROW), 0)
    query_col = lax.broadcasted_iota(jnp.int32, (KEYS, ROW), 1)
    block = picked_block(step, chosen)

    def key_part(sub, carry):
        inner = pl.multiple_of(sub * KEYS, KEYS)
        k = k_ref[pl.ds(inner, KEYS), :]
        v = v_ref[pl.ds(inner, KEYS), :]
        for head in range(heads):
            km[head] = jnp.where(head_lanes_turned(head), k, jnp.zeros_like(k))
        dk[...] = jnp.zeros_like(dk)
        dv[...] = jnp.zeros_like(dv)

        def query_part(query_block, diagonal):
            place = query_block
            rows = pl.ds(pl.multiple_of(place * ROW, ROW), ROW)
            for head in range(heads):
                part = slice(head * ROW, (head + 1) * ROW)
                st = lax.dot_general(k, qm[place, part, :], NT, preferred_element_type=F32)
                dp = lax.dot_general(v, dom[place, part, :], NT, preferred_element_type=F32)
                p = jnp.exp2(st - l_ref[place, head : head + 1, :])
                if diagonal:
                    p = jnp.where(key_row + inner <= query_col, p, 0.0)
                ds = p * (dp - delta[place, head : head + 1, :])
                pt[:, part] = p.astype(BF)
                dst[:, part] = ds.astype(BF)
            dv[...] += lax.dot_general(pt[...], dom[place], NN, preferred_element_type=F32)
            dk[...] += lax.dot_general(dst[...], qm[place], NN, preferred_element_type=F32)
            total = lax.dot_general(dst[:, 0:ROW], km[0], TN, preferred_element_type=F32)
            for head in range(1, heads):
                part = slice(head * ROW, (head + 1) * ROW)
                total += lax.dot_general(dst[:, part], km[head], TN, preferred_element_type=F32)
            dq[rows, :] += total

        query_part(block, True)

        def later(query_block, carry):
            query_part(query_block, False)
            return carry

        lax.fori_loop(block + 1, blocks, later, 0)
        cs = cos_ref[pl.ds(inner, KEYS), :]
        sn = sin_ref[pl.ds(inner, KEYS), :]
        d = dk[...] * (1.0 / LOG2E)
        d1, d2 = d[:, :128], d[:, 128:]
        dkv_ref[pl.ds(inner, KEYS), 0:128] = (d1 * cs + d2 * sn).astype(BF)
        dkv_ref[pl.ds(inner, KEYS), 128:256] = (d2 * cs - d1 * sn).astype(BF)
        dkv_ref[pl.ds(inner, KEYS), 256:512] = dv[...].astype(BF)
        return carry

    lax.fori_loop(0, ROW // KEYS, key_part, 0)

    @pl.when(step == pl.num_programs(0) - 1)
    def _():
        def finish(place, carry):
            rows = pl.ds(pl.multiple_of(place * ROW, ROW), ROW)
            if not last:
                dq_out[rows, :] = dq[rows, :]
            else:
                cs = all_cos[rows, :]
                sn = all_sin[rows, :]
                d = dq[rows, :] * 0.125
                d1, d2 = d[:, :128], d[:, 128:]
                dq_out[rows, 0:128] = (d1 * cs + d2 * sn).astype(BF)
                dq_out[rows, 128:256] = (d2 * cs - d1 * sn).astype(BF)
            return carry

        lax.fori_loop(0, blocks, finish, 0)


def attend_back(me, q, k, v, do, o, level, cos, sin, chosen, last, earlier):
    length = q.shape[0]
    blocks = length // ROW

    def place(step, me):
        return picked_block(step, chosen)

    def whole(width):
        return pl.BlockSpec((length, width), lambda step, me: (0, 0))

    def key_spec(width):
        return pl.BlockSpec((ROW, width), lambda step, me: (place(step, me), 0))

    head_rows = pl.BlockSpec((blocks, 4, ROW), lambda step, me: (0, 0, 0))
    out_specs = [key_spec(512), whole(256)]
    out_shape = [
        jax.ShapeDtypeStruct((length, 512), BF),
        jax.ShapeDtypeStruct((length, 256), BF if last else F32),
    ]
    if not earlier:
        more = [(whole(256), o)]
        out_specs.append(head_rows)
        out_shape.append(jax.ShapeDtypeStruct((blocks, 4, ROW), F32))
    else:
        delta, dq, dkv = earlier
        more = [(whole(128), cos), (whole(128), sin)] if last else []
        more += [(head_rows, delta), (whole(256), dq), (pl.BlockSpec(memory_space=pl.ANY), dkv)]
    grid = pltpu.PrefetchScalarGridSpec(
        num_scalar_prefetch=1,
        grid=(len(chosen),),
        in_specs=[
            whole(256),
            key_spec(256),
            key_spec(256),
            whole(256),
            head_rows,
            key_spec(128),
            key_spec(128),
        ]
        + [spec for spec, _ in more],
        out_specs=out_specs,
        scratch_shapes=[
            pltpu.VMEM((blocks, 4 * ROW, 256), BF),
            pltpu.VMEM((blocks, 4 * ROW, 256), BF),
            pltpu.VMEM((length, 256), F32),
            pltpu.VMEM((KEYS, 256), F32),
            pltpu.VMEM((KEYS, 256), F32),
            pltpu.VMEM((4, KEYS, 256), BF),
            pltpu.VMEM((KEYS, 4 * ROW), BF),
            pltpu.VMEM((KEYS, 4 * ROW), BF),
        ],
    )
    return pl.pallas_call(
        lambda *refs: attend_back_kernel(chosen, not earlier, last, *refs),
        grid_spec=grid,
        out_shape=out_shape,
        input_output_aliases={7 + len(more): 0} if earlier else {},
        compiler_params=pltpu.CompilerParams(vmem_limit_bytes=62 * 2**20),
        cost_estimate=pl.CostEstimate(
            flops=19 * 10**9 * len(chosen), bytes_accessed=20 * 2**20, transcendentals=0
        ),
    )(me, q, k, v, do, level, cos, sin, *[value for _, value in more])


def ring_shards(
    layer_input,
    cotangent,
    counts,
    positions,
    qkv_master,
    qkv_moment,
    qkv_average,
    out_master,
    out_moment,
    out_average,
    gate_up_master,
    gate_up_moment,
    gate_up_average,
    down_master,
    down_moment,
    down_average,
    gains_master,
    gains_moment,
    gains_average,
):
    y, c, h, l, x = (lax.axis_index(name) for name in AXES)
    own = 4 * c + 2 * l + x
    plain_y, plain_c, straight = y == 0, c == 0, c == h
    idle = jnp.zeros((1,), jnp.int32)

    def features(values):
        half = values.shape[-1] // 2
        return jnp.where(
            plain_y, values, jnp.concatenate([values[..., half:], values[..., :half]], axis=-1)
        )

    def both_cores(mine, other):
        return jnp.where(plain_c, mine, other), jnp.where(plain_c, other, mine)

    def gather_near(shard):
        r1 = move(shard, lambda y, c, h, l, x: (y, c, 1 - h, l, x) if c == h else None)
        r2a = move(shard, lambda y, c, h, l, x: (y, 1 - c, h, l, x) if c != h else None)
        r2b = move(shard, lambda y, c, h, l, x: (y, h, c, l, x) if c != h else None)
        near = jnp.stack(both_cores(jnp.where(straight, shard, r1), jnp.where(straight, r2a, r2b)))
        return near, mark(r1, r2a, r2b)

    def scatter_y(blocks, zero=None):
        return blocks[:2], flip(held(blocks[2:], zero), "y")

    def scatter_ch(near, far):
        total = (near.astype(F32) + far.astype(F32)).astype(BF)
        kept, other = both_cores(total[0], total[1])
        r1 = move(kept, lambda y, c, h, l, x: (y, c, 1 - h, l, x) if c != h else None)
        r2a = move(other, lambda y, c, h, l, x: (y, 1 - c, h, l, x) if c == h else None)
        r2b = move(other, lambda y, c, h, l, x: (y, h, c, l, x) if c != h else None)
        return kept, r1, r2a, r2b

    def scatter_own(kept, r1, r2a, r2b):
        return jnp.where(
            straight,
            kept.astype(F32) + r1.astype(F32),
            r2a.astype(F32) + r2b.astype(F32),
        )

    turn = column_order()
    rows_moved = swap_ch(layer_input)
    rows_in = features(rows_moved).astype(F32)
    gains_here = gains_master.astype(BF)
    gains_near = jnp.concatenate(both_cores(gains_here, flip(gains_here, "c")), axis=1)
    gains_all = jnp.concatenate([gains_near, flip(gains_near, "y")], axis=1).astype(F32)
    gain_first, gain_second = gains_all[0], gains_all[1]
    qkv_shard = jnp.dot(qkv_master.astype(BF), turn, preferred_element_type=F32).astype(BF)
    scale_first = rms_scale(rows_in)
    normed_own = (rows_in * scale_first * gain_first).astype(BF)
    qkv_near, near_there = gather_near(held(qkv_shard, mark(rows_moved)))
    qkv_far = flip(qkv_near, "y")
    grad_moved = swap_ch(held(cotangent, near_there))
    qkv_weight = jnp.concatenate([qkv_near, qkv_far]).reshape(2048, 768)

    frequency = rope_theta ** (
        -((jnp.arange(128, dtype=jnp.int32) % 32).astype(F32) * 2.0) / HD
    )
    angles = swap_ch(positions).astype(F32)[:, None] * frequency[None, :]
    cosine, sine = jnp.cos(angles), jnp.sin(angles)
    normed, queries, keys, values = gather_product(
        normed_own, qkv_weight, 256, attention_finish, 1, (cosine, sine)
    )

    count_here = counts.astype(F32)
    count_pair = both_cores(count_here, flip(count_here, "c"))
    pair_total = count_pair[0] + count_pair[1]
    count_total = pair_total + flip(pair_total, "y")
    seq_weight = 4.0 * jnp.where(h == 0, count_pair[0], count_pair[1])[0] / count_total[0]

    first_there = mark(values)
    grad_rows = seq_weight * features(grad_moved).astype(F32)
    grad_out = lax.all_gather(
        held(grad_rows.astype(BF), first_there), RING, axis=0, tiled=True
    )
    out_near, out_there = gather_near(held(out_master.astype(BF), first_there))
    gate_up_shard = jnp.concatenate([gate_up_master[0], gate_up_master[1]], axis=1).astype(BF)
    gate_up_near, gate_up_there = gather_near(held(gate_up_shard, first_there))
    done = attend(idle, queries, keys, values, (7, 0, 6, 1), ())
    stage = out_there + gate_up_there
    out_far = flip(out_near, "y")
    gate_up_far = flip(gate_up_near, "y")
    down_near, down_there = gather_near(held(down_master.astype(BF), gate_up_there))
    out_heads = jnp.concatenate([out_near, out_far]).transpose(1, 0, 2).reshape(256, 2048)
    out_weight = lax.all_gather(out_heads, RING, axis=0, tiled=True)
    done = attend(idle + stage.astype(jnp.int32), queries, keys, values, (5, 2, 4, 3), tuple(done))
    attended, level = done
    gate_up_weight = jnp.concatenate([gate_up_near, gate_up_far]).reshape(2048, 2048)
    down_far = flip(down_near, "y")
    down_weight = jnp.concatenate([down_near, down_far]).transpose(1, 0, 2).reshape(1024, 2048)

    attended_own = (
        lax.all_to_all(attended.reshape(8, ROW, 256), RING, 0, 0)
        .transpose(1, 0, 2)
        .reshape(ROW, 2048)
    )
    residual = rows_in + jnp.dot(attended_own, out_weight, preferred_element_type=F32)
    scale_second = rms_scale(residual)
    normed_second, gate, up, activation = gather_product(
        (residual * scale_second * gain_second).astype(BF),
        gate_up_weight,
        1024,
        feed_forward_finish,
        2,
    )

    grad_act = lax.dot_general(grad_out, down_weight, NT, preferred_element_type=F32)
    g = gate.astype(F32)
    sigmoid = jax.nn.sigmoid(g)
    grad_gate = (grad_act * up.astype(F32) * sigmoid * (1.0 + g * (1.0 - sigmoid))).astype(BF)
    grad_up = (grad_act * g * sigmoid).astype(BF)
    grad_gate_up = jnp.concatenate([grad_gate, grad_up], axis=1)
    grad_normed_second = product_scatter(grad_gate_up, gate_up_weight, NT, 3)
    gate_up_grad = lax.dot_general(
        normed_second, grad_gate_up, TN, preferred_element_type=F32
    ).astype(BF)
    gate_up_y = scatter_y(gate_up_grad.reshape(4, 512, 2048))
    down_grad = lax.dot_general(activation, grad_out, TN, preferred_element_type=F32).astype(BF)
    down_y = scatter_y(down_grad.reshape(1024, 4, 512).transpose(1, 0, 2))
    layer_own = residual + product_scatter(activation, down_weight, NN, 4)
    layer_output = swap_ch(features(layer_own.astype(BF)))

    def norm_grad(values, scale, gain, grad):
        scaled = grad * gain
        back = scale * (
            scaled - values * scale * scale * jnp.mean(scaled * values, axis=-1, keepdims=True)
        )
        return back, jnp.sum(grad * values * scale, axis=0)

    residual_grad, gain_second_part = norm_grad(
        residual, scale_second, gain_second, grad_normed_second
    )
    residual_grad = residual_grad + grad_rows
    residual_low = residual_grad.astype(BF)
    grad_heads = lax.dot_general(residual_low, out_weight, NT, preferred_element_type=F32)
    grad_attended = lax.all_to_all(
        grad_heads.astype(BF).reshape(ROW, 8, 256).transpose(1, 0, 2), RING, 0, 0
    ).reshape(8 * ROW, 256)

    def back(zero, chosen, last, earlier):
        grad_kv, grad_q, *delta = attend_back(
            idle + zero.astype(jnp.int32),
            queries, keys, values, grad_attended, attended, level, cosine, sine, chosen, last, earlier,
        )
        return (delta[0] if delta else earlier[0], grad_q, grad_kv)

    earlier = back(mark(gate_up_y[1]), (0, 7, 1, 6), False, ())
    gate_up_ch = scatter_ch(*gate_up_y)
    down_ch = scatter_ch(*down_y)
    _, grad_q, grad_kv = back(mark(*gate_up_ch[1:]), (2, 5, 3, 4), True, earlier)

    grad_mixture = jnp.concatenate([grad_q, grad_kv], axis=1)
    grad_normed_first = product_scatter(grad_mixture, qkv_weight, NT, 5)
    qkv_grad = lax.dot_general(normed, grad_mixture, TN, preferred_element_type=F32).astype(BF)
    qkv_grad = lax.dot_general(qkv_grad, turn, NT, preferred_element_type=F32).astype(BF)
    qkv_y = scatter_y(qkv_grad.reshape(4, 512, 768))
    out_grad = lax.dot_general(attended_own, residual_low, TN, preferred_element_type=F32)
    out_grad = lax.psum_scatter(out_grad.astype(BF), RING, scatter_dimension=0, tiled=True)
    out_y = scatter_y(out_grad.reshape(256, 4, 512).transpose(1, 0, 2))
    qkv_grad_own = scatter_own(*scatter_ch(*qkv_y))
    out_grad_own = scatter_own(*scatter_ch(*out_y))
    gate_up_grad_own = scatter_own(*gate_up_ch)
    down_grad_own = scatter_own(*down_ch)

    input_back, gain_first_part = norm_grad(rows_in, scale_first, gain_first, grad_normed_first)
    input_grad = swap_ch(features(residual_grad + input_back).astype(BF)).astype(F32)

    gain_grads = jnp.stack([gain_first_part, gain_second_part])
    for bit in "xlch":
        gain_grads = gain_grads + flip(gain_grads, bit)
    gain_grads = gain_grads[:, :1024] + flip(gain_grads[:, 1024:], "y")
    gain_grad_own = jnp.where(plain_c, gain_grads[:, :512], gain_grads[:, 512:])

    rate_unit = float(4 * 8 * ROW) ** (-0.5)
    qkv_new = apply_update(qkv_master, qkv_grad_own, qkv_moment, qkv_average, rate_qkv * rate_unit)
    out_new = apply_update(out_master, out_grad_own, out_moment, out_average, rate_out * rate_unit)
    gate_up_grad_own = jnp.stack([gate_up_grad_own[:, :1024], gate_up_grad_own[:, 1024:]])
    gate_up_new = apply_update(
        gate_up_master, gate_up_grad_own, gate_up_moment, gate_up_average, rate_gate_up * rate_unit
    )
    down_new = apply_update(
        down_master, down_grad_own, down_moment, down_average, rate_down * rate_unit
    )
    gains_new = apply_update(
        gains_master, gain_grad_own, gains_moment, gains_average, rate_gains * rate_unit
    )
    return (layer_output, input_grad) + qkv_new + out_new + gate_up_new + down_new + gains_new


def solution(mesh):
    in_specs = (
        P(("seq", "tp"), None),
        P(("seq", "tp"), None),
        P("seq"),
        P("seq"),
        P("seq", "tp"),
        P("seq", "tp"),
        P("seq", "tp"),
        P("tp", "seq"),
        P("tp", "seq"),
        P("tp", "seq"),
        P(None, "seq", "tp"),
        P(None, "seq", "tp"),
        P(None, "seq", "tp"),
        P("tp", "seq"),
        P("tp", "seq"),
        P("tp", "seq"),
        P(None, "seq"),
        P(None, "seq"),
        P(None, "seq"),
    )
    out_specs = (
        P(("seq", "tp"), None),
        P(("seq", "tp"), None),
        P("seq", "tp"),
        P("seq", "tp"),
        P("seq", "tp"),
        P("seq", "tp"),
        P("tp", "seq"),
        P("tp", "seq"),
        P("tp", "seq"),
        P("tp", "seq"),
        P(None, "seq", "tp"),
        P(None, "seq", "tp"),
        P(None, "seq", "tp"),
        P(None, "seq", "tp"),
        P("tp", "seq"),
        P("tp", "seq"),
        P("tp", "seq"),
        P("tp", "seq"),
        P(None, "seq"),
        P(None, "seq"),
        P(None, "seq"),
        P(None, "seq"),
    )
    if ring_plan_fits(mesh):
        fine = jax.sharding.Mesh(mesh.devices.reshape(2, 2, 2, 2, 2), AXES)
        names = {"seq": ("y", "c"), "tp": ("h", "l", "x")}

        def finer(spec):
            parts = []
            for entry in spec:
                entry = (entry,) if isinstance(entry, str) else (entry or ())
                parts.append(sum((names[name] for name in entry), ()) or None)
            return P(*parts)

        return jax.shard_map(
            ring_shards,
            mesh=fine,
            in_specs=tuple(finer(spec) for spec in in_specs),
            out_specs=tuple(finer(spec) for spec in out_specs),
            check_vma=False,
        )
    return jax.shard_map(shards, mesh=mesh, in_specs=in_specs, out_specs=out_specs, check_vma=False)
```

```python
import jax
import jax.numpy as jnp
from jax import lax
from jax.experimental import pallas as pl
from jax.experimental.pallas import tpu as pltpu
from jax.sharding import PartitionSpec as P

HD = 64


norm_epsilon = 1e-05
rope_theta = 130000.0
momentum_coef = 0.9
average_coef = 0.5
masked_score = -1e30
rate_qkv = 0.004
rate_out = 2.0
rate_gate_up = 0.03
rate_down = 0.009
rate_gains = 0.1


def rms_scale(values):
    return lax.rsqrt(jnp.mean(values * values, axis=-1, keepdims=True) + norm_epsilon)


def rope_tables(positions, head_size):
    frequency = rope_theta ** (-(jnp.arange(head_size // 2, dtype=jnp.float32) * 2.0) / head_size)
    angles = positions.astype(jnp.float32)[:, None] * frequency[None, :]
    return (jnp.cos(angles)[:, None, :], jnp.sin(angles)[:, None, :])


def rotate(vectors, cosine_table, sine_table):
    half_width = vectors.shape[-1] // 2
    lower_half = vectors[..., :half_width]
    upper_half = vectors[..., half_width:]
    return jnp.concatenate(
        [
            lower_half * cosine_table - upper_half * sine_table,
            upper_half * cosine_table + lower_half * sine_table,
        ],
        axis=-1,
    )


def unrotate(grads, cosine_table, sine_table):
    half_width = grads.shape[-1] // 2
    lower_half = grads[..., :half_width]
    upper_half = grads[..., half_width:]
    return jnp.concatenate(
        [
            lower_half * cosine_table + upper_half * sine_table,
            upper_half * cosine_table - lower_half * sine_table,
        ],
        axis=-1,
    )


def norm_back(values, gain, grad):
    scale_rows = rms_scale(values)
    scaled = grad * gain
    back = scale_rows * (
        scaled
        - values * scale_rows * scale_rows * jnp.mean(scaled * values, axis=-1, keepdims=True)
    )
    return (back, jnp.sum(grad * values * scale_rows, axis=0))


def apply_update(master, grad, moment, average, rate):
    moment_new = momentum_coef * moment + grad
    master_new = master - rate * (grad + momentum_coef * moment_new)
    average_new = average_coef * average + (1.0 - average_coef) * master_new
    return (moment_new, average_new, master_new, master_new.astype(jnp.bfloat16))


def shards(
    layer_input,
    cotangent,
    counts,
    positions,
    qkv_master,
    qkv_moment,
    qkv_average,
    out_master,
    out_moment,
    out_average,
    gate_up_master,
    gate_up_moment,
    gate_up_average,
    down_master,
    down_moment,
    down_average,
    gains_master,
    gains_moment,
    gains_average,
):
    tp_size = lax.axis_size("tp")
    seq_size = lax.axis_size("seq")
    own_rows = layer_input.shape[0]
    length = own_rows * tp_size
    qkv_weight, out_weight, gate_up_weight, down_weight, gain_weight = (
        lax.all_gather(qkv_master.astype(jnp.bfloat16), "seq", axis=0, tiled=True),
        lax.all_gather(out_master.astype(jnp.bfloat16), "seq", axis=1, tiled=True),
        lax.all_gather(gate_up_master.astype(jnp.bfloat16), "seq", axis=1, tiled=True),
        lax.all_gather(down_master.astype(jnp.bfloat16), "seq", axis=1, tiled=True),
        lax.all_gather(gains_master.astype(jnp.bfloat16), "seq", axis=1, tiled=True),
    )
    heads_local = qkv_weight.shape[1] // (3 * HD)
    count_total = lax.psum(counts.astype(jnp.float32), "seq")
    seq_weight = seq_size * counts.astype(jnp.float32)[0] / count_total[0]
    gain_first = gain_weight[0].astype(jnp.float32)
    gain_second = gain_weight[1].astype(jnp.float32)
    gathered = lax.all_gather(layer_input, "tp", axis=0, tiled=True)
    inputs = gathered.astype(jnp.float32)
    normed = (inputs * rms_scale(inputs) * gain_first).astype(jnp.bfloat16)
    mixture = jnp.dot(normed, qkv_weight, preferred_element_type=jnp.float32).reshape(
        length, heads_local, 3, HD
    )
    cosine_table, sine_table = rope_tables(positions, HD)
    queries = rotate(mixture[:, :, 0], cosine_table, sine_table).astype(jnp.bfloat16)
    key_rows = rotate(mixture[:, :, 1], cosine_table, sine_table).astype(jnp.bfloat16)
    value_rows = mixture[:, :, 2].astype(jnp.bfloat16)
    block_rows = min(512, length)
    block_count = length // block_rows
    score_scale = HD ** (-0.5)

    def block_scores(block_index):
        key_end = (block_index + 1) * block_rows
        query_block = queries[block_index * block_rows : key_end]
        row_index = block_index * block_rows + jnp.arange(block_rows)
        allowed = jnp.arange(key_end)[None, :] <= row_index[:, None]
        scores = score_scale * jnp.einsum(
            "qhd,khd->hqk", query_block, key_rows[:key_end], preferred_element_type=jnp.float32
        )
        return (query_block, jnp.where(allowed[None], scores, masked_score))

    attended_list = []
    log_totals = []
    for block_index in range(block_count):
        query_block, scores = block_scores(block_index)
        key_end = (block_index + 1) * block_rows
        row_max = jnp.max(scores, axis=-1, keepdims=True)
        exp_scores = jnp.exp(scores - row_max)
        row_total = jnp.sum(exp_scores, axis=-1, keepdims=True)
        soft_scores = (exp_scores / row_total).astype(jnp.bfloat16)
        attended_block = jnp.einsum(
            "hqk,khd->qhd", soft_scores, value_rows[:key_end], preferred_element_type=jnp.float32
        )
        attended_list.append(attended_block.astype(jnp.bfloat16))
        log_totals.append(row_max + jnp.log(row_total))
    attended = jnp.concatenate(attended_list, axis=0).reshape(length, heads_local * HD)
    own_start = lax.axis_index("tp") * own_rows
    input_own = layer_input.astype(jnp.float32)
    branch = lax.psum(
        jnp.dot(attended, out_weight, preferred_element_type=jnp.float32).astype(jnp.bfloat16), "tp"
    ).astype(jnp.float32)
    residual = inputs + branch
    normed_second = (residual * rms_scale(residual) * gain_second).astype(jnp.bfloat16)
    resid_own = lax.dynamic_slice_in_dim(residual, own_start, own_rows, 0)
    gate_pre = jnp.dot(normed_second, gate_up_weight[0], preferred_element_type=jnp.float32)
    up_pre = jnp.dot(normed_second, gate_up_weight[1], preferred_element_type=jnp.float32)
    gate_sigmoid = jax.nn.sigmoid(gate_pre)
    activation = (gate_pre * gate_sigmoid * up_pre).astype(jnp.bfloat16)
    layer_output = (
        resid_own
        + lax.psum_scatter(
            jnp.dot(activation, down_weight, preferred_element_type=jnp.float32).astype(
                jnp.bfloat16
            ),
            "tp",
            scatter_dimension=0,
            tiled=True,
        ).astype(jnp.float32)
    ).astype(jnp.bfloat16)
    cot_all = lax.all_gather(cotangent, "tp", axis=0, tiled=True)
    grad_out = (seq_weight * cot_all.astype(jnp.float32)).astype(jnp.bfloat16)
    grad_down = jnp.einsum("tf,td->fd", activation, grad_out, preferred_element_type=jnp.float32)
    grad_act = jnp.einsum("td,fd->tf", grad_out, down_weight, preferred_element_type=jnp.float32)
    grad_gate = (grad_act * up_pre * gate_sigmoid * (1.0 + gate_pre * (1.0 - gate_sigmoid))).astype(
        jnp.bfloat16
    )
    grad_up = (grad_act * gate_pre * gate_sigmoid).astype(jnp.bfloat16)
    grad_gate_up = jnp.stack(
        [
            jnp.einsum("td,tf->df", normed_second, grad_gate, preferred_element_type=jnp.float32),
            jnp.einsum("td,tf->df", normed_second, grad_up, preferred_element_type=jnp.float32),
        ]
    )
    grad_normed_second = lax.psum_scatter(
        (
            jnp.einsum(
                "tf,df->td", grad_gate, gate_up_weight[0], preferred_element_type=jnp.float32
            )
            + jnp.einsum(
                "tf,df->td", grad_up, gate_up_weight[1], preferred_element_type=jnp.float32
            )
        ).astype(jnp.bfloat16),
        "tp",
        scatter_dimension=0,
        tiled=True,
    ).astype(jnp.float32)
    grad_resid_own, gain_second_part = norm_back(resid_own, gain_second, grad_normed_second)
    grad_resid_own = grad_resid_own + seq_weight * cotangent.astype(jnp.float32)
    resid_grad_rows = lax.all_gather(grad_resid_own.astype(jnp.bfloat16), "tp", axis=0, tiled=True)
    grad_out_proj = jnp.einsum(
        "tc,td->cd", attended, resid_grad_rows, preferred_element_type=jnp.float32
    )
    grad_attended = (
        jnp.einsum("td,cd->tc", resid_grad_rows, out_weight, preferred_element_type=jnp.float32)
        .astype(jnp.bfloat16)
        .reshape(length, heads_local, HD)
    )
    grad_keys = jnp.zeros((length, heads_local, HD), jnp.float32)
    grad_values = jnp.zeros((length, heads_local, HD), jnp.float32)
    query_grads = []
    for block_index in range(block_count):
        key_end = (block_index + 1) * block_rows
        query_block, scores = block_scores(block_index)
        soft_scores = jnp.exp(scores - log_totals[block_index])
        grad_block = grad_attended[block_index * block_rows : key_end]
        grad_soft = jnp.einsum(
            "qhd,khd->hqk", grad_block, value_rows[:key_end], preferred_element_type=jnp.float32
        )
        row_delta = jnp.sum(soft_scores * grad_soft, axis=-1, keepdims=True)
        grad_scores = (soft_scores * (grad_soft - row_delta)).astype(jnp.bfloat16)
        query_grads.append(
            score_scale
            * jnp.einsum(
                "hqk,khd->qhd", grad_scores, key_rows[:key_end], preferred_element_type=jnp.float32
            )
        )
        grad_keys = grad_keys.at[:key_end].add(
            score_scale
            * jnp.einsum(
                "hqk,qhd->khd", grad_scores, query_block, preferred_element_type=jnp.float32
            )
        )
        grad_values = grad_values.at[:key_end].add(
            jnp.einsum(
                "hqk,qhd->khd",
                soft_scores.astype(jnp.bfloat16),
                grad_block,
                preferred_element_type=jnp.float32,
            )
        )
    grad_queries = jnp.concatenate(query_grads, axis=0)
    grad_mixture = (
        jnp.stack(
            [
                unrotate(grad_queries, cosine_table, sine_table),
                unrotate(grad_keys, cosine_table, sine_table),
                grad_values,
            ],
            axis=2,
        )
        .astype(jnp.bfloat16)
        .reshape(length, heads_local * 3 * HD)
    )
    grad_qkv = jnp.einsum("td,tc->dc", normed, grad_mixture, preferred_element_type=jnp.float32)
    grad_normed_first = lax.psum_scatter(
        jnp.einsum(
            "tc,dc->td", grad_mixture, qkv_weight, preferred_element_type=jnp.float32
        ).astype(jnp.bfloat16),
        "tp",
        scatter_dimension=0,
        tiled=True,
    ).astype(jnp.float32)
    grad_input_own, gain_first_part = norm_back(input_own, gain_first, grad_normed_first)
    input_grad = grad_resid_own + grad_input_own
    gain_grads = lax.psum(jnp.stack([gain_first_part, gain_second_part]), ("seq", "tp"))
    gain_grad_own = lax.dynamic_slice_in_dim(
        gain_grads, lax.axis_index("seq") * gains_master.shape[1], gains_master.shape[1], 1
    )
    qkv_grad_own, out_grad_own, gate_up_grad_own, down_grad_own = (
        lax.psum_scatter(
            grad_qkv.astype(jnp.bfloat16), "seq", scatter_dimension=0, tiled=True
        ).astype(jnp.float32),
        lax.psum_scatter(
            grad_out_proj.astype(jnp.bfloat16), "seq", scatter_dimension=1, tiled=True
        ).astype(jnp.float32),
        lax.psum_scatter(
            grad_gate_up.astype(jnp.bfloat16), "seq", scatter_dimension=1, tiled=True
        ).astype(jnp.float32),
        lax.psum_scatter(
            grad_down.astype(jnp.bfloat16), "seq", scatter_dimension=1, tiled=True
        ).astype(jnp.float32),
    )
    rate_unit = float(length * seq_size) ** (-0.5)
    qkv_new = apply_update(qkv_master, qkv_grad_own, qkv_moment, qkv_average, rate_qkv * rate_unit)
    out_new = apply_update(out_master, out_grad_own, out_moment, out_average, rate_out * rate_unit)
    gate_up_new = apply_update(
        gate_up_master, gate_up_grad_own, gate_up_moment, gate_up_average, rate_gate_up * rate_unit
    )
    down_new = apply_update(
        down_master, down_grad_own, down_moment, down_average, rate_down * rate_unit
    )
    gains_new = apply_update(
        gains_master, gain_grad_own, gains_moment, gains_average, rate_gains * rate_unit
    )
    return (
        layer_output,
        input_grad,
        qkv_new[0],
        qkv_new[1],
        qkv_new[2],
        qkv_new[3],
        out_new[0],
        out_new[1],
        out_new[2],
        out_new[3],
        gate_up_new[0],
        gate_up_new[1],
        gate_up_new[2],
        gate_up_new[3],
        down_new[0],
        down_new[1],
        down_new[2],
        down_new[3],
        gains_new[0],
        gains_new[1],
        gains_new[2],
        gains_new[3],
    )


AXES = ("y", "c", "h", "l", "x")
RING = ("c", "l", "x")
MESH = pl.DeviceIdType.MESH
ROW = 512
BF = jnp.bfloat16
F32 = jnp.float32
LOG2E = 1.4426950408889634
NT = (((1,), (1,)), ((), ()))
NN = (((1,), (0,)), ((), ()))
TN = (((0,), (0,)), ((), ()))


def ring_plan_fits(mesh):
    return mesh.shape["seq"] == 4 and mesh.shape["tp"] == 8


def device_pairs(target):
    pairs = []
    for index in range(32):
        y, c, h, l, x = (index >> 4) & 1, (index >> 3) & 1, (index >> 2) & 1, (index >> 1) & 1, index & 1
        goal = target(y, c, h, l, x)
        if goal is not None:
            y, c, h, l, x = goal
            pairs.append((index, 16 * y + 8 * c + 4 * h + 2 * l + x))
    return pairs


def move(values, target):
    return lax.ppermute(values, AXES, device_pairs(target))


def flip(values, bits):
    return move(
        values,
        lambda y, c, h, l, x: (
            y ^ ("y" in bits),
            c ^ ("c" in bits),
            h ^ ("h" in bits),
            l ^ ("l" in bits),
            x ^ ("x" in bits),
        ),
    )


def swap_ch(values):
    return move(values, lambda y, c, h, l, x: (y, h, c, l, x))


def rounded(values):
    return values.astype(BF)


def ring_position():
    c, l, x = (lax.axis_index(name) for name in RING)
    partners = ({"x": 1 - x}, {"l": 1 - l}, {"c": 1 - c})
    return 4 * c + 2 * l + x, partners


def enter_ring(partners):
    barrier = pltpu.get_barrier_semaphore()
    for partner in partners:
        pl.semaphore_signal(barrier, inc=1, device_id=partner, device_id_type=MESH)
    pl.semaphore_wait(barrier, len(partners))


def rows_at(block, part=None):
    if part is None:
        return pl.ds(pl.multiple_of(block * ROW, ROW), ROW)
    half = ROW // 2
    return pl.ds(pl.multiple_of(block * ROW + part * half, half), half)


def remote(source, target, sent, received, device):
    return pltpu.make_async_remote_copy(
        src_ref=source,
        dst_ref=target,
        send_sem=sent,
        recv_sem=received,
        device_id=device,
        device_id_type=MESH,
    )


def places():
    y, c, h, l, x = (lax.axis_index(name) for name in AXES)
    return y, c, h, 4 * c + 2 * l + x


def wide_partners():
    y, c, h, _ = places()
    _, (to_x, to_l, to_c) = ring_position()
    mixed = ({**to_x, **to_l}, {**to_x, **to_c}, {**to_l, **to_c}, {**to_x, **to_l, **to_c})
    across = ({"c": 0, "h": 1 - h}, {"c": 1, "h": 1 - h})
    return (to_x, to_l, to_c) + mixed + ({"y": 1 - y},) + across


class Ring:
    def __init__(self, buffer, size, send, recv):
        self.buffer, self.size, self.send, self.recv = buffer, size, send, recv
        me, (to_x, to_l, to_c) = ring_position()
        self.plan = (
            (me, 0, to_x, me ^ 1),
            (me, 1, to_l, me ^ 2),
            (me, None, to_c, me ^ 4),
            (me, 1, to_x, me ^ 1),
            (me, 0, to_l, me ^ 2),
            (me ^ 1, 0, to_l, me ^ 3),
            (me ^ 2, 1, to_x, me ^ 3),
            (me ^ 1, None, to_c, me ^ 5),
            (me ^ 2, None, to_c, me ^ 6),
            (me ^ 3, None, to_c, me ^ 7),
        )

    def copy(self, index, block):
        _, part, partner, _ = self.plan[index]
        size = self.size if part is None else self.size // 2
        first = block * self.size + (size if part == 1 else 0)
        place = self.buffer.at[pl.ds(pl.multiple_of(first, size), size)]
        return remote(place, place, self.send.at[index], self.recv.at[index], partner)

    def start(self, *indices):
        for index in indices:
            self.copy(index, self.plan[index][0]).start()

    def arrived(self, *indices):
        for index in indices:
            self.copy(index, self.plan[index][3]).wait_recv()

    def sent(self):
        for index in range(10):
            self.copy(index, self.plan[index][0]).wait_send()


class Spread:
    def __init__(self, source, target, near, far, keep):
        self.source, self.target, self.near, self.far, self.keep = source, target, near, far, keep
        _, self.c, self.h, _ = places()

    def local(self):
        return pltpu.make_async_copy(self.source, self.target, self.keep)

    def beside(self):
        return remote(self.source, self.target, self.near.at[0], self.near.at[1], {"c": self.h})

    def across(self, core):
        return remote(
            self.source, self.target, self.far.at[2], self.far.at[core], {"c": self.h, "h": 1 - self.h}
        )

    def start(self):
        self.across(self.c).start()

        @pl.when(self.c == self.h)
        def _():
            self.local().start()

        @pl.when(self.c != self.h)
        def _():
            self.beside().start()

    def arrived(self):
        @pl.when(self.c == self.h)
        def _():
            self.local().wait()
            self.beside().wait_recv()

        @pl.when(self.c != self.h)
        def _():
            self.across(0).wait_recv()
            self.across(1).wait_recv()

    def sent(self):
        self.across(self.c).wait_send()

        @pl.when(self.c != self.h)
        def _():
            self.beside().wait_send()


SPREAD_SEMAPHORES = [
    pltpu.SemaphoreType.DMA((4, 2)),
    pltpu.SemaphoreType.DMA((4, 3)),
    pltpu.SemaphoreType.DMA((4,)),
    pltpu.SemaphoreType.DMA((4, 2)),
    pltpu.SemaphoreType.DMA((4, 2)),
]


class First:
    def __init__(self, refs):
        (self.shard, self.grad), (self.whole, self.moved) = refs[:2], refs[2:4]
        self.w, near, far, keep, self.y_send, self.y_recv, self.grad_sems = refs[4:]
        self.y, self.c, self.h, _ = places()
        first = (2 * self.y + self.c) * 512
        self.pieces = [
            Spread(
                self.shard.at[pl.ds(k * 256, 256)],
                self.w.at[pl.ds(pl.multiple_of(first + k * 256, 256), 256)],
                near.at[k],
                far.at[k],
                keep.at[k],
            )
            for k in range(2)
        ]

    def over_y(self, k, core, y):
        first = (2 * y + core) * 512 + k * 256
        place = self.w.at[pl.ds(pl.multiple_of(first, 256), 256)]
        return remote(place, place, self.y_send.at[k, core], self.y_recv.at[k, core], {"y": 1 - self.y})

    def grad_local(self):
        return pltpu.make_async_copy(self.grad, self.moved, self.grad_sems.at[2])

    def grad_remote(self):
        return remote(
            self.grad, self.moved, self.grad_sems.at[0], self.grad_sems.at[1], {"c": self.h, "h": self.c}
        )

    def run(self, ring):
        for piece in self.pieces:
            piece.start()
        for k in range(2):
            self.pieces[k].arrived()
            for core in range(2):
                self.over_y(k, core, self.y).start()
            if k == 0:
                ring.arrived(0)
                ring.start(5)
                ring.arrived(1)
                ring.start(6)

        @pl.when(self.c == self.h)
        def _():
            self.grad_local().start()

        @pl.when(self.c != self.h)
        def _():
            self.grad_remote().start()

        ring.arrived(2, 3)
        ring.start(7)
        ring.arrived(4)
        ring.start(8)
        for k in range(2):
            for core in range(2):
                self.over_y(k, core, 1 - self.y).wait_recv()
        pltpu.make_async_copy(self.w, self.whole, self.grad_sems.at[3]).start()

    def poll(self, step):
        pass

    def finish(self):
        for piece in self.pieces:
            piece.sent()
        for k in range(2):
            for core in range(2):
                self.over_y(k, core, self.y).wait_send()
        pltpu.make_async_copy(self.w, self.whole, self.grad_sems.at[3]).wait()

        @pl.when(self.c == self.h)
        def _():
            self.grad_local().wait()

        @pl.when(self.c != self.h)
        def _():
            self.grad_remote().wait_recv()
            self.grad_remote().wait_send()


class Second:
    def __init__(self, refs):
        self.shard, self.whole = refs[:2]
        near, far, keep, self.y_send, self.y_recv = refs[2:]
        self.y, c, _, _ = places()
        columns = pl.ds(pl.multiple_of((2 * self.y + c) * 512, 512), 512)
        self.pieces = [
            Spread(
                self.shard.at[pl.ds(k * 512, 512)],
                self.whole.at[pl.ds(k * 512, 512), columns],
                near.at[k],
                far.at[k],
                keep.at[k],
            )
            for k in range(2)
        ]

    def over_y(self, k, y):
        place = self.whole.at[pl.ds(k * 512, 512), pl.ds(pl.multiple_of(y * 1024, 1024), 1024)]
        return remote(place, place, self.y_send.at[k, 0], self.y_recv.at[k, 0], {"y": 1 - self.y})

    def run(self, ring):
        for piece in self.pieces:
            piece.start()

    def poll(self, step):
        @pl.when(step == 1)
        def _():
            self.pieces[0].arrived()
            self.over_y(0, self.y).start()

        @pl.when(step == 4)
        def _():
            self.pieces[1].arrived()
            self.over_y(1, self.y).start()

    def finish(self):
        for k in range(2):
            self.pieces[k].sent()
            self.over_y(k, 1 - self.y).wait_recv()
            self.over_y(k, self.y).wait_send()


def gather_kernel(finish, beside, inputs, outputs, *refs):
    own_ref, refs = refs[0], refs[1:]
    given, refs = refs[:inputs], refs[inputs:]
    full_ref, outs, refs = refs[0], refs[1:4], refs[4:]
    extra_outs, refs = refs[:outputs], refs[outputs:]
    buf, res, send, recv, own_sem, full_sem, out_sem = refs[:7]
    me, _ = ring_position()
    load = pltpu.make_async_copy(own_ref, buf.at[rows_at(me)], own_sem)
    load.start()
    enter_ring(wide_partners())
    load.wait()
    ring = Ring(buf, ROW, send, recv)
    ring.start(0, 1, 2, 3, 4)
    early = beside is First
    if early:
        more = First(given[2:] + extra_outs + refs[7:])
        w_ref, tables = more.w, given[:2]
    else:
        more = Second(given[1:] + extra_outs + refs[7:])
        w_ref, tables = given[0], ()
    more.run(ring)

    def step_body(step, carry):
        block = me ^ ((step >> 1) | ((step & 1) << 2))
        rows = rows_at(block)
        if not early:

            @pl.when(step == 1)
            def _():
                ring.arrived(2)

            @pl.when(step == 2)
            def _():
                ring.arrived(0)
                ring.start(5)
                ring.arrived(1)
                ring.start(6)
                ring.arrived(3)
                ring.start(7)
                ring.arrived(4)
                ring.start(8)

        @pl.when(step == 3)
        def _():
            ring.arrived(7)

        @pl.when(step == 5)
        def _():
            ring.arrived(8)

        @pl.when(step == 6)
        def _():
            ring.arrived(5, 6)
            ring.start(9)

        @pl.when(step == 7)
        def _():
            ring.arrived(9)

        more.poll(step)
        pltpu.make_async_copy(buf.at[rows], full_ref.at[rows], full_sem.at[step]).start()
        turn = step & 1

        def out_copy(which, rows):
            return pltpu.make_async_copy(
                res.at[turn, which], outs[which].at[rows], out_sem.at[turn, which]
            )

        @pl.when(step >= 2)
        def _():
            for which in range(3):
                out_copy(which, rows).wait()

        finish(buf, rows, w_ref, tables, res, turn)
        for which in range(3):
            out_copy(which, rows).start()
        return carry

    lax.fori_loop(0, 8, step_body, 0)
    ring.sent()
    more.finish()

    def drain(step, carry):
        rows = rows_at(step)
        pltpu.make_async_copy(buf.at[rows], full_ref.at[rows], full_sem.at[step]).wait()
        return carry

    lax.fori_loop(0, 8, drain, 0)
    for turn in range(2):
        for which in range(3):
            pltpu.make_async_copy(
                res.at[turn, which], outs[which].at[rows_at(0)], out_sem.at[turn, which]
            ).wait()


def feed_forward_finish(buf, rows, w_ref, tables, res, turn):
    def columns(chunk, carry):
        here = pl.multiple_of(chunk * 256, 256)
        block = buf[rows, :]
        g = jnp.dot(block, w_ref[:, pl.ds(here, 256)], preferred_element_type=F32)
        u = jnp.dot(block, w_ref[:, pl.ds(here + 1024, 256)], preferred_element_type=F32)
        res[turn, 0, :, pl.ds(here, 256)] = rounded(g)
        res[turn, 1, :, pl.ds(here, 256)] = rounded(u)
        res[turn, 2, :, pl.ds(here, 256)] = rounded(g * (1.0 / (1.0 + jnp.exp(-g))) * u)
        return carry

    lax.fori_loop(0, 4, columns, 0)


def attention_finish(buf, rows, w_ref, tables, res, turn):
    block = buf[rows, :]
    cs, sn = tables[0][rows, :], tables[1][rows, :]
    for which in range(2):
        m = jnp.dot(block, w_ref[:, which * 256 : which * 256 + 256], preferred_element_type=F32)
        if which == 0:
            m = m * (0.125 * LOG2E)
        m1, m2 = m[:, :128], m[:, 128:]
        res[turn, which, :, 0:128] = rounded(m1 * cs - m2 * sn)
        res[turn, which, :, 128:256] = rounded(m2 * cs + m1 * sn)
    res[turn, 2] = rounded(jnp.dot(block, w_ref[:, 512:768], preferred_element_type=F32))


def gather_product(own, given, anywhere_given, extra_shapes, width, finish, beside, scratch, number):
    anywhere = pl.BlockSpec(memory_space=pl.ANY)
    vmem = pl.BlockSpec(memory_space=pltpu.VMEM)
    length, depth = 8 * ROW, own.shape[1]
    inputs = len(given) + len(anywhere_given)
    return pl.pallas_call(
        lambda *refs: gather_kernel(finish, beside, inputs, len(extra_shapes), *refs),
        in_specs=[anywhere] + [vmem] * len(given) + [anywhere] * len(anywhere_given),
        out_specs=[anywhere] * (4 + len(extra_shapes)),
        out_shape=[jax.ShapeDtypeStruct((length, depth), BF)]
        + [jax.ShapeDtypeStruct((length, width), BF)] * 3
        + [jax.ShapeDtypeStruct(shape, BF) for shape in extra_shapes],
        scratch_shapes=[
            pltpu.VMEM((length, depth), BF),
            pltpu.VMEM((2, 3, ROW, width), BF),
            pltpu.SemaphoreType.DMA((10,)),
            pltpu.SemaphoreType.DMA((10,)),
            pltpu.SemaphoreType.DMA,
            pltpu.SemaphoreType.DMA((8,)),
            pltpu.SemaphoreType.DMA((2, 3)),
        ]
        + scratch,
        compiler_params=pltpu.CompilerParams(
            collective_id=number, has_side_effects=True, vmem_limit_bytes=56 * 2**20
        ),
        cost_estimate=pl.CostEstimate(
            flops=80 * 10**9, bytes_accessed=30 * 2**20, transcendentals=0
        ),
    )(own, *given, *anywhere_given)


def scatter_kernel(dims, a_ref, w_ref, out_ref, abuf, mine, other, sums, ra, rb, near_x, near_l, send, recv, a_sem):
    me, partners = ring_position()
    to_x, to_l, to_c = partners
    order = (7, 3, 5, 6, 1, 2, 4, 0)

    def load(index):
        return pltpu.make_async_copy(
            a_ref.at[rows_at(me ^ order[index])], abuf.at[index % 2], a_sem.at[index % 2]
        )

    load(0).start()
    enter_ring(partners)

    def copy(index, source, target, partner):
        return pltpu.make_async_remote_copy(
            src_ref=source,
            dst_ref=target,
            send_sem=send.at[index],
            recv_sem=recv.at[index],
            device_id=partner,
            device_id_type=MESH,
        )

    half = ROW // 2
    top, bottom = pl.ds(0, half), pl.ds(half, half)
    copies = [copy(slot, mine.at[slot], other.at[slot], to_c) for slot in range(4)] + [
        copy(4, sums.at[2, top], ra, to_x),
        copy(5, sums.at[2, bottom], rb, to_l),
        copy(6, sums.at[0, top], near_x.at[top], to_x),
        copy(7, sums.at[1, bottom], near_l.at[bottom], to_l),
        copy(8, sums.at[0, bottom], near_x.at[bottom], to_x),
        copy(9, sums.at[1, top], near_l.at[top], to_l),
    ]

    def product(index, store):
        def columns(chunk, carry):
            here = pl.ds(pl.multiple_of(chunk * 256, 256), 256)
            w = w_ref[here, :] if dims == NT else w_ref[:, here]
            store(
                here, lax.dot_general(abuf[index % 2], w, dims, preferred_element_type=F32)
            )
            return carry

        lax.fori_loop(0, 8, columns, 0)

    for index, slot in enumerate(order):
        load(index).wait()
        if index + 1 < 8:
            load(index + 1).start()
        if slot >= 4:

            def store(here, value, slot=slot):
                mine[slot - 4, :, here] = rounded(value)

            product(index, store)
            copies[slot - 4].start()
        elif slot > 0:
            copies[slot].wait_recv()

            def store(here, value, slot=slot):
                sums[slot - 1, :, here] = rounded(value + other[slot, :, here].astype(F32))

            product(index, store)
            if slot == 3:
                copies[4].start()
                copies[5].start()
            if slot == 1:
                copies[6].start()
            if slot == 2:
                copies[7].start()
                copies[5].wait_recv()
                sums[0, bottom, :] = rounded(
                    sums[0, bottom, :].astype(F32) + rb[...].astype(F32)
                )
                copies[8].start()
                copies[4].wait_recv()
                sums[1, top, :] = rounded(sums[1, top, :].astype(F32) + ra[...].astype(F32))
                copies[9].start()
        else:
            copies[0].wait_recv()

            def store(here, value):
                out_ref[:, here] = value + other[0, :, here].astype(F32)

            product(index, store)
    for part, first, second in ((top, 6, 9), (bottom, 8, 7)):
        copies[first].wait_recv()
        copies[second].wait_recv()
        out_ref[part, :] = out_ref[part, :] + (
            near_x[part, :].astype(F32) + near_l[part, :].astype(F32)
        )
    for each in copies:
        each.wait_send()


def product_scatter(a, weight, dims, number):
    anywhere = pl.BlockSpec(memory_space=pl.ANY)
    vmem = pl.BlockSpec(memory_space=pltpu.VMEM)
    depth = a.shape[1]
    width = weight.shape[0] if dims == NT else weight.shape[1]
    return pl.pallas_call(
        lambda *refs: scatter_kernel(dims, *refs),
        in_specs=[anywhere, vmem],
        out_specs=vmem,
        out_shape=jax.ShapeDtypeStruct((ROW, width), F32),
        scratch_shapes=[
            pltpu.VMEM((2, ROW, depth), BF),
            pltpu.VMEM((4, ROW, width), BF),
            pltpu.VMEM((4, ROW, width), BF),
            pltpu.VMEM((3, ROW, width), BF),
            pltpu.VMEM((ROW // 2, width), BF),
            pltpu.VMEM((ROW // 2, width), BF),
            pltpu.VMEM((ROW, width), BF),
            pltpu.VMEM((ROW, width), BF),
            pltpu.SemaphoreType.DMA((10,)),
            pltpu.SemaphoreType.DMA((10,)),
            pltpu.SemaphoreType.DMA((2,)),
        ],
        compiler_params=pltpu.CompilerParams(
            collective_id=number, has_side_effects=True, vmem_limit_bytes=58 * 2**20
        ),
        cost_estimate=pl.CostEstimate(
            flops=80 * 10**9, bytes_accessed=30 * 2**20, transcendentals=0
        ),
    )(a, weight)


def column_order():
    column = lax.broadcasted_iota(jnp.int32, (768, 768), 1)
    row = lax.broadcasted_iota(jnp.int32, (768, 768), 0)
    part, within = column // 256, column % 256
    turned = ((within % 128) // 32) * 192 + part * 64 + (within // 128) * 32 + within % 32
    plain = (within // 64) * 192 + 128 + within % 64
    return (row == jnp.where(part == 2, plain, turned)).astype(BF)


def head_lanes_turned(head):
    lane = lax.broadcasted_iota(jnp.int32, (1, 256), 1)
    return (lane % 128) // 32 == head


def head_lanes_plain(head):
    lane = lax.broadcasted_iota(jnp.int32, (1, 256), 1)
    return lane // 64 == head


def picked_block(step, blocks):
    block = jnp.int32(blocks[0])
    for index in range(1, len(blocks)):
        block = jnp.where(step == index, blocks[index], block)
    return block


def mark(*values):
    return sum(value[(0,) * value.ndim].astype(F32) for value in values) * 0.0


def after(values, zero):
    return values + zero.astype(values.dtype)


def held(values, zero):
    if zero is None:
        return values
    return after(lax.optimization_barrier(values), zero)


class Beside:
    def __init__(self, refs):
        self.out_shard, self.gate_up_shard, self.grad_own = refs[:3]
        self.out_full, self.gate_up, self.grad_full, self.rows_own = refs[3:7]
        (
            near,
            far,
            keep,
            self.y_send,
            self.y_recv,
            out_near,
            out_far,
            out_keep,
            self.out_y,
            grad_send,
            grad_recv,
            out_send,
            out_recv,
            self.row_send,
            self.row_recv,
            self.own_sem,
        ) = refs[7:]
        self.y, self.c, self.h, self.me = places()
        _, _, _, l, x = (lax.axis_index(name) for name in AXES)
        s = 2 * self.y + self.c
        self.pieces = [
            Spread(
                self.gate_up_shard.at[pl.ds(k * 128, 128)],
                self.gate_up.at[pl.ds(pl.multiple_of(s * 512 + k * 128, 128), 128)],
                near.at[k],
                far.at[k],
                keep.at[k],
            )
            for k in range(4)
        ]
        heads = 4 * self.h + 2 * l + x
        self.out_piece = Spread(
            self.out_shard,
            self.out_full.at[
                pl.ds(pl.multiple_of(heads * 256, 256), 256), pl.ds(pl.multiple_of(s * 512, 512), 512)
            ],
            out_near,
            out_far,
            out_keep,
        )
        self.grad_ring = Ring(self.grad_full, ROW, grad_send, grad_recv)
        self.out_ring = Ring(self.out_full, 256, out_send, out_recv)

    def over_y(self, k, core, y):
        first = (2 * y + core) * 512 + k * 128
        place = self.gate_up.at[pl.ds(pl.multiple_of(first, 128), 128)]
        return remote(place, place, self.y_send.at[k, core], self.y_recv.at[k, core], {"y": 1 - self.y})

    def out_over_y(self, y):
        place = self.out_full.at[
            pl.ds(pl.multiple_of(self.me * 256, 256), 256), pl.ds(pl.multiple_of(y * 1024, 1024), 1024)
        ]
        return remote(place, place, self.out_y.at[0], self.out_y.at[1], {"y": 1 - self.y})

    def piece_over_y(self, k):
        self.pieces[k].arrived()
        for core in range(2):
            self.over_y(k, core, self.y).start()

    def begin(self):
        own = pltpu.make_async_copy(self.grad_own, self.grad_full.at[rows_at(self.me)], self.own_sem.at[0])
        own.start()
        enter_ring(wide_partners())
        self.out_piece.start()
        self.pieces[0].start()
        own.wait()
        self.grad_ring.start(0, 1, 2, 3, 4)

    def at(self, step):
        def when(number, *actions):
            @pl.when(step == number)
            def _():
                for action in actions:
                    action()

        def out_on():
            self.out_piece.arrived()
            self.out_over_y(self.y).start()

        def out_ring_on():
            self.out_over_y(1 - self.y).wait_recv()
            self.out_ring.start(0, 1, 2, 3, 4)

        def relay(ring):
            ring.arrived(0)
            ring.start(5)
            ring.arrived(1)
            ring.start(6)

        def relay_core(ring):
            ring.arrived(3)
            ring.start(7)
            ring.arrived(4)
            ring.start(8)

        def relay_last(ring):
            ring.arrived(5, 6)
            ring.start(9)

        when(0, self.begin)
        when(3, out_on, self.pieces[1].start)
        when(6, out_ring_on, lambda: relay(self.grad_ring))
        when(9, lambda: self.piece_over_y(0), self.pieces[2].start)
        when(12, lambda: relay_core(self.grad_ring), lambda: relay(self.out_ring))
        when(14, lambda: self.piece_over_y(1), self.pieces[3].start)
        when(18, lambda: relay_core(self.out_ring), lambda: relay_last(self.grad_ring))
        when(20, lambda: self.piece_over_y(2))
        when(25, lambda: relay_last(self.out_ring))
        when(29, lambda: self.piece_over_y(3))

    def row_local(self, block, o_all):
        columns = pl.ds(pl.multiple_of(self.me * 256, 256), 256)
        return pltpu.make_async_copy(
            o_all.at[rows_at(block)], self.rows_own.at[:, columns], self.own_sem.at[1]
        )

    def row_remote(self, block, o_all, sender):
        columns = pl.ds(pl.multiple_of(sender * 256, 256), 256)
        return remote(
            o_all.at[rows_at(block)],
            self.rows_own.at[:, columns],
            self.row_send.at[block],
            self.row_recv.at[sender],
            {"c": block >> 2, "l": (block >> 1) & 1, "x": block & 1},
        )

    def send_rows(self, block, o_all):
        @pl.when(block == self.me)
        def _():
            self.row_local(block, o_all).start()

        @pl.when(block != self.me)
        def _():
            self.row_remote(block, o_all, self.me).start()

    def end(self, o_all):
        self.out_piece.sent()
        self.out_over_y(self.y).wait_send()
        for k in range(4):
            self.pieces[k].sent()
            for core in range(2):
                self.over_y(k, core, self.y).wait_send()
                self.over_y(k, core, 1 - self.y).wait_recv()
        for ring in (self.grad_ring, self.out_ring):
            ring.arrived(2, 7, 8, 9)
            ring.sent()

        def each(block, carry):
            @pl.when(block == self.me)
            def _():
                self.row_local(block, o_all).wait()

            @pl.when(block != self.me)
            def _():
                self.row_remote(block, o_all, self.me).wait_send()
                self.row_remote(block, o_all, block).wait_recv()

            return carry

        lax.fori_loop(0, 8, each, 0)


def attend_kernel(q_ref, k_ref, v_ref, out_shard, gate_up_shard, grad_own, o_ref, l_ref, *refs):
    beside = Beside((out_shard, gate_up_shard, grad_own) + refs[:4] + refs[8:])
    s_scr, m_scr, acc_scr, o_all = refs[4:8]
    head = pl.program_id(1)
    step = pl.program_id(0) * 4 + head
    block = 7 - pl.program_id(0)
    beside.at(step)
    row = lax.broadcasted_iota(jnp.int32, (ROW, ROW), 0)
    col = lax.broadcasted_iota(jnp.int32, (ROW, ROW), 1)

    def lane_max(s):
        return jnp.maximum(
            jnp.maximum(s[:, :128], s[:, 128:256]), jnp.maximum(s[:, 256:384], s[:, 384:])
        )

    def lane_sum(s):
        return (s[:, :128] + s[:, 128:256]) + (s[:, 256:384] + s[:, 384:])

    def keys_at(key_block):
        return pl.ds(pl.multiple_of(key_block * ROW, ROW), ROW)

    q = q_ref[...]
    qh = jnp.where(head_lanes_turned(head), q, jnp.zeros_like(q))

    def scores(key_block):
        return lax.dot_general(qh, k_ref[keys_at(key_block), :], NT, preferred_element_type=F32)

    s = jnp.where(col <= row, scores(block), masked_score)
    s_scr[block] = s
    m_scr[...] = lane_max(s)

    def first_pass(key_block, carry):
        s = scores(key_block)
        s_scr[key_block] = s
        m_scr[...] = jnp.maximum(m_scr[...], lane_max(s))
        return carry

    lax.fori_loop(0, block, first_pass, 0)
    top = jnp.max(m_scr[...], axis=1, keepdims=True)
    m_scr[...] = jnp.zeros_like(m_scr)
    acc_scr[...] = jnp.zeros_like(acc_scr)

    def second_pass(key_block, carry):
        e = jnp.exp2(s_scr[key_block] - top)
        m_scr[...] += lane_sum(e)
        acc_scr[...] += lax.dot_general(
            e.astype(BF), v_ref[keys_at(key_block), :], NN, preferred_element_type=F32
        )
        return carry

    lax.fori_loop(0, block + 1, second_pass, 0)
    total = jnp.sum(m_scr[...], axis=1, keepdims=True)
    part = rounded(acc_scr[...] * (1.0 / total))
    rows = rows_at(block)

    @pl.when(head == 0)
    def _():
        o_all[rows, :] = part

    @pl.when(head > 0)
    def _():
        o_all[rows, :] = jnp.where(head_lanes_plain(head), part, o_all[rows, :])

    level = jnp.transpose(jnp.broadcast_to(top + jnp.log2(total), (ROW, 128)))[0:4, :]
    row4 = lax.broadcasted_iota(jnp.int32, (4, ROW), 0)
    l_ref[0] = jnp.where(row4 == head, level, l_ref[0])

    @pl.when(head == 3)
    def _():
        o_ref[...] = o_all[rows, :]
        beside.send_rows(block, o_all)

    @pl.when(step == 31)
    def _():
        beside.end(o_all)


def attend(q, k, v, out_shard, gate_up_shard, grad_own):
    length = q.shape[0]
    blocks = length // ROW
    whole = pl.BlockSpec((length, 256), lambda i, head: (0, 0))
    anywhere = pl.BlockSpec(memory_space=pl.ANY)
    dma = pltpu.SemaphoreType.DMA
    return pl.pallas_call(
        attend_kernel,
        grid=(blocks, 4),
        in_specs=[pl.BlockSpec((ROW, 256), lambda i, head: (7 - i, 0)), whole, whole] + [anywhere] * 3,
        out_specs=[
            pl.BlockSpec((ROW, 256), lambda i, head: (7 - i, 0)),
            pl.BlockSpec((1, 4, ROW), lambda i, head: (7 - i, 0, 0)),
        ]
        + [anywhere] * 4,
        out_shape=[
            jax.ShapeDtypeStruct((length, 256), BF),
            jax.ShapeDtypeStruct((blocks, 4, ROW), F32),
            jax.ShapeDtypeStruct((2048, 2048), BF),
            jax.ShapeDtypeStruct((2048, 2048), BF),
            jax.ShapeDtypeStruct((length, 2048), BF),
            jax.ShapeDtypeStruct((ROW, 2048), BF),
        ],
        scratch_shapes=[
            pltpu.VMEM((blocks, ROW, ROW), F32),
            pltpu.VMEM((ROW, 128), F32),
            pltpu.VMEM((ROW, 256), F32),
            pltpu.VMEM((length, 256), BF),
        ]
        + SPREAD_SEMAPHORES
        + [dma((2,)), dma((3,)), dma, dma((2,))]
        + [dma((10,))] * 4
        + [dma((8,)), dma((8,)), dma((2,))],
        compiler_params=pltpu.CompilerParams(
            collective_id=6, has_side_effects=True, vmem_limit_bytes=48 * 2**20
        ),
        cost_estimate=pl.CostEstimate(
            flops=14 * 10**9 * blocks, bytes_accessed=10 * 2**20, transcendentals=0
        ),
    )(q, k, v, out_shard, gate_up_shard, grad_own)


KEYS = 256


def attend_back_kernel(chosen, first, last, me_ref, q_ref, k_ref, v_ref, do_ref, l_ref, cos_ref, sin_ref, *refs):
    if first:
        o_ref, dkv_ref, dq_out, delta = refs[:4]
        rest = refs[4:]
    else:
        if last:
            all_cos, all_sin = refs[:2]
            refs = refs[2:]
        delta, dq_in, _, dkv_ref, dq_out = refs[:5]
        rest = refs[5:]
    qm, dom, dq, dk, dv, km, pt, dst = rest
    heads = 4
    step = pl.program_id(0)
    blocks = q_ref.shape[0] // ROW

    @pl.when(step == 0)
    def _():
        def prepare(place, carry):
            start = pl.multiple_of(place * ROW, ROW)
            q = q_ref[pl.ds(start, ROW), :]
            do = do_ref[pl.ds(start, ROW), :]
            for head in range(heads):
                rows = slice(head * ROW, (head + 1) * ROW)
                qm[place, rows, :] = jnp.where(head_lanes_turned(head), q, jnp.zeros_like(q))
                dom[place, rows, :] = jnp.where(head_lanes_plain(head), do, jnp.zeros_like(do))
            if first:
                product = do.astype(F32) * o_ref[pl.ds(start, ROW), :].astype(F32)
                high = product.astype(BF)
                low = (product - high.astype(F32)).astype(BF)
                head_row = lax.broadcasted_iota(jnp.int32, (8, 256), 0)
                lane = lax.broadcasted_iota(jnp.int32, (8, 256), 1)
                pick = jnp.where(lane // 64 == head_row, 1.0, 0.0).astype(BF)
                sums = lax.dot_general(pick, high, NT, preferred_element_type=F32)
                sums += lax.dot_general(pick, low, NT, preferred_element_type=F32)
                delta[place] = sums[:heads, :]
                dq[pl.ds(start, ROW), :] = jnp.zeros((ROW, 256), F32)
            else:
                dq[pl.ds(start, ROW), :] = dq_in[pl.ds(start, ROW), :]
            return carry

        lax.fori_loop(0, blocks, prepare, 0)

    key_row = lax.broadcasted_iota(jnp.int32, (KEYS, ROW), 0)
    query_col = lax.broadcasted_iota(jnp.int32, (KEYS, ROW), 1)
    block = picked_block(step, chosen)

    def key_part(sub, carry):
        inner = pl.multiple_of(sub * KEYS, KEYS)
        k = k_ref[pl.ds(inner, KEYS), :]
        v = v_ref[pl.ds(inner, KEYS), :]
        for head in range(heads):
            km[head] = jnp.where(head_lanes_turned(head), k, jnp.zeros_like(k))
        dk[...] = jnp.zeros_like(dk)
        dv[...] = jnp.zeros_like(dv)

        def query_part(query_block, diagonal):
            place = query_block
            rows = pl.ds(pl.multiple_of(place * ROW, ROW), ROW)
            for head in range(heads):
                part = slice(head * ROW, (head + 1) * ROW)
                st = lax.dot_general(k, qm[place, part, :], NT, preferred_element_type=F32)
                dp = lax.dot_general(v, dom[place, part, :], NT, preferred_element_type=F32)
                p = jnp.exp2(st - l_ref[place, head : head + 1, :])
                if diagonal:
                    p = jnp.where(key_row + inner <= query_col, p, 0.0)
                ds = p * (dp - delta[place, head : head + 1, :])
                pt[:, part] = p.astype(BF)
                dst[:, part] = ds.astype(BF)
            dv[...] += lax.dot_general(pt[...], dom[place], NN, preferred_element_type=F32)
            dk[...] += lax.dot_general(dst[...], qm[place], NN, preferred_element_type=F32)
            total = lax.dot_general(dst[:, 0:ROW], km[0], TN, preferred_element_type=F32)
            for head in range(1, heads):
                part = slice(head * ROW, (head + 1) * ROW)
                total += lax.dot_general(dst[:, part], km[head], TN, preferred_element_type=F32)
            dq[rows, :] += total

        query_part(block, True)

        def later(query_block, carry):
            query_part(query_block, False)
            return carry

        lax.fori_loop(block + 1, blocks, later, 0)
        cs = cos_ref[pl.ds(inner, KEYS), :]
        sn = sin_ref[pl.ds(inner, KEYS), :]
        d = dk[...] * (1.0 / LOG2E)
        d1, d2 = d[:, :128], d[:, 128:]
        dkv_ref[pl.ds(inner, KEYS), 0:128] = (d1 * cs + d2 * sn).astype(BF)
        dkv_ref[pl.ds(inner, KEYS), 128:256] = (d2 * cs - d1 * sn).astype(BF)
        dkv_ref[pl.ds(inner, KEYS), 256:512] = dv[...].astype(BF)
        return carry

    lax.fori_loop(0, ROW // KEYS, key_part, 0)

    @pl.when(step == pl.num_programs(0) - 1)
    def _():
        def finish(place, carry):
            rows = pl.ds(pl.multiple_of(place * ROW, ROW), ROW)
            if not last:
                dq_out[rows, :] = dq[rows, :]
            else:
                cs = all_cos[rows, :]
                sn = all_sin[rows, :]
                d = dq[rows, :] * 0.125
                d1, d2 = d[:, :128], d[:, 128:]
                dq_out[rows, 0:128] = (d1 * cs + d2 * sn).astype(BF)
                dq_out[rows, 128:256] = (d2 * cs - d1 * sn).astype(BF)
            return carry

        lax.fori_loop(0, blocks, finish, 0)


def attend_back(me, q, k, v, do, o, level, cos, sin, chosen, last, earlier):
    length = q.shape[0]
    blocks = length // ROW

    def place(step, me):
        return picked_block(step, chosen)

    def whole(width):
        return pl.BlockSpec((length, width), lambda step, me: (0, 0))

    def key_spec(width):
        return pl.BlockSpec((ROW, width), lambda step, me: (place(step, me), 0))

    head_rows = pl.BlockSpec((blocks, 4, ROW), lambda step, me: (0, 0, 0))
    out_specs = [key_spec(512), whole(256)]
    out_shape = [
        jax.ShapeDtypeStruct((length, 512), BF),
        jax.ShapeDtypeStruct((length, 256), BF if last else F32),
    ]
    if not earlier:
        more = [(whole(256), o)]
        out_specs.append(head_rows)
        out_shape.append(jax.ShapeDtypeStruct((blocks, 4, ROW), F32))
    else:
        delta, dq, dkv = earlier
        more = [(whole(128), cos), (whole(128), sin)] if last else []
        more += [(head_rows, delta), (whole(256), dq), (pl.BlockSpec(memory_space=pl.ANY), dkv)]
    grid = pltpu.PrefetchScalarGridSpec(
        num_scalar_prefetch=1,
        grid=(len(chosen),),
        in_specs=[
            whole(256),
            key_spec(256),
            key_spec(256),
            whole(256),
            head_rows,
            key_spec(128),
            key_spec(128),
        ]
        + [spec for spec, _ in more],
        out_specs=out_specs,
        scratch_shapes=[
            pltpu.VMEM((blocks, 4 * ROW, 256), BF),
            pltpu.VMEM((blocks, 4 * ROW, 256), BF),
            pltpu.VMEM((length, 256), F32),
            pltpu.VMEM((KEYS, 256), F32),
            pltpu.VMEM((KEYS, 256), F32),
            pltpu.VMEM((4, KEYS, 256), BF),
            pltpu.VMEM((KEYS, 4 * ROW), BF),
            pltpu.VMEM((KEYS, 4 * ROW), BF),
        ],
    )
    return pl.pallas_call(
        lambda *refs: attend_back_kernel(chosen, not earlier, last, *refs),
        grid_spec=grid,
        out_shape=out_shape,
        input_output_aliases={7 + len(more): 0} if earlier else {},
        compiler_params=pltpu.CompilerParams(vmem_limit_bytes=62 * 2**20),
        cost_estimate=pl.CostEstimate(
            flops=19 * 10**9 * len(chosen), bytes_accessed=20 * 2**20, transcendentals=0
        ),
    )(me, q, k, v, do, level, cos, sin, *[value for _, value in more])


def ring_shards(
    layer_input,
    cotangent,
    counts,
    positions,
    qkv_master,
    qkv_moment,
    qkv_average,
    out_master,
    out_moment,
    out_average,
    gate_up_master,
    gate_up_moment,
    gate_up_average,
    down_master,
    down_moment,
    down_average,
    gains_master,
    gains_moment,
    gains_average,
):
    y, c, h, l, x = (lax.axis_index(name) for name in AXES)
    own = 4 * c + 2 * l + x
    plain_y, plain_c, straight = y == 0, c == 0, c == h
    idle = jnp.zeros((1,), jnp.int32)

    def both_y(mine, other, axis):
        return jnp.where(
            plain_y,
            jnp.concatenate([mine, other], axis=axis),
            jnp.concatenate([other, mine], axis=axis),
        )

    def both_cores(mine, other):
        return jnp.where(plain_c, mine, other), jnp.where(plain_c, other, mine)

    def scatter_y(blocks, zero=None):
        mine = lax.dynamic_slice_in_dim(blocks, 2 * y, 2, 0)
        return mine, flip(held(lax.dynamic_slice_in_dim(blocks, 2 * (1 - y), 2, 0), zero), "y")

    def scatter_ch(near, far):
        total = (near.astype(F32) + far.astype(F32)).astype(BF)
        kept, other = both_cores(total[0], total[1])
        r1 = move(kept, lambda y, c, h, l, x: (y, c, 1 - h, l, x) if c != h else None)
        r2a = move(other, lambda y, c, h, l, x: (y, 1 - c, h, l, x) if c == h else None)
        r2b = move(other, lambda y, c, h, l, x: (y, h, c, l, x) if c != h else None)
        return kept, r1, r2a, r2b

    def scatter_own(kept, r1, r2a, r2b):
        return jnp.where(
            straight,
            kept.astype(F32) + r1.astype(F32),
            r2a.astype(F32) + r2b.astype(F32),
        )

    turn = column_order()
    rows_in = swap_ch(layer_input).astype(F32)
    gains_here = gains_master.astype(BF)
    gains_near = jnp.concatenate(both_cores(gains_here, flip(gains_here, "c")), axis=1)
    gains_all = both_y(gains_near, flip(gains_near, "y"), 1).astype(F32)
    gain_first, gain_second = gains_all[0], gains_all[1]
    qkv_shard = jnp.dot(qkv_master.astype(BF), turn, preferred_element_type=F32).astype(BF)
    scale_first = rms_scale(rows_in)
    normed_own = (rows_in * scale_first * gain_first).astype(BF)
    frequency = rope_theta ** (
        -((jnp.arange(128, dtype=jnp.int32) % 32).astype(F32) * 2.0) / HD
    )
    positions_here = jnp.where(straight, positions, flip(positions, "c"))
    angles = positions_here.astype(F32)[:, None] * frequency[None, :]
    cosine, sine = jnp.cos(angles), jnp.sin(angles)
    count_here = counts.astype(F32)
    count_total = count_here + flip(count_here, "c")
    count_total = count_total + flip(count_total, "y")
    grad_here = (4.0 * count_here[0] / count_total[0] * cotangent.astype(F32)).astype(BF)
    normed, queries, keys, values, qkv_weight, grad_own = gather_product(
        normed_own,
        (cosine, sine),
        (qkv_shard, grad_here),
        ((2048, 768), (ROW, 2048)),
        256,
        attention_finish,
        First,
        [pltpu.VMEM((2048, 768), BF)] + SPREAD_SEMAPHORES + [pltpu.SemaphoreType.DMA((4,))],
        1,
    )
    gate_up_shard = jnp.concatenate([gate_up_master[0], gate_up_master[1]], axis=1).astype(BF)
    attended, level, out_weight, gate_up_weight, grad_out, attended_own = attend(
        queries, keys, values, out_master.astype(BF), gate_up_shard, grad_own
    )
    grad_rows = grad_own.astype(F32)
    residual = rows_in + jnp.dot(attended_own, out_weight, preferred_element_type=F32)
    scale_second = rms_scale(residual)
    normed_second, gate, up, activation, down_weight = gather_product(
        (residual * scale_second * gain_second).astype(BF),
        (gate_up_weight,),
        (down_master.astype(BF),),
        ((1024, 2048),),
        1024,
        feed_forward_finish,
        Second,
        SPREAD_SEMAPHORES,
        2,
    )

    grad_act = lax.dot_general(grad_out, down_weight, NT, preferred_element_type=F32)
    g = gate.astype(F32)
    sigmoid = jax.nn.sigmoid(g)
    grad_gate = (grad_act * up.astype(F32) * sigmoid * (1.0 + g * (1.0 - sigmoid))).astype(BF)
    grad_up = (grad_act * g * sigmoid).astype(BF)
    grad_gate_up = jnp.concatenate([grad_gate, grad_up], axis=1)
    grad_normed_second = product_scatter(grad_gate_up, gate_up_weight, NT, 3)
    gate_up_grad = lax.dot_general(
        normed_second, grad_gate_up, TN, preferred_element_type=F32
    ).astype(BF)
    gate_up_y = scatter_y(gate_up_grad.reshape(4, 512, 2048))
    down_grad = lax.dot_general(activation, grad_out, TN, preferred_element_type=F32).astype(BF)
    down_y = scatter_y(down_grad.reshape(1024, 4, 512).transpose(1, 0, 2))
    layer_own = residual + product_scatter(activation, down_weight, NN, 4)
    layer_output = swap_ch(layer_own.astype(BF))

    def norm_grad(values, scale, gain, grad):
        scaled = grad * gain
        back = scale * (
            scaled - values * scale * scale * jnp.mean(scaled * values, axis=-1, keepdims=True)
        )
        return back, jnp.sum(grad * values * scale, axis=0)

    residual_grad, gain_second_part = norm_grad(
        residual, scale_second, gain_second, grad_normed_second
    )
    residual_grad = residual_grad + grad_rows
    residual_low = residual_grad.astype(BF)
    grad_heads = lax.dot_general(residual_low, out_weight, NT, preferred_element_type=F32)
    grad_attended = lax.all_to_all(
        grad_heads.astype(BF).reshape(ROW, 8, 256).transpose(1, 0, 2), RING, 0, 0
    ).reshape(8 * ROW, 256)

    def back(zero, chosen, last, earlier):
        grad_kv, grad_q, *delta = attend_back(
            idle + zero.astype(jnp.int32),
            queries, keys, values, grad_attended, attended, level, cosine, sine, chosen, last, earlier,
        )
        return (delta[0] if delta else earlier[0], grad_q, grad_kv)

    earlier = back(mark(gate_up_y[1]), (0, 7, 1, 6), False, ())
    gate_up_ch = scatter_ch(*gate_up_y)
    down_ch = scatter_ch(*down_y)
    _, grad_q, grad_kv = back(mark(*gate_up_ch[1:]), (2, 5, 3, 4), True, earlier)

    grad_mixture = jnp.concatenate([grad_q, grad_kv], axis=1)
    grad_normed_first = product_scatter(grad_mixture, qkv_weight, NT, 5)
    qkv_grad = lax.dot_general(normed, grad_mixture, TN, preferred_element_type=F32).astype(BF)
    qkv_grad = lax.dot_general(qkv_grad, turn, NT, preferred_element_type=F32).astype(BF)
    qkv_y = scatter_y(qkv_grad.reshape(4, 512, 768))
    out_grad = lax.dot_general(attended_own, residual_low, TN, preferred_element_type=F32)
    out_grad = lax.psum_scatter(out_grad.astype(BF), RING, scatter_dimension=0, tiled=True)
    out_y = scatter_y(out_grad.reshape(256, 4, 512).transpose(1, 0, 2))
    qkv_grad_own = scatter_own(*scatter_ch(*qkv_y))
    out_grad_own = scatter_own(*scatter_ch(*out_y))
    gate_up_grad_own = scatter_own(*gate_up_ch)
    down_grad_own = scatter_own(*down_ch)

    input_back, gain_first_part = norm_grad(rows_in, scale_first, gain_first, grad_normed_first)
    input_grad = swap_ch((residual_grad + input_back).astype(BF)).astype(F32)

    gain_grads = jnp.stack([gain_first_part, gain_second_part])
    for bit in "xlchy":
        gain_grads = gain_grads + flip(gain_grads, bit)
    gain_grad_own = lax.dynamic_slice_in_dim(gain_grads, (2 * y + c) * 512, 512, 1)

    rate_unit = float(4 * 8 * ROW) ** (-0.5)
    qkv_new = apply_update(qkv_master, qkv_grad_own, qkv_moment, qkv_average, rate_qkv * rate_unit)
    out_new = apply_update(out_master, out_grad_own, out_moment, out_average, rate_out * rate_unit)
    gate_up_grad_own = jnp.stack([gate_up_grad_own[:, :1024], gate_up_grad_own[:, 1024:]])
    gate_up_new = apply_update(
        gate_up_master, gate_up_grad_own, gate_up_moment, gate_up_average, rate_gate_up * rate_unit
    )
    down_new = apply_update(
        down_master, down_grad_own, down_moment, down_average, rate_down * rate_unit
    )
    gains_new = apply_update(
        gains_master, gain_grad_own, gains_moment, gains_average, rate_gains * rate_unit
    )
    return (layer_output, input_grad) + qkv_new + out_new + gate_up_new + down_new + gains_new


def solution(mesh):
    in_specs = (
        P(("seq", "tp"), None),
        P(("seq", "tp"), None),
        P("seq"),
        P("seq"),
        P("seq", "tp"),
        P("seq", "tp"),
        P("seq", "tp"),
        P("tp", "seq"),
        P("tp", "seq"),
        P("tp", "seq"),
        P(None, "seq", "tp"),
        P(None, "seq", "tp"),
        P(None, "seq", "tp"),
        P("tp", "seq"),
        P("tp", "seq"),
        P("tp", "seq"),
        P(None, "seq"),
        P(None, "seq"),
        P(None, "seq"),
    )
    out_specs = (
        P(("seq", "tp"), None),
        P(("seq", "tp"), None),
        P("seq", "tp"),
        P("seq", "tp"),
        P("seq", "tp"),
        P("seq", "tp"),
        P("tp", "seq"),
        P("tp", "seq"),
        P("tp", "seq"),
        P("tp", "seq"),
        P(None, "seq", "tp"),
        P(None, "seq", "tp"),
        P(None, "seq", "tp"),
        P(None, "seq", "tp"),
        P("tp", "seq"),
        P("tp", "seq"),
        P("tp", "seq"),
        P("tp", "seq"),
        P(None, "seq"),
        P(None, "seq"),
        P(None, "seq"),
        P(None, "seq"),
    )
    if ring_plan_fits(mesh):
        fine = jax.sharding.Mesh(mesh.devices.reshape(2, 2, 2, 2, 2), AXES)
        names = {"seq": ("y", "c"), "tp": ("h", "l", "x")}

        def finer(spec):
            parts = []
            for entry in spec:
                entry = (entry,) if isinstance(entry, str) else (entry or ())
                parts.append(sum((names[name] for name in entry), ()) or None)
            return P(*parts)

        return jax.shard_map(
            ring_shards,
            mesh=fine,
            in_specs=tuple(finer(spec) for spec in in_specs),
            out_specs=tuple(finer(spec) for spec in out_specs),
            check_vma=False,
        )
    return jax.shard_map(shards, mesh=mesh, in_specs=in_specs, out_specs=out_specs, check_vma=False)
```

```python
import jax
import jax.numpy as jnp
from jax import lax
from jax.experimental import pallas as pl
from jax.experimental.pallas import tpu as pltpu
from jax.sharding import PartitionSpec as P

HD = 64


norm_epsilon = 1e-05
rope_theta = 130000.0
momentum_coef = 0.9
average_coef = 0.5
masked_score = -1e30
rate_qkv = 0.004
rate_out = 2.0
rate_gate_up = 0.03
rate_down = 0.009
rate_gains = 0.1


def rms_scale(values):
    return lax.rsqrt(jnp.mean(values * values, axis=-1, keepdims=True) + norm_epsilon)


def rope_tables(positions, head_size):
    frequency = rope_theta ** (-(jnp.arange(head_size // 2, dtype=jnp.float32) * 2.0) / head_size)
    angles = positions.astype(jnp.float32)[:, None] * frequency[None, :]
    return (jnp.cos(angles)[:, None, :], jnp.sin(angles)[:, None, :])


def rotate(vectors, cosine_table, sine_table):
    half_width = vectors.shape[-1] // 2
    lower_half = vectors[..., :half_width]
    upper_half = vectors[..., half_width:]
    return jnp.concatenate(
        [
            lower_half * cosine_table - upper_half * sine_table,
            upper_half * cosine_table + lower_half * sine_table,
        ],
        axis=-1,
    )


def unrotate(grads, cosine_table, sine_table):
    half_width = grads.shape[-1] // 2
    lower_half = grads[..., :half_width]
    upper_half = grads[..., half_width:]
    return jnp.concatenate(
        [
            lower_half * cosine_table + upper_half * sine_table,
            upper_half * cosine_table - lower_half * sine_table,
        ],
        axis=-1,
    )


def norm_back(values, gain, grad):
    scale_rows = rms_scale(values)
    scaled = grad * gain
    back = scale_rows * (
        scaled
        - values * scale_rows * scale_rows * jnp.mean(scaled * values, axis=-1, keepdims=True)
    )
    return (back, jnp.sum(grad * values * scale_rows, axis=0))


def apply_update(master, grad, moment, average, rate):
    moment_new = momentum_coef * moment + grad
    master_new = master - rate * (grad + momentum_coef * moment_new)
    average_new = average_coef * average + (1.0 - average_coef) * master_new
    return (moment_new, average_new, master_new, master_new.astype(jnp.bfloat16))


def shards(
    layer_input,
    cotangent,
    counts,
    positions,
    qkv_master,
    qkv_moment,
    qkv_average,
    out_master,
    out_moment,
    out_average,
    gate_up_master,
    gate_up_moment,
    gate_up_average,
    down_master,
    down_moment,
    down_average,
    gains_master,
    gains_moment,
    gains_average,
):
    tp_size = lax.axis_size("tp")
    seq_size = lax.axis_size("seq")
    own_rows = layer_input.shape[0]
    length = own_rows * tp_size
    qkv_weight, out_weight, gate_up_weight, down_weight, gain_weight = (
        lax.all_gather(qkv_master.astype(jnp.bfloat16), "seq", axis=0, tiled=True),
        lax.all_gather(out_master.astype(jnp.bfloat16), "seq", axis=1, tiled=True),
        lax.all_gather(gate_up_master.astype(jnp.bfloat16), "seq", axis=1, tiled=True),
        lax.all_gather(down_master.astype(jnp.bfloat16), "seq", axis=1, tiled=True),
        lax.all_gather(gains_master.astype(jnp.bfloat16), "seq", axis=1, tiled=True),
    )
    heads_local = qkv_weight.shape[1] // (3 * HD)
    count_total = lax.psum(counts.astype(jnp.float32), "seq")
    seq_weight = seq_size * counts.astype(jnp.float32)[0] / count_total[0]
    gain_first = gain_weight[0].astype(jnp.float32)
    gain_second = gain_weight[1].astype(jnp.float32)
    gathered = lax.all_gather(layer_input, "tp", axis=0, tiled=True)
    inputs = gathered.astype(jnp.float32)
    normed = (inputs * rms_scale(inputs) * gain_first).astype(jnp.bfloat16)
    mixture = jnp.dot(normed, qkv_weight, preferred_element_type=jnp.float32).reshape(
        length, heads_local, 3, HD
    )
    cosine_table, sine_table = rope_tables(positions, HD)
    queries = rotate(mixture[:, :, 0], cosine_table, sine_table).astype(jnp.bfloat16)
    key_rows = rotate(mixture[:, :, 1], cosine_table, sine_table).astype(jnp.bfloat16)
    value_rows = mixture[:, :, 2].astype(jnp.bfloat16)
    block_rows = min(512, length)
    block_count = length // block_rows
    score_scale = HD ** (-0.5)

    def block_scores(block_index):
        key_end = (block_index + 1) * block_rows
        query_block = queries[block_index * block_rows : key_end]
        row_index = block_index * block_rows + jnp.arange(block_rows)
        allowed = jnp.arange(key_end)[None, :] <= row_index[:, None]
        scores = score_scale * jnp.einsum(
            "qhd,khd->hqk", query_block, key_rows[:key_end], preferred_element_type=jnp.float32
        )
        return (query_block, jnp.where(allowed[None], scores, masked_score))

    attended_list = []
    log_totals = []
    for block_index in range(block_count):
        query_block, scores = block_scores(block_index)
        key_end = (block_index + 1) * block_rows
        row_max = jnp.max(scores, axis=-1, keepdims=True)
        exp_scores = jnp.exp(scores - row_max)
        row_total = jnp.sum(exp_scores, axis=-1, keepdims=True)
        soft_scores = (exp_scores / row_total).astype(jnp.bfloat16)
        attended_block = jnp.einsum(
            "hqk,khd->qhd", soft_scores, value_rows[:key_end], preferred_element_type=jnp.float32
        )
        attended_list.append(attended_block.astype(jnp.bfloat16))
        log_totals.append(row_max + jnp.log(row_total))
    attended = jnp.concatenate(attended_list, axis=0).reshape(length, heads_local * HD)
    own_start = lax.axis_index("tp") * own_rows
    input_own = layer_input.astype(jnp.float32)
    branch = lax.psum(
        jnp.dot(attended, out_weight, preferred_element_type=jnp.float32).astype(jnp.bfloat16), "tp"
    ).astype(jnp.float32)
    residual = inputs + branch
    normed_second = (residual * rms_scale(residual) * gain_second).astype(jnp.bfloat16)
    resid_own = lax.dynamic_slice_in_dim(residual, own_start, own_rows, 0)
    gate_pre = jnp.dot(normed_second, gate_up_weight[0], preferred_element_type=jnp.float32)
    up_pre = jnp.dot(normed_second, gate_up_weight[1], preferred_element_type=jnp.float32)
    gate_sigmoid = jax.nn.sigmoid(gate_pre)
    activation = (gate_pre * gate_sigmoid * up_pre).astype(jnp.bfloat16)
    layer_output = (
        resid_own
        + lax.psum_scatter(
            jnp.dot(activation, down_weight, preferred_element_type=jnp.float32).astype(
                jnp.bfloat16
            ),
            "tp",
            scatter_dimension=0,
            tiled=True,
        ).astype(jnp.float32)
    ).astype(jnp.bfloat16)
    cot_all = lax.all_gather(cotangent, "tp", axis=0, tiled=True)
    grad_out = (seq_weight * cot_all.astype(jnp.float32)).astype(jnp.bfloat16)
    grad_down = jnp.einsum("tf,td->fd", activation, grad_out, preferred_element_type=jnp.float32)
    grad_act = jnp.einsum("td,fd->tf", grad_out, down_weight, preferred_element_type=jnp.float32)
    grad_gate = (grad_act * up_pre * gate_sigmoid * (1.0 + gate_pre * (1.0 - gate_sigmoid))).astype(
        jnp.bfloat16
    )
    grad_up = (grad_act * gate_pre * gate_sigmoid).astype(jnp.bfloat16)
    grad_gate_up = jnp.stack(
        [
            jnp.einsum("td,tf->df", normed_second, grad_gate, preferred_element_type=jnp.float32),
            jnp.einsum("td,tf->df", normed_second, grad_up, preferred_element_type=jnp.float32),
        ]
    )
    grad_normed_second = lax.psum_scatter(
        (
            jnp.einsum(
                "tf,df->td", grad_gate, gate_up_weight[0], preferred_element_type=jnp.float32
            )
            + jnp.einsum(
                "tf,df->td", grad_up, gate_up_weight[1], preferred_element_type=jnp.float32
            )
        ).astype(jnp.bfloat16),
        "tp",
        scatter_dimension=0,
        tiled=True,
    ).astype(jnp.float32)
    grad_resid_own, gain_second_part = norm_back(resid_own, gain_second, grad_normed_second)
    grad_resid_own = grad_resid_own + seq_weight * cotangent.astype(jnp.float32)
    resid_grad_rows = lax.all_gather(grad_resid_own.astype(jnp.bfloat16), "tp", axis=0, tiled=True)
    grad_out_proj = jnp.einsum(
        "tc,td->cd", attended, resid_grad_rows, preferred_element_type=jnp.float32
    )
    grad_attended = (
        jnp.einsum("td,cd->tc", resid_grad_rows, out_weight, preferred_element_type=jnp.float32)
        .astype(jnp.bfloat16)
        .reshape(length, heads_local, HD)
    )
    grad_keys = jnp.zeros((length, heads_local, HD), jnp.float32)
    grad_values = jnp.zeros((length, heads_local, HD), jnp.float32)
    query_grads = []
    for block_index in range(block_count):
        key_end = (block_index + 1) * block_rows
        query_block, scores = block_scores(block_index)
        soft_scores = jnp.exp(scores - log_totals[block_index])
        grad_block = grad_attended[block_index * block_rows : key_end]
        grad_soft = jnp.einsum(
            "qhd,khd->hqk", grad_block, value_rows[:key_end], preferred_element_type=jnp.float32
        )
        row_delta = jnp.sum(soft_scores * grad_soft, axis=-1, keepdims=True)
        grad_scores = (soft_scores * (grad_soft - row_delta)).astype(jnp.bfloat16)
        query_grads.append(
            score_scale
            * jnp.einsum(
                "hqk,khd->qhd", grad_scores, key_rows[:key_end], preferred_element_type=jnp.float32
            )
        )
        grad_keys = grad_keys.at[:key_end].add(
            score_scale
            * jnp.einsum(
                "hqk,qhd->khd", grad_scores, query_block, preferred_element_type=jnp.float32
            )
        )
        grad_values = grad_values.at[:key_end].add(
            jnp.einsum(
                "hqk,qhd->khd",
                soft_scores.astype(jnp.bfloat16),
                grad_block,
                preferred_element_type=jnp.float32,
            )
        )
    grad_queries = jnp.concatenate(query_grads, axis=0)
    grad_mixture = (
        jnp.stack(
            [
                unrotate(grad_queries, cosine_table, sine_table),
                unrotate(grad_keys, cosine_table, sine_table),
                grad_values,
            ],
            axis=2,
        )
        .astype(jnp.bfloat16)
        .reshape(length, heads_local * 3 * HD)
    )
    grad_qkv = jnp.einsum("td,tc->dc", normed, grad_mixture, preferred_element_type=jnp.float32)
    grad_normed_first = lax.psum_scatter(
        jnp.einsum(
            "tc,dc->td", grad_mixture, qkv_weight, preferred_element_type=jnp.float32
        ).astype(jnp.bfloat16),
        "tp",
        scatter_dimension=0,
        tiled=True,
    ).astype(jnp.float32)
    grad_input_own, gain_first_part = norm_back(input_own, gain_first, grad_normed_first)
    input_grad = grad_resid_own + grad_input_own
    gain_grads = lax.psum(jnp.stack([gain_first_part, gain_second_part]), ("seq", "tp"))
    gain_grad_own = lax.dynamic_slice_in_dim(
        gain_grads, lax.axis_index("seq") * gains_master.shape[1], gains_master.shape[1], 1
    )
    qkv_grad_own, out_grad_own, gate_up_grad_own, down_grad_own = (
        lax.psum_scatter(
            grad_qkv.astype(jnp.bfloat16), "seq", scatter_dimension=0, tiled=True
        ).astype(jnp.float32),
        lax.psum_scatter(
            grad_out_proj.astype(jnp.bfloat16), "seq", scatter_dimension=1, tiled=True
        ).astype(jnp.float32),
        lax.psum_scatter(
            grad_gate_up.astype(jnp.bfloat16), "seq", scatter_dimension=1, tiled=True
        ).astype(jnp.float32),
        lax.psum_scatter(
            grad_down.astype(jnp.bfloat16), "seq", scatter_dimension=1, tiled=True
        ).astype(jnp.float32),
    )
    rate_unit = float(length * seq_size) ** (-0.5)
    qkv_new = apply_update(qkv_master, qkv_grad_own, qkv_moment, qkv_average, rate_qkv * rate_unit)
    out_new = apply_update(out_master, out_grad_own, out_moment, out_average, rate_out * rate_unit)
    gate_up_new = apply_update(
        gate_up_master, gate_up_grad_own, gate_up_moment, gate_up_average, rate_gate_up * rate_unit
    )
    down_new = apply_update(
        down_master, down_grad_own, down_moment, down_average, rate_down * rate_unit
    )
    gains_new = apply_update(
        gains_master, gain_grad_own, gains_moment, gains_average, rate_gains * rate_unit
    )
    return (
        layer_output,
        input_grad,
        qkv_new[0],
        qkv_new[1],
        qkv_new[2],
        qkv_new[3],
        out_new[0],
        out_new[1],
        out_new[2],
        out_new[3],
        gate_up_new[0],
        gate_up_new[1],
        gate_up_new[2],
        gate_up_new[3],
        down_new[0],
        down_new[1],
        down_new[2],
        down_new[3],
        gains_new[0],
        gains_new[1],
        gains_new[2],
        gains_new[3],
    )


AXES = ("y", "c", "h", "l", "x")
RING = ("c", "l", "x")
MESH = pl.DeviceIdType.MESH
ROW = 512
BF = jnp.bfloat16
F32 = jnp.float32
LOG2E = 1.4426950408889634
NT = (((1,), (1,)), ((), ()))
NN = (((1,), (0,)), ((), ()))
TN = (((0,), (0,)), ((), ()))


def ring_plan_fits(mesh):
    return mesh.shape["seq"] == 4 and mesh.shape["tp"] == 8


def device_pairs(target):
    pairs = []
    for index in range(32):
        y, c, h, l, x = (index >> 4) & 1, (index >> 3) & 1, (index >> 2) & 1, (index >> 1) & 1, index & 1
        goal = target(y, c, h, l, x)
        if goal is not None:
            y, c, h, l, x = goal
            pairs.append((index, 16 * y + 8 * c + 4 * h + 2 * l + x))
    return pairs


def move(values, target):
    return lax.ppermute(values, AXES, device_pairs(target))


def flip(values, bits):
    return move(
        values,
        lambda y, c, h, l, x: (
            y ^ ("y" in bits),
            c ^ ("c" in bits),
            h ^ ("h" in bits),
            l ^ ("l" in bits),
            x ^ ("x" in bits),
        ),
    )


def swap_ch(values):
    return move(values, lambda y, c, h, l, x: (y, h, c, l, x))


def rounded(values):
    return values.astype(BF)


def ring_position():
    c, l, x = (lax.axis_index(name) for name in RING)
    partners = ({"x": 1 - x}, {"l": 1 - l}, {"c": 1 - c})
    return 4 * c + 2 * l + x, partners


def enter_ring(partners):
    barrier = pltpu.get_barrier_semaphore()
    for partner in partners:
        pl.semaphore_signal(barrier, inc=1, device_id=partner, device_id_type=MESH)
    pl.semaphore_wait(barrier, len(partners))


def rows_at(block, part=None):
    if part is None:
        return pl.ds(pl.multiple_of(block * ROW, ROW), ROW)
    half = ROW // 2
    return pl.ds(pl.multiple_of(block * ROW + part * half, half), half)


def remote(source, target, sent, received, device):
    return pltpu.make_async_remote_copy(
        src_ref=source,
        dst_ref=target,
        send_sem=sent,
        recv_sem=received,
        device_id=device,
        device_id_type=MESH,
    )


def places():
    y, c, h, l, x = (lax.axis_index(name) for name in AXES)
    return y, c, h, 4 * c + 2 * l + x


def wide_partners():
    y, c, h, _ = places()
    _, (to_x, to_l, to_c) = ring_position()
    mixed = ({**to_x, **to_l}, {**to_x, **to_c}, {**to_l, **to_c}, {**to_x, **to_l, **to_c})
    across = ({"c": 0, "h": 1 - h}, {"c": 1, "h": 1 - h})
    return (to_x, to_l, to_c) + mixed + ({"y": 1 - y},) + across


class Ring:
    def __init__(self, buffer, size, send, recv):
        self.buffer, self.size, self.send, self.recv = buffer, size, send, recv
        me, (to_x, to_l, to_c) = ring_position()
        self.plan = (
            (me, 0, to_x, me ^ 1),
            (me, 1, to_l, me ^ 2),
            (me, None, to_c, me ^ 4),
            (me, 1, to_x, me ^ 1),
            (me, 0, to_l, me ^ 2),
            (me ^ 1, 0, to_l, me ^ 3),
            (me ^ 2, 1, to_x, me ^ 3),
            (me ^ 1, None, to_c, me ^ 5),
            (me ^ 2, None, to_c, me ^ 6),
            (me ^ 3, None, to_c, me ^ 7),
        )

    def copy(self, index, block):
        _, part, partner, _ = self.plan[index]
        size = self.size if part is None else self.size // 2
        first = block * self.size + (size if part == 1 else 0)
        place = self.buffer.at[pl.ds(pl.multiple_of(first, size), size)]
        return remote(place, place, self.send.at[index], self.recv.at[index], partner)

    def start(self, *indices):
        for index in indices:
            self.copy(index, self.plan[index][0]).start()

    def arrived(self, *indices):
        for index in indices:
            self.copy(index, self.plan[index][3]).wait_recv()

    def sent(self):
        for index in range(10):
            self.copy(index, self.plan[index][0]).wait_send()


class Spread:
    def __init__(self, source, target, near, far, keep):
        self.source, self.target, self.near, self.far, self.keep = source, target, near, far, keep
        _, self.c, self.h, _ = places()

    def local(self):
        return pltpu.make_async_copy(self.source, self.target, self.keep)

    def beside(self):
        return remote(self.source, self.target, self.near.at[0], self.near.at[1], {"c": self.h})

    def across(self, core):
        return remote(
            self.source, self.target, self.far.at[2], self.far.at[core], {"c": self.h, "h": 1 - self.h}
        )

    def start(self):
        self.across(self.c).start()

        @pl.when(self.c == self.h)
        def _():
            self.local().start()

        @pl.when(self.c != self.h)
        def _():
            self.beside().start()

    def arrived(self):
        @pl.when(self.c == self.h)
        def _():
            self.local().wait()
            self.beside().wait_recv()

        @pl.when(self.c != self.h)
        def _():
            self.across(0).wait_recv()
            self.across(1).wait_recv()

    def sent(self):
        self.across(self.c).wait_send()

        @pl.when(self.c != self.h)
        def _():
            self.beside().wait_send()


SPREAD_SEMAPHORES = [
    pltpu.SemaphoreType.DMA((4, 2)),
    pltpu.SemaphoreType.DMA((4, 3)),
    pltpu.SemaphoreType.DMA((4,)),
    pltpu.SemaphoreType.DMA((4, 2)),
    pltpu.SemaphoreType.DMA((4, 2)),
]


class First:
    def __init__(self, refs):
        (self.shard, self.grad), (self.whole, self.moved) = refs[:2], refs[2:4]
        self.w, near, far, keep, self.y_send, self.y_recv, self.grad_sems = refs[4:]
        self.y, self.c, self.h, _ = places()
        first = (2 * self.y + self.c) * 512
        self.pieces = [
            Spread(
                self.shard.at[pl.ds(k * 256, 256)],
                self.w.at[pl.ds(pl.multiple_of(first + k * 256, 256), 256)],
                near.at[k],
                far.at[k],
                keep.at[k],
            )
            for k in range(2)
        ]

    def over_y(self, k, core, y):
        first = (2 * y + core) * 512 + k * 256
        place = self.w.at[pl.ds(pl.multiple_of(first, 256), 256)]
        return remote(place, place, self.y_send.at[k, core], self.y_recv.at[k, core], {"y": 1 - self.y})

    def grad_local(self):
        return pltpu.make_async_copy(self.grad, self.moved, self.grad_sems.at[2])

    def grad_remote(self):
        return remote(
            self.grad, self.moved, self.grad_sems.at[0], self.grad_sems.at[1], {"c": self.h, "h": self.c}
        )

    def run(self, ring):
        for piece in self.pieces:
            piece.start()
        for k in range(2):
            self.pieces[k].arrived()
            for core in range(2):
                self.over_y(k, core, self.y).start()
            if k == 0:
                ring.arrived(0)
                ring.start(5)
                ring.arrived(1)
                ring.start(6)

        @pl.when(self.c == self.h)
        def _():
            self.grad_local().start()

        @pl.when(self.c != self.h)
        def _():
            self.grad_remote().start()

        ring.arrived(2, 3)
        ring.start(7)
        ring.arrived(4)
        ring.start(8)
        for k in range(2):
            for core in range(2):
                self.over_y(k, core, 1 - self.y).wait_recv()
        pltpu.make_async_copy(self.w, self.whole, self.grad_sems.at[3]).start()

    def poll(self, step):
        pass

    def finish(self):
        for piece in self.pieces:
            piece.sent()
        for k in range(2):
            for core in range(2):
                self.over_y(k, core, self.y).wait_send()
        pltpu.make_async_copy(self.w, self.whole, self.grad_sems.at[3]).wait()

        @pl.when(self.c == self.h)
        def _():
            self.grad_local().wait()

        @pl.when(self.c != self.h)
        def _():
            self.grad_remote().wait_recv()
            self.grad_remote().wait_send()


class Second:
    def __init__(self, refs):
        self.shard, self.whole = refs[:2]
        near, far, keep, self.y_send, self.y_recv = refs[2:]
        self.y, c, _, _ = places()
        columns = pl.ds(pl.multiple_of((2 * self.y + c) * 512, 512), 512)
        self.pieces = [
            Spread(
                self.shard.at[pl.ds(k * 512, 512)],
                self.whole.at[pl.ds(k * 512, 512), columns],
                near.at[k],
                far.at[k],
                keep.at[k],
            )
            for k in range(2)
        ]

    def over_y(self, k, y):
        place = self.whole.at[pl.ds(k * 512, 512), pl.ds(pl.multiple_of(y * 1024, 1024), 1024)]
        return remote(place, place, self.y_send.at[k, 0], self.y_recv.at[k, 0], {"y": 1 - self.y})

    def run(self, ring):
        for piece in self.pieces:
            piece.start()

    def poll(self, step):
        @pl.when(step == 1)
        def _():
            self.pieces[0].arrived()
            self.over_y(0, self.y).start()

        @pl.when(step == 4)
        def _():
            self.pieces[1].arrived()
            self.over_y(1, self.y).start()

    def finish(self):
        for k in range(2):
            self.pieces[k].sent()
            self.over_y(k, 1 - self.y).wait_recv()
            self.over_y(k, self.y).wait_send()


def gather_kernel(finish, beside, inputs, outputs, *refs):
    own_ref, refs = refs[0], refs[1:]
    given, refs = refs[:inputs], refs[inputs:]
    full_ref, outs, refs = refs[0], refs[1:4], refs[4:]
    extra_outs, refs = refs[:outputs], refs[outputs:]
    buf, res, send, recv, own_sem, full_sem, out_sem = refs[:7]
    me, _ = ring_position()
    load = pltpu.make_async_copy(own_ref, buf.at[rows_at(me)], own_sem)
    load.start()
    enter_ring(wide_partners())
    load.wait()
    ring = Ring(buf, ROW, send, recv)
    ring.start(0, 1, 2, 3, 4)
    early = beside is First
    if early:
        more = First(given[2:] + extra_outs + refs[7:])
        w_ref, tables = more.w, given[:2]
    else:
        more = Second(given[1:] + extra_outs + refs[7:])
        w_ref, tables = given[0], ()
    more.run(ring)

    def step_body(step, carry):
        block = me ^ ((step >> 1) | ((step & 1) << 2))
        rows = rows_at(block)
        if not early:

            @pl.when(step == 1)
            def _():
                ring.arrived(2)

            @pl.when(step == 2)
            def _():
                ring.arrived(0)
                ring.start(5)
                ring.arrived(1)
                ring.start(6)
                ring.arrived(3)
                ring.start(7)
                ring.arrived(4)
                ring.start(8)

        @pl.when(step == 3)
        def _():
            ring.arrived(7)

        @pl.when(step == 5)
        def _():
            ring.arrived(8)

        @pl.when(step == 6)
        def _():
            ring.arrived(5, 6)
            ring.start(9)

        @pl.when(step == 7)
        def _():
            ring.arrived(9)

        more.poll(step)
        pltpu.make_async_copy(buf.at[rows], full_ref.at[rows], full_sem.at[step]).start()
        turn = step & 1

        def out_copy(which, rows):
            return pltpu.make_async_copy(
                res.at[turn, which], outs[which].at[rows], out_sem.at[turn, which]
            )

        @pl.when(step >= 2)
        def _():
            for which in range(3):
                out_copy(which, rows).wait()

        finish(buf, rows, w_ref, tables, res, turn)
        for which in range(3):
            out_copy(which, rows).start()
        return carry

    lax.fori_loop(0, 8, step_body, 0)
    ring.sent()
    more.finish()

    def drain(step, carry):
        rows = rows_at(step)
        pltpu.make_async_copy(buf.at[rows], full_ref.at[rows], full_sem.at[step]).wait()
        return carry

    lax.fori_loop(0, 8, drain, 0)
    for turn in range(2):
        for which in range(3):
            pltpu.make_async_copy(
                res.at[turn, which], outs[which].at[rows_at(0)], out_sem.at[turn, which]
            ).wait()


def feed_forward_finish(buf, rows, w_ref, tables, res, turn):
    def columns(chunk, carry):
        here = pl.multiple_of(chunk * 256, 256)
        block = buf[rows, :]
        g = jnp.dot(block, w_ref[:, pl.ds(here, 256)], preferred_element_type=F32)
        u = jnp.dot(block, w_ref[:, pl.ds(here + 1024, 256)], preferred_element_type=F32)
        res[turn, 0, :, pl.ds(here, 256)] = rounded(g)
        res[turn, 1, :, pl.ds(here, 256)] = rounded(u)
        res[turn, 2, :, pl.ds(here, 256)] = rounded(g * (1.0 / (1.0 + jnp.exp(-g))) * u)
        return carry

    lax.fori_loop(0, 4, columns, 0)


def attention_finish(buf, rows, w_ref, tables, res, turn):
    block = buf[rows, :]
    cs, sn = tables[0][rows, :], tables[1][rows, :]
    for which in range(2):
        m = jnp.dot(block, w_ref[:, which * 256 : which * 256 + 256], preferred_element_type=F32)
        if which == 0:
            m = m * (0.125 * LOG2E)
        m1, m2 = m[:, :128], m[:, 128:]
        res[turn, which, :, 0:128] = rounded(m1 * cs - m2 * sn)
        res[turn, which, :, 128:256] = rounded(m2 * cs + m1 * sn)
    res[turn, 2] = rounded(jnp.dot(block, w_ref[:, 512:768], preferred_element_type=F32))


def gather_product(own, given, anywhere_given, extra_shapes, width, finish, beside, scratch, number):
    anywhere = pl.BlockSpec(memory_space=pl.ANY)
    vmem = pl.BlockSpec(memory_space=pltpu.VMEM)
    length, depth = 8 * ROW, own.shape[1]
    inputs = len(given) + len(anywhere_given)
    return pl.pallas_call(
        lambda *refs: gather_kernel(finish, beside, inputs, len(extra_shapes), *refs),
        in_specs=[anywhere] + [vmem] * len(given) + [anywhere] * len(anywhere_given),
        out_specs=[anywhere] * (4 + len(extra_shapes)),
        out_shape=[jax.ShapeDtypeStruct((length, depth), BF)]
        + [jax.ShapeDtypeStruct((length, width), BF)] * 3
        + [jax.ShapeDtypeStruct(shape, BF) for shape in extra_shapes],
        scratch_shapes=[
            pltpu.VMEM((length, depth), BF),
            pltpu.VMEM((2, 3, ROW, width), BF),
            pltpu.SemaphoreType.DMA((10,)),
            pltpu.SemaphoreType.DMA((10,)),
            pltpu.SemaphoreType.DMA,
            pltpu.SemaphoreType.DMA((8,)),
            pltpu.SemaphoreType.DMA((2, 3)),
        ]
        + scratch,
        compiler_params=pltpu.CompilerParams(
            collective_id=number, has_side_effects=True, vmem_limit_bytes=56 * 2**20
        ),
        cost_estimate=pl.CostEstimate(
            flops=80 * 10**9, bytes_accessed=30 * 2**20, transcendentals=0
        ),
    )(own, *given, *anywhere_given)


def scatter_kernel(dims, a_ref, w_ref, out_ref, abuf, mine, other, sums, ra, rb, near_x, near_l, send, recv, a_sem):
    me, partners = ring_position()
    to_x, to_l, to_c = partners
    order = (7, 3, 5, 6, 1, 2, 4, 0)

    def load(index):
        return pltpu.make_async_copy(
            a_ref.at[rows_at(me ^ order[index])], abuf.at[index % 2], a_sem.at[index % 2]
        )

    load(0).start()
    enter_ring(partners)

    def copy(index, source, target, partner):
        return pltpu.make_async_remote_copy(
            src_ref=source,
            dst_ref=target,
            send_sem=send.at[index],
            recv_sem=recv.at[index],
            device_id=partner,
            device_id_type=MESH,
        )

    half = ROW // 2
    top, bottom = pl.ds(0, half), pl.ds(half, half)
    copies = [copy(slot, mine.at[slot], other.at[slot], to_c) for slot in range(4)] + [
        copy(4, sums.at[2, top], ra, to_x),
        copy(5, sums.at[2, bottom], rb, to_l),
        copy(6, sums.at[0, top], near_x.at[top], to_x),
        copy(7, sums.at[1, bottom], near_l.at[bottom], to_l),
        copy(8, sums.at[0, bottom], near_x.at[bottom], to_x),
        copy(9, sums.at[1, top], near_l.at[top], to_l),
    ]

    def product(index, store):
        def columns(chunk, carry):
            here = pl.ds(pl.multiple_of(chunk * 256, 256), 256)
            w = w_ref[here, :] if dims == NT else w_ref[:, here]
            store(
                here, lax.dot_general(abuf[index % 2], w, dims, preferred_element_type=F32)
            )
            return carry

        lax.fori_loop(0, 8, columns, 0)

    for index, slot in enumerate(order):
        load(index).wait()
        if index + 1 < 8:
            load(index + 1).start()
        if slot >= 4:

            def store(here, value, slot=slot):
                mine[slot - 4, :, here] = rounded(value)

            product(index, store)
            copies[slot - 4].start()
        elif slot > 0:
            copies[slot].wait_recv()

            def store(here, value, slot=slot):
                sums[slot - 1, :, here] = rounded(value + other[slot, :, here].astype(F32))

            product(index, store)
            if slot == 3:
                copies[4].start()
                copies[5].start()
            if slot == 1:
                copies[6].start()
            if slot == 2:
                copies[7].start()
                copies[5].wait_recv()
                sums[0, bottom, :] = rounded(
                    sums[0, bottom, :].astype(F32) + rb[...].astype(F32)
                )
                copies[8].start()
                copies[4].wait_recv()
                sums[1, top, :] = rounded(sums[1, top, :].astype(F32) + ra[...].astype(F32))
                copies[9].start()
        else:
            copies[0].wait_recv()

            def store(here, value):
                out_ref[:, here] = value + other[0, :, here].astype(F32)

            product(index, store)
    for part, first, second in ((top, 6, 9), (bottom, 8, 7)):
        copies[first].wait_recv()
        copies[second].wait_recv()
        out_ref[part, :] = out_ref[part, :] + (
            near_x[part, :].astype(F32) + near_l[part, :].astype(F32)
        )
    for each in copies:
        each.wait_send()


def product_scatter(a, weight, dims, number):
    anywhere = pl.BlockSpec(memory_space=pl.ANY)
    vmem = pl.BlockSpec(memory_space=pltpu.VMEM)
    depth = a.shape[1]
    width = weight.shape[0] if dims == NT else weight.shape[1]
    return pl.pallas_call(
        lambda *refs: scatter_kernel(dims, *refs),
        in_specs=[anywhere, vmem],
        out_specs=vmem,
        out_shape=jax.ShapeDtypeStruct((ROW, width), F32),
        scratch_shapes=[
            pltpu.VMEM((2, ROW, depth), BF),
            pltpu.VMEM((4, ROW, width), BF),
            pltpu.VMEM((4, ROW, width), BF),
            pltpu.VMEM((3, ROW, width), BF),
            pltpu.VMEM((ROW // 2, width), BF),
            pltpu.VMEM((ROW // 2, width), BF),
            pltpu.VMEM((ROW, width), BF),
            pltpu.VMEM((ROW, width), BF),
            pltpu.SemaphoreType.DMA((10,)),
            pltpu.SemaphoreType.DMA((10,)),
            pltpu.SemaphoreType.DMA((2,)),
        ],
        compiler_params=pltpu.CompilerParams(
            collective_id=number, has_side_effects=True, vmem_limit_bytes=58 * 2**20
        ),
        cost_estimate=pl.CostEstimate(
            flops=80 * 10**9, bytes_accessed=30 * 2**20, transcendentals=0
        ),
    )(a, weight)


def column_order():
    column = lax.broadcasted_iota(jnp.int32, (768, 768), 1)
    row = lax.broadcasted_iota(jnp.int32, (768, 768), 0)
    part, within = column // 256, column % 256
    turned = ((within % 128) // 32) * 192 + part * 64 + (within // 128) * 32 + within % 32
    plain = (within // 64) * 192 + 128 + within % 64
    return (row == jnp.where(part == 2, plain, turned)).astype(BF)


def head_lanes_turned(head):
    lane = lax.broadcasted_iota(jnp.int32, (1, 256), 1)
    return (lane % 128) // 32 == head


def head_lanes_plain(head):
    lane = lax.broadcasted_iota(jnp.int32, (1, 256), 1)
    return lane // 64 == head


def picked_block(step, blocks):
    block = jnp.int32(blocks[0])
    for index in range(1, len(blocks)):
        block = jnp.where(step == index, blocks[index], block)
    return block


def mark(*values):
    return sum(value[(0,) * value.ndim].astype(F32) for value in values) * 0.0


def after(values, zero):
    return values + zero.astype(values.dtype)


def held(values, zero):
    if zero is None:
        return values
    return after(lax.optimization_barrier(values), zero)


class Beside:
    def __init__(self, refs):
        self.out_shard, self.gate_up_shard, self.grad_own = refs[:3]
        self.out_full, self.gate_up, self.grad_full, self.rows_own = refs[3:7]
        (
            near,
            far,
            keep,
            self.y_send,
            self.y_recv,
            out_near,
            out_far,
            out_keep,
            self.out_y,
            grad_send,
            grad_recv,
            out_send,
            out_recv,
            self.row_send,
            self.row_recv,
            self.own_sem,
        ) = refs[7:]
        self.y, self.c, self.h, self.me = places()
        _, _, _, l, x = (lax.axis_index(name) for name in AXES)
        s = 2 * self.y + self.c
        self.pieces = [
            Spread(
                self.gate_up_shard.at[pl.ds(k * 128, 128)],
                self.gate_up.at[pl.ds(pl.multiple_of(s * 512 + k * 128, 128), 128)],
                near.at[k],
                far.at[k],
                keep.at[k],
            )
            for k in range(4)
        ]
        heads = 4 * self.h + 2 * l + x
        self.out_piece = Spread(
            self.out_shard,
            self.out_full.at[
                pl.ds(pl.multiple_of(heads * 256, 256), 256), pl.ds(pl.multiple_of(s * 512, 512), 512)
            ],
            out_near,
            out_far,
            out_keep,
        )
        self.grad_ring = Ring(self.grad_full, ROW, grad_send, grad_recv)
        self.out_ring = Ring(self.out_full, 256, out_send, out_recv)

    def over_y(self, k, core, y):
        first = (2 * y + core) * 512 + k * 128
        place = self.gate_up.at[pl.ds(pl.multiple_of(first, 128), 128)]
        return remote(place, place, self.y_send.at[k, core], self.y_recv.at[k, core], {"y": 1 - self.y})

    def out_over_y(self, y):
        place = self.out_full.at[
            pl.ds(pl.multiple_of(self.me * 256, 256), 256), pl.ds(pl.multiple_of(y * 1024, 1024), 1024)
        ]
        return remote(place, place, self.out_y.at[0], self.out_y.at[1], {"y": 1 - self.y})

    def piece_over_y(self, k):
        self.pieces[k].arrived()
        for core in range(2):
            self.over_y(k, core, self.y).start()

    def begin(self):
        own = pltpu.make_async_copy(self.grad_own, self.grad_full.at[rows_at(self.me)], self.own_sem.at[0])
        own.start()
        enter_ring(wide_partners())
        self.out_piece.start()
        self.pieces[0].start()
        own.wait()
        self.grad_ring.start(0, 1, 2, 3, 4)

    def at(self, step):
        def when(number, *actions):
            @pl.when(step == number)
            def _():
                for action in actions:
                    action()

        def out_on():
            self.out_piece.arrived()
            self.out_over_y(self.y).start()

        def out_ring_on():
            self.out_over_y(1 - self.y).wait_recv()
            self.out_ring.start(0, 1, 2, 3, 4)

        def relay(ring):
            ring.arrived(0)
            ring.start(5)
            ring.arrived(1)
            ring.start(6)

        def relay_core(ring):
            ring.arrived(3)
            ring.start(7)
            ring.arrived(4)
            ring.start(8)

        def relay_last(ring):
            ring.arrived(5, 6)
            ring.start(9)

        when(0, self.begin)
        when(3, out_on, self.pieces[1].start)
        when(6, out_ring_on, lambda: relay(self.grad_ring))
        when(9, lambda: self.piece_over_y(0), self.pieces[2].start)
        when(12, lambda: relay_core(self.grad_ring), lambda: relay(self.out_ring))
        when(14, lambda: self.piece_over_y(1), self.pieces[3].start)
        when(18, lambda: relay_core(self.out_ring), lambda: relay_last(self.grad_ring))
        when(20, lambda: self.piece_over_y(2))
        when(25, lambda: relay_last(self.out_ring))
        when(29, lambda: self.piece_over_y(3))

    def row_local(self, block, o_all):
        columns = pl.ds(pl.multiple_of(self.me * 256, 256), 256)
        return pltpu.make_async_copy(
            o_all.at[rows_at(block)], self.rows_own.at[:, columns], self.own_sem.at[1]
        )

    def row_remote(self, block, o_all, sender):
        columns = pl.ds(pl.multiple_of(sender * 256, 256), 256)
        return remote(
            o_all.at[rows_at(block)],
            self.rows_own.at[:, columns],
            self.row_send.at[block],
            self.row_recv.at[sender],
            {"c": block >> 2, "l": (block >> 1) & 1, "x": block & 1},
        )

    def send_rows(self, block, o_all):
        @pl.when(block == self.me)
        def _():
            self.row_local(block, o_all).start()

        @pl.when(block != self.me)
        def _():
            self.row_remote(block, o_all, self.me).start()

    def end(self, o_all):
        self.out_piece.sent()
        self.out_over_y(self.y).wait_send()
        for k in range(4):
            self.pieces[k].sent()
            for core in range(2):
                self.over_y(k, core, self.y).wait_send()
                self.over_y(k, core, 1 - self.y).wait_recv()
        for ring in (self.grad_ring, self.out_ring):
            ring.arrived(2, 7, 8, 9)
            ring.sent()

        def each(block, carry):
            @pl.when(block == self.me)
            def _():
                self.row_local(block, o_all).wait()

            @pl.when(block != self.me)
            def _():
                self.row_remote(block, o_all, self.me).wait_send()
                self.row_remote(block, o_all, block).wait_recv()

            return carry

        lax.fori_loop(0, 8, each, 0)


def attend_kernel(q_ref, k_ref, v_ref, out_shard, gate_up_shard, grad_own, o_ref, l_ref, *refs):
    beside = Beside((out_shard, gate_up_shard, grad_own) + refs[:4] + refs[8:])
    s_scr, m_scr, acc_scr, o_all = refs[4:8]
    head = pl.program_id(1)
    step = pl.program_id(0) * 4 + head
    block = 7 - pl.program_id(0)
    beside.at(step)
    row = lax.broadcasted_iota(jnp.int32, (ROW, ROW), 0)
    col = lax.broadcasted_iota(jnp.int32, (ROW, ROW), 1)

    def lane_max(s):
        return jnp.maximum(
            jnp.maximum(s[:, :128], s[:, 128:256]), jnp.maximum(s[:, 256:384], s[:, 384:])
        )

    def lane_sum(s):
        return (s[:, :128] + s[:, 128:256]) + (s[:, 256:384] + s[:, 384:])

    def keys_at(key_block):
        return pl.ds(pl.multiple_of(key_block * ROW, ROW), ROW)

    q = q_ref[...]
    qh = jnp.where(head_lanes_turned(head), q, jnp.zeros_like(q))

    def scores(key_block):
        return lax.dot_general(qh, k_ref[keys_at(key_block), :], NT, preferred_element_type=F32)

    s = jnp.where(col <= row, scores(block), masked_score)
    s_scr[block] = s
    m_scr[...] = lane_max(s)

    def first_pass(key_block, carry):
        s = scores(key_block)
        s_scr[key_block] = s
        m_scr[...] = jnp.maximum(m_scr[...], lane_max(s))
        return carry

    lax.fori_loop(0, block, first_pass, 0)
    top = jnp.max(m_scr[...], axis=1, keepdims=True)
    m_scr[...] = jnp.zeros_like(m_scr)
    acc_scr[...] = jnp.zeros_like(acc_scr)

    def second_pass(key_block, carry):
        e = jnp.exp2(s_scr[key_block] - top)
        m_scr[...] += lane_sum(e)
        acc_scr[...] += lax.dot_general(
            e.astype(BF), v_ref[keys_at(key_block), :], NN, preferred_element_type=F32
        )
        return carry

    lax.fori_loop(0, block + 1, second_pass, 0)
    total = jnp.sum(m_scr[...], axis=1, keepdims=True)
    part = rounded(acc_scr[...] * (1.0 / total))
    rows = rows_at(block)

    @pl.when(head == 0)
    def _():
        o_all[rows, :] = part

    @pl.when(head > 0)
    def _():
        o_all[rows, :] = jnp.where(head_lanes_plain(head), part, o_all[rows, :])

    level = jnp.transpose(jnp.broadcast_to(top + jnp.log2(total), (ROW, 128)))[0:4, :]
    row4 = lax.broadcasted_iota(jnp.int32, (4, ROW), 0)
    l_ref[0] = jnp.where(row4 == head, level, l_ref[0])

    @pl.when(head == 3)
    def _():
        o_ref[...] = o_all[rows, :]
        beside.send_rows(block, o_all)

    @pl.when(step == 31)
    def _():
        beside.end(o_all)


def attend(q, k, v, out_shard, gate_up_shard, grad_own):
    length = q.shape[0]
    blocks = length // ROW
    whole = pl.BlockSpec((length, 256), lambda i, head: (0, 0))
    anywhere = pl.BlockSpec(memory_space=pl.ANY)
    dma = pltpu.SemaphoreType.DMA
    return pl.pallas_call(
        attend_kernel,
        grid=(blocks, 4),
        in_specs=[pl.BlockSpec((ROW, 256), lambda i, head: (7 - i, 0)), whole, whole] + [anywhere] * 3,
        out_specs=[
            pl.BlockSpec((ROW, 256), lambda i, head: (7 - i, 0)),
            pl.BlockSpec((1, 4, ROW), lambda i, head: (7 - i, 0, 0)),
        ]
        + [anywhere] * 4,
        out_shape=[
            jax.ShapeDtypeStruct((length, 256), BF),
            jax.ShapeDtypeStruct((blocks, 4, ROW), F32),
            jax.ShapeDtypeStruct((2048, 2048), BF),
            jax.ShapeDtypeStruct((2048, 2048), BF),
            jax.ShapeDtypeStruct((length, 2048), BF),
            jax.ShapeDtypeStruct((ROW, 2048), BF),
        ],
        scratch_shapes=[
            pltpu.VMEM((blocks, ROW, ROW), F32),
            pltpu.VMEM((ROW, 128), F32),
            pltpu.VMEM((ROW, 256), F32),
            pltpu.VMEM((length, 256), BF),
        ]
        + SPREAD_SEMAPHORES
        + [dma((2,)), dma((3,)), dma, dma((2,))]
        + [dma((10,))] * 4
        + [dma((8,)), dma((8,)), dma((2,))],
        compiler_params=pltpu.CompilerParams(
            collective_id=6, has_side_effects=True, vmem_limit_bytes=48 * 2**20
        ),
        cost_estimate=pl.CostEstimate(
            flops=14 * 10**9 * blocks, bytes_accessed=10 * 2**20, transcendentals=0
        ),
    )(q, k, v, out_shard, gate_up_shard, grad_own)


KEYS = 256


HALF = ROW // 2


class BesideBack:
    DUE = {"a": 8, "b": 9, "c": 11, "d": 12, "D0": 15, "e": 24, "f": 25, "D1": 27, "G0": 37, "g": 48, "h": 49, "G1": 51, "G2": 61, "G3": 70}

    def __init__(self, refs):
        self.heads_own, self.parts, self.gate_up, self.down, self.residual, self.cos, self.sin = refs[:7]
        self.gate_up_sums, self.down_sums, self.layer = refs[7:10]
        (
            self.do,
            self.cs,
            self.sn,
            self.other,
            self.near_x,
            self.near_l,
            self.ra,
            self.rb,
            self.land,
            self.stage,
            self.rest,
            self.row_send,
            self.row_recv,
            self.core_send,
            self.core_recv,
            self.far_send,
            self.far_recv,
            self.y_send,
            self.y_recv,
            self.z_send,
            self.z_recv,
            self.stage_sem,
            self.own_sem,
        ) = refs[10:]
        self.y, self.c, self.h, self.me = places()
        _, (self.to_x, self.to_l, self.to_c) = ring_position()
        self.names = list(self.DUE)
        self.where = {
            "a": (3, 0), "b": (3, 1), "c": (1, 0), "d": (2, 1), "e": (1, 1), "f": (2, 0), "g": (0, 0), "h": (0, 1)
        }

    def far(self, name):
        top, bottom = pl.ds(0, HALF), pl.ds(HALF, HALF)
        other = self.other
        index = "abcdef".index(name)
        source, target, device = (
            (other.at[3, top], self.ra, self.to_x),
            (other.at[3, bottom], self.rb, self.to_l),
            (other.at[1, top], self.near_x.at[top], self.to_x),
            (other.at[2, bottom], self.near_l.at[bottom], self.to_l),
            (other.at[1, bottom], self.near_x.at[bottom], self.to_x),
            (other.at[2, top], self.near_l.at[top], self.to_l),
        )[index]
        return remote(source, target, self.far_send.at[index], self.far_recv.at[index], device)

    def tables(self):
        return (
            pltpu.make_async_copy(self.cos, self.cs, self.own_sem.at[0]),
            pltpu.make_async_copy(self.sin, self.sn, self.own_sem.at[1]),
        )

    def row_local(self):
        columns = pl.ds(pl.multiple_of(self.me * 256, 256), 256)
        return pltpu.make_async_copy(
            self.heads_own.at[:, columns], self.do.at[rows_at(self.me)], self.own_sem.at[2]
        )

    def row_remote(self, block, sender):
        columns = pl.ds(pl.multiple_of(block * 256, 256), 256)
        return remote(
            self.heads_own.at[:, columns],
            self.do.at[rows_at(sender)],
            self.row_send.at[block],
            self.row_recv.at[sender],
            {"c": block >> 2, "l": (block >> 1) & 1, "x": block & 1},
        )

    def core(self, slot):
        return remote(
            self.parts.at[rows_at(self.me ^ (slot | 4))],
            self.other.at[slot],
            self.core_send.at[slot],
            self.core_recv.at[slot],
            self.to_c,
        )

    def piece(self, name, y):
        k = int(name[1])
        if name[0] == "G":
            first = (2 * y + (k >> 1)) * 512 + (k & 1) * 256
            return self.gate_up.at[pl.ds(pl.multiple_of(first, 256), 256)]
        return self.down.at[:, pl.ds(pl.multiple_of((2 * y + k) * 512, 512), 512)]

    def over_y(self, name):
        index = ("D0", "D1", "G0", "G1", "G2", "G3").index(name)
        target = self.land_d.at[int(name[1])] if name[0] == "D" else self.land.at[int(name[1])]
        return remote(
            self.piece(name, 1 - self.y), target, self.y_send.at[index], self.y_recv.at[index], {"y": 1 - self.y}
        )

    def owner(self, name):
        k = int(name[1])
        return k >> 1 if name[0] == "G" else k

    def sum_place(self, name, h):
        k = int(name[1])
        if name[0] == "G":
            return self.gate_up_sums.at[h, pl.ds((k & 1) * 256, 256)]
        return self.down_sums.at[h]

    def over_z(self, name, h):
        index = ("D0", "D1", "G0", "G1", "G2", "G3").index(name)
        source = self.land_d.at[int(name[1])] if name[0] == "D" else self.land.at[int(name[1])]
        group = (0, 0, 1, 2, 1, 2)[index]
        return (
            remote(
                source,
                self.sum_place(name, h),
                self.z_send.at[index],
                self.z_recv.at[group, h],
                {"c": self.owner(name), "h": self.c},
            ),
            pltpu.make_async_copy(source, self.sum_place(name, h), self.z_send.at[index]),
        )

    def stage_copy(self, index):
        name = self.names[index]
        sem = self.stage_sem.at[index % 2]
        if name in self.where:
            slot, half = self.where[name]
            return pltpu.make_async_copy(
                self.parts.at[rows_at(self.me ^ slot, half)], self.stage.at[index % 2], sem
            )
        if name[0] == "G":
            return pltpu.make_async_copy(self.piece(name, self.y), self.stage.at[index % 2], sem)
        return pltpu.make_async_copy(self.piece(name, self.y), self.stage_d.at[index % 2], sem)

    def rest_copy(self, half):
        return pltpu.make_async_copy(self.residual.at[pl.ds(half * HALF, HALF)], self.rest, self.own_sem.at[3])

    def layer_remote(self, half):
        part = pl.ds(half * HALF, HALF)
        return (
            remote(
                self.other.at[0, part],
                self.layer.at[part],
                self.far_send.at[6 + half],
                self.far_recv.at[6 + half],
                {"c": self.h, "h": self.c},
            ),
            pltpu.make_async_copy(self.other.at[0, part], self.layer.at[part], self.far_send.at[6 + half]),
        )

    def either(self, here, pair, method):
        away, local = pair

        @pl.when(here)
        def _():
            getattr(local, method)()

        @pl.when(jnp.logical_not(here))
        def _():
            getattr(away, method)()

    def begin(self):
        for copy in self.tables():
            copy.start()
        self.row_local().start()
        self.stage_copy(0).start()
        self.stage_copy(1).start()
        enter_ring(wide_partners())

        def send(index, carry):
            block = 7 - index

            @pl.when(block != self.me)
            def _():
                self.row_remote(block, self.me).start()

            return carry

        lax.fori_loop(0, 8, send, 0)
        for slot in (3, 1, 2, 0):
            self.core(slot).start()
        self.over_y("D0").start()
        self.over_y("D1").start()
        for copy in self.tables():
            copy.wait()

    def rows_there(self, block):
        @pl.when(block == self.me)
        def _():
            self.row_local().wait()

        @pl.when(block != self.me)
        def _():
            self.row_remote(block, block).wait_recv()

    def add(self, target, terms, count):
        size = target.shape[0] // count

        def chunk(index, carry):
            rows = pl.ds(pl.multiple_of(index * size, size), size)
            total = terms[0][rows, :].astype(F32)
            for term in terms[1:]:
                total += term[rows, :].astype(F32)
            target[rows, :] = rounded(total)
            return carry

        lax.fori_loop(0, count, chunk, 0)

    def work(self, name):
        index = self.names.index(name)
        order = ("D0", "D1", "G0", "G1", "G2", "G3")
        self.stage_copy(index).wait()
        if name in self.where:
            slot, half = self.where[name]
            part = pl.ds(half * HALF, HALF)
            if name in "acd" or name == "g":
                self.core(slot).wait_recv()
            terms = [self.stage.at[index % 2], self.other.at[slot, part]]
            if name == "e":
                self.far("b").wait_recv()
                terms.append(self.rb)
            if name == "f":
                self.far("a").wait_recv()
                terms.append(self.ra)
            if name in "gh":
                for each in ("c", "f") if name == "g" else ("e", "d"):
                    self.far(each).wait_recv()
                self.rest_copy(half).start()
                self.rest_copy(half).wait()
                terms += [self.near_x.at[part], self.near_l.at[part], self.rest]
            self.add(self.other.at[slot, part], terms, 8)
            if name in "gh":
                self.either(self.c == self.h, self.layer_remote(half), "start")
            else:
                self.far(name).start()
        else:
            self.over_y(name).wait_recv()
            if name[0] == "D":
                source, mine = self.land_d.at[int(name[1])], self.stage_d.at[index % 2]
            else:
                source, mine = self.land.at[int(name[1])], self.stage.at[index % 2]
            self.add(source, [mine, source], 8)
            here = jnp.logical_and(self.owner(name) == self.c, self.h == self.c)
            self.either(here, self.over_z(name, self.h), "start")
            place = order.index(name)
            if place + 2 < 6:
                self.over_y(order[place + 2]).start()
        if index + 2 < len(self.names):
            self.stage_copy(index + 2).start()

    def poll(self, unit):
        for name, due in self.DUE.items():

            @pl.when(unit == due)
            def _(name=name):
                self.work(name)

    def end(self):
        def each(block, carry):
            @pl.when(block != self.me)
            def _():
                self.row_remote(block, self.me).wait_send()

            return carry

        lax.fori_loop(0, 8, each, 0)
        for slot in range(4):
            self.core(slot).wait_send()
        for name in "abcdef":
            self.far(name).wait_send()
        for half in range(2):
            pair = self.layer_remote(half)

            @pl.when(self.c == self.h)
            def _(pair=pair):
                pair[1].wait()

            @pl.when(self.c != self.h)
            def _(pair=pair):
                pair[0].wait_send()
                pair[0].wait_recv()

        for name in ("D0", "D1", "G0", "G1", "G2", "G3"):
            self.over_y(name).wait_send()
            here = jnp.logical_and(self.owner(name) == self.c, self.h == self.c)
            pair = self.over_z(name, self.h)

            @pl.when(here)
            def _(pair=pair):
                pair[1].wait()

            @pl.when(jnp.logical_not(here))
            def _(pair=pair):
                pair[0].wait_send()

        for h in range(2):
            here = jnp.logical_and(h == self.h, self.c == self.h)
            for name in ("D0", "G0", "G1"):

                @pl.when(jnp.logical_not(here))
                def _(name=name, h=h):
                    self.over_z(name, h)[0].wait_recv()


def attend_back_kernel(q_ref, k_ref, v_ref, o_ref, l_ref, *refs):
    given, (dkv_ref, dq_out), outs = refs[:7], refs[7:9], refs[9:12]
    qm, dom, delta, dq, dk, dv, km, pt, dst = refs[12:21]
    land_d, stage_d = refs[21:23]
    beside = BesideBack(given + outs + refs[23:])
    beside.land_d, beside.stage_d = land_d, stage_d
    heads = 4
    i, sub = pl.program_id(0), pl.program_id(1)
    block = 7 - i
    blocks = 8
    unit = i * (i + 1) + sub * (i + 1)
    rows_here = rows_at(block)

    @pl.when(jnp.logical_and(i == 0, sub == 0))
    def _():
        beside.begin()

    @pl.when(sub == 0)
    def _():
        beside.rows_there(block)
        q = q_ref[...]
        do = beside.do[rows_here, :]
        for head in range(heads):
            part = slice(head * ROW, (head + 1) * ROW)
            qm[block, part, :] = jnp.where(head_lanes_turned(head), q, jnp.zeros_like(q))
            dom[block, part, :] = jnp.where(head_lanes_plain(head), do, jnp.zeros_like(do))
        product = do.astype(F32) * o_ref[...].astype(F32)
        high = rounded(product)
        low = rounded(product - high.astype(F32))
        head_row = lax.broadcasted_iota(jnp.int32, (8, 256), 0)
        lane = lax.broadcasted_iota(jnp.int32, (8, 256), 1)
        pick = jnp.where(lane // 64 == head_row, 1.0, 0.0).astype(BF)
        sums = lax.dot_general(pick, high, NT, preferred_element_type=F32)
        sums += lax.dot_general(pick, low, NT, preferred_element_type=F32)
        delta[block] = sums[:heads, :]
        dq[rows_here, :] = jnp.zeros((ROW, 256), F32)

    beside.poll(unit)
    key_row = lax.broadcasted_iota(jnp.int32, (KEYS, ROW), 0)
    query_col = lax.broadcasted_iota(jnp.int32, (KEYS, ROW), 1)
    inner = pl.multiple_of(sub * KEYS, KEYS)
    k = k_ref[pl.ds(inner, KEYS), :]
    v = v_ref[pl.ds(inner, KEYS), :]
    for head in range(heads):
        km[head] = jnp.where(head_lanes_turned(head), k, jnp.zeros_like(k))
    dk[...] = jnp.zeros_like(dk)
    dv[...] = jnp.zeros_like(dv)

    def query_part(place, diagonal):
        rows = rows_at(place)
        for head in range(heads):
            part = slice(head * ROW, (head + 1) * ROW)
            st = lax.dot_general(k, qm[place, part, :], NT, preferred_element_type=F32)
            dp = lax.dot_general(v, dom[place, part, :], NT, preferred_element_type=F32)
            p = jnp.exp2(st - l_ref[place, head : head + 1, :])
            if diagonal:
                p = jnp.where(key_row + inner <= query_col, p, 0.0)
            ds = p * (dp - delta[place, head : head + 1, :])
            pt[:, part] = p.astype(BF)
            dst[:, part] = ds.astype(BF)
        dv[...] += lax.dot_general(pt[...], dom[place], NN, preferred_element_type=F32)
        dk[...] += lax.dot_general(dst[...], qm[place], NN, preferred_element_type=F32)
        total = lax.dot_general(dst[:, 0:ROW], km[0], TN, preferred_element_type=F32)
        for head in range(1, heads):
            part = slice(head * ROW, (head + 1) * ROW)
            total += lax.dot_general(dst[:, part], km[head], TN, preferred_element_type=F32)
        dq[rows, :] += total

    query_part(block, True)

    def later(query_block, carry):
        beside.poll(unit + query_block - block)
        query_part(query_block, False)
        return carry

    lax.fori_loop(block + 1, blocks, later, 0)
    table = pl.ds(pl.multiple_of(block * ROW + inner, KEYS), KEYS)
    cs, sn = beside.cs[table, :], beside.sn[table, :]
    d = dk[...] * (1.0 / LOG2E)
    d1, d2 = d[:, :128], d[:, 128:]
    dkv_ref[pl.ds(inner, KEYS), 0:128] = rounded(d1 * cs + d2 * sn)
    dkv_ref[pl.ds(inner, KEYS), 128:256] = rounded(d2 * cs - d1 * sn)
    dkv_ref[pl.ds(inner, KEYS), 256:512] = rounded(dv[...])

    @pl.when(jnp.logical_and(i == 7, sub == 1))
    def _():
        def finish(place, carry):
            rows = rows_at(place)
            cs, sn = beside.cs[rows, :], beside.sn[rows, :]
            d = dq[rows, :] * 0.125
            d1, d2 = d[:, :128], d[:, 128:]
            beside.do[rows, 0:128] = rounded(d1 * cs + d2 * sn)
            beside.do[rows, 128:256] = rounded(d2 * cs - d1 * sn)
            return carry

        lax.fori_loop(0, blocks, finish, 0)
        copy = pltpu.make_async_copy(beside.do, dq_out, beside.own_sem.at[4])
        copy.start()
        copy.wait()
        beside.end()


def attend_back(q, k, v, o, level, heads_own, parts, gate_up, down, residual, cos, sin):
    length = q.shape[0]
    blocks = length // ROW
    dma = pltpu.SemaphoreType.DMA
    anywhere = pl.BlockSpec(memory_space=pl.ANY)

    def key_spec(width):
        return pl.BlockSpec((ROW, width), lambda i, sub: (7 - i, 0))

    return pl.pallas_call(
        attend_back_kernel,
        grid=(blocks, 2),
        in_specs=[key_spec(256)] * 4
        + [pl.BlockSpec((blocks, 4, ROW), lambda i, sub: (0, 0, 0))]
        + [anywhere] * 7,
        out_specs=[key_spec(512)] + [anywhere] * 4,
        out_shape=[
            jax.ShapeDtypeStruct((length, 512), BF),
            jax.ShapeDtypeStruct((length, 256), BF),
            jax.ShapeDtypeStruct((2, 512, 2048), BF),
            jax.ShapeDtypeStruct((2, 1024, 512), BF),
            jax.ShapeDtypeStruct((ROW, 2048), BF),
        ],
        scratch_shapes=[
            pltpu.VMEM((blocks, 4 * ROW, 256), BF),
            pltpu.VMEM((blocks, 4 * ROW, 256), BF),
            pltpu.VMEM((blocks, 4, ROW), F32),
            pltpu.VMEM((length, 256), F32),
            pltpu.VMEM((KEYS, 256), F32),
            pltpu.VMEM((KEYS, 256), F32),
            pltpu.VMEM((4, KEYS, 256), BF),
            pltpu.VMEM((KEYS, 4 * ROW), BF),
            pltpu.VMEM((KEYS, 4 * ROW), BF),
            pltpu.VMEM((2, 1024, 512), BF),
            pltpu.VMEM((2, 1024, 512), BF),
            pltpu.VMEM((length, 256), BF),
            pltpu.VMEM((length, 128), F32),
            pltpu.VMEM((length, 128), F32),
            pltpu.VMEM((4, ROW, 2048), BF),
            pltpu.VMEM((ROW, 2048), BF),
            pltpu.VMEM((ROW, 2048), BF),
            pltpu.VMEM((HALF, 2048), BF),
            pltpu.VMEM((HALF, 2048), BF),
            pltpu.VMEM((4, 256, 2048), BF),
            pltpu.VMEM((2, 256, 2048), BF),
            pltpu.VMEM((HALF, 2048), F32),
            dma((8,)),
            dma((8,)),
            dma((4,)),
            dma((4,)),
            dma((8,)),
            dma((8,)),
            dma((6,)),
            dma((6,)),
            dma((6,)),
            dma((3, 2)),
            dma((2,)),
            dma((5,)),
        ],
        compiler_params=pltpu.CompilerParams(
            collective_id=7, has_side_effects=True, vmem_limit_bytes=63 * 2**20
        ),
        cost_estimate=pl.CostEstimate(
            flops=19 * 10**9 * blocks, bytes_accessed=20 * 2**20, transcendentals=0
        ),
    )(q, k, v, o, level, heads_own, parts, gate_up, down, residual, cos, sin)


def ring_shards(
    layer_input,
    cotangent,
    counts,
    positions,
    qkv_master,
    qkv_moment,
    qkv_average,
    out_master,
    out_moment,
    out_average,
    gate_up_master,
    gate_up_moment,
    gate_up_average,
    down_master,
    down_moment,
    down_average,
    gains_master,
    gains_moment,
    gains_average,
):
    y, c, h, l, x = (lax.axis_index(name) for name in AXES)
    own = 4 * c + 2 * l + x
    plain_y, plain_c, straight = y == 0, c == 0, c == h

    def both_y(mine, other, axis):
        return jnp.where(
            plain_y,
            jnp.concatenate([mine, other], axis=axis),
            jnp.concatenate([other, mine], axis=axis),
        )

    def both_cores(mine, other):
        return jnp.where(plain_c, mine, other), jnp.where(plain_c, other, mine)

    def scatter_y(blocks, zero=None):
        mine = lax.dynamic_slice_in_dim(blocks, 2 * y, 2, 0)
        return mine, flip(held(lax.dynamic_slice_in_dim(blocks, 2 * (1 - y), 2, 0), zero), "y")

    def scatter_ch(near, far):
        total = (near.astype(F32) + far.astype(F32)).astype(BF)
        kept, other = both_cores(total[0], total[1])
        r1 = move(kept, lambda y, c, h, l, x: (y, c, 1 - h, l, x) if c != h else None)
        r2a = move(other, lambda y, c, h, l, x: (y, 1 - c, h, l, x) if c == h else None)
        r2b = move(other, lambda y, c, h, l, x: (y, h, c, l, x) if c != h else None)
        return kept, r1, r2a, r2b

    def scatter_own(kept, r1, r2a, r2b):
        return jnp.where(
            straight,
            kept.astype(F32) + r1.astype(F32),
            r2a.astype(F32) + r2b.astype(F32),
        )

    turn = column_order()
    rows_in = swap_ch(layer_input).astype(F32)
    gains_here = gains_master.astype(BF)
    gains_near = jnp.concatenate(both_cores(gains_here, flip(gains_here, "c")), axis=1)
    gains_all = both_y(gains_near, flip(gains_near, "y"), 1).astype(F32)
    gain_first, gain_second = gains_all[0], gains_all[1]
    qkv_shard = jnp.dot(qkv_master.astype(BF), turn, preferred_element_type=F32).astype(BF)
    scale_first = rms_scale(rows_in)
    normed_own = (rows_in * scale_first * gain_first).astype(BF)
    frequency = rope_theta ** (
        -((jnp.arange(128, dtype=jnp.int32) % 32).astype(F32) * 2.0) / HD
    )
    positions_here = jnp.where(straight, positions, flip(positions, "c"))
    angles = positions_here.astype(F32)[:, None] * frequency[None, :]
    cosine, sine = jnp.cos(angles), jnp.sin(angles)
    count_here = counts.astype(F32)
    count_total = count_here + flip(count_here, "c")
    count_total = count_total + flip(count_total, "y")
    grad_here = (4.0 * count_here[0] / count_total[0] * cotangent.astype(F32)).astype(BF)
    normed, queries, keys, values, qkv_weight, grad_own = gather_product(
        normed_own,
        (cosine, sine),
        (qkv_shard, grad_here),
        ((2048, 768), (ROW, 2048)),
        256,
        attention_finish,
        First,
        [pltpu.VMEM((2048, 768), BF)] + SPREAD_SEMAPHORES + [pltpu.SemaphoreType.DMA((4,))],
        1,
    )
    gate_up_shard = jnp.concatenate([gate_up_master[0], gate_up_master[1]], axis=1).astype(BF)
    attended, level, out_weight, gate_up_weight, grad_out, attended_own = attend(
        queries, keys, values, out_master.astype(BF), gate_up_shard, grad_own
    )
    grad_rows = grad_own.astype(F32)
    residual = rows_in + jnp.dot(attended_own, out_weight, preferred_element_type=F32)
    scale_second = rms_scale(residual)
    normed_second, gate, up, activation, down_weight = gather_product(
        (residual * scale_second * gain_second).astype(BF),
        (gate_up_weight,),
        (down_master.astype(BF),),
        ((1024, 2048),),
        1024,
        feed_forward_finish,
        Second,
        SPREAD_SEMAPHORES,
        2,
    )

    grad_act = lax.dot_general(grad_out, down_weight, NT, preferred_element_type=F32)
    g = gate.astype(F32)
    sigmoid = jax.nn.sigmoid(g)
    grad_gate = (grad_act * up.astype(F32) * sigmoid * (1.0 + g * (1.0 - sigmoid))).astype(BF)
    grad_up = (grad_act * g * sigmoid).astype(BF)
    grad_gate_up = jnp.concatenate([grad_gate, grad_up], axis=1)
    grad_normed_second = product_scatter(grad_gate_up, gate_up_weight, NT, 3)
    gate_up_grad = lax.dot_general(
        normed_second, grad_gate_up, TN, preferred_element_type=F32
    ).astype(BF)
    down_grad = lax.dot_general(activation, grad_out, TN, preferred_element_type=F32).astype(BF)
    layer_parts = jnp.dot(activation, down_weight, preferred_element_type=F32).astype(BF)

    def norm_grad(values, scale, gain, grad):
        scaled = grad * gain
        back = scale * (
            scaled - values * scale * scale * jnp.mean(scaled * values, axis=-1, keepdims=True)
        )
        return back, jnp.sum(grad * values * scale, axis=0)

    residual_grad, gain_second_part = norm_grad(
        residual, scale_second, gain_second, grad_normed_second
    )
    residual_grad = residual_grad + grad_rows
    residual_low = residual_grad.astype(BF)
    grad_heads = lax.dot_general(residual_low, out_weight, NT, preferred_element_type=F32).astype(BF)
    grad_kv, grad_q, gate_up_sums, down_sums, layer_output = attend_back(
        queries, keys, values, attended, level, grad_heads, layer_parts, gate_up_grad, down_grad, residual, cosine, sine
    )
    gate_up_grad_own = gate_up_sums[0].astype(F32) + gate_up_sums[1].astype(F32)
    down_grad_own = down_sums[0].astype(F32) + down_sums[1].astype(F32)

    grad_mixture = jnp.concatenate([grad_q, grad_kv], axis=1)
    grad_normed_first = product_scatter(grad_mixture, qkv_weight, NT, 5)
    qkv_grad = lax.dot_general(normed, grad_mixture, TN, preferred_element_type=F32).astype(BF)
    qkv_grad = lax.dot_general(qkv_grad, turn, NT, preferred_element_type=F32).astype(BF)
    qkv_y = scatter_y(qkv_grad.reshape(4, 512, 768))
    out_grad = lax.dot_general(attended_own, residual_low, TN, preferred_element_type=F32)
    out_grad = lax.psum_scatter(out_grad.astype(BF), RING, scatter_dimension=0, tiled=True)
    out_y = scatter_y(out_grad.reshape(256, 4, 512).transpose(1, 0, 2))
    qkv_grad_own = scatter_own(*scatter_ch(*qkv_y))
    out_grad_own = scatter_own(*scatter_ch(*out_y))

    input_back, gain_first_part = norm_grad(rows_in, scale_first, gain_first, grad_normed_first)
    input_grad = swap_ch((residual_grad + input_back).astype(BF)).astype(F32)

    gain_grads = jnp.stack([gain_first_part, gain_second_part])
    for bit in "xlchy":
        gain_grads = gain_grads + flip(gain_grads, bit)
    gain_grad_own = lax.dynamic_slice_in_dim(gain_grads, (2 * y + c) * 512, 512, 1)

    rate_unit = float(4 * 8 * ROW) ** (-0.5)
    qkv_new = apply_update(qkv_master, qkv_grad_own, qkv_moment, qkv_average, rate_qkv * rate_unit)
    out_new = apply_update(out_master, out_grad_own, out_moment, out_average, rate_out * rate_unit)
    gate_up_grad_own = jnp.stack([gate_up_grad_own[:, :1024], gate_up_grad_own[:, 1024:]])
    gate_up_new = apply_update(
        gate_up_master, gate_up_grad_own, gate_up_moment, gate_up_average, rate_gate_up * rate_unit
    )
    down_new = apply_update(
        down_master, down_grad_own, down_moment, down_average, rate_down * rate_unit
    )
    gains_new = apply_update(
        gains_master, gain_grad_own, gains_moment, gains_average, rate_gains * rate_unit
    )
    return (layer_output, input_grad) + qkv_new + out_new + gate_up_new + down_new + gains_new


def solution(mesh):
    in_specs = (
        P(("seq", "tp"), None),
        P(("seq", "tp"), None),
        P("seq"),
        P("seq"),
        P("seq", "tp"),
        P("seq", "tp"),
        P("seq", "tp"),
        P("tp", "seq"),
        P("tp", "seq"),
        P("tp", "seq"),
        P(None, "seq", "tp"),
        P(None, "seq", "tp"),
        P(None, "seq", "tp"),
        P("tp", "seq"),
        P("tp", "seq"),
        P("tp", "seq"),
        P(None, "seq"),
        P(None, "seq"),
        P(None, "seq"),
    )
    out_specs = (
        P(("seq", "tp"), None),
        P(("seq", "tp"), None),
        P("seq", "tp"),
        P("seq", "tp"),
        P("seq", "tp"),
        P("seq", "tp"),
        P("tp", "seq"),
        P("tp", "seq"),
        P("tp", "seq"),
        P("tp", "seq"),
        P(None, "seq", "tp"),
        P(None, "seq", "tp"),
        P(None, "seq", "tp"),
        P(None, "seq", "tp"),
        P("tp", "seq"),
        P("tp", "seq"),
        P("tp", "seq"),
        P("tp", "seq"),
        P(None, "seq"),
        P(None, "seq"),
        P(None, "seq"),
        P(None, "seq"),
    )
    if ring_plan_fits(mesh):
        fine = jax.sharding.Mesh(mesh.devices.reshape(2, 2, 2, 2, 2), AXES)
        names = {"seq": ("y", "c"), "tp": ("h", "l", "x")}

        def finer(spec):
            parts = []
            for entry in spec:
                entry = (entry,) if isinstance(entry, str) else (entry or ())
                parts.append(sum((names[name] for name in entry), ()) or None)
            return P(*parts)

        return jax.shard_map(
            ring_shards,
            mesh=fine,
            in_specs=tuple(finer(spec) for spec in in_specs),
            out_specs=tuple(finer(spec) for spec in out_specs),
            check_vma=False,
        )
    return jax.shard_map(shards, mesh=mesh, in_specs=in_specs, out_specs=out_specs, check_vma=False)
```

```python
import jax
import jax.numpy as jnp
from jax import lax
from jax.experimental import pallas as pl
from jax.experimental.pallas import tpu as pltpu
from jax.sharding import PartitionSpec as P

HD = 64


norm_epsilon = 1e-05
rope_theta = 130000.0
momentum_coef = 0.9
average_coef = 0.5
masked_score = -1e30
rate_qkv = 0.004
rate_out = 2.0
rate_gate_up = 0.03
rate_down = 0.009
rate_gains = 0.1


def rms_scale(values):
    return lax.rsqrt(jnp.mean(values * values, axis=-1, keepdims=True) + norm_epsilon)


def rope_tables(positions, head_size):
    frequency = rope_theta ** (-(jnp.arange(head_size // 2, dtype=jnp.float32) * 2.0) / head_size)
    angles = positions.astype(jnp.float32)[:, None] * frequency[None, :]
    return (jnp.cos(angles)[:, None, :], jnp.sin(angles)[:, None, :])


def rotate(vectors, cosine_table, sine_table):
    half_width = vectors.shape[-1] // 2
    lower_half = vectors[..., :half_width]
    upper_half = vectors[..., half_width:]
    return jnp.concatenate(
        [
            lower_half * cosine_table - upper_half * sine_table,
            upper_half * cosine_table + lower_half * sine_table,
        ],
        axis=-1,
    )


def unrotate(grads, cosine_table, sine_table):
    half_width = grads.shape[-1] // 2
    lower_half = grads[..., :half_width]
    upper_half = grads[..., half_width:]
    return jnp.concatenate(
        [
            lower_half * cosine_table + upper_half * sine_table,
            upper_half * cosine_table - lower_half * sine_table,
        ],
        axis=-1,
    )


def norm_back(values, gain, grad):
    scale_rows = rms_scale(values)
    scaled = grad * gain
    back = scale_rows * (
        scaled
        - values * scale_rows * scale_rows * jnp.mean(scaled * values, axis=-1, keepdims=True)
    )
    return (back, jnp.sum(grad * values * scale_rows, axis=0))


def apply_update(master, grad, moment, average, rate):
    moment_new = momentum_coef * moment + grad
    master_new = master - rate * (grad + momentum_coef * moment_new)
    average_new = average_coef * average + (1.0 - average_coef) * master_new
    return (moment_new, average_new, master_new, master_new.astype(jnp.bfloat16))


def shards(
    layer_input,
    cotangent,
    counts,
    positions,
    qkv_master,
    qkv_moment,
    qkv_average,
    out_master,
    out_moment,
    out_average,
    gate_up_master,
    gate_up_moment,
    gate_up_average,
    down_master,
    down_moment,
    down_average,
    gains_master,
    gains_moment,
    gains_average,
):
    tp_size = lax.axis_size("tp")
    seq_size = lax.axis_size("seq")
    own_rows = layer_input.shape[0]
    length = own_rows * tp_size
    qkv_weight, out_weight, gate_up_weight, down_weight, gain_weight = (
        lax.all_gather(qkv_master.astype(jnp.bfloat16), "seq", axis=0, tiled=True),
        lax.all_gather(out_master.astype(jnp.bfloat16), "seq", axis=1, tiled=True),
        lax.all_gather(gate_up_master.astype(jnp.bfloat16), "seq", axis=1, tiled=True),
        lax.all_gather(down_master.astype(jnp.bfloat16), "seq", axis=1, tiled=True),
        lax.all_gather(gains_master.astype(jnp.bfloat16), "seq", axis=1, tiled=True),
    )
    heads_local = qkv_weight.shape[1] // (3 * HD)
    count_total = lax.psum(counts.astype(jnp.float32), "seq")
    seq_weight = seq_size * counts.astype(jnp.float32)[0] / count_total[0]
    gain_first = gain_weight[0].astype(jnp.float32)
    gain_second = gain_weight[1].astype(jnp.float32)
    gathered = lax.all_gather(layer_input, "tp", axis=0, tiled=True)
    inputs = gathered.astype(jnp.float32)
    normed = (inputs * rms_scale(inputs) * gain_first).astype(jnp.bfloat16)
    mixture = jnp.dot(normed, qkv_weight, preferred_element_type=jnp.float32).reshape(
        length, heads_local, 3, HD
    )
    cosine_table, sine_table = rope_tables(positions, HD)
    queries = rotate(mixture[:, :, 0], cosine_table, sine_table).astype(jnp.bfloat16)
    key_rows = rotate(mixture[:, :, 1], cosine_table, sine_table).astype(jnp.bfloat16)
    value_rows = mixture[:, :, 2].astype(jnp.bfloat16)
    block_rows = min(512, length)
    block_count = length // block_rows
    score_scale = HD ** (-0.5)

    def block_scores(block_index):
        key_end = (block_index + 1) * block_rows
        query_block = queries[block_index * block_rows : key_end]
        row_index = block_index * block_rows + jnp.arange(block_rows)
        allowed = jnp.arange(key_end)[None, :] <= row_index[:, None]
        scores = score_scale * jnp.einsum(
            "qhd,khd->hqk", query_block, key_rows[:key_end], preferred_element_type=jnp.float32
        )
        return (query_block, jnp.where(allowed[None], scores, masked_score))

    attended_list = []
    log_totals = []
    for block_index in range(block_count):
        query_block, scores = block_scores(block_index)
        key_end = (block_index + 1) * block_rows
        row_max = jnp.max(scores, axis=-1, keepdims=True)
        exp_scores = jnp.exp(scores - row_max)
        row_total = jnp.sum(exp_scores, axis=-1, keepdims=True)
        soft_scores = (exp_scores / row_total).astype(jnp.bfloat16)
        attended_block = jnp.einsum(
            "hqk,khd->qhd", soft_scores, value_rows[:key_end], preferred_element_type=jnp.float32
        )
        attended_list.append(attended_block.astype(jnp.bfloat16))
        log_totals.append(row_max + jnp.log(row_total))
    attended = jnp.concatenate(attended_list, axis=0).reshape(length, heads_local * HD)
    own_start = lax.axis_index("tp") * own_rows
    input_own = layer_input.astype(jnp.float32)
    branch = lax.psum(
        jnp.dot(attended, out_weight, preferred_element_type=jnp.float32).astype(jnp.bfloat16), "tp"
    ).astype(jnp.float32)
    residual = inputs + branch
    normed_second = (residual * rms_scale(residual) * gain_second).astype(jnp.bfloat16)
    resid_own = lax.dynamic_slice_in_dim(residual, own_start, own_rows, 0)
    gate_pre = jnp.dot(normed_second, gate_up_weight[0], preferred_element_type=jnp.float32)
    up_pre = jnp.dot(normed_second, gate_up_weight[1], preferred_element_type=jnp.float32)
    gate_sigmoid = jax.nn.sigmoid(gate_pre)
    activation = (gate_pre * gate_sigmoid * up_pre).astype(jnp.bfloat16)
    layer_output = (
        resid_own
        + lax.psum_scatter(
            jnp.dot(activation, down_weight, preferred_element_type=jnp.float32).astype(
                jnp.bfloat16
            ),
            "tp",
            scatter_dimension=0,
            tiled=True,
        ).astype(jnp.float32)
    ).astype(jnp.bfloat16)
    cot_all = lax.all_gather(cotangent, "tp", axis=0, tiled=True)
    grad_out = (seq_weight * cot_all.astype(jnp.float32)).astype(jnp.bfloat16)
    grad_down = jnp.einsum("tf,td->fd", activation, grad_out, preferred_element_type=jnp.float32)
    grad_act = jnp.einsum("td,fd->tf", grad_out, down_weight, preferred_element_type=jnp.float32)
    grad_gate = (grad_act * up_pre * gate_sigmoid * (1.0 + gate_pre * (1.0 - gate_sigmoid))).astype(
        jnp.bfloat16
    )
    grad_up = (grad_act * gate_pre * gate_sigmoid).astype(jnp.bfloat16)
    grad_gate_up = jnp.stack(
        [
            jnp.einsum("td,tf->df", normed_second, grad_gate, preferred_element_type=jnp.float32),
            jnp.einsum("td,tf->df", normed_second, grad_up, preferred_element_type=jnp.float32),
        ]
    )
    grad_normed_second = lax.psum_scatter(
        (
            jnp.einsum(
                "tf,df->td", grad_gate, gate_up_weight[0], preferred_element_type=jnp.float32
            )
            + jnp.einsum(
                "tf,df->td", grad_up, gate_up_weight[1], preferred_element_type=jnp.float32
            )
        ).astype(jnp.bfloat16),
        "tp",
        scatter_dimension=0,
        tiled=True,
    ).astype(jnp.float32)
    grad_resid_own, gain_second_part = norm_back(resid_own, gain_second, grad_normed_second)
    grad_resid_own = grad_resid_own + seq_weight * cotangent.astype(jnp.float32)
    resid_grad_rows = lax.all_gather(grad_resid_own.astype(jnp.bfloat16), "tp", axis=0, tiled=True)
    grad_out_proj = jnp.einsum(
        "tc,td->cd", attended, resid_grad_rows, preferred_element_type=jnp.float32
    )
    grad_attended = (
        jnp.einsum("td,cd->tc", resid_grad_rows, out_weight, preferred_element_type=jnp.float32)
        .astype(jnp.bfloat16)
        .reshape(length, heads_local, HD)
    )
    grad_keys = jnp.zeros((length, heads_local, HD), jnp.float32)
    grad_values = jnp.zeros((length, heads_local, HD), jnp.float32)
    query_grads = []
    for block_index in range(block_count):
        key_end = (block_index + 1) * block_rows
        query_block, scores = block_scores(block_index)
        soft_scores = jnp.exp(scores - log_totals[block_index])
        grad_block = grad_attended[block_index * block_rows : key_end]
        grad_soft = jnp.einsum(
            "qhd,khd->hqk", grad_block, value_rows[:key_end], preferred_element_type=jnp.float32
        )
        row_delta = jnp.sum(soft_scores * grad_soft, axis=-1, keepdims=True)
        grad_scores = (soft_scores * (grad_soft - row_delta)).astype(jnp.bfloat16)
        query_grads.append(
            score_scale
            * jnp.einsum(
                "hqk,khd->qhd", grad_scores, key_rows[:key_end], preferred_element_type=jnp.float32
            )
        )
        grad_keys = grad_keys.at[:key_end].add(
            score_scale
            * jnp.einsum(
                "hqk,qhd->khd", grad_scores, query_block, preferred_element_type=jnp.float32
            )
        )
        grad_values = grad_values.at[:key_end].add(
            jnp.einsum(
                "hqk,qhd->khd",
                soft_scores.astype(jnp.bfloat16),
                grad_block,
                preferred_element_type=jnp.float32,
            )
        )
    grad_queries = jnp.concatenate(query_grads, axis=0)
    grad_mixture = (
        jnp.stack(
            [
                unrotate(grad_queries, cosine_table, sine_table),
                unrotate(grad_keys, cosine_table, sine_table),
                grad_values,
            ],
            axis=2,
        )
        .astype(jnp.bfloat16)
        .reshape(length, heads_local * 3 * HD)
    )
    grad_qkv = jnp.einsum("td,tc->dc", normed, grad_mixture, preferred_element_type=jnp.float32)
    grad_normed_first = lax.psum_scatter(
        jnp.einsum(
            "tc,dc->td", grad_mixture, qkv_weight, preferred_element_type=jnp.float32
        ).astype(jnp.bfloat16),
        "tp",
        scatter_dimension=0,
        tiled=True,
    ).astype(jnp.float32)
    grad_input_own, gain_first_part = norm_back(input_own, gain_first, grad_normed_first)
    input_grad = grad_resid_own + grad_input_own
    gain_grads = lax.psum(jnp.stack([gain_first_part, gain_second_part]), ("seq", "tp"))
    gain_grad_own = lax.dynamic_slice_in_dim(
        gain_grads, lax.axis_index("seq") * gains_master.shape[1], gains_master.shape[1], 1
    )
    qkv_grad_own, out_grad_own, gate_up_grad_own, down_grad_own = (
        lax.psum_scatter(
            grad_qkv.astype(jnp.bfloat16), "seq", scatter_dimension=0, tiled=True
        ).astype(jnp.float32),
        lax.psum_scatter(
            grad_out_proj.astype(jnp.bfloat16), "seq", scatter_dimension=1, tiled=True
        ).astype(jnp.float32),
        lax.psum_scatter(
            grad_gate_up.astype(jnp.bfloat16), "seq", scatter_dimension=1, tiled=True
        ).astype(jnp.float32),
        lax.psum_scatter(
            grad_down.astype(jnp.bfloat16), "seq", scatter_dimension=1, tiled=True
        ).astype(jnp.float32),
    )
    rate_unit = float(length * seq_size) ** (-0.5)
    qkv_new = apply_update(qkv_master, qkv_grad_own, qkv_moment, qkv_average, rate_qkv * rate_unit)
    out_new = apply_update(out_master, out_grad_own, out_moment, out_average, rate_out * rate_unit)
    gate_up_new = apply_update(
        gate_up_master, gate_up_grad_own, gate_up_moment, gate_up_average, rate_gate_up * rate_unit
    )
    down_new = apply_update(
        down_master, down_grad_own, down_moment, down_average, rate_down * rate_unit
    )
    gains_new = apply_update(
        gains_master, gain_grad_own, gains_moment, gains_average, rate_gains * rate_unit
    )
    return (
        layer_output,
        input_grad,
        qkv_new[0],
        qkv_new[1],
        qkv_new[2],
        qkv_new[3],
        out_new[0],
        out_new[1],
        out_new[2],
        out_new[3],
        gate_up_new[0],
        gate_up_new[1],
        gate_up_new[2],
        gate_up_new[3],
        down_new[0],
        down_new[1],
        down_new[2],
        down_new[3],
        gains_new[0],
        gains_new[1],
        gains_new[2],
        gains_new[3],
    )


AXES = ("y", "c", "h", "l", "x")
RING = ("c", "l", "x")
MESH = pl.DeviceIdType.MESH
ROW = 512
BF = jnp.bfloat16
F32 = jnp.float32
LOG2E = 1.4426950408889634
NT = (((1,), (1,)), ((), ()))
NN = (((1,), (0,)), ((), ()))
TN = (((0,), (0,)), ((), ()))


def ring_plan_fits(mesh):
    return mesh.shape["seq"] == 4 and mesh.shape["tp"] == 8


def device_pairs(target):
    pairs = []
    for index in range(32):
        y, c, h, l, x = (index >> 4) & 1, (index >> 3) & 1, (index >> 2) & 1, (index >> 1) & 1, index & 1
        goal = target(y, c, h, l, x)
        if goal is not None:
            y, c, h, l, x = goal
            pairs.append((index, 16 * y + 8 * c + 4 * h + 2 * l + x))
    return pairs


def move(values, target):
    return lax.ppermute(values, AXES, device_pairs(target))


def flip(values, bits):
    return move(
        values,
        lambda y, c, h, l, x: (
            y ^ ("y" in bits),
            c ^ ("c" in bits),
            h ^ ("h" in bits),
            l ^ ("l" in bits),
            x ^ ("x" in bits),
        ),
    )


def swap_ch(values):
    return move(values, lambda y, c, h, l, x: (y, h, c, l, x))


def rounded(values):
    return values.astype(BF)


def ring_position():
    c, l, x = (lax.axis_index(name) for name in RING)
    partners = ({"x": 1 - x}, {"l": 1 - l}, {"c": 1 - c})
    return 4 * c + 2 * l + x, partners


def enter_ring(partners):
    barrier = pltpu.get_barrier_semaphore()
    for partner in partners:
        pl.semaphore_signal(barrier, inc=1, device_id=partner, device_id_type=MESH)
    pl.semaphore_wait(barrier, len(partners))


def rows_at(block, part=None):
    if part is None:
        return pl.ds(pl.multiple_of(block * ROW, ROW), ROW)
    half = ROW // 2
    return pl.ds(pl.multiple_of(block * ROW + part * half, half), half)


def remote(source, target, sent, received, device):
    return pltpu.make_async_remote_copy(
        src_ref=source,
        dst_ref=target,
        send_sem=sent,
        recv_sem=received,
        device_id=device,
        device_id_type=MESH,
    )


def places():
    y, c, h, l, x = (lax.axis_index(name) for name in AXES)
    return y, c, h, 4 * c + 2 * l + x


def wide_partners():
    y, c, h, _ = places()
    _, (to_x, to_l, to_c) = ring_position()
    mixed = ({**to_x, **to_l}, {**to_x, **to_c}, {**to_l, **to_c}, {**to_x, **to_l, **to_c})
    across = ({"c": 0, "h": 1 - h}, {"c": 1, "h": 1 - h})
    return (to_x, to_l, to_c) + mixed + ({"y": 1 - y},) + across


class Ring:
    def __init__(self, buffer, size, send, recv):
        self.buffer, self.size, self.send, self.recv = buffer, size, send, recv
        me, (to_x, to_l, to_c) = ring_position()
        self.plan = (
            (me, 0, to_x, me ^ 1),
            (me, 1, to_l, me ^ 2),
            (me, None, to_c, me ^ 4),
            (me, 1, to_x, me ^ 1),
            (me, 0, to_l, me ^ 2),
            (me ^ 1, 0, to_l, me ^ 3),
            (me ^ 2, 1, to_x, me ^ 3),
            (me ^ 1, None, to_c, me ^ 5),
            (me ^ 2, None, to_c, me ^ 6),
            (me ^ 3, None, to_c, me ^ 7),
        )

    def copy(self, index, block):
        _, part, partner, _ = self.plan[index]
        size = self.size if part is None else self.size // 2
        first = block * self.size + (size if part == 1 else 0)
        place = self.buffer.at[pl.ds(pl.multiple_of(first, size), size)]
        return remote(place, place, self.send.at[index], self.recv.at[index], partner)

    def start(self, *indices):
        for index in indices:
            self.copy(index, self.plan[index][0]).start()

    def arrived(self, *indices):
        for index in indices:
            self.copy(index, self.plan[index][3]).wait_recv()

    def sent(self):
        for index in range(10):
            self.copy(index, self.plan[index][0]).wait_send()


class Spread:
    def __init__(self, source, target, near, far, keep):
        self.source, self.target, self.near, self.far, self.keep = source, target, near, far, keep
        _, self.c, self.h, _ = places()

    def local(self):
        return pltpu.make_async_copy(self.source, self.target, self.keep)

    def beside(self):
        return remote(self.source, self.target, self.near.at[0], self.near.at[1], {"c": self.h})

    def across(self, core):
        return remote(
            self.source, self.target, self.far.at[2], self.far.at[core], {"c": self.h, "h": 1 - self.h}
        )

    def start(self):
        self.across(self.c).start()

        @pl.when(self.c == self.h)
        def _():
            self.local().start()

        @pl.when(self.c != self.h)
        def _():
            self.beside().start()

    def arrived(self):
        @pl.when(self.c == self.h)
        def _():
            self.local().wait()
            self.beside().wait_recv()

        @pl.when(self.c != self.h)
        def _():
            self.across(0).wait_recv()
            self.across(1).wait_recv()

    def sent(self):
        self.across(self.c).wait_send()

        @pl.when(self.c != self.h)
        def _():
            self.beside().wait_send()


SPREAD_SEMAPHORES = [
    pltpu.SemaphoreType.DMA((4, 2)),
    pltpu.SemaphoreType.DMA((4, 3)),
    pltpu.SemaphoreType.DMA((4,)),
    pltpu.SemaphoreType.DMA((4, 2)),
    pltpu.SemaphoreType.DMA((4, 2)),
]


class First:
    def __init__(self, refs):
        (self.shard, self.grad), (self.whole, self.moved) = refs[:2], refs[2:4]
        self.w, near, far, keep, self.y_send, self.y_recv, self.grad_sems = refs[4:]
        self.y, self.c, self.h, _ = places()
        first = (2 * self.y + self.c) * 512
        self.pieces = [
            Spread(
                self.shard.at[pl.ds(k * 256, 256)],
                self.w.at[pl.ds(pl.multiple_of(first + k * 256, 256), 256)],
                near.at[k],
                far.at[k],
                keep.at[k],
            )
            for k in range(2)
        ]

    def over_y(self, k, core, y):
        first = (2 * y + core) * 512 + k * 256
        place = self.w.at[pl.ds(pl.multiple_of(first, 256), 256)]
        return remote(place, place, self.y_send.at[k, core], self.y_recv.at[k, core], {"y": 1 - self.y})

    def grad_local(self):
        return pltpu.make_async_copy(self.grad, self.moved, self.grad_sems.at[2])

    def grad_remote(self):
        return remote(
            self.grad, self.moved, self.grad_sems.at[0], self.grad_sems.at[1], {"c": self.h, "h": self.c}
        )

    def run(self, ring):
        for piece in self.pieces:
            piece.start()
        for k in range(2):
            self.pieces[k].arrived()
            for core in range(2):
                self.over_y(k, core, self.y).start()
            if k == 0:
                ring.arrived(0)
                ring.start(5)
                ring.arrived(1)
                ring.start(6)

        @pl.when(self.c == self.h)
        def _():
            self.grad_local().start()

        @pl.when(self.c != self.h)
        def _():
            self.grad_remote().start()

        ring.arrived(2, 3)
        ring.start(7)
        ring.arrived(4)
        ring.start(8)
        for k in range(2):
            for core in range(2):
                self.over_y(k, core, 1 - self.y).wait_recv()
        pltpu.make_async_copy(self.w, self.whole, self.grad_sems.at[3]).start()

    def poll(self, step):
        pass

    def finish(self):
        for piece in self.pieces:
            piece.sent()
        for k in range(2):
            for core in range(2):
                self.over_y(k, core, self.y).wait_send()
        pltpu.make_async_copy(self.w, self.whole, self.grad_sems.at[3]).wait()

        @pl.when(self.c == self.h)
        def _():
            self.grad_local().wait()

        @pl.when(self.c != self.h)
        def _():
            self.grad_remote().wait_recv()
            self.grad_remote().wait_send()


class Second:
    def __init__(self, refs):
        self.shard, self.whole = refs[:2]
        near, far, keep, self.y_send, self.y_recv = refs[2:]
        self.y, c, _, _ = places()
        columns = pl.ds(pl.multiple_of((2 * self.y + c) * 512, 512), 512)
        self.pieces = [
            Spread(
                self.shard.at[pl.ds(k * 512, 512)],
                self.whole.at[pl.ds(k * 512, 512), columns],
                near.at[k],
                far.at[k],
                keep.at[k],
            )
            for k in range(2)
        ]

    def over_y(self, k, y):
        place = self.whole.at[pl.ds(k * 512, 512), pl.ds(pl.multiple_of(y * 1024, 1024), 1024)]
        return remote(place, place, self.y_send.at[k, 0], self.y_recv.at[k, 0], {"y": 1 - self.y})

    def run(self, ring):
        for piece in self.pieces:
            piece.start()

    def poll(self, step):
        @pl.when(step == 1)
        def _():
            self.pieces[0].arrived()
            self.over_y(0, self.y).start()

        @pl.when(step == 4)
        def _():
            self.pieces[1].arrived()
            self.over_y(1, self.y).start()

    def finish(self):
        for k in range(2):
            self.pieces[k].sent()
            self.over_y(k, 1 - self.y).wait_recv()
            self.over_y(k, self.y).wait_send()


def gather_kernel(finish, beside, inputs, outputs, *refs):
    own_ref, refs = refs[0], refs[1:]
    given, refs = refs[:inputs], refs[inputs:]
    full_ref, outs, refs = refs[0], refs[1:4], refs[4:]
    extra_outs, refs = refs[:outputs], refs[outputs:]
    buf, res, send, recv, own_sem, full_sem, out_sem = refs[:7]
    me, _ = ring_position()
    load = pltpu.make_async_copy(own_ref, buf.at[rows_at(me)], own_sem)
    load.start()
    enter_ring(wide_partners())
    load.wait()
    ring = Ring(buf, ROW, send, recv)
    ring.start(0, 1, 2, 3, 4)
    early = beside is First
    if early:
        more = First(given[2:] + extra_outs + refs[7:])
        w_ref, tables = more.w, given[:2]
    else:
        more = Second(given[1:] + extra_outs + refs[7:])
        w_ref, tables = given[0], ()
    more.run(ring)

    def step_body(step, carry):
        block = me ^ ((step >> 1) | ((step & 1) << 2))
        rows = rows_at(block)
        if not early:

            @pl.when(step == 1)
            def _():
                ring.arrived(2)

            @pl.when(step == 2)
            def _():
                ring.arrived(0)
                ring.start(5)
                ring.arrived(1)
                ring.start(6)
                ring.arrived(3)
                ring.start(7)
                ring.arrived(4)
                ring.start(8)

        @pl.when(step == 3)
        def _():
            ring.arrived(7)

        @pl.when(step == 5)
        def _():
            ring.arrived(8)

        @pl.when(step == 6)
        def _():
            ring.arrived(5, 6)
            ring.start(9)

        @pl.when(step == 7)
        def _():
            ring.arrived(9)

        more.poll(step)
        pltpu.make_async_copy(buf.at[rows], full_ref.at[rows], full_sem.at[step]).start()
        turn = step & 1

        def out_copy(which, rows):
            return pltpu.make_async_copy(
                res.at[turn, which], outs[which].at[rows], out_sem.at[turn, which]
            )

        @pl.when(step >= 2)
        def _():
            for which in range(3):
                out_copy(which, rows).wait()

        finish(buf, rows, w_ref, tables, res, turn)
        for which in range(3):
            out_copy(which, rows).start()
        return carry

    lax.fori_loop(0, 8, step_body, 0)
    ring.sent()
    more.finish()

    def drain(step, carry):
        rows = rows_at(step)
        pltpu.make_async_copy(buf.at[rows], full_ref.at[rows], full_sem.at[step]).wait()
        return carry

    lax.fori_loop(0, 8, drain, 0)
    for turn in range(2):
        for which in range(3):
            pltpu.make_async_copy(
                res.at[turn, which], outs[which].at[rows_at(0)], out_sem.at[turn, which]
            ).wait()


def feed_forward_finish(buf, rows, w_ref, tables, res, turn):
    def columns(chunk, carry):
        here = pl.multiple_of(chunk * 256, 256)
        block = buf[rows, :]
        g = jnp.dot(block, w_ref[:, pl.ds(here, 256)], preferred_element_type=F32)
        u = jnp.dot(block, w_ref[:, pl.ds(here + 1024, 256)], preferred_element_type=F32)
        res[turn, 0, :, pl.ds(here, 256)] = rounded(g)
        res[turn, 1, :, pl.ds(here, 256)] = rounded(u)
        res[turn, 2, :, pl.ds(here, 256)] = rounded(g * (1.0 / (1.0 + jnp.exp(-g))) * u)
        return carry

    lax.fori_loop(0, 4, columns, 0)


def attention_finish(buf, rows, w_ref, tables, res, turn):
    block = buf[rows, :]
    cs, sn = tables[0][rows, :], tables[1][rows, :]
    for which in range(2):
        m = jnp.dot(block, w_ref[:, which * 256 : which * 256 + 256], preferred_element_type=F32)
        if which == 0:
            m = m * (0.125 * LOG2E)
        m1, m2 = m[:, :128], m[:, 128:]
        res[turn, which, :, 0:128] = rounded(m1 * cs - m2 * sn)
        res[turn, which, :, 128:256] = rounded(m2 * cs + m1 * sn)
    res[turn, 2] = rounded(jnp.dot(block, w_ref[:, 512:768], preferred_element_type=F32))


def gather_product(own, given, anywhere_given, extra_shapes, width, finish, beside, scratch, number):
    anywhere = pl.BlockSpec(memory_space=pl.ANY)
    vmem = pl.BlockSpec(memory_space=pltpu.VMEM)
    length, depth = 8 * ROW, own.shape[1]
    inputs = len(given) + len(anywhere_given)
    return pl.pallas_call(
        lambda *refs: gather_kernel(finish, beside, inputs, len(extra_shapes), *refs),
        in_specs=[anywhere] + [vmem] * len(given) + [anywhere] * len(anywhere_given),
        out_specs=[anywhere] * (4 + len(extra_shapes)),
        out_shape=[jax.ShapeDtypeStruct((length, depth), BF)]
        + [jax.ShapeDtypeStruct((length, width), BF)] * 3
        + [jax.ShapeDtypeStruct(shape, BF) for shape in extra_shapes],
        scratch_shapes=[
            pltpu.VMEM((length, depth), BF),
            pltpu.VMEM((2, 3, ROW, width), BF),
            pltpu.SemaphoreType.DMA((10,)),
            pltpu.SemaphoreType.DMA((10,)),
            pltpu.SemaphoreType.DMA,
            pltpu.SemaphoreType.DMA((8,)),
            pltpu.SemaphoreType.DMA((2, 3)),
        ]
        + scratch,
        compiler_params=pltpu.CompilerParams(
            collective_id=number, has_side_effects=True, vmem_limit_bytes=56 * 2**20
        ),
        cost_estimate=pl.CostEstimate(
            flops=80 * 10**9, bytes_accessed=30 * 2**20, transcendentals=0
        ),
    )(own, *given, *anywhere_given)


def scatter_kernel(dims, beside, a_ref, w_ref, *refs):
    given, refs = refs[:beside], refs[beside:]
    out_ref, refs = refs[0], refs[1:]
    more_outs, refs = refs[: 2 * beside], refs[2 * beside :]
    abuf, mine, other, sums, ra, rb, near_x, near_l, send, recv, a_sem = refs[:11]
    me, partners = ring_position()
    to_x, to_l, to_c = partners
    order = (7, 3, 5, 6, 1, 2, 4, 0)

    def load(index):
        return pltpu.make_async_copy(
            a_ref.at[rows_at(me ^ order[index])], abuf.at[index % 2], a_sem.at[index % 2]
        )

    load(0).start()
    enter_ring(wide_partners() if beside else partners)
    if beside:
        tail = WeightTail(given + more_outs + refs[11:])
        tail.begin()

    def copy(index, source, target, partner):
        return pltpu.make_async_remote_copy(
            src_ref=source,
            dst_ref=target,
            send_sem=send.at[index],
            recv_sem=recv.at[index],
            device_id=partner,
            device_id_type=MESH,
        )

    half = ROW // 2
    top, bottom = pl.ds(0, half), pl.ds(half, half)
    copies = [copy(slot, mine.at[slot], other.at[slot], to_c) for slot in range(4)] + [
        copy(4, sums.at[2, top], ra, to_x),
        copy(5, sums.at[2, bottom], rb, to_l),
        copy(6, sums.at[0, top], near_x.at[top], to_x),
        copy(7, sums.at[1, bottom], near_l.at[bottom], to_l),
        copy(8, sums.at[0, bottom], near_x.at[bottom], to_x),
        copy(9, sums.at[1, top], near_l.at[top], to_l),
    ]

    def product(index, store):
        def columns(chunk, carry):
            here = pl.ds(pl.multiple_of(chunk * 256, 256), 256)
            w = w_ref[here, :] if dims == NT else w_ref[:, here]
            store(
                here, lax.dot_general(abuf[index % 2], w, dims, preferred_element_type=F32)
            )
            return carry

        lax.fori_loop(0, 8, columns, 0)

    for index, slot in enumerate(order):
        load(index).wait()
        if index + 1 < 8:
            load(index + 1).start()
        if slot >= 4:

            def store(here, value, slot=slot):
                mine[slot - 4, :, here] = rounded(value)

            product(index, store)
            copies[slot - 4].start()
        elif slot > 0:
            copies[slot].wait_recv()

            def store(here, value, slot=slot):
                sums[slot - 1, :, here] = rounded(value + other[slot, :, here].astype(F32))

            product(index, store)
            if slot == 3:
                copies[4].start()
                copies[5].start()
            if slot == 1:
                copies[6].start()
            if slot == 2:
                copies[7].start()
                copies[5].wait_recv()
                sums[0, bottom, :] = rounded(
                    sums[0, bottom, :].astype(F32) + rb[...].astype(F32)
                )
                copies[8].start()
                copies[4].wait_recv()
                sums[1, top, :] = rounded(sums[1, top, :].astype(F32) + ra[...].astype(F32))
                copies[9].start()
        else:
            copies[0].wait_recv()

            def store(here, value):
                out_ref[:, here] = value + other[0, :, here].astype(F32)

            product(index, store)
    if beside:
        tail.run()
    for part, first, second in ((top, 6, 9), (bottom, 8, 7)):
        copies[first].wait_recv()
        copies[second].wait_recv()
        out_ref[part, :] = out_ref[part, :] + (
            near_x[part, :].astype(F32) + near_l[part, :].astype(F32)
        )
    for each in copies:
        each.wait_send()
    if beside:
        tail.end()


class WeightTail:
    def __init__(self, refs):
        self.grad, self.totals, self.landing, stage, result, y_sems, z_sems, stage_sems = refs
        self.y, _, _, _ = places()
        self.names = [("Q", 0, 0), ("Q", 1, 0)]
        self.pieces = PieceSums(
            self.names,
            self.piece,
            lambda name: self.landing.at[name[1]],
            lambda name, h: self.totals.at[h],
            y_sems,
            z_sems,
        )
        self.sums = Sums(stage, result, stage_sems)
        for name in self.names:
            self.sums.item(
                0,
                512,
                [self.piece(name, self.y), self.landing.at[name[1]]],
                self.pieces.sends(name),
                [lambda name=name: self.pieces.over_y(name).wait_recv()],
            )

    def piece(self, name, y):
        return self.grad.at[pl.ds(pl.multiple_of((2 * y + name[1]) * 512, 512), 512)]

    def begin(self):
        for name in self.names:
            self.pieces.over_y(name).start()

    def run(self):
        for k in range(2):
            self.sums.load(k)
            self.sums.add(k)

    def end(self):
        self.sums.last_sent()
        self.pieces.end()


def product_scatter(a, weight, dims, number, *grad):
    anywhere = pl.BlockSpec(memory_space=pl.ANY)
    vmem = pl.BlockSpec(memory_space=pltpu.VMEM)
    depth = a.shape[1]
    width = weight.shape[0] if dims == NT else weight.shape[1]
    return pl.pallas_call(
        lambda *refs: scatter_kernel(dims, len(grad), *refs),
        in_specs=[anywhere, vmem] + [anywhere] * len(grad),
        out_specs=[vmem] + [anywhere] * (2 * len(grad)),
        out_shape=[jax.ShapeDtypeStruct((ROW, width), F32)]
        + [jax.ShapeDtypeStruct((2, 512, 768), BF)] * (2 * len(grad)),
        scratch_shapes=[
            pltpu.VMEM((2, ROW, depth), BF),
            pltpu.VMEM((4, ROW, width), BF),
            pltpu.VMEM((4, ROW, width), BF),
            pltpu.VMEM((3, ROW, width), BF),
            pltpu.VMEM((ROW // 2, width), BF),
            pltpu.VMEM((ROW // 2, width), BF),
            pltpu.VMEM((ROW, width), BF),
            pltpu.VMEM((ROW, width), BF),
            pltpu.SemaphoreType.DMA((10,)),
            pltpu.SemaphoreType.DMA((10,)),
            pltpu.SemaphoreType.DMA((2,)),
        ]
        + [
            pltpu.VMEM((2, 2, 512, 768), BF),
            pltpu.VMEM((2, 512, 768), BF),
            pltpu.SemaphoreType.DMA((2, 2)),
            pltpu.SemaphoreType.DMA((3, 2)),
            pltpu.SemaphoreType.DMA((2, 5)),
        ]
        * len(grad),
        compiler_params=pltpu.CompilerParams(
            collective_id=number, has_side_effects=True, vmem_limit_bytes=58 * 2**20
        ),
        cost_estimate=pl.CostEstimate(
            flops=80 * 10**9, bytes_accessed=30 * 2**20, transcendentals=0
        ),
    )(a, weight, *grad)


def column_order():
    column = lax.broadcasted_iota(jnp.int32, (768, 768), 1)
    row = lax.broadcasted_iota(jnp.int32, (768, 768), 0)
    part, within = column // 256, column % 256
    turned = ((within % 128) // 32) * 192 + part * 64 + (within // 128) * 32 + within % 32
    plain = (within // 64) * 192 + 128 + within % 64
    return (row == jnp.where(part == 2, plain, turned)).astype(BF)


def head_lanes_turned(head):
    lane = lax.broadcasted_iota(jnp.int32, (1, 256), 1)
    return (lane % 128) // 32 == head


def head_lanes_plain(head):
    lane = lax.broadcasted_iota(jnp.int32, (1, 256), 1)
    return lane // 64 == head


def picked_block(step, blocks):
    block = jnp.int32(blocks[0])
    for index in range(1, len(blocks)):
        block = jnp.where(step == index, blocks[index], block)
    return block


def mark(*values):
    return sum(value[(0,) * value.ndim].astype(F32) for value in values) * 0.0


def after(values, zero):
    return values + zero.astype(values.dtype)


def held(values, zero):
    if zero is None:
        return values
    return after(lax.optimization_barrier(values), zero)


class Beside:
    def __init__(self, refs):
        self.out_shard, self.gate_up_shard, self.grad_own = refs[:3]
        self.out_full, self.gate_up, self.grad_full, self.rows_own = refs[3:7]
        (
            near,
            far,
            keep,
            self.y_send,
            self.y_recv,
            out_near,
            out_far,
            out_keep,
            self.out_y,
            grad_send,
            grad_recv,
            out_send,
            out_recv,
            self.row_send,
            self.row_recv,
            self.own_sem,
        ) = refs[7:]
        self.y, self.c, self.h, self.me = places()
        _, _, _, l, x = (lax.axis_index(name) for name in AXES)
        s = 2 * self.y + self.c
        self.pieces = [
            Spread(
                self.gate_up_shard.at[pl.ds(k * 128, 128)],
                self.gate_up.at[pl.ds(pl.multiple_of(s * 512 + k * 128, 128), 128)],
                near.at[k],
                far.at[k],
                keep.at[k],
            )
            for k in range(4)
        ]
        heads = 4 * self.h + 2 * l + x
        self.out_piece = Spread(
            self.out_shard,
            self.out_full.at[
                pl.ds(pl.multiple_of(heads * 256, 256), 256), pl.ds(pl.multiple_of(s * 512, 512), 512)
            ],
            out_near,
            out_far,
            out_keep,
        )
        self.grad_ring = Ring(self.grad_full, ROW, grad_send, grad_recv)
        self.out_ring = Ring(self.out_full, 256, out_send, out_recv)

    def over_y(self, k, core, y):
        first = (2 * y + core) * 512 + k * 128
        place = self.gate_up.at[pl.ds(pl.multiple_of(first, 128), 128)]
        return remote(place, place, self.y_send.at[k, core], self.y_recv.at[k, core], {"y": 1 - self.y})

    def out_over_y(self, y):
        place = self.out_full.at[
            pl.ds(pl.multiple_of(self.me * 256, 256), 256), pl.ds(pl.multiple_of(y * 1024, 1024), 1024)
        ]
        return remote(place, place, self.out_y.at[0], self.out_y.at[1], {"y": 1 - self.y})

    def piece_over_y(self, k):
        self.pieces[k].arrived()
        for core in range(2):
            self.over_y(k, core, self.y).start()

    def begin(self):
        own = pltpu.make_async_copy(self.grad_own, self.grad_full.at[rows_at(self.me)], self.own_sem.at[0])
        own.start()
        enter_ring(wide_partners())
        self.out_piece.start()
        self.pieces[0].start()
        own.wait()
        self.grad_ring.start(0, 1, 2, 3, 4)

    def at(self, step):
        def when(number, *actions):
            @pl.when(step == number)
            def _():
                for action in actions:
                    action()

        def out_on():
            self.out_piece.arrived()
            self.out_over_y(self.y).start()

        def out_ring_on():
            self.out_over_y(1 - self.y).wait_recv()
            self.out_ring.start(0, 1, 2, 3, 4)

        def relay(ring):
            ring.arrived(0)
            ring.start(5)
            ring.arrived(1)
            ring.start(6)

        def relay_core(ring):
            ring.arrived(3)
            ring.start(7)
            ring.arrived(4)
            ring.start(8)

        def relay_last(ring):
            ring.arrived(5, 6)
            ring.start(9)

        when(0, self.begin)
        when(3, out_on, self.pieces[1].start)
        when(6, out_ring_on, lambda: relay(self.grad_ring))
        when(9, lambda: self.piece_over_y(0), self.pieces[2].start)
        when(12, lambda: relay_core(self.grad_ring), lambda: relay(self.out_ring))
        when(14, lambda: self.piece_over_y(1), self.pieces[3].start)
        when(18, lambda: relay_core(self.out_ring), lambda: relay_last(self.grad_ring))
        when(20, lambda: self.piece_over_y(2))
        when(25, lambda: relay_last(self.out_ring))
        when(29, lambda: self.piece_over_y(3))

    def row_local(self, block, o_all):
        columns = pl.ds(pl.multiple_of(self.me * 256, 256), 256)
        return pltpu.make_async_copy(
            o_all.at[rows_at(block)], self.rows_own.at[:, columns], self.own_sem.at[1]
        )

    def row_remote(self, block, o_all, sender):
        columns = pl.ds(pl.multiple_of(sender * 256, 256), 256)
        return remote(
            o_all.at[rows_at(block)],
            self.rows_own.at[:, columns],
            self.row_send.at[block],
            self.row_recv.at[sender],
            {"c": block >> 2, "l": (block >> 1) & 1, "x": block & 1},
        )

    def send_rows(self, block, o_all):
        @pl.when(block == self.me)
        def _():
            self.row_local(block, o_all).start()

        @pl.when(block != self.me)
        def _():
            self.row_remote(block, o_all, self.me).start()

    def end(self, o_all):
        self.out_piece.sent()
        self.out_over_y(self.y).wait_send()
        for k in range(4):
            self.pieces[k].sent()
            for core in range(2):
                self.over_y(k, core, self.y).wait_send()
                self.over_y(k, core, 1 - self.y).wait_recv()
        for ring in (self.grad_ring, self.out_ring):
            ring.arrived(2, 7, 8, 9)
            ring.sent()

        def each(block, carry):
            @pl.when(block == self.me)
            def _():
                self.row_local(block, o_all).wait()

            @pl.when(block != self.me)
            def _():
                self.row_remote(block, o_all, self.me).wait_send()
                self.row_remote(block, o_all, block).wait_recv()

            return carry

        lax.fori_loop(0, 8, each, 0)


def attend_kernel(q_ref, k_ref, v_ref, out_shard, gate_up_shard, grad_own, o_ref, l_ref, *refs):
    beside = Beside((out_shard, gate_up_shard, grad_own) + refs[:4] + refs[8:])
    s_scr, m_scr, acc_scr, o_all = refs[4:8]
    head = pl.program_id(1)
    step = pl.program_id(0) * 4 + head
    block = 7 - pl.program_id(0)
    beside.at(step)
    row = lax.broadcasted_iota(jnp.int32, (ROW, ROW), 0)
    col = lax.broadcasted_iota(jnp.int32, (ROW, ROW), 1)

    def lane_max(s):
        return jnp.maximum(
            jnp.maximum(s[:, :128], s[:, 128:256]), jnp.maximum(s[:, 256:384], s[:, 384:])
        )

    def lane_sum(s):
        return (s[:, :128] + s[:, 128:256]) + (s[:, 256:384] + s[:, 384:])

    def keys_at(key_block):
        return pl.ds(pl.multiple_of(key_block * ROW, ROW), ROW)

    q = q_ref[...]
    qh = jnp.where(head_lanes_turned(head), q, jnp.zeros_like(q))

    def scores(key_block):
        return lax.dot_general(qh, k_ref[keys_at(key_block), :], NT, preferred_element_type=F32)

    s = jnp.where(col <= row, scores(block), masked_score)
    s_scr[block] = s
    m_scr[...] = lane_max(s)

    def first_pass(key_block, carry):
        s = scores(key_block)
        s_scr[key_block] = s
        m_scr[...] = jnp.maximum(m_scr[...], lane_max(s))
        return carry

    lax.fori_loop(0, block, first_pass, 0)
    top = jnp.max(m_scr[...], axis=1, keepdims=True)
    m_scr[...] = jnp.zeros_like(m_scr)
    acc_scr[...] = jnp.zeros_like(acc_scr)

    def second_pass(key_block, carry):
        e = jnp.exp2(s_scr[key_block] - top)
        m_scr[...] += lane_sum(e)
        acc_scr[...] += lax.dot_general(
            e.astype(BF), v_ref[keys_at(key_block), :], NN, preferred_element_type=F32
        )
        return carry

    lax.fori_loop(0, block + 1, second_pass, 0)
    total = jnp.sum(m_scr[...], axis=1, keepdims=True)
    part = rounded(acc_scr[...] * (1.0 / total))
    rows = rows_at(block)

    @pl.when(head == 0)
    def _():
        o_all[rows, :] = part

    @pl.when(head > 0)
    def _():
        o_all[rows, :] = jnp.where(head_lanes_plain(head), part, o_all[rows, :])

    level = jnp.transpose(jnp.broadcast_to(top + jnp.log2(total), (ROW, 128)))[0:4, :]
    row4 = lax.broadcasted_iota(jnp.int32, (4, ROW), 0)
    l_ref[0] = jnp.where(row4 == head, level, l_ref[0])

    @pl.when(head == 3)
    def _():
        o_ref[...] = o_all[rows, :]
        beside.send_rows(block, o_all)

    @pl.when(step == 31)
    def _():
        beside.end(o_all)


def attend(q, k, v, out_shard, gate_up_shard, grad_own):
    length = q.shape[0]
    blocks = length // ROW
    whole = pl.BlockSpec((length, 256), lambda i, head: (0, 0))
    anywhere = pl.BlockSpec(memory_space=pl.ANY)
    dma = pltpu.SemaphoreType.DMA
    return pl.pallas_call(
        attend_kernel,
        grid=(blocks, 4),
        in_specs=[pl.BlockSpec((ROW, 256), lambda i, head: (7 - i, 0)), whole, whole] + [anywhere] * 3,
        out_specs=[
            pl.BlockSpec((ROW, 256), lambda i, head: (7 - i, 0)),
            pl.BlockSpec((1, 4, ROW), lambda i, head: (7 - i, 0, 0)),
        ]
        + [anywhere] * 4,
        out_shape=[
            jax.ShapeDtypeStruct((length, 256), BF),
            jax.ShapeDtypeStruct((blocks, 4, ROW), F32),
            jax.ShapeDtypeStruct((2048, 2048), BF),
            jax.ShapeDtypeStruct((2048, 2048), BF),
            jax.ShapeDtypeStruct((length, 2048), BF),
            jax.ShapeDtypeStruct((ROW, 2048), BF),
        ],
        scratch_shapes=[
            pltpu.VMEM((blocks, ROW, ROW), F32),
            pltpu.VMEM((ROW, 128), F32),
            pltpu.VMEM((ROW, 256), F32),
            pltpu.VMEM((length, 256), BF),
        ]
        + SPREAD_SEMAPHORES
        + [dma((2,)), dma((3,)), dma, dma((2,))]
        + [dma((10,))] * 4
        + [dma((8,)), dma((8,)), dma((2,))],
        compiler_params=pltpu.CompilerParams(
            collective_id=6, has_side_effects=True, vmem_limit_bytes=48 * 2**20
        ),
        cost_estimate=pl.CostEstimate(
            flops=14 * 10**9 * blocks, bytes_accessed=10 * 2**20, transcendentals=0
        ),
    )(q, k, v, out_shard, gate_up_shard, grad_own)


KEYS = 256


class Sums:
    def __init__(self, stage, result, stage_sems):
        self.stage, self.result, self.stage_sems = stage, result, stage_sems
        self.items = []

    def item(self, due, rows, terms, sends, waits=(), extra=None, then=None):
        self.items.append((due, rows, terms, sends, waits, extra, then))

    def loads(self, k):
        _, rows, terms, _, _, extra, _ = self.items[k]
        turn = k % 2
        copies = [
            pltpu.make_async_copy(
                term, self.stage.at[turn, index, pl.ds(0, rows)], self.stage_sems.at[turn, index]
            )
            for index, term in enumerate(terms)
        ]
        if extra is not None:
            copies.append(pltpu.make_async_copy(extra[0], extra[1], self.stage_sems.at[turn, 4]))
        return copies

    def load(self, k):
        for wait in self.items[k][4]:
            wait()
        for copy in self.loads(k):
            copy.start()

    def add(self, k):
        _, rows, terms, sends, _, extra, then = self.items[k]
        turn = k % 2
        for copy in self.loads(k):
            copy.wait()
        if k >= 2:
            self.sent(k - 2)
        target = self.result.at[turn]
        size = rows // 8

        def chunk(index, carry):
            here = pl.ds(pl.multiple_of(index * size, size), size)
            total = self.stage[turn, 0, here, :].astype(F32)
            for term in range(1, len(terms)):
                total += self.stage[turn, term, here, :].astype(F32)
            if extra is not None:
                total += extra[1][here, :]
            target[here, :] = rounded(total)
            return carry

        lax.fori_loop(0, 8, chunk, 0)
        for here, away, local in sends(self.result.at[turn, pl.ds(0, rows)]):
            self.either(here, away, local, "start")
        if then is not None:
            then()

    def either(self, here, away, local, method):
        if here is None:
            getattr(away(), method)()
            return

        @pl.when(here)
        def _():
            getattr(local(), "wait" if method == "wait_send" else method)()

        @pl.when(jnp.logical_not(here))
        def _():
            getattr(away(), method)()

    def sent(self, k):
        _, rows, _, sends, _, _, _ = self.items[k]
        for here, away, local in sends(self.result.at[k % 2, pl.ds(0, rows)]):
            self.either(here, away, local, "wait_send")

    def poll(self, unit):
        for k, item in enumerate(self.items):

            @pl.when(unit == item[0])
            def _(k=k):
                self.load(k)

            @pl.when(unit == item[0] + 1)
            def _(k=k):
                self.add(k)

    def last_sent(self):
        for k in range(len(self.items) - 2, len(self.items)):
            self.sent(k)


def half_columns(half):
    return pl.ds(half * 1024, 1024)


class RingSum:
    def __init__(self, parts, size, core_land, far_land, core_sems, far_sems):
        self.parts, self.size, self.core_land, self.far_land = parts, size, core_land, far_land
        self.core_sems, self.far_sems = core_sems, far_sems
        self.me, (self.to_x, self.to_l, self.to_c) = ring_position()

    def block(self, slot):
        return pl.ds(pl.multiple_of((self.me ^ slot) * self.size, self.size), self.size)

    def core(self, slot):
        return remote(
            self.parts.at[self.block(slot | 4)],
            self.core_land.at[slot],
            self.core_sems.at[0, slot],
            self.core_sems.at[1, slot],
            self.to_c,
        )

    def begin(self):
        for slot in (3, 1, 2, 0):
            self.core(slot).start()

    def far(self, index, source):
        device = self.to_x if index in (0, 2, 4) else self.to_l
        return remote(
            source, self.far_land.at[index], self.far_sems.at[0, index], self.far_sems.at[1, index], device
        )

    def landed(self, index):
        return lambda: self.far(index, self.far_land.at[index]).wait_recv()

    def terms(self, slot, half):
        return [
            self.parts.at[self.block(slot), half_columns(half)],
            self.core_land.at[slot, :, half_columns(half)],
        ]

    def add_to(self, sums, due, last_sends, extra):
        def items():
            core = lambda slot: (lambda: self.core(slot).wait_recv())
            send = lambda index: (lambda source: [(None, lambda: self.far(index, source), None)])
            yield 0, self.terms(3, 0), send(0), [core(3)], None
            yield 1, self.terms(3, 1), send(1), [], None
            yield 2, self.terms(1, 0), send(2), [core(1)], None
            yield 3, self.terms(2, 1), send(3), [core(2)], None
            yield 4, self.terms(1, 1) + [self.far_land.at[1]], send(4), [self.landed(1)], None
            yield 5, self.terms(2, 0) + [self.far_land.at[0]], send(5), [self.landed(0)], None
            yield (
                6,
                self.terms(0, 0) + [self.far_land.at[2], self.far_land.at[5]],
                last_sends(0),
                [core(0), self.landed(2), self.landed(5)],
                extra(0),
            )
            yield (
                7,
                self.terms(0, 1) + [self.far_land.at[4], self.far_land.at[3]],
                last_sends(1),
                [self.landed(4), self.landed(3)],
                extra(1),
            )

        return [
            (due[index], self.size, terms, sends, waits, more) for index, terms, sends, waits, more in items()
        ]

    def end(self):
        for slot in range(4):
            self.core(slot).wait_send()


class PieceSums:
    def __init__(self, names, piece, landing, sums_at, y_sems, z_sems):
        self.names, self.piece, self.landing, self.sums_at = names, piece, landing, sums_at
        self.y_sems, self.z_sems = y_sems, z_sems
        self.y, self.c, self.h, _ = places()

    def core_of(self, name):
        return name[1]

    def over_y(self, name):
        index = self.names.index(name)
        return remote(
            self.piece(name, 1 - self.y),
            self.landing(name),
            self.y_sems.at[0, index],
            self.y_sems.at[1, index],
            {"y": 1 - self.y},
        )

    def group(self, name):
        groups = []
        for each in self.names:
            key = (each[0], each[2])
            if key not in groups:
                groups.append(key)
        return groups.index((name[0], name[2])), groups

    def over_z(self, name, h, source):
        index = self.names.index(name)
        target = self.sums_at(name, h)
        return (
            lambda: remote(
                source,
                target,
                self.z_sems.at[0, index],
                self.z_sems.at[1 + h, self.group(name)[0]],
                {"c": self.core_of(name), "h": self.c},
            ),
            lambda: pltpu.make_async_copy(source, target, self.z_sems.at[0, index]),
        )

    def sends(self, name):
        here = jnp.logical_and(self.core_of(name) == self.c, self.h == self.c)
        return lambda source: [(here, *self.over_z(name, self.h, source))]

    def end(self):
        for name in self.names:
            self.over_y(name).wait_send()
        self.owned()

    def owned(self):
        seen = []
        for name in self.names:
            group, _ = self.group(name)
            if group in seen:
                continue
            seen.append(group)
            for h in range(2):
                here = jnp.logical_and(h == self.h, self.c == self.h)

                @pl.when(jnp.logical_not(here))
                def _(name=name, h=h):
                    self.over_z(name, h, self.sums_at(name, h))[0]().wait_recv()


class BesideBack:
    def __init__(self, refs):
        self.heads_own, self.parts, self.gate_up, self.down, self.out, self.residual, self.cos, self.sin = refs[:8]
        (
            self.gate_up_sums,
            self.down_sums,
            self.out_sums,
            self.layer,
            core_land,
            far_land,
            self.y_land,
            out_core_land,
            out_far_land,
            self.out_own,
            self.out_y_land,
        ) = refs[8:19]
        (
            self.do,
            self.cs,
            self.sn,
            stage,
            result,
            self.rest,
            self.row_send,
            self.row_recv,
            core_sems,
            far_sems,
            out_core_sems,
            out_far_sems,
            self.layer_sems,
            y_sems,
            z_sems,
            self.out_sems,
            out_y_sems,
            out_z_sems,
            stage_sems,
            self.own_sem,
        ) = refs[19:]
        self.y, self.c, self.h, self.me = places()
        self.sums = Sums(stage, result, stage_sems)
        self.layer_ring = RingSum(self.parts, ROW, core_land, far_land, core_sems, far_sems)
        self.out_ring = RingSum(self.out, 256, out_core_land, out_far_land, out_core_sems, out_far_sems)
        names = [("D", 0, 0), ("D", 1, 0), ("G", 0, 0), ("G", 0, 1), ("G", 1, 0), ("G", 1, 1)]
        self.pieces = PieceSums(names, self.piece, lambda name: self.y_land.at[names.index(name)], self.sums_at, y_sems, z_sems)
        self.names = names
        out_names = [("O", 0, 0), ("O", 1, 0)]
        self.out_pieces = PieceSums(out_names, None, None, self.sums_at, out_y_sems, out_z_sems)
        work = self.layer_ring.add_to(
            self.sums, (8, 9, 10, 11, 25, 26, 46, 47), self.layer_sends, self.residual_half
        )
        work += self.out_ring.add_to(
            self.sums, (28, 29, 30, 31, 51, 52, 63, 64), self.out_sends, lambda half: None
        )
        for name, due in zip(names, (13, 24, 36, 48, 58, 69)):
            work.append((due, ROW, [self.piece(name, self.y), self.y_land.at[names.index(name)]], self.pieces.sends(name), [self.arrived(name)], None))
        work.sort(key=lambda item: item[0])
        for item in work:
            self.sums.item(*item)

    def arrived(self, name):
        def wait():
            self.pieces.over_y(name).wait_recv()
            place = self.names.index(name) + 2
            if place < 6:
                self.pieces.over_y(self.names[place]).start()

        return wait

    def residual_half(self, half):
        return (self.residual.at[:, half_columns(half)], self.rest)

    def layer_sends(self, half):
        def sends(source):
            target = self.layer.at[:, half_columns(half)]
            return [
                (
                    self.c == self.h,
                    lambda: remote(
                        source,
                        target,
                        self.layer_sems.at[0, half],
                        self.layer_sems.at[1, half],
                        {"c": self.h, "h": self.c},
                    ),
                    lambda: pltpu.make_async_copy(source, target, self.layer_sems.at[0, half]),
                )
            ]

        return sends

    def out_sends(self, half):
        def sends(source):
            return [
                (
                    self.y == half,
                    lambda: remote(
                        source, self.out_y_land, self.out_sems.at[half], self.out_sems.at[2], {"y": 1 - self.y}
                    ),
                    lambda: pltpu.make_async_copy(source, self.out_own, self.out_sems.at[half]),
                )
            ]

        return sends

    def piece(self, name, y):
        kind, core, half = name
        rows = pl.ds(pl.multiple_of((2 * y + core) * 512, 512), 512)
        if kind == "G":
            return self.gate_up.at[rows, half_columns(half)]
        return self.down.at[rows]

    def sums_at(self, name, h):
        kind, _, half = name
        if kind == "G":
            return self.gate_up_sums.at[h, :, half_columns(half)]
        return self.down_sums.at[h] if kind == "D" else self.out_sums.at[h]

    def tables(self):
        return (
            pltpu.make_async_copy(self.cos, self.cs, self.own_sem.at[0]),
            pltpu.make_async_copy(self.sin, self.sn, self.own_sem.at[1]),
        )

    def row_local(self):
        columns = pl.ds(pl.multiple_of(self.me * 256, 256), 256)
        return pltpu.make_async_copy(
            self.heads_own.at[:, columns], self.do.at[rows_at(self.me)], self.own_sem.at[2]
        )

    def row_remote(self, block, sender):
        columns = pl.ds(pl.multiple_of(block * 256, 256), 256)
        return remote(
            self.heads_own.at[:, columns],
            self.do.at[rows_at(sender)],
            self.row_send.at[block],
            self.row_recv.at[sender],
            {"c": block >> 2, "l": (block >> 1) & 1, "x": block & 1},
        )

    def begin(self):
        for copy in self.tables():
            copy.start()
        self.row_local().start()
        enter_ring(wide_partners())

        def send(index, carry):
            block = 7 - index

            @pl.when(block != self.me)
            def _():
                self.row_remote(block, self.me).start()

            return carry

        lax.fori_loop(0, 8, send, 0)
        self.layer_ring.begin()
        self.out_ring.begin()
        for name in self.names[:2]:
            self.pieces.over_y(name).start()
        for copy in self.tables():
            copy.wait()

    def rows_there(self, block):
        @pl.when(block == self.me)
        def _():
            self.row_local().wait()

        @pl.when(block != self.me)
        def _():
            self.row_remote(block, block).wait_recv()

    def poll(self, unit):
        self.sums.poll(unit)

    def end(self):
        def each(block, carry):
            @pl.when(block != self.me)
            def _():
                self.row_remote(block, self.me).wait_send()

            return carry

        lax.fori_loop(0, 8, each, 0)
        self.sums.last_sent()
        remote(
            self.out_own, self.out_y_land, self.out_sems.at[0], self.out_sems.at[2], {"y": 1 - self.y}
        ).wait_recv()
        terms = [self.out_own, self.out_y_land]
        count = len(self.sums.items)

        def owners(source):
            sends = []
            for name in self.out_pieces.names:
                part = source.at[:, pl.ds(name[1] * 512, 512)]
                sends += self.out_pieces.sends(name)(part)
            return sends

        self.sums.item(0, 256, terms, owners)
        self.sums.load(count)
        for copy in self.sums.loads(count):
            copy.wait()
        turn = count % 2
        total = self.sums.stage[turn, 0, 0:256, :].astype(F32) + self.sums.stage[turn, 1, 0:256, :].astype(F32)
        self.sums.result[turn, 0:256, :] = rounded(total)
        for here, away, local in owners(self.sums.result.at[turn, pl.ds(0, 256)]):
            self.sums.either(here, away, local, "start")
        self.layer_ring.end()
        self.out_ring.end()
        self.pieces.end()
        for here, away, local in owners(self.sums.result.at[turn, pl.ds(0, 256)]):
            self.sums.either(here, away, local, "wait_send")
        self.out_pieces.owned()

        @pl.when(self.c != self.h)
        def _():
            for half in range(2):
                remote(
                    self.layer.at[:, half_columns(half)],
                    self.layer.at[:, half_columns(half)],
                    self.layer_sems.at[0, half],
                    self.layer_sems.at[1, half],
                    {"c": self.h, "h": self.c},
                ).wait_recv()


def attend_back_kernel(q_ref, k_ref, v_ref, o_ref, l_ref, *refs):
    given, (dkv_ref, dq_out), outs = refs[:8], refs[8:10], refs[10:21]
    qm, dom, delta, dq, dk, dv, km, pt, dst = refs[21:30]
    beside = BesideBack(given + outs + refs[30:])
    heads = 4
    i, sub = pl.program_id(0), pl.program_id(1)
    block = 7 - i
    blocks = 8
    unit = i * (i + 1) + sub * (i + 1)
    rows_here = rows_at(block)

    @pl.when(jnp.logical_and(i == 0, sub == 0))
    def _():
        beside.begin()

    @pl.when(sub == 0)
    def _():
        beside.rows_there(block)
        q = q_ref[...]
        do = beside.do[rows_here, :]
        for head in range(heads):
            part = slice(head * ROW, (head + 1) * ROW)
            qm[block, part, :] = jnp.where(head_lanes_turned(head), q, jnp.zeros_like(q))
            dom[block, part, :] = jnp.where(head_lanes_plain(head), do, jnp.zeros_like(do))
        product = do.astype(F32) * o_ref[...].astype(F32)
        high = rounded(product)
        low = rounded(product - high.astype(F32))
        head_row = lax.broadcasted_iota(jnp.int32, (8, 256), 0)
        lane = lax.broadcasted_iota(jnp.int32, (8, 256), 1)
        pick = jnp.where(lane // 64 == head_row, 1.0, 0.0).astype(BF)
        sums = lax.dot_general(pick, high, NT, preferred_element_type=F32)
        sums += lax.dot_general(pick, low, NT, preferred_element_type=F32)
        delta[block] = sums[:heads, :]
        dq[rows_here, :] = jnp.zeros((ROW, 256), F32)

    beside.poll(unit)
    key_row = lax.broadcasted_iota(jnp.int32, (KEYS, ROW), 0)
    query_col = lax.broadcasted_iota(jnp.int32, (KEYS, ROW), 1)
    inner = pl.multiple_of(sub * KEYS, KEYS)
    k = k_ref[pl.ds(inner, KEYS), :]
    v = v_ref[pl.ds(inner, KEYS), :]
    for head in range(heads):
        km[head] = jnp.where(head_lanes_turned(head), k, jnp.zeros_like(k))
    dk[...] = jnp.zeros_like(dk)
    dv[...] = jnp.zeros_like(dv)

    def query_part(place, diagonal):
        rows = rows_at(place)
        for head in range(heads):
            part = slice(head * ROW, (head + 1) * ROW)
            st = lax.dot_general(k, qm[place, part, :], NT, preferred_element_type=F32)
            dp = lax.dot_general(v, dom[place, part, :], NT, preferred_element_type=F32)
            p = jnp.exp2(st - l_ref[place, head : head + 1, :])
            if diagonal:
                p = jnp.where(key_row + inner <= query_col, p, 0.0)
            ds = p * (dp - delta[place, head : head + 1, :])
            pt[:, part] = p.astype(BF)
            dst[:, part] = ds.astype(BF)
        dv[...] += lax.dot_general(pt[...], dom[place], NN, preferred_element_type=F32)
        dk[...] += lax.dot_general(dst[...], qm[place], NN, preferred_element_type=F32)
        total = lax.dot_general(dst[:, 0:ROW], km[0], TN, preferred_element_type=F32)
        for head in range(1, heads):
            part = slice(head * ROW, (head + 1) * ROW)
            total += lax.dot_general(dst[:, part], km[head], TN, preferred_element_type=F32)
        dq[rows, :] += total

    query_part(block, True)

    def later(query_block, carry):
        beside.poll(unit + query_block - block)
        query_part(query_block, False)
        return carry

    lax.fori_loop(block + 1, blocks, later, 0)
    table = pl.ds(pl.multiple_of(block * ROW + inner, KEYS), KEYS)
    cs, sn = beside.cs[table, :], beside.sn[table, :]
    d = dk[...] * (1.0 / LOG2E)
    d1, d2 = d[:, :128], d[:, 128:]
    dkv_ref[pl.ds(inner, KEYS), 0:128] = rounded(d1 * cs + d2 * sn)
    dkv_ref[pl.ds(inner, KEYS), 128:256] = rounded(d2 * cs - d1 * sn)
    dkv_ref[pl.ds(inner, KEYS), 256:512] = rounded(dv[...])

    @pl.when(jnp.logical_and(i == 7, sub == 1))
    def _():
        def finish(place, carry):
            rows = rows_at(place)
            cs, sn = beside.cs[rows, :], beside.sn[rows, :]
            d = dq[rows, :] * 0.125
            d1, d2 = d[:, :128], d[:, 128:]
            beside.do[rows, 0:128] = rounded(d1 * cs + d2 * sn)
            beside.do[rows, 128:256] = rounded(d2 * cs - d1 * sn)
            return carry

        lax.fori_loop(0, blocks, finish, 0)
        copy = pltpu.make_async_copy(beside.do, dq_out, beside.own_sem.at[4])
        copy.start()
        copy.wait()
        beside.end()


def attend_back(q, k, v, o, level, heads_own, parts, gate_up, down, out, residual, cos, sin):
    length = q.shape[0]
    blocks = length // ROW
    dma = pltpu.SemaphoreType.DMA
    anywhere = pl.BlockSpec(memory_space=pl.ANY)

    def key_spec(width):
        return pl.BlockSpec((ROW, width), lambda i, sub: (7 - i, 0))

    shapes = [
        (2, 512, 2048),
        (2, 512, 1024),
        (2, 256, 512),
        (ROW, 2048),
        (4, ROW, 2048),
        (6, ROW, 1024),
        (6, 512, 1024),
        (4, 256, 2048),
        (6, 256, 1024),
        (256, 1024),
        (256, 1024),
    ]
    return pl.pallas_call(
        attend_back_kernel,
        grid=(blocks, 2),
        in_specs=[key_spec(256)] * 4
        + [pl.BlockSpec((blocks, 4, ROW), lambda i, sub: (0, 0, 0))]
        + [anywhere] * 8,
        out_specs=[key_spec(512)] + [anywhere] * (1 + len(shapes)),
        out_shape=[jax.ShapeDtypeStruct((length, 512), BF), jax.ShapeDtypeStruct((length, 256), BF)]
        + [jax.ShapeDtypeStruct(shape, BF) for shape in shapes],
        scratch_shapes=[
            pltpu.VMEM((blocks, 4 * ROW, 256), BF),
            pltpu.VMEM((blocks, 4 * ROW, 256), BF),
            pltpu.VMEM((blocks, 4, ROW), F32),
            pltpu.VMEM((length, 256), F32),
            pltpu.VMEM((KEYS, 256), F32),
            pltpu.VMEM((KEYS, 256), F32),
            pltpu.VMEM((4, KEYS, 256), BF),
            pltpu.VMEM((KEYS, 4 * ROW), BF),
            pltpu.VMEM((KEYS, 4 * ROW), BF),
            pltpu.VMEM((length, 256), BF),
            pltpu.VMEM((length, 128), F32),
            pltpu.VMEM((length, 128), F32),
            pltpu.VMEM((2, 4, ROW, 1024), BF),
            pltpu.VMEM((2, ROW, 1024), BF),
            pltpu.VMEM((ROW, 1024), F32),
            dma((8,)),
            dma((8,)),
            dma((2, 4)),
            dma((2, 6)),
            dma((2, 4)),
            dma((2, 6)),
            dma((2, 2)),
            dma((2, 6)),
            dma((3, 6)),
            dma((3,)),
            dma((2, 2)),
            dma((3, 2)),
            dma((2, 5)),
            dma((5,)),
        ],
        compiler_params=pltpu.CompilerParams(
            collective_id=7, has_side_effects=True, vmem_limit_bytes=60 * 2**20
        ),
        cost_estimate=pl.CostEstimate(
            flops=19 * 10**9 * blocks, bytes_accessed=20 * 2**20, transcendentals=0
        ),
    )(q, k, v, o, level, heads_own, parts, gate_up, down, out, residual, cos, sin)


def ring_shards(
    layer_input,
    cotangent,
    counts,
    positions,
    qkv_master,
    qkv_moment,
    qkv_average,
    out_master,
    out_moment,
    out_average,
    gate_up_master,
    gate_up_moment,
    gate_up_average,
    down_master,
    down_moment,
    down_average,
    gains_master,
    gains_moment,
    gains_average,
):
    y, c, h, l, x = (lax.axis_index(name) for name in AXES)
    own = 4 * c + 2 * l + x
    plain_y, plain_c, straight = y == 0, c == 0, c == h

    def both_y(mine, other, axis):
        return jnp.where(
            plain_y,
            jnp.concatenate([mine, other], axis=axis),
            jnp.concatenate([other, mine], axis=axis),
        )

    def both_cores(mine, other):
        return jnp.where(plain_c, mine, other), jnp.where(plain_c, other, mine)

    turn = column_order()
    rows_in = swap_ch(layer_input).astype(F32)
    gains_here = gains_master.astype(BF)
    gains_near = jnp.concatenate(both_cores(gains_here, flip(gains_here, "c")), axis=1)
    gains_all = both_y(gains_near, flip(gains_near, "y"), 1).astype(F32)
    gain_first, gain_second = gains_all[0], gains_all[1]
    qkv_shard = jnp.dot(qkv_master.astype(BF), turn, preferred_element_type=F32).astype(BF)
    scale_first = rms_scale(rows_in)
    normed_own = (rows_in * scale_first * gain_first).astype(BF)
    frequency = rope_theta ** (
        -((jnp.arange(128, dtype=jnp.int32) % 32).astype(F32) * 2.0) / HD
    )
    positions_here = jnp.where(straight, positions, flip(positions, "c"))
    angles = positions_here.astype(F32)[:, None] * frequency[None, :]
    cosine, sine = jnp.cos(angles), jnp.sin(angles)
    count_here = counts.astype(F32)
    count_total = count_here + flip(count_here, "c")
    count_total = count_total + flip(count_total, "y")
    grad_here = (4.0 * count_here[0] / count_total[0] * cotangent.astype(F32)).astype(BF)
    normed, queries, keys, values, qkv_weight, grad_own = gather_product(
        normed_own,
        (cosine, sine),
        (qkv_shard, grad_here),
        ((2048, 768), (ROW, 2048)),
        256,
        attention_finish,
        First,
        [pltpu.VMEM((2048, 768), BF)] + SPREAD_SEMAPHORES + [pltpu.SemaphoreType.DMA((4,))],
        1,
    )
    gate_up_shard = jnp.concatenate([gate_up_master[0], gate_up_master[1]], axis=1).astype(BF)
    attended, level, out_weight, gate_up_weight, grad_out, attended_own = attend(
        queries, keys, values, out_master.astype(BF), gate_up_shard, grad_own
    )
    grad_rows = grad_own.astype(F32)
    residual = rows_in + jnp.dot(attended_own, out_weight, preferred_element_type=F32)
    scale_second = rms_scale(residual)
    normed_second, gate, up, activation, down_weight = gather_product(
        (residual * scale_second * gain_second).astype(BF),
        (gate_up_weight,),
        (down_master.astype(BF),),
        ((1024, 2048),),
        1024,
        feed_forward_finish,
        Second,
        SPREAD_SEMAPHORES,
        2,
    )

    grad_act = lax.dot_general(grad_out, down_weight, NT, preferred_element_type=F32)
    g = gate.astype(F32)
    sigmoid = jax.nn.sigmoid(g)
    grad_gate = (grad_act * up.astype(F32) * sigmoid * (1.0 + g * (1.0 - sigmoid))).astype(BF)
    grad_up = (grad_act * g * sigmoid).astype(BF)
    grad_gate_up = jnp.concatenate([grad_gate, grad_up], axis=1)
    grad_normed_second = product_scatter(grad_gate_up, gate_up_weight, NT, 3)[0]
    gate_up_grad = lax.dot_general(
        normed_second, grad_gate_up, TN, preferred_element_type=F32
    ).astype(BF)
    down_grad = lax.dot_general(grad_out, activation, TN, preferred_element_type=F32).astype(BF)
    layer_parts = jnp.dot(activation, down_weight, preferred_element_type=F32).astype(BF)

    def norm_grad(values, scale, gain, grad):
        scaled = grad * gain
        back = scale * (
            scaled - values * scale * scale * jnp.mean(scaled * values, axis=-1, keepdims=True)
        )
        return back, jnp.sum(grad * values * scale, axis=0)

    residual_grad, gain_second_part = norm_grad(
        residual, scale_second, gain_second, grad_normed_second
    )
    residual_grad = residual_grad + grad_rows
    residual_low = residual_grad.astype(BF)
    grad_heads = lax.dot_general(residual_low, out_weight, NT, preferred_element_type=F32).astype(BF)
    out_grad = lax.dot_general(attended_own, residual_low, TN, preferred_element_type=F32).astype(BF)
    grad_kv, grad_q, gate_up_sums, down_sums, out_sums, layer_output, *_ = attend_back(
        queries, keys, values, attended, level, grad_heads, layer_parts, gate_up_grad, down_grad, out_grad, residual, cosine, sine
    )
    gate_up_grad_own = gate_up_sums[0].astype(F32) + gate_up_sums[1].astype(F32)
    down_grad_own = (down_sums[0].astype(F32) + down_sums[1].astype(F32)).T
    out_grad_own = out_sums[0].astype(F32) + out_sums[1].astype(F32)

    grad_mixture = jnp.concatenate([grad_q, grad_kv], axis=1)
    qkv_grad = lax.dot_general(normed, grad_mixture, TN, preferred_element_type=F32).astype(BF)
    qkv_grad = lax.dot_general(qkv_grad, turn, NT, preferred_element_type=F32).astype(BF)
    grad_normed_first, qkv_sums, _ = product_scatter(grad_mixture, qkv_weight, NT, 5, qkv_grad)
    qkv_grad_own = qkv_sums[0].astype(F32) + qkv_sums[1].astype(F32)

    input_back, gain_first_part = norm_grad(rows_in, scale_first, gain_first, grad_normed_first)
    input_grad = swap_ch((residual_grad + input_back).astype(BF)).astype(F32)

    gain_grads = jnp.stack([gain_first_part, gain_second_part])
    for bit in "xlchy":
        gain_grads = gain_grads + flip(gain_grads, bit)
    gain_grad_own = lax.dynamic_slice_in_dim(gain_grads, (2 * y + c) * 512, 512, 1)

    rate_unit = float(4 * 8 * ROW) ** (-0.5)
    qkv_new = apply_update(qkv_master, qkv_grad_own, qkv_moment, qkv_average, rate_qkv * rate_unit)
    out_new = apply_update(out_master, out_grad_own, out_moment, out_average, rate_out * rate_unit)
    gate_up_grad_own = jnp.stack([gate_up_grad_own[:, :1024], gate_up_grad_own[:, 1024:]])
    gate_up_new = apply_update(
        gate_up_master, gate_up_grad_own, gate_up_moment, gate_up_average, rate_gate_up * rate_unit
    )
    down_new = apply_update(
        down_master, down_grad_own, down_moment, down_average, rate_down * rate_unit
    )
    gains_new = apply_update(
        gains_master, gain_grad_own, gains_moment, gains_average, rate_gains * rate_unit
    )
    return (layer_output, input_grad) + qkv_new + out_new + gate_up_new + down_new + gains_new


def solution(mesh):
    in_specs = (
        P(("seq", "tp"), None),
        P(("seq", "tp"), None),
        P("seq"),
        P("seq"),
        P("seq", "tp"),
        P("seq", "tp"),
        P("seq", "tp"),
        P("tp", "seq"),
        P("tp", "seq"),
        P("tp", "seq"),
        P(None, "seq", "tp"),
        P(None, "seq", "tp"),
        P(None, "seq", "tp"),
        P("tp", "seq"),
        P("tp", "seq"),
        P("tp", "seq"),
        P(None, "seq"),
        P(None, "seq"),
        P(None, "seq"),
    )
    out_specs = (
        P(("seq", "tp"), None),
        P(("seq", "tp"), None),
        P("seq", "tp"),
        P("seq", "tp"),
        P("seq", "tp"),
        P("seq", "tp"),
        P("tp", "seq"),
        P("tp", "seq"),
        P("tp", "seq"),
        P("tp", "seq"),
        P(None, "seq", "tp"),
        P(None, "seq", "tp"),
        P(None, "seq", "tp"),
        P(None, "seq", "tp"),
        P("tp", "seq"),
        P("tp", "seq"),
        P("tp", "seq"),
        P("tp", "seq"),
        P(None, "seq"),
        P(None, "seq"),
        P(None, "seq"),
        P(None, "seq"),
    )
    if ring_plan_fits(mesh):
        fine = jax.sharding.Mesh(mesh.devices.reshape(2, 2, 2, 2, 2), AXES)
        names = {"seq": ("y", "c"), "tp": ("h", "l", "x")}

        def finer(spec):
            parts = []
            for entry in spec:
                entry = (entry,) if isinstance(entry, str) else (entry or ())
                parts.append(sum((names[name] for name in entry), ()) or None)
            return P(*parts)

        return jax.shard_map(
            ring_shards,
            mesh=fine,
            in_specs=tuple(finer(spec) for spec in in_specs),
            out_specs=tuple(finer(spec) for spec in out_specs),
            check_vma=False,
        )
    return jax.shard_map(shards, mesh=mesh, in_specs=in_specs, out_specs=out_specs, check_vma=False)
```

```python
import jax
import jax.numpy as jnp
from jax import lax
from jax.experimental import pallas as pl
from jax.experimental.pallas import tpu as pltpu
from jax.sharding import PartitionSpec as P

HD = 64


norm_epsilon = 1e-05
rope_theta = 130000.0
momentum_coef = 0.9
average_coef = 0.5
masked_score = -1e30
rate_qkv = 0.004
rate_out = 2.0
rate_gate_up = 0.03
rate_down = 0.009
rate_gains = 0.1


def rms_scale(values):
    return lax.rsqrt(jnp.mean(values * values, axis=-1, keepdims=True) + norm_epsilon)


def rope_tables(positions, head_size):
    frequency = rope_theta ** (-(jnp.arange(head_size // 2, dtype=jnp.float32) * 2.0) / head_size)
    angles = positions.astype(jnp.float32)[:, None] * frequency[None, :]
    return (jnp.cos(angles)[:, None, :], jnp.sin(angles)[:, None, :])


def rotate(vectors, cosine_table, sine_table):
    half_width = vectors.shape[-1] // 2
    lower_half = vectors[..., :half_width]
    upper_half = vectors[..., half_width:]
    return jnp.concatenate(
        [
            lower_half * cosine_table - upper_half * sine_table,
            upper_half * cosine_table + lower_half * sine_table,
        ],
        axis=-1,
    )


def unrotate(grads, cosine_table, sine_table):
    half_width = grads.shape[-1] // 2
    lower_half = grads[..., :half_width]
    upper_half = grads[..., half_width:]
    return jnp.concatenate(
        [
            lower_half * cosine_table + upper_half * sine_table,
            upper_half * cosine_table - lower_half * sine_table,
        ],
        axis=-1,
    )


def norm_back(values, gain, grad):
    scale_rows = rms_scale(values)
    scaled = grad * gain
    back = scale_rows * (
        scaled
        - values * scale_rows * scale_rows * jnp.mean(scaled * values, axis=-1, keepdims=True)
    )
    return (back, jnp.sum(grad * values * scale_rows, axis=0))


def apply_update(master, grad, moment, average, rate):
    moment_new = momentum_coef * moment + grad
    master_new = master - rate * (grad + momentum_coef * moment_new)
    average_new = average_coef * average + (1.0 - average_coef) * master_new
    return (moment_new, average_new, master_new, master_new.astype(jnp.bfloat16))


def shards(
    layer_input,
    cotangent,
    counts,
    positions,
    qkv_master,
    qkv_moment,
    qkv_average,
    out_master,
    out_moment,
    out_average,
    gate_up_master,
    gate_up_moment,
    gate_up_average,
    down_master,
    down_moment,
    down_average,
    gains_master,
    gains_moment,
    gains_average,
):
    tp_size = lax.axis_size("tp")
    seq_size = lax.axis_size("seq")
    own_rows = layer_input.shape[0]
    length = own_rows * tp_size
    qkv_weight, out_weight, gate_up_weight, down_weight, gain_weight = (
        lax.all_gather(qkv_master.astype(jnp.bfloat16), "seq", axis=0, tiled=True),
        lax.all_gather(out_master.astype(jnp.bfloat16), "seq", axis=1, tiled=True),
        lax.all_gather(gate_up_master.astype(jnp.bfloat16), "seq", axis=1, tiled=True),
        lax.all_gather(down_master.astype(jnp.bfloat16), "seq", axis=1, tiled=True),
        lax.all_gather(gains_master.astype(jnp.bfloat16), "seq", axis=1, tiled=True),
    )
    heads_local = qkv_weight.shape[1] // (3 * HD)
    count_total = lax.psum(counts.astype(jnp.float32), "seq")
    seq_weight = seq_size * counts.astype(jnp.float32)[0] / count_total[0]
    gain_first = gain_weight[0].astype(jnp.float32)
    gain_second = gain_weight[1].astype(jnp.float32)
    gathered = lax.all_gather(layer_input, "tp", axis=0, tiled=True)
    inputs = gathered.astype(jnp.float32)
    normed = (inputs * rms_scale(inputs) * gain_first).astype(jnp.bfloat16)
    mixture = jnp.dot(normed, qkv_weight, preferred_element_type=jnp.float32).reshape(
        length, heads_local, 3, HD
    )
    cosine_table, sine_table = rope_tables(positions, HD)
    queries = rotate(mixture[:, :, 0], cosine_table, sine_table).astype(jnp.bfloat16)
    key_rows = rotate(mixture[:, :, 1], cosine_table, sine_table).astype(jnp.bfloat16)
    value_rows = mixture[:, :, 2].astype(jnp.bfloat16)
    block_rows = min(512, length)
    block_count = length // block_rows
    score_scale = HD ** (-0.5)

    def block_scores(block_index):
        key_end = (block_index + 1) * block_rows
        query_block = queries[block_index * block_rows : key_end]
        row_index = block_index * block_rows + jnp.arange(block_rows)
        allowed = jnp.arange(key_end)[None, :] <= row_index[:, None]
        scores = score_scale * jnp.einsum(
            "qhd,khd->hqk", query_block, key_rows[:key_end], preferred_element_type=jnp.float32
        )
        return (query_block, jnp.where(allowed[None], scores, masked_score))

    attended_list = []
    log_totals = []
    for block_index in range(block_count):
        query_block, scores = block_scores(block_index)
        key_end = (block_index + 1) * block_rows
        row_max = jnp.max(scores, axis=-1, keepdims=True)
        exp_scores = jnp.exp(scores - row_max)
        row_total = jnp.sum(exp_scores, axis=-1, keepdims=True)
        soft_scores = (exp_scores / row_total).astype(jnp.bfloat16)
        attended_block = jnp.einsum(
            "hqk,khd->qhd", soft_scores, value_rows[:key_end], preferred_element_type=jnp.float32
        )
        attended_list.append(attended_block.astype(jnp.bfloat16))
        log_totals.append(row_max + jnp.log(row_total))
    attended = jnp.concatenate(attended_list, axis=0).reshape(length, heads_local * HD)
    own_start = lax.axis_index("tp") * own_rows
    input_own = layer_input.astype(jnp.float32)
    branch = lax.psum(
        jnp.dot(attended, out_weight, preferred_element_type=jnp.float32).astype(jnp.bfloat16), "tp"
    ).astype(jnp.float32)
    residual = inputs + branch
    normed_second = (residual * rms_scale(residual) * gain_second).astype(jnp.bfloat16)
    resid_own = lax.dynamic_slice_in_dim(residual, own_start, own_rows, 0)
    gate_pre = jnp.dot(normed_second, gate_up_weight[0], preferred_element_type=jnp.float32)
    up_pre = jnp.dot(normed_second, gate_up_weight[1], preferred_element_type=jnp.float32)
    gate_sigmoid = jax.nn.sigmoid(gate_pre)
    activation = (gate_pre * gate_sigmoid * up_pre).astype(jnp.bfloat16)
    layer_output = (
        resid_own
        + lax.psum_scatter(
            jnp.dot(activation, down_weight, preferred_element_type=jnp.float32).astype(
                jnp.bfloat16
            ),
            "tp",
            scatter_dimension=0,
            tiled=True,
        ).astype(jnp.float32)
    ).astype(jnp.bfloat16)
    cot_all = lax.all_gather(cotangent, "tp", axis=0, tiled=True)
    grad_out = (seq_weight * cot_all.astype(jnp.float32)).astype(jnp.bfloat16)
    grad_down = jnp.einsum("tf,td->fd", activation, grad_out, preferred_element_type=jnp.float32)
    grad_act = jnp.einsum("td,fd->tf", grad_out, down_weight, preferred_element_type=jnp.float32)
    grad_gate = (grad_act * up_pre * gate_sigmoid * (1.0 + gate_pre * (1.0 - gate_sigmoid))).astype(
        jnp.bfloat16
    )
    grad_up = (grad_act * gate_pre * gate_sigmoid).astype(jnp.bfloat16)
    grad_gate_up = jnp.stack(
        [
            jnp.einsum("td,tf->df", normed_second, grad_gate, preferred_element_type=jnp.float32),
            jnp.einsum("td,tf->df", normed_second, grad_up, preferred_element_type=jnp.float32),
        ]
    )
    grad_normed_second = lax.psum_scatter(
        (
            jnp.einsum(
                "tf,df->td", grad_gate, gate_up_weight[0], preferred_element_type=jnp.float32
            )
            + jnp.einsum(
                "tf,df->td", grad_up, gate_up_weight[1], preferred_element_type=jnp.float32
            )
        ).astype(jnp.bfloat16),
        "tp",
        scatter_dimension=0,
        tiled=True,
    ).astype(jnp.float32)
    grad_resid_own, gain_second_part = norm_back(resid_own, gain_second, grad_normed_second)
    grad_resid_own = grad_resid_own + seq_weight * cotangent.astype(jnp.float32)
    resid_grad_rows = lax.all_gather(grad_resid_own.astype(jnp.bfloat16), "tp", axis=0, tiled=True)
    grad_out_proj = jnp.einsum(
        "tc,td->cd", attended, resid_grad_rows, preferred_element_type=jnp.float32
    )
    grad_attended = (
        jnp.einsum("td,cd->tc", resid_grad_rows, out_weight, preferred_element_type=jnp.float32)
        .astype(jnp.bfloat16)
        .reshape(length, heads_local, HD)
    )
    grad_keys = jnp.zeros((length, heads_local, HD), jnp.float32)
    grad_values = jnp.zeros((length, heads_local, HD), jnp.float32)
    query_grads = []
    for block_index in range(block_count):
        key_end = (block_index + 1) * block_rows
        query_block, scores = block_scores(block_index)
        soft_scores = jnp.exp(scores - log_totals[block_index])
        grad_block = grad_attended[block_index * block_rows : key_end]
        grad_soft = jnp.einsum(
            "qhd,khd->hqk", grad_block, value_rows[:key_end], preferred_element_type=jnp.float32
        )
        row_delta = jnp.sum(soft_scores * grad_soft, axis=-1, keepdims=True)
        grad_scores = (soft_scores * (grad_soft - row_delta)).astype(jnp.bfloat16)
        query_grads.append(
            score_scale
            * jnp.einsum(
                "hqk,khd->qhd", grad_scores, key_rows[:key_end], preferred_element_type=jnp.float32
            )
        )
        grad_keys = grad_keys.at[:key_end].add(
            score_scale
            * jnp.einsum(
                "hqk,qhd->khd", grad_scores, query_block, preferred_element_type=jnp.float32
            )
        )
        grad_values = grad_values.at[:key_end].add(
            jnp.einsum(
                "hqk,qhd->khd",
                soft_scores.astype(jnp.bfloat16),
                grad_block,
                preferred_element_type=jnp.float32,
            )
        )
    grad_queries = jnp.concatenate(query_grads, axis=0)
    grad_mixture = (
        jnp.stack(
            [
                unrotate(grad_queries, cosine_table, sine_table),
                unrotate(grad_keys, cosine_table, sine_table),
                grad_values,
            ],
            axis=2,
        )
        .astype(jnp.bfloat16)
        .reshape(length, heads_local * 3 * HD)
    )
    grad_qkv = jnp.einsum("td,tc->dc", normed, grad_mixture, preferred_element_type=jnp.float32)
    grad_normed_first = lax.psum_scatter(
        jnp.einsum(
            "tc,dc->td", grad_mixture, qkv_weight, preferred_element_type=jnp.float32
        ).astype(jnp.bfloat16),
        "tp",
        scatter_dimension=0,
        tiled=True,
    ).astype(jnp.float32)
    grad_input_own, gain_first_part = norm_back(input_own, gain_first, grad_normed_first)
    input_grad = grad_resid_own + grad_input_own
    gain_grads = lax.psum(jnp.stack([gain_first_part, gain_second_part]), ("seq", "tp"))
    gain_grad_own = lax.dynamic_slice_in_dim(
        gain_grads, lax.axis_index("seq") * gains_master.shape[1], gains_master.shape[1], 1
    )
    qkv_grad_own, out_grad_own, gate_up_grad_own, down_grad_own = (
        lax.psum_scatter(
            grad_qkv.astype(jnp.bfloat16), "seq", scatter_dimension=0, tiled=True
        ).astype(jnp.float32),
        lax.psum_scatter(
            grad_out_proj.astype(jnp.bfloat16), "seq", scatter_dimension=1, tiled=True
        ).astype(jnp.float32),
        lax.psum_scatter(
            grad_gate_up.astype(jnp.bfloat16), "seq", scatter_dimension=1, tiled=True
        ).astype(jnp.float32),
        lax.psum_scatter(
            grad_down.astype(jnp.bfloat16), "seq", scatter_dimension=1, tiled=True
        ).astype(jnp.float32),
    )
    rate_unit = float(length * seq_size) ** (-0.5)
    qkv_new = apply_update(qkv_master, qkv_grad_own, qkv_moment, qkv_average, rate_qkv * rate_unit)
    out_new = apply_update(out_master, out_grad_own, out_moment, out_average, rate_out * rate_unit)
    gate_up_new = apply_update(
        gate_up_master, gate_up_grad_own, gate_up_moment, gate_up_average, rate_gate_up * rate_unit
    )
    down_new = apply_update(
        down_master, down_grad_own, down_moment, down_average, rate_down * rate_unit
    )
    gains_new = apply_update(
        gains_master, gain_grad_own, gains_moment, gains_average, rate_gains * rate_unit
    )
    return (
        layer_output,
        input_grad,
        qkv_new[0],
        qkv_new[1],
        qkv_new[2],
        qkv_new[3],
        out_new[0],
        out_new[1],
        out_new[2],
        out_new[3],
        gate_up_new[0],
        gate_up_new[1],
        gate_up_new[2],
        gate_up_new[3],
        down_new[0],
        down_new[1],
        down_new[2],
        down_new[3],
        gains_new[0],
        gains_new[1],
        gains_new[2],
        gains_new[3],
    )


AXES = ("y", "c", "h", "l", "x")
RING = ("c", "l", "x")
MESH = pl.DeviceIdType.MESH
ROW = 512
BF = jnp.bfloat16
F32 = jnp.float32
LOG2E = 1.4426950408889634
NT = (((1,), (1,)), ((), ()))
NN = (((1,), (0,)), ((), ()))
TN = (((0,), (0,)), ((), ()))


def ring_plan_fits(mesh):
    return mesh.shape["seq"] == 4 and mesh.shape["tp"] == 8


def device_pairs(target):
    pairs = []
    for index in range(32):
        y, c, h, l, x = (index >> 4) & 1, (index >> 3) & 1, (index >> 2) & 1, (index >> 1) & 1, index & 1
        goal = target(y, c, h, l, x)
        if goal is not None:
            y, c, h, l, x = goal
            pairs.append((index, 16 * y + 8 * c + 4 * h + 2 * l + x))
    return pairs


def move(values, target):
    return lax.ppermute(values, AXES, device_pairs(target))


def flip(values, bits):
    return move(
        values,
        lambda y, c, h, l, x: (
            y ^ ("y" in bits),
            c ^ ("c" in bits),
            h ^ ("h" in bits),
            l ^ ("l" in bits),
            x ^ ("x" in bits),
        ),
    )


def swap_ch(values):
    return move(values, lambda y, c, h, l, x: (y, h, c, l, x))


def rounded(values):
    return values.astype(BF)


def ring_position():
    c, l, x = (lax.axis_index(name) for name in RING)
    partners = ({"x": 1 - x}, {"l": 1 - l}, {"c": 1 - c})
    return 4 * c + 2 * l + x, partners


def enter_ring(partners):
    barrier = pltpu.get_barrier_semaphore()
    for partner in partners:
        pl.semaphore_signal(barrier, inc=1, device_id=partner, device_id_type=MESH)
    pl.semaphore_wait(barrier, len(partners))


def rows_at(block, part=None):
    if part is None:
        return pl.ds(pl.multiple_of(block * ROW, ROW), ROW)
    half = ROW // 2
    return pl.ds(pl.multiple_of(block * ROW + part * half, half), half)


def remote(source, target, sent, received, device):
    return pltpu.make_async_remote_copy(
        src_ref=source,
        dst_ref=target,
        send_sem=sent,
        recv_sem=received,
        device_id=device,
        device_id_type=MESH,
    )


def places():
    y, c, h, l, x = (lax.axis_index(name) for name in AXES)
    return y, c, h, 4 * c + 2 * l + x


def wide_partners():
    y, c, h, _ = places()
    _, (to_x, to_l, to_c) = ring_position()
    mixed = ({**to_x, **to_l}, {**to_x, **to_c}, {**to_l, **to_c}, {**to_x, **to_l, **to_c})
    across = ({"c": 0, "h": 1 - h}, {"c": 1, "h": 1 - h})
    return (to_x, to_l, to_c) + mixed + ({"y": 1 - y},) + across


class Ring:
    def __init__(self, buffer, size, send, recv, lean=False, own=None, cut=None):
        self.buffer, self.size, self.send, self.recv, self.own = buffer, size, send, recv, own
        self.cut = size // 2 if cut is None else cut
        me, (to_x, to_l, to_c) = ring_position()
        self.plan = (
            (me, 0, to_x, me ^ 1),
            (me, 1, to_l, me ^ 2),
            (me, None, to_c, me ^ 4),
            (me, 1, to_x, me ^ 1),
            (me, 0, to_l, me ^ 2),
            (me ^ 1, 0, to_l, me ^ 3),
            (me ^ 2, 1, to_x, me ^ 3),
            (me ^ 1, None, to_c, me ^ 5),
            (me ^ 2, None, to_c, me ^ 6),
            (me ^ 3, None, to_c, me ^ 7),
        )
        if lean:
            self.plan = self.plan[:5] + ((me ^ 2, 0, to_x, me ^ 3),) + self.plan[6:]

    def copy(self, index, block):
        _, part, partner, _ = self.plan[index]
        size = (self.cut, self.size - self.cut, self.size)[2 if part is None else part]
        offset = self.cut if part == 1 else 0
        place = self.buffer.at[pl.ds(pl.multiple_of(block * self.size + offset, 128), size)]
        source = place
        if self.own is not None and index < 5:
            source = self.own.at[pl.ds(offset, size)]
        return remote(source, place, self.send.at[index], self.recv.at[index], partner)

    def start(self, *indices):
        for index in indices:
            self.copy(index, self.plan[index][0]).start()

    def arrived(self, *indices):
        for index in indices:
            self.copy(index, self.plan[index][3]).wait_recv()

    def sent(self):
        for index in range(10):
            self.copy(index, self.plan[index][0]).wait_send()


class Spread:
    def __init__(self, source, target, near, far, keep, stage=None):
        self.source, self.target, self.near, self.far, self.keep = source, target, near, far, keep
        self.stage = stage
        _, self.c, self.h, _ = places()

    def local(self):
        return pltpu.make_async_copy(
            self.source, self.target if self.stage is None else self.stage, self.keep
        )

    def beside(self):
        return remote(self.source, self.target, self.near.at[0], self.near.at[1], {"c": self.h})

    def across(self, core):
        return remote(
            self.source, self.target, self.far.at[2], self.far.at[core], {"c": self.h, "h": 1 - self.h}
        )

    def start(self):
        self.across(self.c).start()

        @pl.when(self.c == self.h)
        def _():
            self.local().start()

        @pl.when(self.c != self.h)
        def _():
            self.beside().start()

    def arrived(self):
        @pl.when(self.c == self.h)
        def _():
            self.local().wait()
            if self.stage is not None:
                copy = pltpu.make_async_copy(self.stage, self.target, self.keep)
                copy.start()
                copy.wait()
            self.beside().wait_recv()

        @pl.when(self.c != self.h)
        def _():
            self.across(0).wait_recv()
            self.across(1).wait_recv()

    def sent(self):
        self.across(self.c).wait_send()

        @pl.when(self.c != self.h)
        def _():
            self.beside().wait_send()


SPREAD_SEMAPHORES = [
    pltpu.SemaphoreType.DMA((4, 2)),
    pltpu.SemaphoreType.DMA((4, 3)),
    pltpu.SemaphoreType.DMA((4,)),
    pltpu.SemaphoreType.DMA((4, 2)),
    pltpu.SemaphoreType.DMA((4, 2)),
]


class First:
    def __init__(self, refs):
        (self.shard, self.grad), (self.whole, self.moved) = refs[:2], refs[2:4]
        self.w, near, far, keep, self.y_send, self.y_recv, self.grad_sems, self.stage = refs[4:]
        self.y, self.c, self.h, _ = places()
        first = (2 * self.y + self.c) * 512
        self.pieces = [
            Spread(
                self.shard.at[pl.ds(k * 256, 256)],
                self.w.at[pl.ds(pl.multiple_of(first + k * 256, 256), 256)],
                near.at[k],
                far.at[k],
                keep.at[k],
            )
            for k in range(2)
        ]

    def over_y(self, k, core, y):
        first = (2 * y + core) * 512 + k * 256
        place = self.w.at[pl.ds(pl.multiple_of(first, 256), 256)]
        return remote(place, place, self.y_send.at[k, core], self.y_recv.at[k, core], {"y": 1 - self.y})

    def grad_load(self):
        return pltpu.make_async_copy(self.grad, self.stage, self.grad_sems.at[2])

    def grad_local(self):
        return pltpu.make_async_copy(self.stage, self.moved, self.grad_sems.at[2])

    def grad_remote(self):
        return remote(
            self.grad, self.moved, self.grad_sems.at[0], self.grad_sems.at[1], {"c": self.h, "h": self.c}
        )

    def run(self, ring):
        for piece in self.pieces:
            piece.start()

        @pl.when(self.c == self.h)
        def _():
            self.grad_load().start()

        for k in range(2):
            self.pieces[k].arrived()
            for core in range(2):
                self.over_y(k, core, self.y).start()
            if k == 0:
                ring.arrived(1)
                ring.start(6)

        @pl.when(self.c == self.h)
        def _():
            self.grad_load().wait()
            self.grad_local().start()

        @pl.when(self.c != self.h)
        def _():
            self.grad_remote().start()

        ring.arrived(4)
        ring.start(5, 8)
        ring.arrived(2, 0, 3)
        ring.start(7)
        for k in range(2):
            for core in range(2):
                self.over_y(k, core, 1 - self.y).wait_recv()
        pltpu.make_async_copy(self.w, self.whole, self.grad_sems.at[3]).start()

    def finish(self):
        for piece in self.pieces:
            piece.sent()
        for k in range(2):
            for core in range(2):
                self.over_y(k, core, self.y).wait_send()
        pltpu.make_async_copy(self.w, self.whole, self.grad_sems.at[3]).wait()

        @pl.when(self.c == self.h)
        def _():
            self.grad_local().wait()

        @pl.when(self.c != self.h)
        def _():
            self.grad_remote().wait_recv()
            self.grad_remote().wait_send()


class Second:
    def __init__(self, refs):
        self.shard, self.whole = refs[:2]
        near, far, keep, self.y_send, self.y_recv, stage = refs[2:]
        self.y, c, _, _ = places()
        columns = pl.ds(pl.multiple_of((2 * self.y + c) * 512, 512), 512)
        self.pieces = [
            Spread(
                self.shard.at[pl.ds(k * 512, 512)],
                self.whole.at[pl.ds(k * 512, 512), columns],
                near.at[k],
                far.at[k],
                keep.at[k],
                stage.at[k],
            )
            for k in range(2)
        ]

    def over_y(self, k, y):
        place = self.whole.at[pl.ds(k * 512, 512), pl.ds(pl.multiple_of(y * 1024, 1024), 1024)]
        return remote(place, place, self.y_send.at[k, 0], self.y_recv.at[k, 0], {"y": 1 - self.y})

    def run(self, ring):
        for piece in self.pieces:
            piece.start()

    def on(self, k):
        self.pieces[k].arrived()
        self.over_y(k, self.y).start()

    def finish(self):
        for k in range(2):
            self.pieces[k].sent()
            self.over_y(k, 1 - self.y).wait_recv()
            self.over_y(k, self.y).wait_send()


def gather_kernel(finish, beside, inputs, outputs, *refs):
    own_ref, refs = refs[0], refs[1:]
    given, refs = refs[:inputs], refs[inputs:]
    full_ref, outs, refs = refs[0], refs[1:4], refs[4:]
    extra_outs, refs = refs[:outputs], refs[outputs:]
    buf, res, send, recv, own_sem, full_sem, out_sem = refs[:7]
    me, _ = ring_position()
    load = pltpu.make_async_copy(own_ref, buf.at[rows_at(me)], own_sem)
    load.start()
    enter_ring(wide_partners())
    load.wait()
    early = beside is First
    ring = Ring(buf, ROW, send, recv, lean=early, cut=256 if early else 128)
    ring.start(0, 1, 2, 3, 4)
    if early:
        more = First(given[2:] + extra_outs + refs[7:])
        w_ref, tables = more.w, given[:2]
    else:
        more = Second(given[1:] + extra_outs + refs[7:])
        w_ref, tables = given[0], ()
    more.run(ring)

    def step_body(step, carry):
        block = me ^ ((step >> 1) | ((step & 1) << 2))
        rows = rows_at(block)
        if not early:

            @pl.when(step == 1)
            def _():
                ring.arrived(2)

            @pl.when(step == 2)
            def _():
                ring.arrived(0)
                ring.start(5)
                ring.arrived(1)
                ring.start(6)
                more.on(0)
                ring.arrived(3)
                ring.start(7)
                more.on(1)
                ring.arrived(4)
                ring.start(8)

        @pl.when(step == 3)
        def _():
            ring.arrived(7)

        @pl.when(step == 5)
        def _():
            ring.arrived(8)

        @pl.when(step == 6)
        def _():
            ring.arrived(5, 6)
            ring.start(9)

        @pl.when(step == 7)
        def _():
            ring.arrived(9)

        pltpu.make_async_copy(buf.at[rows], full_ref.at[rows], full_sem.at[step]).start()
        turn = step & 1

        def out_copy(which, rows):
            return pltpu.make_async_copy(
                res.at[turn, which], outs[which].at[rows], out_sem.at[turn, which]
            )

        @pl.when(step >= 2)
        def _():
            for which in range(3):
                out_copy(which, rows).wait()

        finish(buf, rows, w_ref, tables, res, turn)
        for which in range(3):
            out_copy(which, rows).start()
        return carry

    lax.fori_loop(0, 8, step_body, 0)
    ring.sent()
    more.finish()

    def drain(step, carry):
        rows = rows_at(step)
        pltpu.make_async_copy(buf.at[rows], full_ref.at[rows], full_sem.at[step]).wait()
        return carry

    lax.fori_loop(0, 8, drain, 0)
    for turn in range(2):
        for which in range(3):
            pltpu.make_async_copy(
                res.at[turn, which], outs[which].at[rows_at(0)], out_sem.at[turn, which]
            ).wait()


def feed_forward_finish(buf, rows, w_ref, tables, res, turn):
    def columns(chunk, carry):
        here = pl.multiple_of(chunk * 256, 256)
        block = buf[rows, :]
        g = jnp.dot(block, w_ref[:, pl.ds(here, 256)], preferred_element_type=F32)
        u = jnp.dot(block, w_ref[:, pl.ds(here + 1024, 256)], preferred_element_type=F32)
        res[turn, 0, :, pl.ds(here, 256)] = rounded(g)
        res[turn, 1, :, pl.ds(here, 256)] = rounded(u)
        res[turn, 2, :, pl.ds(here, 256)] = rounded(g * (1.0 / (1.0 + jnp.exp(-g))) * u)
        return carry

    lax.fori_loop(0, 4, columns, 0)


def attention_finish(buf, rows, w_ref, tables, res, turn):
    block = buf[rows, :]
    cs, sn = tables[0][rows, :], tables[1][rows, :]
    for which in range(2):
        m = jnp.dot(block, w_ref[:, which * 256 : which * 256 + 256], preferred_element_type=F32)
        if which == 0:
            m = m * (0.125 * LOG2E)
        m1, m2 = m[:, :128], m[:, 128:]
        res[turn, which, :, 0:128] = rounded(m1 * cs - m2 * sn)
        res[turn, which, :, 128:256] = rounded(m2 * cs + m1 * sn)
    res[turn, 2] = rounded(jnp.dot(block, w_ref[:, 512:768], preferred_element_type=F32))


def gather_product(own, given, anywhere_given, extra_shapes, width, finish, beside, scratch, number):
    anywhere = pl.BlockSpec(memory_space=pl.ANY)
    vmem = pl.BlockSpec(memory_space=pltpu.VMEM)
    length, depth = 8 * ROW, own.shape[1]
    inputs = len(given) + len(anywhere_given)
    return pl.pallas_call(
        lambda *refs: gather_kernel(finish, beside, inputs, len(extra_shapes), *refs),
        in_specs=[anywhere] + [vmem] * len(given) + [anywhere] * len(anywhere_given),
        out_specs=[anywhere] * (4 + len(extra_shapes)),
        out_shape=[jax.ShapeDtypeStruct((length, depth), BF)]
        + [jax.ShapeDtypeStruct((length, width), BF)] * 3
        + [jax.ShapeDtypeStruct(shape, BF) for shape in extra_shapes],
        scratch_shapes=[
            pltpu.VMEM((length, depth), BF),
            pltpu.VMEM((2, 3, ROW, width), BF),
            pltpu.SemaphoreType.DMA((10,)),
            pltpu.SemaphoreType.DMA((10,)),
            pltpu.SemaphoreType.DMA,
            pltpu.SemaphoreType.DMA((8,)),
            pltpu.SemaphoreType.DMA((2, 3)),
        ]
        + scratch,
        compiler_params=pltpu.CompilerParams(
            collective_id=number, has_side_effects=True, vmem_limit_bytes=56 * 2**20
        ),
        cost_estimate=pl.CostEstimate(
            flops=80 * 10**9, bytes_accessed=30 * 2**20, transcendentals=0
        ),
    )(own, *given, *anywhere_given)


def scatter_kernel(dims, cut, kind, *refs):
    beside = 2 if kind == 2 else 0
    if kind == 3:
        grad_ref, gate_ref, up_ref, down_ref, w_ref, out_ref, a_ref = refs[:7]
        refs = refs[7:]
        grad_buf, gate_buf, up_buf, made_sem = refs[11:]
    else:
        a_ref, w_ref, refs = refs[0], refs[1], refs[2:]
        given, refs = refs[:beside], refs[beside:]
        out_ref, refs = refs[0], refs[1:]
        more_outs, refs = refs[: 3 if beside else 0], refs[3 if beside else 0 :]
    abuf, mine, other, sums, ra, rb, near_x, near_l, send, recv, a_sem = refs[:11]
    me, partners = ring_position()
    to_x, to_l, to_c = partners
    order = (7, 3, 5, 6, 1, 2, 4, 0)

    def load(index):
        rows, turn = rows_at(me ^ order[index]), index % 2
        if kind == 3:
            pairs = ((grad_ref, grad_buf), (gate_ref, gate_buf), (up_ref, up_buf))
        else:
            pairs = ((a_ref, abuf),)
        return [
            pltpu.make_async_copy(ref.at[rows], buf.at[turn], a_sem.at[turn, k])
            for k, (ref, buf) in enumerate(pairs)
        ]

    def made(index):
        return pltpu.make_async_copy(
            abuf.at[index % 2], a_ref.at[rows_at(me ^ order[index])], made_sem.at[index % 2]
        )

    def make(index):
        turn = index % 2
        if index >= 2:
            made(index - 2).wait()

        def columns(chunk, carry):
            start = pl.multiple_of(chunk * 256, 256)
            here, there = pl.ds(start, 256), pl.ds(start + 1024, 256)
            d = lax.dot_general(grad_buf[turn], down_ref[here, :], NT, preferred_element_type=F32)
            g = gate_buf[turn, :, here].astype(F32)
            u = up_buf[turn, :, here].astype(F32)
            sigmoid = 1.0 / (1.0 + jnp.exp(-g))
            abuf[turn, :, here] = rounded(d * u * sigmoid * (1.0 + g * (1.0 - sigmoid)))
            abuf[turn, :, there] = rounded(d * g * sigmoid)
            return carry

        lax.fori_loop(0, 4, columns, 0)
        made(index).start()

    for each in load(0):
        each.start()
    enter_ring(wide_partners() if beside else partners)
    if beside:
        tail = WeightTail(given + more_outs + refs[11:])
        tail.begin()

    def copy(index, source, target, partner):
        return pltpu.make_async_remote_copy(
            src_ref=source,
            dst_ref=target,
            send_sem=send.at[index],
            recv_sem=recv.at[index],
            device_id=partner,
            device_id_type=MESH,
        )

    top, bottom = pl.ds(0, cut), pl.ds(cut, ROW - cut)
    turns = {3: 0, 1: 1, 2: 0, 0: 1}
    copies = [copy(slot, mine.at[turns[slot]], other.at[slot], to_c) for slot in range(4)] + [
        copy(4, sums.at[2, top], ra, to_x),
        copy(5, sums.at[2, bottom], rb, to_l),
        copy(6, sums.at[0, top], near_x.at[top], to_x),
        copy(7, sums.at[1, bottom], near_l.at[bottom], to_l),
        copy(8, sums.at[0, bottom], near_x.at[bottom], to_x),
        copy(9, sums.at[1, top], near_l.at[top], to_l),
    ]

    def product(index, store):
        def columns(chunk, carry):
            here = pl.ds(pl.multiple_of(chunk * 256, 256), 256)
            w = w_ref[here, :] if dims == NT else w_ref[:, here]
            store(
                here, lax.dot_general(abuf[index % 2], w, dims, preferred_element_type=F32)
            )
            return carry

        lax.fori_loop(0, 8, columns, 0)

    for index, slot in enumerate(order):
        for each in load(index):
            each.wait()
        if index + 1 < 8:
            for each in load(index + 1):
                each.start()
        if kind == 3:
            make(index)
        if slot >= 4:
            if slot in (6, 4):
                copies[3 if slot == 6 else 1].wait_send()

            def store(here, value, slot=slot):
                mine[turns[slot - 4], :, here] = rounded(value)

            product(index, store)
            copies[slot - 4].start()
        elif slot > 0:
            copies[slot].wait_recv()

            def store(here, value, slot=slot):
                sums[slot - 1, :, here] = rounded(value + other[slot, :, here].astype(F32))

            product(index, store)
            if slot == 3:
                copies[4].start()
                copies[5].start()
            if slot == 1:
                copies[6].start()
            if slot == 2:
                copies[7].start()
                copies[5].wait_recv()
                sums[0, bottom, :] = rounded(
                    sums[0, bottom, :].astype(F32) + rb[...].astype(F32)
                )
                copies[8].start()
                copies[4].wait_recv()
                sums[1, top, :] = rounded(sums[1, top, :].astype(F32) + ra[...].astype(F32))
                copies[9].start()
        else:
            copies[0].wait_recv()

            def store(here, value):
                out_ref[:, here] = value + other[0, :, here].astype(F32)

            product(index, store)
    if beside:
        tail.run()
    for part, first, second in ((top, 6, 9), (bottom, 8, 7)):
        copies[first].wait_recv()
        copies[second].wait_recv()
        out_ref[part, :] = out_ref[part, :] + (
            near_x[part, :].astype(F32) + near_l[part, :].astype(F32)
        )
    for index, each in enumerate(copies):
        if index not in (1, 3):
            each.wait_send()
    if kind == 3:
        made(6).wait()
        made(7).wait()
    if beside:
        tail.end()


class WeightTail:
    def __init__(self, refs):
        self.grad, self.layer, self.totals, self.landing, self.layer_out = refs[:5]
        stage, result, y_sems, z_sems, stage_sems, self.layer_stage, self.layer_sems = refs[5:]
        self.y, self.c, self.h, _ = places()
        self.names = [("Q", 0, 0), ("Q", 1, 0)]
        self.pieces = PieceSums(
            self.names,
            self.piece,
            lambda name: self.landing.at[name[1]],
            lambda name, h: self.totals.at[h],
            y_sems,
            z_sems,
        )
        self.sums = Sums(stage, result, stage_sems)
        for name in self.names:
            self.sums.item(
                0,
                512,
                [self.piece(name, self.y), self.landing.at[name[1]]],
                self.pieces.sends(name),
                [lambda name=name: self.pieces.over_y(name).wait_recv()],
            )

    def piece(self, name, y):
        return self.grad.at[pl.ds(pl.multiple_of((2 * y + name[1]) * 512, 512), 512)]

    def layer_load(self):
        return pltpu.make_async_copy(self.layer, self.layer_stage, self.layer_sems.at[2])

    def layer_local(self):
        return pltpu.make_async_copy(self.layer_stage, self.layer_out, self.layer_sems.at[2])

    def layer_remote(self):
        return remote(
            self.layer, self.layer_out, self.layer_sems.at[0], self.layer_sems.at[1], {"c": self.h, "h": self.c}
        )

    def begin(self):
        for name in self.names:
            self.pieces.over_y(name).start()

        @pl.when(self.c == self.h)
        def _():
            self.layer_load().start()

        @pl.when(self.c != self.h)
        def _():
            self.layer_remote().start()

    def run(self):
        @pl.when(self.c == self.h)
        def _():
            self.layer_load().wait()
            self.layer_local().start()

        for k in range(2):
            self.sums.load(k)
            self.sums.add(k)

    def end(self):
        self.sums.last_sent()
        self.pieces.end()

        @pl.when(self.c == self.h)
        def _():
            self.layer_local().wait()

        @pl.when(self.c != self.h)
        def _():
            self.layer_remote().wait_recv()
            self.layer_remote().wait_send()


def scatter_scratch(depth, width, cut):
    return [
        pltpu.VMEM((2, ROW, depth), BF),
        pltpu.VMEM((2, ROW, width), BF),
        pltpu.VMEM((4, ROW, width), BF),
        pltpu.VMEM((3, ROW, width), BF),
        pltpu.VMEM((cut, width), BF),
        pltpu.VMEM((ROW - cut, width), BF),
        pltpu.VMEM((ROW, width), BF),
        pltpu.VMEM((ROW, width), BF),
        pltpu.SemaphoreType.DMA((10,)),
        pltpu.SemaphoreType.DMA((10,)),
        pltpu.SemaphoreType.DMA((2, 3)),
    ]


def feed_forward_back(grad, gate, up, down_weight, gate_up_weight, number):
    anywhere = pl.BlockSpec(memory_space=pl.ANY)
    vmem = pl.BlockSpec(memory_space=pltpu.VMEM)
    return pl.pallas_call(
        lambda *refs: scatter_kernel(NT, ROW // 2, 3, *refs),
        in_specs=[anywhere] * 3 + [vmem] * 2,
        out_specs=[vmem, anywhere],
        out_shape=[
            jax.ShapeDtypeStruct((ROW, 2048), F32),
            jax.ShapeDtypeStruct((8 * ROW, 2048), BF),
        ],
        scratch_shapes=scatter_scratch(2048, 2048, ROW // 2)
        + [
            pltpu.VMEM((2, ROW, 2048), BF),
            pltpu.VMEM((2, ROW, 1024), BF),
            pltpu.VMEM((2, ROW, 1024), BF),
            pltpu.SemaphoreType.DMA((2,)),
        ],
        compiler_params=pltpu.CompilerParams(
            collective_id=number, has_side_effects=True, vmem_limit_bytes=62 * 2**20
        ),
        cost_estimate=pl.CostEstimate(
            flops=80 * 10**9, bytes_accessed=60 * 2**20, transcendentals=0
        ),
    )(grad, gate, up, down_weight, gate_up_weight)


def product_scatter(a, weight, dims, number, *more):
    anywhere = pl.BlockSpec(memory_space=pl.ANY)
    vmem = pl.BlockSpec(memory_space=pltpu.VMEM)
    depth = a.shape[1]
    width = weight.shape[0] if dims == NT else weight.shape[1]
    cut = 384 if more else 256
    return pl.pallas_call(
        lambda *refs: scatter_kernel(dims, cut, len(more), *refs),
        in_specs=[anywhere, vmem] + [anywhere] * len(more),
        out_specs=[vmem] + [anywhere] * (3 if more else 0),
        out_shape=[jax.ShapeDtypeStruct((ROW, width), F32)]
        + [
            jax.ShapeDtypeStruct((2, 512, 768), BF),
            jax.ShapeDtypeStruct((2, 512, 768), BF),
            jax.ShapeDtypeStruct((ROW, 2048), BF),
        ]
        * bool(more),
        scratch_shapes=scatter_scratch(depth, width, cut)
        + [
            pltpu.VMEM((2, 2, 512, 768), BF),
            pltpu.VMEM((2, 512, 768), BF),
            pltpu.SemaphoreType.DMA((2, 2)),
            pltpu.SemaphoreType.DMA((3, 2)),
            pltpu.SemaphoreType.DMA((2, 5)),
            pltpu.VMEM((ROW, 2048), BF),
            pltpu.SemaphoreType.DMA((3,)),
        ]
        * bool(more),
        compiler_params=pltpu.CompilerParams(
            collective_id=number, has_side_effects=True, vmem_limit_bytes=58 * 2**20
        ),
        cost_estimate=pl.CostEstimate(
            flops=80 * 10**9, bytes_accessed=30 * 2**20, transcendentals=0
        ),
    )(a, weight, *more)


def column_order():
    column = lax.broadcasted_iota(jnp.int32, (768, 768), 1)
    row = lax.broadcasted_iota(jnp.int32, (768, 768), 0)
    part, within = column // 256, column % 256
    turned = ((within % 128) // 32) * 192 + part * 64 + (within // 128) * 32 + within % 32
    plain = (within // 64) * 192 + 128 + within % 64
    return (row == jnp.where(part == 2, plain, turned)).astype(BF)


def head_lanes_turned(head):
    lane = lax.broadcasted_iota(jnp.int32, (1, 256), 1)
    return (lane % 128) // 32 == head


def head_lanes_plain(head):
    lane = lax.broadcasted_iota(jnp.int32, (1, 256), 1)
    return lane // 64 == head


def picked_block(step, blocks):
    block = jnp.int32(blocks[0])
    for index in range(1, len(blocks)):
        block = jnp.where(step == index, blocks[index], block)
    return block


def mark(*values):
    return sum(value[(0,) * value.ndim].astype(F32) for value in values) * 0.0


def after(values, zero):
    return values + zero.astype(values.dtype)


def held(values, zero):
    if zero is None:
        return values
    return after(lax.optimization_barrier(values), zero)


class Beside:
    def __init__(self, refs):
        self.out_shard, self.gate_up_shard, self.grad_own = refs[:3]
        self.out_full, self.gate_up, self.grad_full, self.rows_own = refs[3:7]
        (
            near,
            far,
            keep,
            self.y_send,
            self.y_recv,
            out_near,
            out_far,
            out_keep,
            self.out_y,
            grad_send,
            grad_recv,
            out_send,
            out_recv,
            self.row_send,
            self.row_recv,
            self.own_sem,
            stage,
            out_stage,
            self.grad_stage,
        ) = refs[7:]
        self.y, self.c, self.h, self.me = places()
        _, _, _, l, x = (lax.axis_index(name) for name in AXES)
        s = 2 * self.y + self.c
        self.pieces = [
            Spread(
                self.gate_up_shard.at[pl.ds(k * 128, 128)],
                self.gate_up.at[pl.ds(pl.multiple_of(s * 512 + k * 128, 128), 128)],
                near.at[k],
                far.at[k],
                keep.at[k],
                stage.at[k],
            )
            for k in range(4)
        ]
        heads = 4 * self.h + 2 * l + x
        self.out_piece = Spread(
            self.out_shard,
            self.out_full.at[
                pl.ds(pl.multiple_of(heads * 256, 256), 256), pl.ds(pl.multiple_of(s * 512, 512), 512)
            ],
            out_near,
            out_far,
            out_keep,
            out_stage,
        )
        self.grad_ring = Ring(self.grad_full, ROW, grad_send, grad_recv, lean=True, own=self.grad_stage)
        self.out_ring = Ring(self.out_full, 256, out_send, out_recv)

    def over_y(self, k, core, y):
        first = (2 * y + core) * 512 + k * 128
        place = self.gate_up.at[pl.ds(pl.multiple_of(first, 128), 128)]
        return remote(place, place, self.y_send.at[k, core], self.y_recv.at[k, core], {"y": 1 - self.y})

    def out_over_y(self, y):
        place = self.out_full.at[
            pl.ds(pl.multiple_of(self.me * 256, 256), 256), pl.ds(pl.multiple_of(y * 1024, 1024), 1024)
        ]
        return remote(place, place, self.out_y.at[0], self.out_y.at[1], {"y": 1 - self.y})

    def piece_over_y(self, k):
        self.pieces[k].arrived()
        for core in range(2):
            self.over_y(k, core, self.y).start()

    def own_out(self):
        return pltpu.make_async_copy(
            self.grad_stage, self.grad_full.at[rows_at(self.me)], self.own_sem.at[0]
        )

    def begin(self):
        own = pltpu.make_async_copy(self.grad_own, self.grad_stage, self.own_sem.at[0])
        own.start()
        enter_ring(wide_partners())
        self.out_piece.start()
        own.wait()
        self.grad_ring.start(0, 1, 2, 3, 4)
        self.own_out().start()

    def at(self, step):
        def when(number, *actions):
            @pl.when(step == number)
            def _():
                for action in actions:
                    action()

        def out_on():
            self.out_piece.arrived()
            self.out_over_y(self.y).start()
            self.pieces[0].start()

        def out_ring_on():
            self.out_over_y(1 - self.y).wait_recv()
            self.out_ring.start(0, 1, 2, 3, 4)
            self.pieces[1].start()

        def grad_one():
            self.grad_ring.arrived(1)
            self.grad_ring.start(6)

        def grad_two():
            self.grad_ring.arrived(4)
            self.grad_ring.start(5, 8)
            self.grad_ring.arrived(0, 3)
            self.grad_ring.start(7)

        def out_one():
            self.out_ring.arrived(0)
            self.out_ring.start(5)
            self.out_ring.arrived(1)
            self.out_ring.start(6)

        def out_two():
            self.out_ring.arrived(3)
            self.out_ring.start(7)
            self.out_ring.arrived(4)
            self.out_ring.start(8)

        when(0, self.begin)
        when(3, out_on)
        when(6, out_ring_on)
        when(7, grad_one)
        when(9, lambda: self.piece_over_y(0), self.pieces[2].start)
        when(11, grad_two)
        when(14, lambda: self.piece_over_y(1), self.pieces[3].start)
        when(16, out_one)
        when(19, lambda: self.piece_over_y(2))
        when(22, out_two)
        when(28, lambda: self.piece_over_y(3))

    def row_local(self, block, o_all):
        columns = pl.ds(pl.multiple_of(self.me * 256, 256), 256)
        return pltpu.make_async_copy(
            o_all.at[rows_at(block)], self.rows_own.at[:, columns], self.own_sem.at[1]
        )

    def row_remote(self, block, o_all, sender):
        columns = pl.ds(pl.multiple_of(sender * 256, 256), 256)
        return remote(
            o_all.at[rows_at(block)],
            self.rows_own.at[:, columns],
            self.row_send.at[block],
            self.row_recv.at[sender],
            {"c": block >> 2, "l": (block >> 1) & 1, "x": block & 1},
        )

    def send_rows(self, block, o_all):
        @pl.when(block == self.me)
        def _():
            self.row_local(block, o_all).start()

        @pl.when(block != self.me)
        def _():
            self.row_remote(block, o_all, self.me).start()

    def end(self, o_all):
        for ring in (self.out_ring, self.grad_ring):
            ring.arrived(5, 6)
            ring.start(9)
        self.own_out().wait()
        self.out_piece.sent()
        self.out_over_y(self.y).wait_send()
        for k in range(4):
            self.pieces[k].sent()
            for core in range(2):
                self.over_y(k, core, self.y).wait_send()
                self.over_y(k, core, 1 - self.y).wait_recv()
        for ring in (self.grad_ring, self.out_ring):
            ring.arrived(2, 7, 8, 9)
            ring.sent()

        def each(block, carry):
            @pl.when(block == self.me)
            def _():
                self.row_local(block, o_all).wait()

            @pl.when(block != self.me)
            def _():
                self.row_remote(block, o_all, self.me).wait_send()
                self.row_remote(block, o_all, block).wait_recv()

            return carry

        lax.fori_loop(0, 8, each, 0)


def attend_kernel(q_ref, k_ref, v_ref, out_shard, gate_up_shard, grad_own, o_ref, l_ref, *refs):
    beside = Beside((out_shard, gate_up_shard, grad_own) + refs[:4] + refs[8:])
    s_scr, m_scr, acc_scr, o_all = refs[4:8]
    head = pl.program_id(1)
    step = pl.program_id(0) * 4 + head
    block = 7 - pl.program_id(0)
    beside.at(step)
    row = lax.broadcasted_iota(jnp.int32, (ROW, ROW), 0)
    col = lax.broadcasted_iota(jnp.int32, (ROW, ROW), 1)

    def lane_max(s):
        return jnp.maximum(
            jnp.maximum(s[:, :128], s[:, 128:256]), jnp.maximum(s[:, 256:384], s[:, 384:])
        )

    def lane_sum(s):
        return (s[:, :128] + s[:, 128:256]) + (s[:, 256:384] + s[:, 384:])

    def keys_at(key_block):
        return pl.ds(pl.multiple_of(key_block * ROW, ROW), ROW)

    q = q_ref[...]
    qh = jnp.where(head_lanes_turned(head), q, jnp.zeros_like(q))

    def scores(key_block):
        return lax.dot_general(qh, k_ref[keys_at(key_block), :], NT, preferred_element_type=F32)

    s = jnp.where(col <= row, scores(block), masked_score)
    s_scr[block] = s
    m_scr[...] = lane_max(s)

    def first_pass(key_block, carry):
        s = scores(key_block)
        s_scr[key_block] = s
        m_scr[...] = jnp.maximum(m_scr[...], lane_max(s))
        return carry

    lax.fori_loop(0, block, first_pass, 0)
    top = jnp.max(m_scr[...], axis=1, keepdims=True)
    m_scr[...] = jnp.zeros_like(m_scr)
    acc_scr[...] = jnp.zeros_like(acc_scr)

    def second_pass(key_block, carry):
        e = jnp.exp2(s_scr[key_block] - top)
        m_scr[...] += lane_sum(e)
        acc_scr[...] += lax.dot_general(
            e.astype(BF), v_ref[keys_at(key_block), :], NN, preferred_element_type=F32
        )
        return carry

    lax.fori_loop(0, block + 1, second_pass, 0)
    total = jnp.sum(m_scr[...], axis=1, keepdims=True)
    part = rounded(acc_scr[...] * (1.0 / total))
    rows = rows_at(block)

    @pl.when(head == 0)
    def _():
        o_all[rows, :] = part

    @pl.when(head > 0)
    def _():
        o_all[rows, :] = jnp.where(head_lanes_plain(head), part, o_all[rows, :])

    level = jnp.transpose(jnp.broadcast_to(top + jnp.log2(total), (ROW, 128)))[0:4, :]
    row4 = lax.broadcasted_iota(jnp.int32, (4, ROW), 0)
    l_ref[0] = jnp.where(row4 == head, level, l_ref[0])

    @pl.when(head == 3)
    def _():
        o_ref[...] = o_all[rows, :]
        beside.send_rows(block, o_all)

    @pl.when(step == 31)
    def _():
        beside.end(o_all)


def attend(q, k, v, out_shard, gate_up_shard, grad_own):
    length = q.shape[0]
    blocks = length // ROW
    whole = pl.BlockSpec((length, 256), lambda i, head: (0, 0))
    anywhere = pl.BlockSpec(memory_space=pl.ANY)
    dma = pltpu.SemaphoreType.DMA
    return pl.pallas_call(
        attend_kernel,
        grid=(blocks, 4),
        in_specs=[pl.BlockSpec((ROW, 256), lambda i, head: (7 - i, 0)), whole, whole] + [anywhere] * 3,
        out_specs=[
            pl.BlockSpec((ROW, 256), lambda i, head: (7 - i, 0)),
            pl.BlockSpec((1, 4, ROW), lambda i, head: (7 - i, 0, 0)),
        ]
        + [anywhere] * 4,
        out_shape=[
            jax.ShapeDtypeStruct((length, 256), BF),
            jax.ShapeDtypeStruct((blocks, 4, ROW), F32),
            jax.ShapeDtypeStruct((2048, 2048), BF),
            jax.ShapeDtypeStruct((2048, 2048), BF),
            jax.ShapeDtypeStruct((length, 2048), BF),
            jax.ShapeDtypeStruct((ROW, 2048), BF),
        ],
        scratch_shapes=[
            pltpu.VMEM((blocks, ROW, ROW), F32),
            pltpu.VMEM((ROW, 128), F32),
            pltpu.VMEM((ROW, 256), F32),
            pltpu.VMEM((length, 256), BF),
        ]
        + SPREAD_SEMAPHORES
        + [dma((2,)), dma((3,)), dma, dma((2,))]
        + [dma((10,))] * 4
        + [dma((8,)), dma((8,)), dma((2,))]
        + [pltpu.VMEM((4, 128, 2048), BF), pltpu.VMEM((256, 512), BF), pltpu.VMEM((ROW, 2048), BF)],
        compiler_params=pltpu.CompilerParams(
            collective_id=6, has_side_effects=True, vmem_limit_bytes=48 * 2**20
        ),
        cost_estimate=pl.CostEstimate(
            flops=14 * 10**9 * blocks, bytes_accessed=10 * 2**20, transcendentals=0
        ),
    )(q, k, v, out_shard, gate_up_shard, grad_own)


KEYS = 256


class Sums:
    def __init__(self, stage, result, stage_sems):
        self.stage, self.result, self.stage_sems = stage, result, stage_sems
        self.items = []

    def item(self, due, rows, terms, sends, waits=(), extra=None, then=None):
        self.items.append((due, rows, terms, sends, waits, extra, then))

    def loads(self, k):
        _, rows, terms, _, _, extra, _ = self.items[k]
        turn = k % 2
        copies = [
            pltpu.make_async_copy(
                term, self.stage.at[turn, index, pl.ds(0, rows)], self.stage_sems.at[turn, index]
            )
            for index, term in enumerate(terms)
        ]
        if extra is not None:
            copies.append(pltpu.make_async_copy(extra[0], extra[1], self.stage_sems.at[turn, 4]))
        return copies

    def load(self, k):
        for wait in self.items[k][4]:
            wait()
        for copy in self.loads(k):
            copy.start()

    def add(self, k):
        _, rows, terms, sends, _, extra, then = self.items[k]
        turn = k % 2
        for copy in self.loads(k):
            copy.wait()
        if k >= 2:
            self.sent(k - 2)
        target = self.result.at[turn]
        size = rows // 8

        def chunk(index, carry):
            here = pl.ds(pl.multiple_of(index * size, size), size)
            total = self.stage[turn, 0, here, :].astype(F32)
            for term in range(1, len(terms)):
                total += self.stage[turn, term, here, :].astype(F32)
            if extra is not None:
                total += extra[1][here, :]
            target[here, :] = rounded(total)
            return carry

        lax.fori_loop(0, 8, chunk, 0)
        for here, away, local in sends(self.result.at[turn, pl.ds(0, rows)]):
            self.either(here, away, local, "start")
        if then is not None:
            then()

    def either(self, here, away, local, method):
        if local is None:
            getattr(away(), method)()
            return
        if away is None:
            getattr(local(), "wait" if method == "wait_send" else method)()
            return

        @pl.when(here)
        def _():
            getattr(local(), "wait" if method == "wait_send" else method)()

        @pl.when(jnp.logical_not(here))
        def _():
            getattr(away(), method)()

    def sent(self, k):
        _, rows, _, sends, _, _, _ = self.items[k]
        for here, away, local in sends(self.result.at[k % 2, pl.ds(0, rows)]):
            self.either(here, away, local, "wait_send")

    def poll(self, unit):
        for k, item in enumerate(self.items):

            @pl.when(unit == item[0])
            def _(k=k):
                self.load(k)

            @pl.when(unit == item[0] + 1)
            def _(k=k):
                self.add(k)

    def last_sent(self):
        for k in range(len(self.items) - 2, len(self.items)):
            self.sent(k)


def half_columns(half):
    return pl.ds(half * 1024, 1024)


class RingSum:
    def __init__(self, parts, size, core_land, far_land, core_sems, far_sems, lean):
        self.lean = lean
        self.parts, self.size, self.core_land, self.far_land = parts, size, core_land, far_land
        self.core_sems, self.far_sems = core_sems, far_sems
        self.me, (self.to_x, self.to_l, self.to_c) = ring_position()

    def block(self, slot):
        return pl.ds(pl.multiple_of((self.me ^ slot) * self.size, self.size), self.size)

    def core(self, slot):
        return remote(
            self.parts.at[self.block(slot | 4)],
            self.core_land.at[slot],
            self.core_sems.at[0, slot],
            self.core_sems.at[1, slot],
            self.to_c,
        )

    def begin(self):
        for slot in (3, 1, 2, 0):
            self.core(slot).start()

    def far(self, index, source):
        device = self.to_x if index in ((0, 1, 2, 3) if self.lean else (0, 2, 4)) else self.to_l
        return remote(
            source, self.far_land.at[index], self.far_sems.at[0, index], self.far_sems.at[1, index], device
        )

    def landed(self, index):
        return lambda: self.far(index, self.far_land.at[index]).wait_recv()

    def terms(self, slot, half):
        return [
            self.parts.at[self.block(slot), half_columns(half)],
            self.core_land.at[slot, :, half_columns(half)],
        ]

    def work(self, due, last_sends, extra):
        if self.lean:
            plan = ((3, 0), (3, 1), (1, 0), (1, 1), (2, 0, 0), (2, 1, 1), (0, 0, 2, 4), (0, 1, 3, 5))
        else:
            plan = ((3, 0), (3, 1), (1, 0), (2, 1), (1, 1, 1), (2, 0, 0), (0, 0, 2, 5), (0, 1, 4, 3))
        first = {}
        for index in sorted(range(8), key=lambda index: due[index]):
            first.setdefault(plan[index][0], index)
        items = []
        for index, (slot, half, *landings) in enumerate(plan):
            waits = [self.landed(landing) for landing in landings]
            if first[slot] == index:
                waits.append(lambda slot=slot: self.core(slot).wait_recv())
            if index < 6:
                sends = lambda source, index=index: [(None, lambda: self.far(index, source), None)]
            else:
                sends = last_sends(half)
            terms = self.terms(slot, half) + [self.far_land.at[landing] for landing in landings]
            items.append((due[index], self.size, terms, sends, waits, extra(half) if index >= 6 else None))
        return items

    def end(self):
        for slot in range(4):
            self.core(slot).wait_send()


class PieceSums:
    def __init__(self, names, piece, landing, sums_at, y_sems, z_sems):
        self.names, self.piece, self.landing, self.sums_at = names, piece, landing, sums_at
        self.y_sems, self.z_sems = y_sems, z_sems
        self.y, self.c, self.h, _ = places()

    def core_of(self, name):
        return name[1]

    def over_y(self, name):
        index = self.names.index(name)
        return remote(
            self.piece(name, 1 - self.y),
            self.landing(name),
            self.y_sems.at[0, index],
            self.y_sems.at[1, index],
            {"y": 1 - self.y},
        )

    def group(self, name):
        groups = []
        for each in self.names:
            key = (each[0], each[2])
            if key not in groups:
                groups.append(key)
        return groups.index((name[0], name[2])), groups

    def over_z(self, name, h, source):
        index = self.names.index(name)
        target = self.sums_at(name, h)
        return (
            lambda: remote(
                source,
                target,
                self.z_sems.at[0, index],
                self.z_sems.at[1 + h, self.group(name)[0]],
                {"c": self.core_of(name), "h": self.c},
            ),
            lambda: pltpu.make_async_copy(source, target, self.z_sems.at[0, index]),
        )

    def sends(self, name):
        here = jnp.logical_and(self.core_of(name) == self.c, self.h == self.c)
        return lambda source: [(here, *self.over_z(name, self.h, source))]

    def end(self):
        for name in self.names:
            self.over_y(name).wait_send()
        self.owned()

    def owned(self):
        seen = []
        for name in self.names:
            group, _ = self.group(name)
            if group in seen:
                continue
            seen.append(group)
            for h in range(2):
                here = jnp.logical_and(h == self.h, self.c == self.h)

                @pl.when(jnp.logical_not(here))
                def _(name=name, h=h):
                    self.over_z(name, h, self.sums_at(name, h))[0]().wait_recv()


class BesideBack:
    def __init__(self, refs):
        self.heads_own, self.parts, self.gate_up, self.down, self.out, self.residual, self.cos, self.sin = refs[:8]
        (
            self.gate_up_sums,
            self.down_sums,
            self.out_sums,
            self.layer,
            core_land,
            far_land,
            self.y_land,
            out_core_land,
            out_far_land,
            self.out_own,
            self.out_y_land,
        ) = refs[8:19]
        (
            self.do,
            self.cs,
            self.sn,
            stage,
            result,
            self.rest,
            self.row_send,
            self.row_recv,
            core_sems,
            far_sems,
            out_core_sems,
            out_far_sems,
            self.layer_sems,
            y_sems,
            z_sems,
            self.out_sems,
            out_y_sems,
            out_z_sems,
            stage_sems,
            self.own_sem,
        ) = refs[19:]
        self.y, self.c, self.h, self.me = places()
        self.sums = Sums(stage, result, stage_sems)
        self.layer_ring = RingSum(self.parts, ROW, core_land, far_land, core_sems, far_sems, True)
        self.out_ring = RingSum(
            self.out, 256, out_core_land, out_far_land, out_core_sems, out_far_sems, False
        )
        names = [("D", 0, 0), ("D", 1, 0), ("G", 0, 0), ("G", 0, 1), ("G", 1, 0), ("G", 1, 1)]
        self.pieces = PieceSums(names, self.piece, lambda name: self.y_land.at[names.index(name)], self.sums_at, y_sems, z_sems)
        self.names = names
        out_names = [("O", 0, 0), ("O", 1, 0)]
        self.out_pieces = PieceSums(out_names, None, None, self.sums_at, out_y_sems, out_z_sems)
        work = self.layer_ring.work((22, 35, 48, 61, 36, 56, 62, 70), self.layer_sends, self.residual_half)
        work += self.out_ring.work((1, 2, 8, 14, 15, 25, 37, 26), self.out_sends, lambda half: None)
        for name, due in zip(names, (3, 16, 29, 44, 57, 69)):
            terms = [self.piece(name, self.y), self.y_land.at[names.index(name)]]
            work.append((due, ROW, terms, self.pieces.sends(name), [self.arrived(name)], None))
        work.append((64, 256, [self.out_own, self.out_y_land], self.out_owners, [self.out_landed], None))
        work.sort(key=lambda item: item[0])
        for item in work:
            self.sums.item(*item)

    def arrived(self, name):
        def wait():
            self.pieces.over_y(name).wait_recv()
            place = self.names.index(name) + 1
            if place < 6:
                self.pieces.over_y(self.names[place]).start()

        return wait

    def out_landed(self):
        remote(
            self.out_own, self.out_y_land, self.out_sems.at[0], self.out_sems.at[2], {"y": 1 - self.y}
        ).wait_recv()

    def out_owners(self, source):
        sends = []
        for name in self.out_pieces.names:
            sends += self.out_pieces.sends(name)(source.at[:, pl.ds(name[1] * 512, 512)])
        return sends

    def residual_half(self, half):
        return (self.residual.at[:, half_columns(half)], self.rest)

    def layer_sends(self, half):
        def sends(source):
            return [
                (
                    None,
                    None,
                    lambda: pltpu.make_async_copy(
                        source, self.layer.at[:, half_columns(half)], self.layer_sems.at[half]
                    ),
                )
            ]

        return sends

    def out_sends(self, half):
        def sends(source):
            return [
                (
                    self.y == half,
                    lambda: remote(
                        source, self.out_y_land, self.out_sems.at[half], self.out_sems.at[2], {"y": 1 - self.y}
                    ),
                    lambda: pltpu.make_async_copy(source, self.out_own, self.out_sems.at[half]),
                )
            ]

        return sends

    def piece(self, name, y):
        kind, core, half = name
        rows = pl.ds(pl.multiple_of((2 * y + core) * 512, 512), 512)
        if kind == "G":
            return self.gate_up.at[rows, half_columns(half)]
        return self.down.at[rows]

    def sums_at(self, name, h):
        kind, _, half = name
        if kind == "G":
            return self.gate_up_sums.at[h, :, half_columns(half)]
        return self.down_sums.at[h] if kind == "D" else self.out_sums.at[h]

    def tables(self):
        return (
            pltpu.make_async_copy(self.cos, self.cs, self.own_sem.at[0]),
            pltpu.make_async_copy(self.sin, self.sn, self.own_sem.at[1]),
        )

    def row_local(self):
        columns = pl.ds(pl.multiple_of(self.me * 256, 256), 256)
        return pltpu.make_async_copy(
            self.heads_own.at[:, columns], self.do.at[rows_at(self.me)], self.own_sem.at[2]
        )

    def row_remote(self, block, sender):
        columns = pl.ds(pl.multiple_of(block * 256, 256), 256)
        return remote(
            self.heads_own.at[:, columns],
            self.do.at[rows_at(sender)],
            self.row_send.at[block],
            self.row_recv.at[sender],
            {"c": block >> 2, "l": (block >> 1) & 1, "x": block & 1},
        )

    def begin(self):
        for copy in self.tables():
            copy.start()
        self.row_local().start()
        enter_ring(wide_partners())

        def send(index, carry):
            block = 7 - index

            @pl.when(block != self.me)
            def _():
                self.row_remote(block, self.me).start()

            return carry

        lax.fori_loop(0, 8, send, 0)
        self.layer_ring.begin()
        self.out_ring.begin()
        self.pieces.over_y(self.names[0]).start()
        for copy in self.tables():
            copy.wait()

    def rows_there(self, block):
        @pl.when(block == self.me)
        def _():
            self.row_local().wait()

        @pl.when(block != self.me)
        def _():
            self.row_remote(block, block).wait_recv()

    def poll(self, unit):
        self.sums.poll(unit)

    def end(self):
        def each(block, carry):
            @pl.when(block != self.me)
            def _():
                self.row_remote(block, self.me).wait_send()

            return carry

        lax.fori_loop(0, 8, each, 0)
        self.sums.last_sent()
        self.layer_ring.end()
        self.out_ring.end()
        self.pieces.end()
        self.out_pieces.owned()


def attend_back_kernel(q_ref, k_ref, v_ref, o_ref, l_ref, *refs):
    given, (dkv_ref, dq_out), outs = refs[:8], refs[8:10], refs[10:21]
    qm, dom, delta, dq, dk, dv, km, pt, dst = refs[21:30]
    beside = BesideBack(given + outs + refs[30:])
    heads = 4
    i, sub = pl.program_id(0), pl.program_id(1)
    block = 7 - i
    blocks = 8
    unit = i * (i + 1) + sub * (i + 1)
    rows_here = rows_at(block)

    @pl.when(jnp.logical_and(i == 0, sub == 0))
    def _():
        beside.begin()

    @pl.when(sub == 0)
    def _():
        beside.rows_there(block)
        q = q_ref[...]
        do = beside.do[rows_here, :]
        for head in range(heads):
            part = slice(head * ROW, (head + 1) * ROW)
            qm[block, part, :] = jnp.where(head_lanes_turned(head), q, jnp.zeros_like(q))
            dom[block, part, :] = jnp.where(head_lanes_plain(head), do, jnp.zeros_like(do))
        product = do.astype(F32) * o_ref[...].astype(F32)
        high = rounded(product)
        low = rounded(product - high.astype(F32))
        head_row = lax.broadcasted_iota(jnp.int32, (8, 256), 0)
        lane = lax.broadcasted_iota(jnp.int32, (8, 256), 1)
        pick = jnp.where(lane // 64 == head_row, 1.0, 0.0).astype(BF)
        sums = lax.dot_general(pick, high, NT, preferred_element_type=F32)
        sums += lax.dot_general(pick, low, NT, preferred_element_type=F32)
        delta[block] = sums[:heads, :]
        dq[rows_here, :] = jnp.zeros((ROW, 256), F32)

    beside.poll(unit)
    key_row = lax.broadcasted_iota(jnp.int32, (KEYS, ROW), 0)
    query_col = lax.broadcasted_iota(jnp.int32, (KEYS, ROW), 1)
    inner = pl.multiple_of(sub * KEYS, KEYS)
    k = k_ref[pl.ds(inner, KEYS), :]
    v = v_ref[pl.ds(inner, KEYS), :]
    for head in range(heads):
        km[head] = jnp.where(head_lanes_turned(head), k, jnp.zeros_like(k))
    dk[...] = jnp.zeros_like(dk)
    dv[...] = jnp.zeros_like(dv)

    def query_part(place, diagonal):
        rows = rows_at(place)
        for head in range(heads):
            part = slice(head * ROW, (head + 1) * ROW)
            st = lax.dot_general(k, qm[place, part, :], NT, preferred_element_type=F32)
            dp = lax.dot_general(v, dom[place, part, :], NT, preferred_element_type=F32)
            p = jnp.exp2(st - l_ref[place, head : head + 1, :])
            if diagonal:
                p = jnp.where(key_row + inner <= query_col, p, 0.0)
            ds = p * (dp - delta[place, head : head + 1, :])
            pt[:, part] = p.astype(BF)
            dst[:, part] = ds.astype(BF)
        dv[...] += lax.dot_general(pt[...], dom[place], NN, preferred_element_type=F32)
        dk[...] += lax.dot_general(dst[...], qm[place], NN, preferred_element_type=F32)
        total = lax.dot_general(dst[:, 0:ROW], km[0], TN, preferred_element_type=F32)
        for head in range(1, heads):
            part = slice(head * ROW, (head + 1) * ROW)
            total += lax.dot_general(dst[:, part], km[head], TN, preferred_element_type=F32)
        dq[rows, :] += total

    query_part(block, True)

    def later(query_block, carry):
        beside.poll(unit + query_block - block)
        query_part(query_block, False)
        return carry

    lax.fori_loop(block + 1, blocks, later, 0)
    table = pl.ds(pl.multiple_of(block * ROW + inner, KEYS), KEYS)
    cs, sn = beside.cs[table, :], beside.sn[table, :]
    d = dk[...] * (1.0 / LOG2E)
    d1, d2 = d[:, :128], d[:, 128:]
    dkv_ref[pl.ds(inner, KEYS), 0:128] = rounded(d1 * cs + d2 * sn)
    dkv_ref[pl.ds(inner, KEYS), 128:256] = rounded(d2 * cs - d1 * sn)
    dkv_ref[pl.ds(inner, KEYS), 256:512] = rounded(dv[...])

    @pl.when(jnp.logical_and(i == 7, sub == 1))
    def _():
        def finish(place, carry):
            rows = rows_at(place)
            cs, sn = beside.cs[rows, :], beside.sn[rows, :]
            d = dq[rows, :] * 0.125
            d1, d2 = d[:, :128], d[:, 128:]
            beside.do[rows, 0:128] = rounded(d1 * cs + d2 * sn)
            beside.do[rows, 128:256] = rounded(d2 * cs - d1 * sn)
            return carry

        lax.fori_loop(0, blocks, finish, 0)
        copy = pltpu.make_async_copy(beside.do, dq_out, beside.own_sem.at[4])
        copy.start()
        copy.wait()
        beside.end()


def attend_back(q, k, v, o, level, heads_own, parts, gate_up, down, out, residual, cos, sin):
    length = q.shape[0]
    blocks = length // ROW
    dma = pltpu.SemaphoreType.DMA
    anywhere = pl.BlockSpec(memory_space=pl.ANY)

    def key_spec(width):
        return pl.BlockSpec((ROW, width), lambda i, sub: (7 - i, 0))

    shapes = [
        (2, 512, 2048),
        (2, 512, 1024),
        (2, 256, 512),
        (ROW, 2048),
        (4, ROW, 2048),
        (6, ROW, 1024),
        (6, 512, 1024),
        (4, 256, 2048),
        (6, 256, 1024),
        (256, 1024),
        (256, 1024),
    ]
    return pl.pallas_call(
        attend_back_kernel,
        grid=(blocks, 2),
        in_specs=[key_spec(256)] * 4
        + [pl.BlockSpec((blocks, 4, ROW), lambda i, sub: (0, 0, 0))]
        + [anywhere] * 8,
        out_specs=[key_spec(512)] + [anywhere] * (1 + len(shapes)),
        out_shape=[jax.ShapeDtypeStruct((length, 512), BF), jax.ShapeDtypeStruct((length, 256), BF)]
        + [jax.ShapeDtypeStruct(shape, BF) for shape in shapes],
        scratch_shapes=[
            pltpu.VMEM((blocks, 4 * ROW, 256), BF),
            pltpu.VMEM((blocks, 4 * ROW, 256), BF),
            pltpu.VMEM((blocks, 4, ROW), F32),
            pltpu.VMEM((length, 256), F32),
            pltpu.VMEM((KEYS, 256), F32),
            pltpu.VMEM((KEYS, 256), F32),
            pltpu.VMEM((4, KEYS, 256), BF),
            pltpu.VMEM((KEYS, 4 * ROW), BF),
            pltpu.VMEM((KEYS, 4 * ROW), BF),
            pltpu.VMEM((length, 256), BF),
            pltpu.VMEM((length, 128), F32),
            pltpu.VMEM((length, 128), F32),
            pltpu.VMEM((2, 4, ROW, 1024), BF),
            pltpu.VMEM((2, ROW, 1024), BF),
            pltpu.VMEM((ROW, 1024), F32),
            dma((8,)),
            dma((8,)),
            dma((2, 4)),
            dma((2, 6)),
            dma((2, 4)),
            dma((2, 6)),
            dma((2,)),
            dma((2, 6)),
            dma((3, 6)),
            dma((3,)),
            dma((2, 2)),
            dma((3, 2)),
            dma((2, 5)),
            dma((5,)),
        ],
        compiler_params=pltpu.CompilerParams(
            collective_id=7, has_side_effects=True, vmem_limit_bytes=60 * 2**20
        ),
        cost_estimate=pl.CostEstimate(
            flops=19 * 10**9 * blocks, bytes_accessed=20 * 2**20, transcendentals=0
        ),
    )(q, k, v, o, level, heads_own, parts, gate_up, down, out, residual, cos, sin)


def ring_shards(
    layer_input,
    cotangent,
    counts,
    positions,
    qkv_master,
    qkv_moment,
    qkv_average,
    out_master,
    out_moment,
    out_average,
    gate_up_master,
    gate_up_moment,
    gate_up_average,
    down_master,
    down_moment,
    down_average,
    gains_master,
    gains_moment,
    gains_average,
):
    y, c, h, l, x = (lax.axis_index(name) for name in AXES)
    own = 4 * c + 2 * l + x
    plain_y, plain_c, straight = y == 0, c == 0, c == h

    def both_y(mine, other, axis):
        return jnp.where(
            plain_y,
            jnp.concatenate([mine, other], axis=axis),
            jnp.concatenate([other, mine], axis=axis),
        )

    def both_cores(mine, other):
        return jnp.where(plain_c, mine, other), jnp.where(plain_c, other, mine)

    turn = column_order()
    rows_in = swap_ch(layer_input).astype(F32)
    gains_here = gains_master.astype(BF)
    gains_near = jnp.concatenate(both_cores(gains_here, flip(gains_here, "c")), axis=1)
    gains_all = both_y(gains_near, flip(gains_near, "y"), 1).astype(F32)
    gain_first, gain_second = gains_all[0], gains_all[1]
    qkv_shard = jnp.dot(qkv_master.astype(BF), turn, preferred_element_type=F32).astype(BF)
    scale_first = rms_scale(rows_in)
    normed_own = (rows_in * scale_first * gain_first).astype(BF)
    frequency = rope_theta ** (
        -((jnp.arange(128, dtype=jnp.int32) % 32).astype(F32) * 2.0) / HD
    )
    positions_here = jnp.where(straight, positions, flip(positions, "c"))
    angles = positions_here.astype(F32)[:, None] * frequency[None, :]
    cosine, sine = jnp.cos(angles), jnp.sin(angles)
    count_here = counts.astype(F32)
    count_total = count_here + flip(count_here, "c")
    count_total = count_total + flip(count_total, "y")
    grad_here = (4.0 * count_here[0] / count_total[0] * cotangent.astype(F32)).astype(BF)
    normed, queries, keys, values, qkv_weight, grad_own = gather_product(
        normed_own,
        (cosine, sine),
        (qkv_shard, grad_here),
        ((2048, 768), (ROW, 2048)),
        256,
        attention_finish,
        First,
        [pltpu.VMEM((2048, 768), BF)]
        + SPREAD_SEMAPHORES
        + [pltpu.SemaphoreType.DMA((4,)), pltpu.VMEM((ROW, 2048), BF)],
        1,
    )
    gate_up_shard = jnp.concatenate([gate_up_master[0], gate_up_master[1]], axis=1).astype(BF)
    attended, level, out_weight, gate_up_weight, grad_out, attended_own = attend(
        queries, keys, values, out_master.astype(BF), gate_up_shard, grad_own
    )
    grad_rows = grad_own.astype(F32)
    residual = rows_in + jnp.dot(attended_own, out_weight, preferred_element_type=F32)
    scale_second = rms_scale(residual)
    normed_second, gate, up, activation, down_weight = gather_product(
        (residual * scale_second * gain_second).astype(BF),
        (gate_up_weight,),
        (down_master.astype(BF),),
        ((1024, 2048),),
        1024,
        feed_forward_finish,
        Second,
        SPREAD_SEMAPHORES + [pltpu.VMEM((2, 512, 512), BF)],
        2,
    )

    grad_normed_second, grad_gate_up = feed_forward_back(
        grad_out, gate, up, down_weight, gate_up_weight, 3
    )
    gate_up_grad = lax.dot_general(
        normed_second, grad_gate_up, TN, preferred_element_type=F32
    ).astype(BF)
    down_grad = lax.dot_general(grad_out, activation, TN, preferred_element_type=F32).astype(BF)
    layer_parts = jnp.dot(activation, down_weight, preferred_element_type=F32).astype(BF)

    def norm_grad(values, scale, gain, grad):
        scaled = grad * gain
        back = scale * (
            scaled - values * scale * scale * jnp.mean(scaled * values, axis=-1, keepdims=True)
        )
        return back, jnp.sum(grad * values * scale, axis=0)

    residual_grad, gain_second_part = norm_grad(
        residual, scale_second, gain_second, grad_normed_second
    )
    residual_grad = residual_grad + grad_rows
    residual_low = residual_grad.astype(BF)
    grad_heads = lax.dot_general(residual_low, out_weight, NT, preferred_element_type=F32).astype(BF)
    out_grad = lax.dot_general(attended_own, residual_low, TN, preferred_element_type=F32).astype(BF)
    grad_kv, grad_q, gate_up_sums, down_sums, out_sums, layer_own, *_ = attend_back(
        queries, keys, values, attended, level, grad_heads, layer_parts, gate_up_grad, down_grad, out_grad, residual, cosine, sine
    )
    gate_up_grad_own = gate_up_sums[0].astype(F32) + gate_up_sums[1].astype(F32)
    unit = jnp.eye(512, dtype=BF)
    down_grad_own = lax.dot_general(
        down_sums.reshape(1024, 1024), jnp.concatenate([unit, unit]), TN, preferred_element_type=F32
    )
    out_grad_own = out_sums[0].astype(F32) + out_sums[1].astype(F32)

    grad_mixture = jnp.concatenate([grad_q, grad_kv], axis=1)
    qkv_grad = lax.dot_general(normed, grad_mixture, TN, preferred_element_type=F32).astype(BF)
    qkv_grad = lax.dot_general(qkv_grad, turn, NT, preferred_element_type=F32).astype(BF)
    grad_normed_first, qkv_sums, _, layer_output = product_scatter(
        grad_mixture, qkv_weight, NT, 5, qkv_grad, layer_own
    )
    qkv_grad_own = qkv_sums[0].astype(F32) + qkv_sums[1].astype(F32)

    input_back, gain_first_part = norm_grad(rows_in, scale_first, gain_first, grad_normed_first)
    input_grad = swap_ch((residual_grad + input_back).astype(BF)).astype(F32)

    gain_grads = jnp.stack([gain_first_part, gain_second_part])
    for bit in "xlchy":
        gain_grads = gain_grads + flip(gain_grads, bit)
    gain_grad_own = lax.dynamic_slice_in_dim(gain_grads, (2 * y + c) * 512, 512, 1)

    rate_unit = float(4 * 8 * ROW) ** (-0.5)
    qkv_new = apply_update(qkv_master, qkv_grad_own, qkv_moment, qkv_average, rate_qkv * rate_unit)
    out_new = apply_update(out_master, out_grad_own, out_moment, out_average, rate_out * rate_unit)
    gate_up_grad_own = jnp.stack([gate_up_grad_own[:, :1024], gate_up_grad_own[:, 1024:]])
    gate_up_new = apply_update(
        gate_up_master, gate_up_grad_own, gate_up_moment, gate_up_average, rate_gate_up * rate_unit
    )
    down_new = apply_update(
        down_master, down_grad_own, down_moment, down_average, rate_down * rate_unit
    )
    gains_new = apply_update(
        gains_master, gain_grad_own, gains_moment, gains_average, rate_gains * rate_unit
    )
    return (layer_output, input_grad) + qkv_new + out_new + gate_up_new + down_new + gains_new


def solution(mesh):
    in_specs = (
        P(("seq", "tp"), None),
        P(("seq", "tp"), None),
        P("seq"),
        P("seq"),
        P("seq", "tp"),
        P("seq", "tp"),
        P("seq", "tp"),
        P("tp", "seq"),
        P("tp", "seq"),
        P("tp", "seq"),
        P(None, "seq", "tp"),
        P(None, "seq", "tp"),
        P(None, "seq", "tp"),
        P("tp", "seq"),
        P("tp", "seq"),
        P("tp", "seq"),
        P(None, "seq"),
        P(None, "seq"),
        P(None, "seq"),
    )
    out_specs = (
        P(("seq", "tp"), None),
        P(("seq", "tp"), None),
        P("seq", "tp"),
        P("seq", "tp"),
        P("seq", "tp"),
        P("seq", "tp"),
        P("tp", "seq"),
        P("tp", "seq"),
        P("tp", "seq"),
        P("tp", "seq"),
        P(None, "seq", "tp"),
        P(None, "seq", "tp"),
        P(None, "seq", "tp"),
        P(None, "seq", "tp"),
        P("tp", "seq"),
        P("tp", "seq"),
        P("tp", "seq"),
        P("tp", "seq"),
        P(None, "seq"),
        P(None, "seq"),
        P(None, "seq"),
        P(None, "seq"),
    )
    if ring_plan_fits(mesh):
        fine = jax.sharding.Mesh(mesh.devices.reshape(2, 2, 2, 2, 2), AXES)
        names = {"seq": ("y", "c"), "tp": ("h", "l", "x")}

        def finer(spec):
            parts = []
            for entry in spec:
                entry = (entry,) if isinstance(entry, str) else (entry or ())
                parts.append(sum((names[name] for name in entry), ()) or None)
            return P(*parts)

        return jax.shard_map(
            ring_shards,
            mesh=fine,
            in_specs=tuple(finer(spec) for spec in in_specs),
            out_specs=tuple(finer(spec) for spec in out_specs),
            check_vma=False,
        )
    return jax.shard_map(shards, mesh=mesh, in_specs=in_specs, out_specs=out_specs, check_vma=False)
```

```python
import jax
import jax.numpy as jnp
from jax import lax
from jax.experimental import pallas as pl
from jax.experimental.pallas import tpu as pltpu
from jax.sharding import PartitionSpec as P

HD = 64


norm_epsilon = 1e-05
rope_theta = 130000.0
momentum_coef = 0.9
average_coef = 0.5
masked_score = -1e30
rate_qkv = 0.004
rate_out = 2.0
rate_gate_up = 0.03
rate_down = 0.009
rate_gains = 0.1


def rms_scale(values):
    return lax.rsqrt(jnp.mean(values * values, axis=-1, keepdims=True) + norm_epsilon)


def rope_tables(positions, head_size):
    frequency = rope_theta ** (-(jnp.arange(head_size // 2, dtype=jnp.float32) * 2.0) / head_size)
    angles = positions.astype(jnp.float32)[:, None] * frequency[None, :]
    return (jnp.cos(angles)[:, None, :], jnp.sin(angles)[:, None, :])


def rotate(vectors, cosine_table, sine_table):
    half_width = vectors.shape[-1] // 2
    lower_half = vectors[..., :half_width]
    upper_half = vectors[..., half_width:]
    return jnp.concatenate(
        [
            lower_half * cosine_table - upper_half * sine_table,
            upper_half * cosine_table + lower_half * sine_table,
        ],
        axis=-1,
    )


def unrotate(grads, cosine_table, sine_table):
    half_width = grads.shape[-1] // 2
    lower_half = grads[..., :half_width]
    upper_half = grads[..., half_width:]
    return jnp.concatenate(
        [
            lower_half * cosine_table + upper_half * sine_table,
            upper_half * cosine_table - lower_half * sine_table,
        ],
        axis=-1,
    )


def norm_back(values, gain, grad):
    scale_rows = rms_scale(values)
    scaled = grad * gain
    back = scale_rows * (
        scaled
        - values * scale_rows * scale_rows * jnp.mean(scaled * values, axis=-1, keepdims=True)
    )
    return (back, jnp.sum(grad * values * scale_rows, axis=0))


def apply_update(master, grad, moment, average, rate):
    moment_new = momentum_coef * moment + grad
    master_new = master - rate * (grad + momentum_coef * moment_new)
    average_new = average_coef * average + (1.0 - average_coef) * master_new
    return (moment_new, average_new, master_new, master_new.astype(jnp.bfloat16))


def shards(
    layer_input,
    cotangent,
    counts,
    positions,
    qkv_master,
    qkv_moment,
    qkv_average,
    out_master,
    out_moment,
    out_average,
    gate_up_master,
    gate_up_moment,
    gate_up_average,
    down_master,
    down_moment,
    down_average,
    gains_master,
    gains_moment,
    gains_average,
):
    tp_size = lax.axis_size("tp")
    seq_size = lax.axis_size("seq")
    own_rows = layer_input.shape[0]
    length = own_rows * tp_size
    qkv_weight, out_weight, gate_up_weight, down_weight, gain_weight = (
        lax.all_gather(qkv_master.astype(jnp.bfloat16), "seq", axis=0, tiled=True),
        lax.all_gather(out_master.astype(jnp.bfloat16), "seq", axis=1, tiled=True),
        lax.all_gather(gate_up_master.astype(jnp.bfloat16), "seq", axis=1, tiled=True),
        lax.all_gather(down_master.astype(jnp.bfloat16), "seq", axis=1, tiled=True),
        lax.all_gather(gains_master.astype(jnp.bfloat16), "seq", axis=1, tiled=True),
    )
    heads_local = qkv_weight.shape[1] // (3 * HD)
    count_total = lax.psum(counts.astype(jnp.float32), "seq")
    seq_weight = seq_size * counts.astype(jnp.float32)[0] / count_total[0]
    gain_first = gain_weight[0].astype(jnp.float32)
    gain_second = gain_weight[1].astype(jnp.float32)
    gathered = lax.all_gather(layer_input, "tp", axis=0, tiled=True)
    inputs = gathered.astype(jnp.float32)
    normed = (inputs * rms_scale(inputs) * gain_first).astype(jnp.bfloat16)
    mixture = jnp.dot(normed, qkv_weight, preferred_element_type=jnp.float32).reshape(
        length, heads_local, 3, HD
    )
    cosine_table, sine_table = rope_tables(positions, HD)
    queries = rotate(mixture[:, :, 0], cosine_table, sine_table).astype(jnp.bfloat16)
    key_rows = rotate(mixture[:, :, 1], cosine_table, sine_table).astype(jnp.bfloat16)
    value_rows = mixture[:, :, 2].astype(jnp.bfloat16)
    block_rows = min(512, length)
    block_count = length // block_rows
    score_scale = HD ** (-0.5)

    def block_scores(block_index):
        key_end = (block_index + 1) * block_rows
        query_block = queries[block_index * block_rows : key_end]
        row_index = block_index * block_rows + jnp.arange(block_rows)
        allowed = jnp.arange(key_end)[None, :] <= row_index[:, None]
        scores = score_scale * jnp.einsum(
            "qhd,khd->hqk", query_block, key_rows[:key_end], preferred_element_type=jnp.float32
        )
        return (query_block, jnp.where(allowed[None], scores, masked_score))

    attended_list = []
    log_totals = []
    for block_index in range(block_count):
        query_block, scores = block_scores(block_index)
        key_end = (block_index + 1) * block_rows
        row_max = jnp.max(scores, axis=-1, keepdims=True)
        exp_scores = jnp.exp(scores - row_max)
        row_total = jnp.sum(exp_scores, axis=-1, keepdims=True)
        soft_scores = (exp_scores / row_total).astype(jnp.bfloat16)
        attended_block = jnp.einsum(
            "hqk,khd->qhd", soft_scores, value_rows[:key_end], preferred_element_type=jnp.float32
        )
        attended_list.append(attended_block.astype(jnp.bfloat16))
        log_totals.append(row_max + jnp.log(row_total))
    attended = jnp.concatenate(attended_list, axis=0).reshape(length, heads_local * HD)
    own_start = lax.axis_index("tp") * own_rows
    input_own = layer_input.astype(jnp.float32)
    branch = lax.psum(
        jnp.dot(attended, out_weight, preferred_element_type=jnp.float32).astype(jnp.bfloat16), "tp"
    ).astype(jnp.float32)
    residual = inputs + branch
    normed_second = (residual * rms_scale(residual) * gain_second).astype(jnp.bfloat16)
    resid_own = lax.dynamic_slice_in_dim(residual, own_start, own_rows, 0)
    gate_pre = jnp.dot(normed_second, gate_up_weight[0], preferred_element_type=jnp.float32)
    up_pre = jnp.dot(normed_second, gate_up_weight[1], preferred_element_type=jnp.float32)
    gate_sigmoid = jax.nn.sigmoid(gate_pre)
    activation = (gate_pre * gate_sigmoid * up_pre).astype(jnp.bfloat16)
    layer_output = (
        resid_own
        + lax.psum_scatter(
            jnp.dot(activation, down_weight, preferred_element_type=jnp.float32).astype(
                jnp.bfloat16
            ),
            "tp",
            scatter_dimension=0,
            tiled=True,
        ).astype(jnp.float32)
    ).astype(jnp.bfloat16)
    cot_all = lax.all_gather(cotangent, "tp", axis=0, tiled=True)
    grad_out = (seq_weight * cot_all.astype(jnp.float32)).astype(jnp.bfloat16)
    grad_down = jnp.einsum("tf,td->fd", activation, grad_out, preferred_element_type=jnp.float32)
    grad_act = jnp.einsum("td,fd->tf", grad_out, down_weight, preferred_element_type=jnp.float32)
    grad_gate = (grad_act * up_pre * gate_sigmoid * (1.0 + gate_pre * (1.0 - gate_sigmoid))).astype(
        jnp.bfloat16
    )
    grad_up = (grad_act * gate_pre * gate_sigmoid).astype(jnp.bfloat16)
    grad_gate_up = jnp.stack(
        [
            jnp.einsum("td,tf->df", normed_second, grad_gate, preferred_element_type=jnp.float32),
            jnp.einsum("td,tf->df", normed_second, grad_up, preferred_element_type=jnp.float32),
        ]
    )
    grad_normed_second = lax.psum_scatter(
        (
            jnp.einsum(
                "tf,df->td", grad_gate, gate_up_weight[0], preferred_element_type=jnp.float32
            )
            + jnp.einsum(
                "tf,df->td", grad_up, gate_up_weight[1], preferred_element_type=jnp.float32
            )
        ).astype(jnp.bfloat16),
        "tp",
        scatter_dimension=0,
        tiled=True,
    ).astype(jnp.float32)
    grad_resid_own, gain_second_part = norm_back(resid_own, gain_second, grad_normed_second)
    grad_resid_own = grad_resid_own + seq_weight * cotangent.astype(jnp.float32)
    resid_grad_rows = lax.all_gather(grad_resid_own.astype(jnp.bfloat16), "tp", axis=0, tiled=True)
    grad_out_proj = jnp.einsum(
        "tc,td->cd", attended, resid_grad_rows, preferred_element_type=jnp.float32
    )
    grad_attended = (
        jnp.einsum("td,cd->tc", resid_grad_rows, out_weight, preferred_element_type=jnp.float32)
        .astype(jnp.bfloat16)
        .reshape(length, heads_local, HD)
    )
    grad_keys = jnp.zeros((length, heads_local, HD), jnp.float32)
    grad_values = jnp.zeros((length, heads_local, HD), jnp.float32)
    query_grads = []
    for block_index in range(block_count):
        key_end = (block_index + 1) * block_rows
        query_block, scores = block_scores(block_index)
        soft_scores = jnp.exp(scores - log_totals[block_index])
        grad_block = grad_attended[block_index * block_rows : key_end]
        grad_soft = jnp.einsum(
            "qhd,khd->hqk", grad_block, value_rows[:key_end], preferred_element_type=jnp.float32
        )
        row_delta = jnp.sum(soft_scores * grad_soft, axis=-1, keepdims=True)
        grad_scores = (soft_scores * (grad_soft - row_delta)).astype(jnp.bfloat16)
        query_grads.append(
            score_scale
            * jnp.einsum(
                "hqk,khd->qhd", grad_scores, key_rows[:key_end], preferred_element_type=jnp.float32
            )
        )
        grad_keys = grad_keys.at[:key_end].add(
            score_scale
            * jnp.einsum(
                "hqk,qhd->khd", grad_scores, query_block, preferred_element_type=jnp.float32
            )
        )
        grad_values = grad_values.at[:key_end].add(
            jnp.einsum(
                "hqk,qhd->khd",
                soft_scores.astype(jnp.bfloat16),
                grad_block,
                preferred_element_type=jnp.float32,
            )
        )
    grad_queries = jnp.concatenate(query_grads, axis=0)
    grad_mixture = (
        jnp.stack(
            [
                unrotate(grad_queries, cosine_table, sine_table),
                unrotate(grad_keys, cosine_table, sine_table),
                grad_values,
            ],
            axis=2,
        )
        .astype(jnp.bfloat16)
        .reshape(length, heads_local * 3 * HD)
    )
    grad_qkv = jnp.einsum("td,tc->dc", normed, grad_mixture, preferred_element_type=jnp.float32)
    grad_normed_first = lax.psum_scatter(
        jnp.einsum(
            "tc,dc->td", grad_mixture, qkv_weight, preferred_element_type=jnp.float32
        ).astype(jnp.bfloat16),
        "tp",
        scatter_dimension=0,
        tiled=True,
    ).astype(jnp.float32)
    grad_input_own, gain_first_part = norm_back(input_own, gain_first, grad_normed_first)
    input_grad = grad_resid_own + grad_input_own
    gain_grads = lax.psum(jnp.stack([gain_first_part, gain_second_part]), ("seq", "tp"))
    gain_grad_own = lax.dynamic_slice_in_dim(
        gain_grads, lax.axis_index("seq") * gains_master.shape[1], gains_master.shape[1], 1
    )
    qkv_grad_own, out_grad_own, gate_up_grad_own, down_grad_own = (
        lax.psum_scatter(
            grad_qkv.astype(jnp.bfloat16), "seq", scatter_dimension=0, tiled=True
        ).astype(jnp.float32),
        lax.psum_scatter(
            grad_out_proj.astype(jnp.bfloat16), "seq", scatter_dimension=1, tiled=True
        ).astype(jnp.float32),
        lax.psum_scatter(
            grad_gate_up.astype(jnp.bfloat16), "seq", scatter_dimension=1, tiled=True
        ).astype(jnp.float32),
        lax.psum_scatter(
            grad_down.astype(jnp.bfloat16), "seq", scatter_dimension=1, tiled=True
        ).astype(jnp.float32),
    )
    rate_unit = float(length * seq_size) ** (-0.5)
    qkv_new = apply_update(qkv_master, qkv_grad_own, qkv_moment, qkv_average, rate_qkv * rate_unit)
    out_new = apply_update(out_master, out_grad_own, out_moment, out_average, rate_out * rate_unit)
    gate_up_new = apply_update(
        gate_up_master, gate_up_grad_own, gate_up_moment, gate_up_average, rate_gate_up * rate_unit
    )
    down_new = apply_update(
        down_master, down_grad_own, down_moment, down_average, rate_down * rate_unit
    )
    gains_new = apply_update(
        gains_master, gain_grad_own, gains_moment, gains_average, rate_gains * rate_unit
    )
    return (
        layer_output,
        input_grad,
        qkv_new[0],
        qkv_new[1],
        qkv_new[2],
        qkv_new[3],
        out_new[0],
        out_new[1],
        out_new[2],
        out_new[3],
        gate_up_new[0],
        gate_up_new[1],
        gate_up_new[2],
        gate_up_new[3],
        down_new[0],
        down_new[1],
        down_new[2],
        down_new[3],
        gains_new[0],
        gains_new[1],
        gains_new[2],
        gains_new[3],
    )


AXES = ("y", "c", "h", "l", "x")
RING = ("c", "l", "x")
MESH = pl.DeviceIdType.MESH
ROW = 512
BF = jnp.bfloat16
F32 = jnp.float32
LOG2E = 1.4426950408889634
NT = (((1,), (1,)), ((), ()))
NN = (((1,), (0,)), ((), ()))
TN = (((0,), (0,)), ((), ()))


def ring_plan_fits(mesh):
    return mesh.shape["seq"] == 4 and mesh.shape["tp"] == 8


def device_pairs(target):
    pairs = []
    for index in range(32):
        y, c, h, l, x = (index >> 4) & 1, (index >> 3) & 1, (index >> 2) & 1, (index >> 1) & 1, index & 1
        goal = target(y, c, h, l, x)
        if goal is not None:
            y, c, h, l, x = goal
            pairs.append((index, 16 * y + 8 * c + 4 * h + 2 * l + x))
    return pairs


def move(values, target):
    return lax.ppermute(values, AXES, device_pairs(target))


def flip(values, bits):
    return move(
        values,
        lambda y, c, h, l, x: (
            y ^ ("y" in bits),
            c ^ ("c" in bits),
            h ^ ("h" in bits),
            l ^ ("l" in bits),
            x ^ ("x" in bits),
        ),
    )


def swap_ch(values):
    return move(values, lambda y, c, h, l, x: (y, h, c, l, x))


def rounded(values):
    return values.astype(BF)


def ring_position():
    c, l, x = (lax.axis_index(name) for name in RING)
    partners = ({"x": 1 - x}, {"l": 1 - l}, {"c": 1 - c})
    return 4 * c + 2 * l + x, partners


def enter_ring(partners):
    barrier = pltpu.get_barrier_semaphore()
    for partner in partners:
        pl.semaphore_signal(barrier, inc=1, device_id=partner, device_id_type=MESH)
    pl.semaphore_wait(barrier, len(partners))


def rows_at(block, part=None):
    if part is None:
        return pl.ds(pl.multiple_of(block * ROW, ROW), ROW)
    half = ROW // 2
    return pl.ds(pl.multiple_of(block * ROW + part * half, half), half)


def remote(source, target, sent, received, device):
    return pltpu.make_async_remote_copy(
        src_ref=source,
        dst_ref=target,
        send_sem=sent,
        recv_sem=received,
        device_id=device,
        device_id_type=MESH,
    )


def places():
    y, c, h, l, x = (lax.axis_index(name) for name in AXES)
    return y, c, h, 4 * c + 2 * l + x


def wide_partners():
    y, c, h, _ = places()
    _, (to_x, to_l, to_c) = ring_position()
    mixed = ({**to_x, **to_l}, {**to_x, **to_c}, {**to_l, **to_c}, {**to_x, **to_l, **to_c})
    across = ({"c": 0, "h": 1 - h}, {"c": 1, "h": 1 - h})
    return (to_x, to_l, to_c) + mixed + ({"y": 1 - y},) + across


class Ring:
    def __init__(self, buffer, size, send, recv, lean=False, own=None, cut=None):
        self.buffer, self.size, self.send, self.recv, self.own = buffer, size, send, recv, own
        self.cut = size // 2 if cut is None else cut
        me, (to_x, to_l, to_c) = ring_position()
        self.plan = (
            (me, 0, to_x, me ^ 1),
            (me, 1, to_l, me ^ 2),
            (me, None, to_c, me ^ 4),
            (me, 1, to_x, me ^ 1),
            (me, 0, to_l, me ^ 2),
            (me ^ 1, 0, to_l, me ^ 3),
            (me ^ 2, 1, to_x, me ^ 3),
            (me ^ 1, None, to_c, me ^ 5),
            (me ^ 2, None, to_c, me ^ 6),
            (me ^ 3, None, to_c, me ^ 7),
        )
        if lean:
            self.plan = self.plan[:5] + ((me ^ 2, 0, to_x, me ^ 3),) + self.plan[6:]

    def copy(self, index, block):
        _, part, partner, _ = self.plan[index]
        size = (self.cut, self.size - self.cut, self.size)[2 if part is None else part]
        offset = self.cut if part == 1 else 0
        place = self.buffer.at[pl.ds(pl.multiple_of(block * self.size + offset, 128), size)]
        source = place
        if self.own is not None and index < 5:
            source = self.own.at[pl.ds(offset, size)]
        return remote(source, place, self.send.at[index], self.recv.at[index], partner)

    def start(self, *indices):
        for index in indices:
            self.copy(index, self.plan[index][0]).start()

    def arrived(self, *indices):
        for index in indices:
            self.copy(index, self.plan[index][3]).wait_recv()

    def sent(self):
        for index in range(10):
            self.copy(index, self.plan[index][0]).wait_send()


class Spread:
    def __init__(self, source, target, near, far, keep, stage=None):
        self.source, self.target, self.near, self.far, self.keep = source, target, near, far, keep
        self.stage = stage
        _, self.c, self.h, _ = places()

    def local(self):
        return pltpu.make_async_copy(
            self.source, self.target if self.stage is None else self.stage, self.keep
        )

    def beside(self):
        return remote(self.source, self.target, self.near.at[0], self.near.at[1], {"c": self.h})

    def across(self, core):
        return remote(
            self.source, self.target, self.far.at[2], self.far.at[core], {"c": self.h, "h": 1 - self.h}
        )

    def start(self):
        self.across(self.c).start()

        @pl.when(self.c == self.h)
        def _():
            self.local().start()

        @pl.when(self.c != self.h)
        def _():
            self.beside().start()

    def arrived(self):
        @pl.when(self.c == self.h)
        def _():
            self.local().wait()
            if self.stage is not None:
                copy = pltpu.make_async_copy(self.stage, self.target, self.keep)
                copy.start()
                copy.wait()
            self.beside().wait_recv()

        @pl.when(self.c != self.h)
        def _():
            self.across(0).wait_recv()
            self.across(1).wait_recv()

    def sent(self):
        self.across(self.c).wait_send()

        @pl.when(self.c != self.h)
        def _():
            self.beside().wait_send()


SPREAD_SEMAPHORES = [
    pltpu.SemaphoreType.DMA((4, 2)),
    pltpu.SemaphoreType.DMA((4, 3)),
    pltpu.SemaphoreType.DMA((4,)),
    pltpu.SemaphoreType.DMA((4, 2)),
    pltpu.SemaphoreType.DMA((4, 2)),
]


class First:
    def __init__(self, refs):
        (self.shard, self.grad), (self.whole, self.moved) = refs[:2], refs[2:4]
        self.w, near, far, keep, self.y_send, self.y_recv, self.grad_sems, self.stage = refs[4:]
        self.y, self.c, self.h, _ = places()
        first = (2 * self.y + self.c) * 512
        self.pieces = [
            Spread(
                self.shard.at[pl.ds(k * 256, 256)],
                self.w.at[pl.ds(pl.multiple_of(first + k * 256, 256), 256)],
                near.at[k],
                far.at[k],
                keep.at[k],
            )
            for k in range(2)
        ]

    def over_y(self, k, core, y):
        first = (2 * y + core) * 512 + k * 256
        place = self.w.at[pl.ds(pl.multiple_of(first, 256), 256)]
        return remote(place, place, self.y_send.at[k, core], self.y_recv.at[k, core], {"y": 1 - self.y})

    def grad_load(self):
        return pltpu.make_async_copy(self.grad, self.stage, self.grad_sems.at[2])

    def grad_local(self):
        return pltpu.make_async_copy(self.stage, self.moved, self.grad_sems.at[2])

    def grad_remote(self):
        return remote(
            self.grad, self.moved, self.grad_sems.at[0], self.grad_sems.at[1], {"c": self.h, "h": self.c}
        )

    def run(self, ring):
        for piece in self.pieces:
            piece.start()

        @pl.when(self.c == self.h)
        def _():
            self.grad_load().start()

        for k in range(2):
            self.pieces[k].arrived()
            for core in range(2):
                self.over_y(k, core, self.y).start()
            if k == 0:
                ring.arrived(1)
                ring.start(6)

        @pl.when(self.c == self.h)
        def _():
            self.grad_load().wait()
            self.grad_local().start()

        @pl.when(self.c != self.h)
        def _():
            self.grad_remote().start()

        ring.arrived(4)
        ring.start(5, 8)
        ring.arrived(2, 0, 3)
        ring.start(7)
        for k in range(2):
            for core in range(2):
                self.over_y(k, core, 1 - self.y).wait_recv()
        pltpu.make_async_copy(self.w, self.whole, self.grad_sems.at[3]).start()

    def finish(self):
        for piece in self.pieces:
            piece.sent()
        for k in range(2):
            for core in range(2):
                self.over_y(k, core, self.y).wait_send()
        pltpu.make_async_copy(self.w, self.whole, self.grad_sems.at[3]).wait()

        @pl.when(self.c == self.h)
        def _():
            self.grad_local().wait()

        @pl.when(self.c != self.h)
        def _():
            self.grad_remote().wait_recv()
            self.grad_remote().wait_send()


class Second:
    def __init__(self, refs):
        self.shard, self.whole = refs[:2]
        near, far, keep, self.y_send, self.y_recv, stage = refs[2:]
        self.y, c, _, _ = places()
        columns = pl.ds(pl.multiple_of((2 * self.y + c) * 512, 512), 512)
        self.pieces = [
            Spread(
                self.shard.at[pl.ds(k * 512, 512)],
                self.whole.at[pl.ds(k * 512, 512), columns],
                near.at[k],
                far.at[k],
                keep.at[k],
                stage.at[k],
            )
            for k in range(2)
        ]

    def over_y(self, k, y):
        place = self.whole.at[pl.ds(k * 512, 512), pl.ds(pl.multiple_of(y * 1024, 1024), 1024)]
        return remote(place, place, self.y_send.at[k, 0], self.y_recv.at[k, 0], {"y": 1 - self.y})

    def run(self, ring):
        for piece in self.pieces:
            piece.start()

    def on(self, k):
        self.pieces[k].arrived()
        self.over_y(k, self.y).start()

    def finish(self):
        for k in range(2):
            self.pieces[k].sent()
            self.over_y(k, 1 - self.y).wait_recv()
            self.over_y(k, self.y).wait_send()


def gather_kernel(finish, beside, inputs, outputs, *refs):
    own_ref, refs = refs[0], refs[1:]
    given, refs = refs[:inputs], refs[inputs:]
    full_ref, outs, refs = refs[0], refs[1:4], refs[4:]
    extra_outs, refs = refs[:outputs], refs[outputs:]
    buf, res, send, recv, own_sem, full_sem, out_sem = refs[:7]
    me, _ = ring_position()
    load = pltpu.make_async_copy(own_ref, buf.at[rows_at(me)], own_sem)
    load.start()
    enter_ring(wide_partners())
    load.wait()
    early = beside is First
    ring = Ring(buf, ROW, send, recv, lean=early, cut=256 if early else 128)
    ring.start(0, 1, 2, 3, 4)
    if early:
        more = First(given[2:] + extra_outs + refs[7:])
        w_ref, tables = more.w, given[:2]
    else:
        more = Second(given[1:] + extra_outs + refs[7:])
        w_ref, tables = given[0], ()
    more.run(ring)

    def step_body(step, carry):
        block = me ^ ((step >> 1) | ((step & 1) << 2))
        rows = rows_at(block)
        if not early:

            @pl.when(step == 1)
            def _():
                ring.arrived(2)

            @pl.when(step == 2)
            def _():
                ring.arrived(0)
                ring.start(5)
                ring.arrived(1)
                ring.start(6)
                more.on(0)
                ring.arrived(3)
                ring.start(7)
                more.on(1)
                ring.arrived(4)
                ring.start(8)

        @pl.when(step == 3)
        def _():
            ring.arrived(7)

        @pl.when(step == 5)
        def _():
            ring.arrived(8)

        @pl.when(step == 6)
        def _():
            ring.arrived(5, 6)
            ring.start(9)

        @pl.when(step == 7)
        def _():
            ring.arrived(9)

        pltpu.make_async_copy(buf.at[rows], full_ref.at[rows], full_sem.at[step]).start()
        turn = step & 1

        def out_copy(which, rows):
            return pltpu.make_async_copy(
                res.at[turn, which], outs[which].at[rows], out_sem.at[turn, which]
            )

        @pl.when(step >= 2)
        def _():
            for which in range(3):
                out_copy(which, rows).wait()

        finish(buf, rows, w_ref, tables, res, turn)
        for which in range(3):
            out_copy(which, rows).start()
        return carry

    lax.fori_loop(0, 8, step_body, 0)
    ring.sent()
    more.finish()

    def drain(step, carry):
        rows = rows_at(step)
        pltpu.make_async_copy(buf.at[rows], full_ref.at[rows], full_sem.at[step]).wait()
        return carry

    lax.fori_loop(0, 8, drain, 0)
    for turn in range(2):
        for which in range(3):
            pltpu.make_async_copy(
                res.at[turn, which], outs[which].at[rows_at(0)], out_sem.at[turn, which]
            ).wait()


def feed_forward_finish(buf, rows, w_ref, tables, res, turn):
    def columns(chunk, carry):
        here = pl.multiple_of(chunk * 256, 256)
        block = buf[rows, :]
        g = jnp.dot(block, w_ref[:, pl.ds(here, 256)], preferred_element_type=F32)
        u = jnp.dot(block, w_ref[:, pl.ds(here + 1024, 256)], preferred_element_type=F32)
        res[turn, 0, :, pl.ds(here, 256)] = rounded(g)
        res[turn, 1, :, pl.ds(here, 256)] = rounded(u)
        res[turn, 2, :, pl.ds(here, 256)] = rounded(g * (1.0 / (1.0 + jnp.exp(-g))) * u)
        return carry

    lax.fori_loop(0, 4, columns, 0)


def attention_finish(buf, rows, w_ref, tables, res, turn):
    block = buf[rows, :]
    cs, sn = tables[0][rows, :], tables[1][rows, :]
    for which in range(2):
        m = jnp.dot(block, w_ref[:, which * 256 : which * 256 + 256], preferred_element_type=F32)
        if which == 0:
            m = m * (0.125 * LOG2E)
        m1, m2 = m[:, :128], m[:, 128:]
        res[turn, which, :, 0:128] = rounded(m1 * cs - m2 * sn)
        res[turn, which, :, 128:256] = rounded(m2 * cs + m1 * sn)
    res[turn, 2] = rounded(jnp.dot(block, w_ref[:, 512:768], preferred_element_type=F32))


def gather_product(own, given, anywhere_given, extra_shapes, width, finish, beside, scratch, number):
    anywhere = pl.BlockSpec(memory_space=pl.ANY)
    vmem = pl.BlockSpec(memory_space=pltpu.VMEM)
    length, depth = 8 * ROW, own.shape[1]
    inputs = len(given) + len(anywhere_given)
    return pl.pallas_call(
        lambda *refs: gather_kernel(finish, beside, inputs, len(extra_shapes), *refs),
        in_specs=[anywhere] + [vmem] * len(given) + [anywhere] * len(anywhere_given),
        out_specs=[anywhere] * (4 + len(extra_shapes)),
        out_shape=[jax.ShapeDtypeStruct((length, depth), BF)]
        + [jax.ShapeDtypeStruct((length, width), BF)] * 3
        + [jax.ShapeDtypeStruct(shape, BF) for shape in extra_shapes],
        scratch_shapes=[
            pltpu.VMEM((length, depth), BF),
            pltpu.VMEM((2, 3, ROW, width), BF),
            pltpu.SemaphoreType.DMA((10,)),
            pltpu.SemaphoreType.DMA((10,)),
            pltpu.SemaphoreType.DMA,
            pltpu.SemaphoreType.DMA((8,)),
            pltpu.SemaphoreType.DMA((2, 3)),
        ]
        + scratch,
        compiler_params=pltpu.CompilerParams(
            collective_id=number, has_side_effects=True, vmem_limit_bytes=56 * 2**20
        ),
        cost_estimate=pl.CostEstimate(
            flops=80 * 10**9, bytes_accessed=30 * 2**20, transcendentals=0
        ),
    )(own, *given, *anywhere_given)


def scatter_kernel(dims, cut, kind, *refs):
    beside = 2 if kind == 2 else 0
    if kind == 3:
        grad_ref, gate_ref, up_ref, down_ref, w_ref, out_ref, a_ref = refs[:7]
        refs = refs[7:]
        grad_buf, gate_buf, up_buf, made_sem = refs[11:]
    else:
        a_ref, w_ref, refs = refs[0], refs[1], refs[2:]
        given, refs = refs[:beside], refs[beside:]
        out_ref, refs = refs[0], refs[1:]
        more_outs, refs = refs[: 3 if beside else 0], refs[3 if beside else 0 :]
    abuf, mine, other, sums, ra, rb, near_x, near_l, send, recv, a_sem = refs[:11]
    me, partners = ring_position()
    to_x, to_l, to_c = partners
    order = (7, 3, 5, 6, 1, 2, 4, 0)

    def load(index):
        rows, turn = rows_at(me ^ order[index]), index % 2
        if kind == 3:
            pairs = ((grad_ref, grad_buf), (gate_ref, gate_buf), (up_ref, up_buf))
        else:
            pairs = ((a_ref, abuf),)
        return [
            pltpu.make_async_copy(ref.at[rows], buf.at[turn], a_sem.at[turn, k])
            for k, (ref, buf) in enumerate(pairs)
        ]

    def made(index):
        return pltpu.make_async_copy(
            abuf.at[index % 2], a_ref.at[rows_at(me ^ order[index])], made_sem.at[index % 2]
        )

    def make(index):
        turn = index % 2
        if index >= 2:
            made(index - 2).wait()

        def columns(chunk, carry):
            start = pl.multiple_of(chunk * 256, 256)
            here, there = pl.ds(start, 256), pl.ds(start + 1024, 256)
            d = lax.dot_general(grad_buf[turn], down_ref[here, :], NT, preferred_element_type=F32)
            g = gate_buf[turn, :, here].astype(F32)
            u = up_buf[turn, :, here].astype(F32)
            sigmoid = 1.0 / (1.0 + jnp.exp(-g))
            abuf[turn, :, here] = rounded(d * u * sigmoid * (1.0 + g * (1.0 - sigmoid)))
            abuf[turn, :, there] = rounded(d * g * sigmoid)
            return carry

        lax.fori_loop(0, 4, columns, 0)
        made(index).start()

    for each in load(0):
        each.start()
    enter_ring(wide_partners() if beside else partners)
    if beside:
        tail = WeightTail(given + more_outs + refs[11:])
        tail.begin()

    def copy(index, source, target, partner):
        return pltpu.make_async_remote_copy(
            src_ref=source,
            dst_ref=target,
            send_sem=send.at[index],
            recv_sem=recv.at[index],
            device_id=partner,
            device_id_type=MESH,
        )

    top, bottom = pl.ds(0, cut), pl.ds(cut, ROW - cut)
    turns = {3: 0, 1: 1, 2: 0, 0: 1}
    copies = [copy(slot, mine.at[turns[slot]], other.at[slot], to_c) for slot in range(4)] + [
        copy(4, sums.at[2, top], ra, to_x),
        copy(5, sums.at[2, bottom], rb, to_l),
        copy(6, sums.at[0, top], near_x.at[top], to_x),
        copy(7, sums.at[1, bottom], near_l.at[bottom], to_l),
        copy(8, sums.at[0, bottom], near_x.at[bottom], to_x),
        copy(9, sums.at[1, top], near_l.at[top], to_l),
    ]

    def product(index, store):
        def columns(chunk, carry):
            here = pl.ds(pl.multiple_of(chunk * 256, 256), 256)
            w = w_ref[here, :] if dims == NT else w_ref[:, here]
            store(
                here, lax.dot_general(abuf[index % 2], w, dims, preferred_element_type=F32)
            )
            return carry

        lax.fori_loop(0, 8, columns, 0)

    for index, slot in enumerate(order):
        for each in load(index):
            each.wait()
        if index + 1 < 8:
            for each in load(index + 1):
                each.start()
        if kind == 3:
            make(index)
        if slot >= 4:
            if slot in (6, 4):
                copies[3 if slot == 6 else 1].wait_send()

            def store(here, value, slot=slot):
                mine[turns[slot - 4], :, here] = rounded(value)

            product(index, store)
            copies[slot - 4].start()
        elif slot > 0:
            copies[slot].wait_recv()

            def store(here, value, slot=slot):
                sums[slot - 1, :, here] = rounded(value + other[slot, :, here].astype(F32))

            product(index, store)
            if slot == 3:
                copies[4].start()
                copies[5].start()
            if slot == 1:
                copies[6].start()
            if slot == 2:
                copies[7].start()
                copies[5].wait_recv()
                sums[0, bottom, :] = rounded(
                    sums[0, bottom, :].astype(F32) + rb[...].astype(F32)
                )
                copies[8].start()
                copies[4].wait_recv()
                sums[1, top, :] = rounded(sums[1, top, :].astype(F32) + ra[...].astype(F32))
                copies[9].start()
        else:
            copies[0].wait_recv()

            def store(here, value):
                out_ref[:, here] = value + other[0, :, here].astype(F32)

            product(index, store)
    if beside:
        tail.run()
    for part, first, second in ((top, 6, 9), (bottom, 8, 7)):
        copies[first].wait_recv()
        copies[second].wait_recv()
        out_ref[part, :] = out_ref[part, :] + (
            near_x[part, :].astype(F32) + near_l[part, :].astype(F32)
        )
    for index, each in enumerate(copies):
        if index not in (1, 3):
            each.wait_send()
    if kind == 3:
        made(6).wait()
        made(7).wait()
    if beside:
        tail.end()


class WeightTail:
    def __init__(self, refs):
        self.grad, self.layer, self.totals, self.landing, self.layer_out = refs[:5]
        stage, result, y_sems, z_sems, stage_sems, self.layer_stage, self.layer_sems = refs[5:]
        self.y, self.c, self.h, _ = places()
        self.names = [("Q", 0, 0), ("Q", 1, 0)]
        self.pieces = PieceSums(
            self.names,
            self.piece,
            lambda name: self.landing.at[name[1]],
            lambda name, h: self.totals.at[h],
            y_sems,
            z_sems,
        )
        self.sums = Sums(stage, result, stage_sems)
        for name in self.names:
            self.sums.item(
                0,
                512,
                [self.piece(name, self.y), self.landing.at[name[1]]],
                self.pieces.sends(name),
                [lambda name=name: self.pieces.over_y(name).wait_recv()],
            )

    def piece(self, name, y):
        return self.grad.at[pl.ds(pl.multiple_of((2 * y + name[1]) * 512, 512), 512)]

    def layer_load(self):
        return pltpu.make_async_copy(self.layer, self.layer_stage, self.layer_sems.at[2])

    def layer_local(self):
        return pltpu.make_async_copy(self.layer_stage, self.layer_out, self.layer_sems.at[2])

    def layer_remote(self):
        return remote(
            self.layer, self.layer_out, self.layer_sems.at[0], self.layer_sems.at[1], {"c": self.h, "h": self.c}
        )

    def begin(self):
        for name in self.names:
            self.pieces.over_y(name).start()

        @pl.when(self.c == self.h)
        def _():
            self.layer_load().start()

        @pl.when(self.c != self.h)
        def _():
            self.layer_remote().start()

    def run(self):
        @pl.when(self.c == self.h)
        def _():
            self.layer_load().wait()
            self.layer_local().start()

        for k in range(2):
            self.sums.load(k)
            self.sums.add(k)

    def end(self):
        self.sums.last_sent()
        self.pieces.end()

        @pl.when(self.c == self.h)
        def _():
            self.layer_local().wait()

        @pl.when(self.c != self.h)
        def _():
            self.layer_remote().wait_recv()
            self.layer_remote().wait_send()


def scatter_scratch(depth, width, cut):
    return [
        pltpu.VMEM((2, ROW, depth), BF),
        pltpu.VMEM((2, ROW, width), BF),
        pltpu.VMEM((4, ROW, width), BF),
        pltpu.VMEM((3, ROW, width), BF),
        pltpu.VMEM((cut, width), BF),
        pltpu.VMEM((ROW - cut, width), BF),
        pltpu.VMEM((ROW, width), BF),
        pltpu.VMEM((ROW, width), BF),
        pltpu.SemaphoreType.DMA((10,)),
        pltpu.SemaphoreType.DMA((10,)),
        pltpu.SemaphoreType.DMA((2, 3)),
    ]


def feed_forward_back(grad, gate, up, down_weight, gate_up_weight, number):
    anywhere = pl.BlockSpec(memory_space=pl.ANY)
    vmem = pl.BlockSpec(memory_space=pltpu.VMEM)
    return pl.pallas_call(
        lambda *refs: scatter_kernel(NT, ROW // 2, 3, *refs),
        in_specs=[anywhere] * 3 + [vmem] * 2,
        out_specs=[vmem, anywhere],
        out_shape=[
            jax.ShapeDtypeStruct((ROW, 2048), F32),
            jax.ShapeDtypeStruct((8 * ROW, 2048), BF),
        ],
        scratch_shapes=scatter_scratch(2048, 2048, ROW // 2)
        + [
            pltpu.VMEM((2, ROW, 2048), BF),
            pltpu.VMEM((2, ROW, 1024), BF),
            pltpu.VMEM((2, ROW, 1024), BF),
            pltpu.SemaphoreType.DMA((2,)),
        ],
        compiler_params=pltpu.CompilerParams(
            collective_id=number, has_side_effects=True, vmem_limit_bytes=62 * 2**20
        ),
        cost_estimate=pl.CostEstimate(
            flops=80 * 10**9, bytes_accessed=60 * 2**20, transcendentals=0
        ),
    )(grad, gate, up, down_weight, gate_up_weight)


def product_scatter(a, weight, dims, number, *more):
    anywhere = pl.BlockSpec(memory_space=pl.ANY)
    vmem = pl.BlockSpec(memory_space=pltpu.VMEM)
    depth = a.shape[1]
    width = weight.shape[0] if dims == NT else weight.shape[1]
    cut = 384 if more else 256
    return pl.pallas_call(
        lambda *refs: scatter_kernel(dims, cut, len(more), *refs),
        in_specs=[anywhere, vmem] + [anywhere] * len(more),
        out_specs=[vmem] + [anywhere] * (3 if more else 0),
        out_shape=[jax.ShapeDtypeStruct((ROW, width), F32)]
        + [
            jax.ShapeDtypeStruct((2, 512, 768), BF),
            jax.ShapeDtypeStruct((2, 512, 768), BF),
            jax.ShapeDtypeStruct((ROW, 2048), BF),
        ]
        * bool(more),
        scratch_shapes=scatter_scratch(depth, width, cut)
        + [
            pltpu.VMEM((2, 2, 512, 768), BF),
            pltpu.VMEM((2, 512, 768), BF),
            pltpu.SemaphoreType.DMA((2, 2)),
            pltpu.SemaphoreType.DMA((3, 2)),
            pltpu.SemaphoreType.DMA((2, 5)),
            pltpu.VMEM((ROW, 2048), BF),
            pltpu.SemaphoreType.DMA((3,)),
        ]
        * bool(more),
        compiler_params=pltpu.CompilerParams(
            collective_id=number, has_side_effects=True, vmem_limit_bytes=58 * 2**20
        ),
        cost_estimate=pl.CostEstimate(
            flops=80 * 10**9, bytes_accessed=30 * 2**20, transcendentals=0
        ),
    )(a, weight, *more)


def column_order():
    column = lax.broadcasted_iota(jnp.int32, (768, 768), 1)
    row = lax.broadcasted_iota(jnp.int32, (768, 768), 0)
    part, within = column // 256, column % 256
    turned = ((within % 128) // 32) * 192 + part * 64 + (within // 128) * 32 + within % 32
    plain = (within // 64) * 192 + 128 + within % 64
    return (row == jnp.where(part == 2, plain, turned)).astype(BF)


def head_lanes_turned(head):
    lane = lax.broadcasted_iota(jnp.int32, (1, 256), 1)
    return (lane % 128) // 32 == head


def head_lanes_plain(head):
    lane = lax.broadcasted_iota(jnp.int32, (1, 256), 1)
    return lane // 64 == head


def picked_block(step, blocks):
    block = jnp.int32(blocks[0])
    for index in range(1, len(blocks)):
        block = jnp.where(step == index, blocks[index], block)
    return block


def mark(*values):
    return sum(value[(0,) * value.ndim].astype(F32) for value in values) * 0.0


def after(values, zero):
    return values + zero.astype(values.dtype)


def held(values, zero):
    if zero is None:
        return values
    return after(lax.optimization_barrier(values), zero)


class Beside:
    def __init__(self, refs):
        self.out_shard, self.gate_up_shard, self.grad_own = refs[:3]
        self.out_full, self.gate_up, self.grad_full, self.rows_own = refs[3:7]
        (
            near,
            far,
            keep,
            self.y_send,
            self.y_recv,
            out_near,
            out_far,
            out_keep,
            self.out_y,
            grad_send,
            grad_recv,
            out_send,
            out_recv,
            self.row_send,
            self.row_recv,
            self.own_sem,
            stage,
            out_stage,
            self.grad_stage,
        ) = refs[7:]
        self.y, self.c, self.h, self.me = places()
        _, _, _, l, x = (lax.axis_index(name) for name in AXES)
        s = 2 * self.y + self.c
        self.pieces = [
            Spread(
                self.gate_up_shard.at[pl.ds(k * 128, 128)],
                self.gate_up.at[pl.ds(pl.multiple_of(s * 512 + k * 128, 128), 128)],
                near.at[k],
                far.at[k],
                keep.at[k],
                stage.at[k],
            )
            for k in range(4)
        ]
        heads = 4 * self.h + 2 * l + x
        self.out_piece = Spread(
            self.out_shard,
            self.out_full.at[
                pl.ds(pl.multiple_of(heads * 256, 256), 256), pl.ds(pl.multiple_of(s * 512, 512), 512)
            ],
            out_near,
            out_far,
            out_keep,
            out_stage,
        )
        self.grad_ring = Ring(self.grad_full, ROW, grad_send, grad_recv, lean=True, own=self.grad_stage)
        self.out_ring = Ring(self.out_full, 256, out_send, out_recv)

    def over_y(self, k, core, y):
        first = (2 * y + core) * 512 + k * 128
        place = self.gate_up.at[pl.ds(pl.multiple_of(first, 128), 128)]
        return remote(place, place, self.y_send.at[k, core], self.y_recv.at[k, core], {"y": 1 - self.y})

    def out_over_y(self, y):
        place = self.out_full.at[
            pl.ds(pl.multiple_of(self.me * 256, 256), 256), pl.ds(pl.multiple_of(y * 1024, 1024), 1024)
        ]
        return remote(place, place, self.out_y.at[0], self.out_y.at[1], {"y": 1 - self.y})

    def piece_over_y(self, k):
        self.pieces[k].arrived()
        for core in range(2):
            self.over_y(k, core, self.y).start()

    def own_out(self):
        return pltpu.make_async_copy(
            self.grad_stage, self.grad_full.at[rows_at(self.me)], self.own_sem.at[0]
        )

    def begin(self):
        own = pltpu.make_async_copy(self.grad_own, self.grad_stage, self.own_sem.at[0])
        own.start()
        enter_ring(wide_partners())
        self.out_piece.start()
        own.wait()
        self.grad_ring.start(0, 1, 2, 3, 4)
        self.own_out().start()

    def at(self, step):
        def when(number, *actions):
            @pl.when(step == number)
            def _():
                for action in actions:
                    action()

        def out_on():
            self.out_piece.arrived()
            self.out_over_y(self.y).start()
            self.pieces[0].start()

        def out_ring_on():
            self.out_over_y(1 - self.y).wait_recv()
            self.out_ring.start(0, 1, 2, 3, 4)
            self.pieces[1].start()

        def grad_one():
            self.grad_ring.arrived(1)
            self.grad_ring.start(6)

        def grad_two():
            self.grad_ring.arrived(4)
            self.grad_ring.start(5, 8)
            self.grad_ring.arrived(0, 3)
            self.grad_ring.start(7)

        def out_one():
            self.out_ring.arrived(0)
            self.out_ring.start(5)
            self.out_ring.arrived(1)
            self.out_ring.start(6)

        def out_two():
            self.out_ring.arrived(3)
            self.out_ring.start(7)
            self.out_ring.arrived(4)
            self.out_ring.start(8)

        when(0, self.begin)
        when(3, out_on)
        when(6, out_ring_on)
        when(7, grad_one)
        when(9, lambda: self.piece_over_y(0), self.pieces[2].start)
        when(11, grad_two)
        when(14, lambda: self.piece_over_y(1), self.pieces[3].start)
        when(16, out_one)
        when(19, lambda: self.piece_over_y(2))
        when(22, out_two)
        when(28, lambda: self.piece_over_y(3))

    def row_local(self, block, o_all):
        columns = pl.ds(pl.multiple_of(self.me * 256, 256), 256)
        return pltpu.make_async_copy(
            o_all.at[rows_at(block)], self.rows_own.at[:, columns], self.own_sem.at[1]
        )

    def row_remote(self, block, o_all, sender):
        columns = pl.ds(pl.multiple_of(sender * 256, 256), 256)
        return remote(
            o_all.at[rows_at(block)],
            self.rows_own.at[:, columns],
            self.row_send.at[block],
            self.row_recv.at[sender],
            {"c": block >> 2, "l": (block >> 1) & 1, "x": block & 1},
        )

    def send_rows(self, block, o_all):
        @pl.when(block == self.me)
        def _():
            self.row_local(block, o_all).start()

        @pl.when(block != self.me)
        def _():
            self.row_remote(block, o_all, self.me).start()

    def end(self, o_all):
        for ring in (self.out_ring, self.grad_ring):
            ring.arrived(5, 6)
            ring.start(9)
        self.own_out().wait()
        self.out_piece.sent()
        self.out_over_y(self.y).wait_send()
        for k in range(4):
            self.pieces[k].sent()
            for core in range(2):
                self.over_y(k, core, self.y).wait_send()
                self.over_y(k, core, 1 - self.y).wait_recv()
        for ring in (self.grad_ring, self.out_ring):
            ring.arrived(2, 7, 8, 9)
            ring.sent()

        def each(block, carry):
            @pl.when(block == self.me)
            def _():
                self.row_local(block, o_all).wait()

            @pl.when(block != self.me)
            def _():
                self.row_remote(block, o_all, self.me).wait_send()
                self.row_remote(block, o_all, block).wait_recv()

            return carry

        lax.fori_loop(0, 8, each, 0)


def attend_kernel(q_ref, k_ref, v_ref, out_shard, gate_up_shard, grad_own, o_ref, l_ref, *refs):
    beside = Beside((out_shard, gate_up_shard, grad_own) + refs[:4] + refs[8:])
    s_scr, m_scr, acc_scr, o_all = refs[4:8]
    head = pl.program_id(1)
    step = pl.program_id(0) * 4 + head
    block = 7 - pl.program_id(0)
    beside.at(step)
    row = lax.broadcasted_iota(jnp.int32, (ROW, ROW), 0)
    col = lax.broadcasted_iota(jnp.int32, (ROW, ROW), 1)

    def lane_max(s):
        return jnp.maximum(
            jnp.maximum(s[:, :128], s[:, 128:256]), jnp.maximum(s[:, 256:384], s[:, 384:])
        )

    def lane_sum(s):
        return (s[:, :128] + s[:, 128:256]) + (s[:, 256:384] + s[:, 384:])

    def keys_at(key_block):
        return pl.ds(pl.multiple_of(key_block * ROW, ROW), ROW)

    q = q_ref[...]
    qh = jnp.where(head_lanes_turned(head), q, jnp.zeros_like(q))

    def scores(key_block):
        return lax.dot_general(qh, k_ref[keys_at(key_block), :], NT, preferred_element_type=F32)

    s = jnp.where(col <= row, scores(block), masked_score)
    s_scr[block] = s
    m_scr[...] = lane_max(s)

    def first_pass(key_block, carry):
        s = scores(key_block)
        s_scr[key_block] = s
        m_scr[...] = jnp.maximum(m_scr[...], lane_max(s))
        return carry

    lax.fori_loop(0, block, first_pass, 0)
    top = jnp.max(m_scr[...], axis=1, keepdims=True)
    m_scr[...] = jnp.zeros_like(m_scr)
    acc_scr[...] = jnp.zeros_like(acc_scr)

    def second_pass(key_block, carry):
        e = jnp.exp2(s_scr[key_block] - top)
        m_scr[...] += lane_sum(e)
        acc_scr[...] += lax.dot_general(
            e.astype(BF), v_ref[keys_at(key_block), :], NN, preferred_element_type=F32
        )
        return carry

    lax.fori_loop(0, block + 1, second_pass, 0)
    total = jnp.sum(m_scr[...], axis=1, keepdims=True)
    part = rounded(acc_scr[...] * (1.0 / total))
    rows = rows_at(block)

    @pl.when(head == 0)
    def _():
        o_all[rows, :] = part

    @pl.when(head > 0)
    def _():
        o_all[rows, :] = jnp.where(head_lanes_plain(head), part, o_all[rows, :])

    level = jnp.transpose(jnp.broadcast_to(top + jnp.log2(total), (ROW, 128)))[0:4, :]
    row4 = lax.broadcasted_iota(jnp.int32, (4, ROW), 0)
    l_ref[0] = jnp.where(row4 == head, level, l_ref[0])

    @pl.when(head == 3)
    def _():
        o_ref[...] = o_all[rows, :]
        beside.send_rows(block, o_all)

    @pl.when(step == 31)
    def _():
        beside.end(o_all)


def attend(q, k, v, out_shard, gate_up_shard, grad_own):
    length = q.shape[0]
    blocks = length // ROW
    whole = pl.BlockSpec((length, 256), lambda i, head: (0, 0))
    anywhere = pl.BlockSpec(memory_space=pl.ANY)
    dma = pltpu.SemaphoreType.DMA
    return pl.pallas_call(
        attend_kernel,
        grid=(blocks, 4),
        in_specs=[pl.BlockSpec((ROW, 256), lambda i, head: (7 - i, 0)), whole, whole] + [anywhere] * 3,
        out_specs=[
            pl.BlockSpec((ROW, 256), lambda i, head: (7 - i, 0)),
            pl.BlockSpec((1, 4, ROW), lambda i, head: (7 - i, 0, 0)),
        ]
        + [anywhere] * 4,
        out_shape=[
            jax.ShapeDtypeStruct((length, 256), BF),
            jax.ShapeDtypeStruct((blocks, 4, ROW), F32),
            jax.ShapeDtypeStruct((2048, 2048), BF),
            jax.ShapeDtypeStruct((2048, 2048), BF),
            jax.ShapeDtypeStruct((length, 2048), BF),
            jax.ShapeDtypeStruct((ROW, 2048), BF),
        ],
        scratch_shapes=[
            pltpu.VMEM((blocks, ROW, ROW), F32),
            pltpu.VMEM((ROW, 128), F32),
            pltpu.VMEM((ROW, 256), F32),
            pltpu.VMEM((length, 256), BF),
        ]
        + SPREAD_SEMAPHORES
        + [dma((2,)), dma((3,)), dma, dma((2,))]
        + [dma((10,))] * 4
        + [dma((8,)), dma((8,)), dma((2,))]
        + [pltpu.VMEM((4, 128, 2048), BF), pltpu.VMEM((256, 512), BF), pltpu.VMEM((ROW, 2048), BF)],
        compiler_params=pltpu.CompilerParams(
            collective_id=6, has_side_effects=True, vmem_limit_bytes=48 * 2**20
        ),
        cost_estimate=pl.CostEstimate(
            flops=14 * 10**9 * blocks, bytes_accessed=10 * 2**20, transcendentals=0
        ),
    )(q, k, v, out_shard, gate_up_shard, grad_own)


KEYS = 256


class Sums:
    def __init__(self, stage, result, stage_sems):
        self.stage, self.result, self.stage_sems = stage, result, stage_sems
        self.depth = result.shape[0]
        self.items = []
        self.early = ()

    def item(self, due, rows, terms, sends, waits=(), extra=None, then=None):
        self.items.append((due, rows, terms, sends, waits, extra, then))

    def loads(self, k):
        _, rows, terms, _, _, extra, _ = self.items[k]
        turn = k % 2
        copies = [
            pltpu.make_async_copy(
                term, self.stage.at[turn, index, pl.ds(0, rows)], self.stage_sems.at[turn, index]
            )
            for index, term in enumerate(terms)
        ]
        if extra is not None:
            copies.append(pltpu.make_async_copy(extra[0], extra[1], self.stage_sems.at[turn, 4]))
        return copies

    def load(self, k):
        for wait in self.items[k][4]:
            wait()
        for copy in self.loads(k):
            copy.start()

    def add(self, k):
        _, rows, terms, sends, _, extra, then = self.items[k]
        turn = k % 2
        for copy in self.loads(k):
            copy.wait()
        if k >= self.depth and k - self.depth not in self.early:
            self.sent(k - self.depth)
        target = self.result.at[k % self.depth]
        size = rows // 8

        def chunk(index, carry):
            here = pl.ds(pl.multiple_of(index * size, size), size)
            total = self.stage[turn, 0, here, :].astype(F32)
            for term in range(1, len(terms)):
                total += self.stage[turn, term, here, :].astype(F32)
            if extra is not None:
                total += extra[1][here, :]
            target[here, :] = rounded(total)
            return carry

        lax.fori_loop(0, 8, chunk, 0)
        for here, away, local in sends(self.result.at[k % self.depth, pl.ds(0, rows)]):
            self.either(here, away, local, "start")
        if then is not None:
            then()

    def either(self, here, away, local, method):
        if local is None:
            getattr(away(), method)()
            return
        if away is None:
            getattr(local(), "wait" if method == "wait_send" else method)()
            return

        @pl.when(here)
        def _():
            getattr(local(), "wait" if method == "wait_send" else method)()

        @pl.when(jnp.logical_not(here))
        def _():
            getattr(away(), method)()

    def sent(self, k):
        _, rows, _, sends, _, _, _ = self.items[k]
        for here, away, local in sends(self.result.at[k % self.depth, pl.ds(0, rows)]):
            self.either(here, away, local, "wait_send")

    def poll(self, unit):
        for k, item in enumerate(self.items):

            @pl.when(unit == item[0])
            def _(k=k):
                self.load(k)

            @pl.when(unit == item[0] + 1)
            def _(k=k):
                self.add(k)

    def last_sent(self):
        for k in range(max(len(self.items) - self.depth, 0), len(self.items)):
            if k not in self.early:
                self.sent(k)


def half_columns(half):
    return pl.ds(half * 1024, 1024)


class RingSum:
    def __init__(self, parts, size, core_land, far_land, core_sems, far_sems, lean):
        self.lean = lean
        self.parts, self.size, self.core_land, self.far_land = parts, size, core_land, far_land
        self.core_sems, self.far_sems = core_sems, far_sems
        self.me, (self.to_x, self.to_l, self.to_c) = ring_position()

    def block(self, slot):
        return pl.ds(pl.multiple_of((self.me ^ slot) * self.size, self.size), self.size)

    def core(self, slot):
        return remote(
            self.parts.at[self.block(slot | 4)],
            self.core_land.at[slot],
            self.core_sems.at[0, slot],
            self.core_sems.at[1, slot],
            self.to_c,
        )

    def begin(self):
        for slot in (3, 1, 2, 0):
            self.core(slot).start()

    def far(self, index, source):
        device = self.to_x if index in ((0, 1, 2, 3) if self.lean else (0, 2, 4)) else self.to_l
        return remote(
            source, self.far_land.at[index], self.far_sems.at[0, index], self.far_sems.at[1, index], device
        )

    def landed(self, index):
        return lambda: self.far(index, self.far_land.at[index]).wait_recv()

    def terms(self, slot, half):
        return [
            self.parts.at[self.block(slot), half_columns(half)],
            self.core_land.at[slot, :, half_columns(half)],
        ]

    def work(self, due, last_sends, extra):
        if self.lean:
            plan = ((3, 0), (3, 1), (1, 0), (1, 1), (2, 0, 0), (2, 1, 1), (0, 0, 2, 4), (0, 1, 3, 5))
        else:
            plan = ((3, 0), (3, 1), (1, 0), (2, 1), (1, 1, 1), (2, 0, 0), (0, 0, 2, 5), (0, 1, 4, 3))
        first = {}
        for index in sorted(range(8), key=lambda index: due[index]):
            first.setdefault(plan[index][0], index)
        items = []
        for index, (slot, half, *landings) in enumerate(plan):
            waits = [self.landed(landing) for landing in landings]
            if first[slot] == index:
                waits.append(lambda slot=slot: self.core(slot).wait_recv())
            if index < 6:
                sends = lambda source, index=index: [(None, lambda: self.far(index, source), None)]
            else:
                sends = last_sends(half)
            terms = self.terms(slot, half) + [self.far_land.at[landing] for landing in landings]
            items.append((due[index], self.size, terms, sends, waits, extra(half) if index >= 6 else None))
        return items

    def end(self):
        for slot in range(4):
            self.core(slot).wait_send()


class PieceSums:
    def __init__(self, names, piece, landing, sums_at, y_sems, z_sems):
        self.names, self.piece, self.landing, self.sums_at = names, piece, landing, sums_at
        self.y_sems, self.z_sems = y_sems, z_sems
        self.y, self.c, self.h, _ = places()

    def core_of(self, name):
        return name[1]

    def over_y(self, name):
        index = self.names.index(name)
        return remote(
            self.piece(name, 1 - self.y),
            self.landing(name),
            self.y_sems.at[0, index],
            self.y_sems.at[1, index],
            {"y": 1 - self.y},
        )

    def group(self, name):
        groups = []
        for each in self.names:
            key = (each[0], each[2])
            if key not in groups:
                groups.append(key)
        return groups.index((name[0], name[2])), groups

    def over_z(self, name, h, source):
        index = self.names.index(name)
        target = self.sums_at(name, h)
        return (
            lambda: remote(
                source,
                target,
                self.z_sems.at[0, index],
                self.z_sems.at[1 + h, self.group(name)[0]],
                {"c": self.core_of(name), "h": self.c},
            ),
            lambda: pltpu.make_async_copy(source, target, self.z_sems.at[0, index]),
        )

    def sends(self, name):
        here = jnp.logical_and(self.core_of(name) == self.c, self.h == self.c)
        return lambda source: [(here, *self.over_z(name, self.h, source))]

    def end(self):
        for name in self.names:
            self.over_y(name).wait_send()
        self.owned()

    def owned(self):
        seen = []
        for name in self.names:
            group, _ = self.group(name)
            if group in seen:
                continue
            seen.append(group)
            for h in range(2):
                here = jnp.logical_and(h == self.h, self.c == self.h)

                @pl.when(jnp.logical_not(here))
                def _(name=name, h=h):
                    self.over_z(name, h, self.sums_at(name, h))[0]().wait_recv()


class BesideBack:
    def __init__(self, refs):
        self.heads_own, self.parts, self.gate_up, self.down, self.out, self.residual, self.cos, self.sin = refs[:8]
        (
            self.gate_up_sums,
            self.down_sums,
            self.out_sums,
            self.layer,
            core_land,
            far_land,
            self.y_land,
            out_core_land,
            out_far_land,
            self.out_own,
            self.out_y_land,
        ) = refs[8:19]
        (
            self.do,
            self.cs,
            self.sn,
            stage,
            result,
            self.rest,
            self.row_send,
            self.row_recv,
            core_sems,
            far_sems,
            out_core_sems,
            out_far_sems,
            self.layer_sems,
            y_sems,
            z_sems,
            self.out_sems,
            out_y_sems,
            out_z_sems,
            stage_sems,
            self.own_sem,
        ) = refs[19:]
        self.y, self.c, self.h, self.me = places()
        self.sums = Sums(stage, result, stage_sems)
        self.layer_ring = RingSum(self.parts, ROW, core_land, far_land, core_sems, far_sems, True)
        self.out_ring = RingSum(
            self.out, 256, out_core_land, out_far_land, out_core_sems, out_far_sems, False
        )
        names = [("D", 0, 0), ("D", 1, 0), ("G", 0, 0), ("G", 0, 1), ("G", 1, 0), ("G", 1, 1)]
        self.pieces = PieceSums(names, self.piece, lambda name: self.y_land.at[names.index(name)], self.sums_at, y_sems, z_sems)
        self.names = names
        out_names = [("O", 0, 0), ("O", 1, 0)]
        self.out_pieces = PieceSums(out_names, None, None, self.sums_at, out_y_sems, out_z_sems)
        work = self.layer_ring.work((22, 35, 48, 61, 36, 56, 62, 70), self.layer_sends, self.residual_half)
        work += self.out_ring.work((1, 2, 8, 14, 15, 25, 37, 26), self.out_sends, lambda half: None)
        for name, due in zip(names, (3, 16, 29, 44, 57, 69)):
            terms = [self.piece(name, self.y), self.y_land.at[names.index(name)]]
            work.append((due, ROW, terms, self.pieces.sends(name), [self.arrived(name)], None))
        work.append((64, 256, [self.out_own, self.out_y_land], self.out_owners, [self.out_landed], None))
        work.sort(key=lambda item: item[0])
        for item in work:
            self.sums.item(*item)
        last = [item[0] for item in work].index(64)
        depth = self.sums.depth
        self.sums.early = [k for k, item in enumerate(work) if item[0] in (37, 26) and k + depth >= last]

    def arrived(self, name):
        def wait():
            self.pieces.over_y(name).wait_recv()
            place = self.names.index(name) + 1
            if place < 6:
                self.pieces.over_y(self.names[place]).start()

        return wait

    def out_landed(self):
        for k in self.sums.early:
            self.sums.sent(k)
        remote(
            self.out_own, self.out_y_land, self.out_sems.at[0], self.out_sems.at[2], {"y": 1 - self.y}
        ).wait_recv()

    def out_owners(self, source):
        sends = []
        for name in self.out_pieces.names:
            sends += self.out_pieces.sends(name)(source.at[:, pl.ds(name[1] * 512, 512)])
        return sends

    def residual_half(self, half):
        return (self.residual.at[:, half_columns(half)], self.rest)

    def layer_sends(self, half):
        def sends(source):
            return [
                (
                    None,
                    None,
                    lambda: pltpu.make_async_copy(
                        source, self.layer.at[:, half_columns(half)], self.layer_sems.at[half]
                    ),
                )
            ]

        return sends

    def out_sends(self, half):
        def sends(source):
            return [
                (
                    self.y == half,
                    lambda: remote(
                        source, self.out_y_land, self.out_sems.at[half], self.out_sems.at[2], {"y": 1 - self.y}
                    ),
                    lambda: pltpu.make_async_copy(source, self.out_own, self.out_sems.at[half]),
                )
            ]

        return sends

    def piece(self, name, y):
        kind, core, half = name
        rows = pl.ds(pl.multiple_of((2 * y + core) * 512, 512), 512)
        if kind == "G":
            return self.gate_up.at[rows, half_columns(half)]
        return self.down.at[rows]

    def sums_at(self, name, h):
        kind, _, half = name
        if kind == "G":
            return self.gate_up_sums.at[h, :, half_columns(half)]
        return self.down_sums.at[h] if kind == "D" else self.out_sums.at[h]

    def tables(self):
        return (
            pltpu.make_async_copy(self.cos, self.cs, self.own_sem.at[0]),
            pltpu.make_async_copy(self.sin, self.sn, self.own_sem.at[1]),
        )

    def row_local(self):
        columns = pl.ds(pl.multiple_of(self.me * 256, 256), 256)
        return pltpu.make_async_copy(
            self.heads_own.at[:, columns], self.do.at[rows_at(self.me)], self.own_sem.at[2]
        )

    def row_remote(self, block, sender):
        columns = pl.ds(pl.multiple_of(block * 256, 256), 256)
        return remote(
            self.heads_own.at[:, columns],
            self.do.at[rows_at(sender)],
            self.row_send.at[block],
            self.row_recv.at[sender],
            {"c": block >> 2, "l": (block >> 1) & 1, "x": block & 1},
        )

    def begin(self):
        for copy in self.tables():
            copy.start()
        self.row_local().start()
        enter_ring(wide_partners())

        def send(index, carry):
            block = 7 - index

            @pl.when(block != self.me)
            def _():
                self.row_remote(block, self.me).start()

            return carry

        lax.fori_loop(0, 8, send, 0)
        self.layer_ring.begin()
        self.out_ring.begin()
        self.pieces.over_y(self.names[0]).start()
        for copy in self.tables():
            copy.wait()

    def rows_there(self, block):
        @pl.when(block == self.me)
        def _():
            self.row_local().wait()

        @pl.when(block != self.me)
        def _():
            self.row_remote(block, block).wait_recv()

    def poll(self, unit):
        self.sums.poll(unit)

    def end(self):
        def each(block, carry):
            @pl.when(block != self.me)
            def _():
                self.row_remote(block, self.me).wait_send()

            return carry

        lax.fori_loop(0, 8, each, 0)
        self.sums.last_sent()
        self.layer_ring.end()
        self.out_ring.end()
        self.pieces.end()
        self.out_pieces.owned()


def attend_back_kernel(q_ref, k_ref, v_ref, o_ref, l_ref, *refs):
    given, (dkv_ref, dq_out), outs = refs[:8], refs[8:10], refs[10:21]
    qm, dom, delta, dq, dk, dv, km, pt, dst = refs[21:30]
    beside = BesideBack(given + outs + refs[30:])
    heads = 4
    i, sub = pl.program_id(0), pl.program_id(1)
    block = 7 - i
    blocks = 8
    unit = i * (i + 1) + sub * (i + 1)
    rows_here = rows_at(block)

    @pl.when(jnp.logical_and(i == 0, sub == 0))
    def _():
        beside.begin()

    @pl.when(sub == 0)
    def _():
        beside.rows_there(block)
        q = q_ref[...]
        do = beside.do[rows_here, :]
        for head in range(heads):
            part = slice(head * ROW, (head + 1) * ROW)
            qm[block, part, :] = jnp.where(head_lanes_turned(head), q, jnp.zeros_like(q))
            dom[block, part, :] = jnp.where(head_lanes_plain(head), do, jnp.zeros_like(do))
        product = do.astype(F32) * o_ref[...].astype(F32)
        high = rounded(product)
        low = rounded(product - high.astype(F32))
        head_row = lax.broadcasted_iota(jnp.int32, (8, 256), 0)
        lane = lax.broadcasted_iota(jnp.int32, (8, 256), 1)
        pick = jnp.where(lane // 64 == head_row, 1.0, 0.0).astype(BF)
        sums = lax.dot_general(pick, high, NT, preferred_element_type=F32)
        sums += lax.dot_general(pick, low, NT, preferred_element_type=F32)
        delta[block] = sums[:heads, :]
        dq[rows_here, :] = jnp.zeros((ROW, 256), F32)

    beside.poll(unit)
    key_row = lax.broadcasted_iota(jnp.int32, (KEYS, ROW), 0)
    query_col = lax.broadcasted_iota(jnp.int32, (KEYS, ROW), 1)
    inner = pl.multiple_of(sub * KEYS, KEYS)
    k = k_ref[pl.ds(inner, KEYS), :]
    v = v_ref[pl.ds(inner, KEYS), :]
    for head in range(heads):
        km[head] = jnp.where(head_lanes_turned(head), k, jnp.zeros_like(k))
    dk[...] = jnp.zeros_like(dk)
    dv[...] = jnp.zeros_like(dv)

    def query_part(place, diagonal):
        rows = rows_at(place)
        for head in range(heads):
            part = slice(head * ROW, (head + 1) * ROW)
            st = lax.dot_general(k, qm[place, part, :], NT, preferred_element_type=F32)
            dp = lax.dot_general(v, dom[place, part, :], NT, preferred_element_type=F32)
            p = jnp.exp2(st - l_ref[place, head : head + 1, :])
            if diagonal:
                p = jnp.where(key_row + inner <= query_col, p, 0.0)
            ds = p * (dp - delta[place, head : head + 1, :])
            pt[:, part] = p.astype(BF)
            dst[:, part] = ds.astype(BF)
        dv[...] += lax.dot_general(pt[...], dom[place], NN, preferred_element_type=F32)
        dk[...] += lax.dot_general(dst[...], qm[place], NN, preferred_element_type=F32)
        total = lax.dot_general(dst[:, 0:ROW], km[0], TN, preferred_element_type=F32)
        for head in range(1, heads):
            part = slice(head * ROW, (head + 1) * ROW)
            total += lax.dot_general(dst[:, part], km[head], TN, preferred_element_type=F32)
        dq[rows, :] += total

    query_part(block, True)

    def later(query_block, carry):
        beside.poll(unit + query_block - block)
        query_part(query_block, False)
        return carry

    lax.fori_loop(block + 1, blocks, later, 0)
    table = pl.ds(pl.multiple_of(block * ROW + inner, KEYS), KEYS)
    cs, sn = beside.cs[table, :], beside.sn[table, :]
    d = dk[...] * (1.0 / LOG2E)
    d1, d2 = d[:, :128], d[:, 128:]
    dkv_ref[pl.ds(inner, KEYS), 0:128] = rounded(d1 * cs + d2 * sn)
    dkv_ref[pl.ds(inner, KEYS), 128:256] = rounded(d2 * cs - d1 * sn)
    dkv_ref[pl.ds(inner, KEYS), 256:512] = rounded(dv[...])

    @pl.when(jnp.logical_and(i == 7, sub == 1))
    def _():
        def finish(place, carry):
            rows = rows_at(place)
            cs, sn = beside.cs[rows, :], beside.sn[rows, :]
            d = dq[rows, :] * 0.125
            d1, d2 = d[:, :128], d[:, 128:]
            beside.do[rows, 0:128] = rounded(d1 * cs + d2 * sn)
            beside.do[rows, 128:256] = rounded(d2 * cs - d1 * sn)
            return carry

        lax.fori_loop(0, blocks, finish, 0)
        copy = pltpu.make_async_copy(beside.do, dq_out, beside.own_sem.at[4])
        copy.start()
        copy.wait()
        beside.end()


def attend_back(q, k, v, o, level, heads_own, parts, gate_up, down, out, residual, cos, sin):
    length = q.shape[0]
    blocks = length // ROW
    dma = pltpu.SemaphoreType.DMA
    anywhere = pl.BlockSpec(memory_space=pl.ANY)

    def key_spec(width):
        return pl.BlockSpec((ROW, width), lambda i, sub: (7 - i, 0))

    shapes = [
        (2, 512, 2048),
        (2, 512, 1024),
        (2, 256, 512),
        (ROW, 2048),
        (4, ROW, 2048),
        (6, ROW, 1024),
        (6, 512, 1024),
        (4, 256, 2048),
        (6, 256, 1024),
        (256, 1024),
        (256, 1024),
    ]
    return pl.pallas_call(
        attend_back_kernel,
        grid=(blocks, 2),
        in_specs=[key_spec(256)] * 4
        + [pl.BlockSpec((blocks, 4, ROW), lambda i, sub: (0, 0, 0))]
        + [anywhere] * 8,
        out_specs=[key_spec(512)] + [anywhere] * (1 + len(shapes)),
        out_shape=[jax.ShapeDtypeStruct((length, 512), BF), jax.ShapeDtypeStruct((length, 256), BF)]
        + [jax.ShapeDtypeStruct(shape, BF) for shape in shapes],
        scratch_shapes=[
            pltpu.VMEM((blocks, 4 * ROW, 256), BF),
            pltpu.VMEM((blocks, 4 * ROW, 256), BF),
            pltpu.VMEM((blocks, 4, ROW), F32),
            pltpu.VMEM((length, 256), F32),
            pltpu.VMEM((KEYS, 256), F32),
            pltpu.VMEM((KEYS, 256), F32),
            pltpu.VMEM((4, KEYS, 256), BF),
            pltpu.VMEM((KEYS, 4 * ROW), BF),
            pltpu.VMEM((KEYS, 4 * ROW), BF),
            pltpu.VMEM((length, 256), BF),
            pltpu.VMEM((length, 128), F32),
            pltpu.VMEM((length, 128), F32),
            pltpu.VMEM((2, 4, ROW, 1024), BF),
            pltpu.VMEM((8, ROW, 1024), BF),
            pltpu.VMEM((ROW, 1024), F32),
            dma((8,)),
            dma((8,)),
            dma((2, 4)),
            dma((2, 6)),
            dma((2, 4)),
            dma((2, 6)),
            dma((2,)),
            dma((2, 6)),
            dma((3, 6)),
            dma((3,)),
            dma((2, 2)),
            dma((3, 2)),
            dma((2, 5)),
            dma((5,)),
        ],
        compiler_params=pltpu.CompilerParams(
            collective_id=7, has_side_effects=True, vmem_limit_bytes=60 * 2**20
        ),
        cost_estimate=pl.CostEstimate(
            flops=19 * 10**9 * blocks, bytes_accessed=20 * 2**20, transcendentals=0
        ),
    )(q, k, v, o, level, heads_own, parts, gate_up, down, out, residual, cos, sin)


def ring_shards(
    layer_input,
    cotangent,
    counts,
    positions,
    qkv_master,
    qkv_moment,
    qkv_average,
    out_master,
    out_moment,
    out_average,
    gate_up_master,
    gate_up_moment,
    gate_up_average,
    down_master,
    down_moment,
    down_average,
    gains_master,
    gains_moment,
    gains_average,
):
    y, c, h, l, x = (lax.axis_index(name) for name in AXES)
    own = 4 * c + 2 * l + x
    plain_y, plain_c, straight = y == 0, c == 0, c == h

    def both_y(mine, other, axis):
        return jnp.where(
            plain_y,
            jnp.concatenate([mine, other], axis=axis),
            jnp.concatenate([other, mine], axis=axis),
        )

    def both_cores(mine, other):
        return jnp.where(plain_c, mine, other), jnp.where(plain_c, other, mine)

    turn = column_order()
    rows_in = swap_ch(layer_input).astype(F32)
    gains_here = gains_master.astype(BF)
    gains_near = jnp.concatenate(both_cores(gains_here, flip(gains_here, "c")), axis=1)
    gains_all = both_y(gains_near, flip(gains_near, "y"), 1).astype(F32)
    gain_first, gain_second = gains_all[0], gains_all[1]
    qkv_shard = jnp.dot(qkv_master.astype(BF), turn, preferred_element_type=F32).astype(BF)
    scale_first = rms_scale(rows_in)
    normed_own = (rows_in * scale_first * gain_first).astype(BF)
    frequency = rope_theta ** (
        -((jnp.arange(128, dtype=jnp.int32) % 32).astype(F32) * 2.0) / HD
    )
    positions_here = jnp.where(straight, positions, flip(positions, "c"))
    angles = positions_here.astype(F32)[:, None] * frequency[None, :]
    cosine, sine = jnp.cos(angles), jnp.sin(angles)
    count_here = counts.astype(F32)
    count_total = count_here + flip(count_here, "c")
    count_total = count_total + flip(count_total, "y")
    grad_here = (4.0 * count_here[0] / count_total[0] * cotangent.astype(F32)).astype(BF)
    normed, queries, keys, values, qkv_weight, grad_own = gather_product(
        normed_own,
        (cosine, sine),
        (qkv_shard, grad_here),
        ((2048, 768), (ROW, 2048)),
        256,
        attention_finish,
        First,
        [pltpu.VMEM((2048, 768), BF)]
        + SPREAD_SEMAPHORES
        + [pltpu.SemaphoreType.DMA((4,)), pltpu.VMEM((ROW, 2048), BF)],
        1,
    )
    gate_up_shard = jnp.concatenate([gate_up_master[0], gate_up_master[1]], axis=1).astype(BF)
    attended, level, out_weight, gate_up_weight, grad_out, attended_own = attend(
        queries, keys, values, out_master.astype(BF), gate_up_shard, grad_own
    )
    grad_rows = grad_own.astype(F32)
    residual = rows_in + jnp.dot(attended_own, out_weight, preferred_element_type=F32)
    scale_second = rms_scale(residual)
    normed_second, gate, up, activation, down_weight = gather_product(
        (residual * scale_second * gain_second).astype(BF),
        (gate_up_weight,),
        (down_master.astype(BF),),
        ((1024, 2048),),
        1024,
        feed_forward_finish,
        Second,
        SPREAD_SEMAPHORES + [pltpu.VMEM((2, 512, 512), BF)],
        2,
    )

    grad_normed_second, grad_gate_up = feed_forward_back(
        grad_out, gate, up, down_weight, gate_up_weight, 3
    )
    gate_up_grad = lax.dot_general(
        normed_second, grad_gate_up, TN, preferred_element_type=F32
    ).astype(BF)
    down_grad = lax.dot_general(grad_out, activation, TN, preferred_element_type=F32).astype(BF)
    layer_parts = jnp.dot(activation, down_weight, preferred_element_type=F32).astype(BF)

    def norm_grad(values, scale, gain, grad):
        scaled = grad * gain
        back = scale * (
            scaled - values * scale * scale * jnp.mean(scaled * values, axis=-1, keepdims=True)
        )
        return back, jnp.sum(grad * values * scale, axis=0)

    residual_grad, gain_second_part = norm_grad(
        residual, scale_second, gain_second, grad_normed_second
    )
    residual_grad = residual_grad + grad_rows
    residual_low = residual_grad.astype(BF)
    grad_heads = lax.dot_general(residual_low, out_weight, NT, preferred_element_type=F32).astype(BF)
    out_grad = lax.dot_general(attended_own, residual_low, TN, preferred_element_type=F32).astype(BF)
    grad_kv, grad_q, gate_up_sums, down_sums, out_sums, layer_own, *_ = attend_back(
        queries, keys, values, attended, level, grad_heads, layer_parts, gate_up_grad, down_grad, out_grad, residual, cosine, sine
    )
    gate_up_grad_own = gate_up_sums[0].astype(F32) + gate_up_sums[1].astype(F32)
    unit = jnp.eye(512, dtype=BF)
    down_grad_own = lax.dot_general(
        down_sums.reshape(1024, 1024), jnp.concatenate([unit, unit]), TN, preferred_element_type=F32
    )
    out_grad_own = out_sums[0].astype(F32) + out_sums[1].astype(F32)

    grad_mixture = jnp.concatenate([grad_q, grad_kv], axis=1)
    qkv_grad = lax.dot_general(normed, grad_mixture, TN, preferred_element_type=F32).astype(BF)
    qkv_grad = lax.dot_general(qkv_grad, turn, NT, preferred_element_type=F32).astype(BF)
    grad_normed_first, qkv_sums, _, layer_output = product_scatter(
        grad_mixture, qkv_weight, NT, 5, qkv_grad, layer_own
    )
    qkv_grad_own = qkv_sums[0].astype(F32) + qkv_sums[1].astype(F32)

    input_back, gain_first_part = norm_grad(rows_in, scale_first, gain_first, grad_normed_first)
    input_grad = swap_ch((residual_grad + input_back).astype(BF)).astype(F32)

    gain_grads = jnp.stack([gain_first_part, gain_second_part])
    for bit in "xlchy":
        gain_grads = gain_grads + flip(gain_grads, bit)
    gain_grad_own = lax.dynamic_slice_in_dim(gain_grads, (2 * y + c) * 512, 512, 1)

    rate_unit = float(4 * 8 * ROW) ** (-0.5)
    qkv_new = apply_update(qkv_master, qkv_grad_own, qkv_moment, qkv_average, rate_qkv * rate_unit)
    out_new = apply_update(out_master, out_grad_own, out_moment, out_average, rate_out * rate_unit)
    gate_up_grad_own = jnp.stack([gate_up_grad_own[:, :1024], gate_up_grad_own[:, 1024:]])
    gate_up_new = apply_update(
        gate_up_master, gate_up_grad_own, gate_up_moment, gate_up_average, rate_gate_up * rate_unit
    )
    down_new = apply_update(
        down_master, down_grad_own, down_moment, down_average, rate_down * rate_unit
    )
    gains_new = apply_update(
        gains_master, gain_grad_own, gains_moment, gains_average, rate_gains * rate_unit
    )
    return (layer_output, input_grad) + qkv_new + out_new + gate_up_new + down_new + gains_new


def solution(mesh):
    in_specs = (
        P(("seq", "tp"), None),
        P(("seq", "tp"), None),
        P("seq"),
        P("seq"),
        P("seq", "tp"),
        P("seq", "tp"),
        P("seq", "tp"),
        P("tp", "seq"),
        P("tp", "seq"),
        P("tp", "seq"),
        P(None, "seq", "tp"),
        P(None, "seq", "tp"),
        P(None, "seq", "tp"),
        P("tp", "seq"),
        P("tp", "seq"),
        P("tp", "seq"),
        P(None, "seq"),
        P(None, "seq"),
        P(None, "seq"),
    )
    out_specs = (
        P(("seq", "tp"), None),
        P(("seq", "tp"), None),
        P("seq", "tp"),
        P("seq", "tp"),
        P("seq", "tp"),
        P("seq", "tp"),
        P("tp", "seq"),
        P("tp", "seq"),
        P("tp", "seq"),
        P("tp", "seq"),
        P(None, "seq", "tp"),
        P(None, "seq", "tp"),
        P(None, "seq", "tp"),
        P(None, "seq", "tp"),
        P("tp", "seq"),
        P("tp", "seq"),
        P("tp", "seq"),
        P("tp", "seq"),
        P(None, "seq"),
        P(None, "seq"),
        P(None, "seq"),
        P(None, "seq"),
    )
    if ring_plan_fits(mesh):
        fine = jax.sharding.Mesh(mesh.devices.reshape(2, 2, 2, 2, 2), AXES)
        names = {"seq": ("y", "c"), "tp": ("h", "l", "x")}

        def finer(spec):
            parts = []
            for entry in spec:
                entry = (entry,) if isinstance(entry, str) else (entry or ())
                parts.append(sum((names[name] for name in entry), ()) or None)
            return P(*parts)

        return jax.shard_map(
            ring_shards,
            mesh=fine,
            in_specs=tuple(finer(spec) for spec in in_specs),
            out_specs=tuple(finer(spec) for spec in out_specs),
            check_vma=False,
        )
    return jax.shard_map(shards, mesh=mesh, in_specs=in_specs, out_specs=out_specs, check_vma=False)
```

```python
import jax
import jax.numpy as jnp
from jax import lax
from jax.experimental import pallas as pl
from jax.experimental.pallas import tpu as pltpu
from jax.sharding import PartitionSpec as P

HD = 64


norm_epsilon = 1e-05
rope_theta = 130000.0
momentum_coef = 0.9
average_coef = 0.5
masked_score = -1e30
rate_qkv = 0.004
rate_out = 2.0
rate_gate_up = 0.03
rate_down = 0.009
rate_gains = 0.1


def rms_scale(values):
    return lax.rsqrt(jnp.mean(values * values, axis=-1, keepdims=True) + norm_epsilon)


def rope_tables(positions, head_size):
    frequency = rope_theta ** (-(jnp.arange(head_size // 2, dtype=jnp.float32) * 2.0) / head_size)
    angles = positions.astype(jnp.float32)[:, None] * frequency[None, :]
    return (jnp.cos(angles)[:, None, :], jnp.sin(angles)[:, None, :])


def rotate(vectors, cosine_table, sine_table):
    half_width = vectors.shape[-1] // 2
    lower_half = vectors[..., :half_width]
    upper_half = vectors[..., half_width:]
    return jnp.concatenate(
        [
            lower_half * cosine_table - upper_half * sine_table,
            upper_half * cosine_table + lower_half * sine_table,
        ],
        axis=-1,
    )


def unrotate(grads, cosine_table, sine_table):
    half_width = grads.shape[-1] // 2
    lower_half = grads[..., :half_width]
    upper_half = grads[..., half_width:]
    return jnp.concatenate(
        [
            lower_half * cosine_table + upper_half * sine_table,
            upper_half * cosine_table - lower_half * sine_table,
        ],
        axis=-1,
    )


def norm_back(values, gain, grad):
    scale_rows = rms_scale(values)
    scaled = grad * gain
    back = scale_rows * (
        scaled
        - values * scale_rows * scale_rows * jnp.mean(scaled * values, axis=-1, keepdims=True)
    )
    return (back, jnp.sum(grad * values * scale_rows, axis=0))


def apply_update(master, grad, moment, average, rate):
    moment_new = momentum_coef * moment + grad
    master_new = master - rate * (grad + momentum_coef * moment_new)
    average_new = average_coef * average + (1.0 - average_coef) * master_new
    return (moment_new, average_new, master_new, master_new.astype(jnp.bfloat16))


def shards(
    layer_input,
    cotangent,
    counts,
    positions,
    qkv_master,
    qkv_moment,
    qkv_average,
    out_master,
    out_moment,
    out_average,
    gate_up_master,
    gate_up_moment,
    gate_up_average,
    down_master,
    down_moment,
    down_average,
    gains_master,
    gains_moment,
    gains_average,
):
    tp_size = lax.axis_size("tp")
    seq_size = lax.axis_size("seq")
    own_rows = layer_input.shape[0]
    length = own_rows * tp_size
    qkv_weight, out_weight, gate_up_weight, down_weight, gain_weight = (
        lax.all_gather(qkv_master.astype(jnp.bfloat16), "seq", axis=0, tiled=True),
        lax.all_gather(out_master.astype(jnp.bfloat16), "seq", axis=1, tiled=True),
        lax.all_gather(gate_up_master.astype(jnp.bfloat16), "seq", axis=1, tiled=True),
        lax.all_gather(down_master.astype(jnp.bfloat16), "seq", axis=1, tiled=True),
        lax.all_gather(gains_master.astype(jnp.bfloat16), "seq", axis=1, tiled=True),
    )
    heads_local = qkv_weight.shape[1] // (3 * HD)
    count_total = lax.psum(counts.astype(jnp.float32), "seq")
    seq_weight = seq_size * counts.astype(jnp.float32)[0] / count_total[0]
    gain_first = gain_weight[0].astype(jnp.float32)
    gain_second = gain_weight[1].astype(jnp.float32)
    gathered = lax.all_gather(layer_input, "tp", axis=0, tiled=True)
    inputs = gathered.astype(jnp.float32)
    normed = (inputs * rms_scale(inputs) * gain_first).astype(jnp.bfloat16)
    mixture = jnp.dot(normed, qkv_weight, preferred_element_type=jnp.float32).reshape(
        length, heads_local, 3, HD
    )
    cosine_table, sine_table = rope_tables(positions, HD)
    queries = rotate(mixture[:, :, 0], cosine_table, sine_table).astype(jnp.bfloat16)
    key_rows = rotate(mixture[:, :, 1], cosine_table, sine_table).astype(jnp.bfloat16)
    value_rows = mixture[:, :, 2].astype(jnp.bfloat16)
    block_rows = min(512, length)
    block_count = length // block_rows
    score_scale = HD ** (-0.5)

    def block_scores(block_index):
        key_end = (block_index + 1) * block_rows
        query_block = queries[block_index * block_rows : key_end]
        row_index = block_index * block_rows + jnp.arange(block_rows)
        allowed = jnp.arange(key_end)[None, :] <= row_index[:, None]
        scores = score_scale * jnp.einsum(
            "qhd,khd->hqk", query_block, key_rows[:key_end], preferred_element_type=jnp.float32
        )
        return (query_block, jnp.where(allowed[None], scores, masked_score))

    attended_list = []
    log_totals = []
    for block_index in range(block_count):
        query_block, scores = block_scores(block_index)
        key_end = (block_index + 1) * block_rows
        row_max = jnp.max(scores, axis=-1, keepdims=True)
        exp_scores = jnp.exp(scores - row_max)
        row_total = jnp.sum(exp_scores, axis=-1, keepdims=True)
        soft_scores = (exp_scores / row_total).astype(jnp.bfloat16)
        attended_block = jnp.einsum(
            "hqk,khd->qhd", soft_scores, value_rows[:key_end], preferred_element_type=jnp.float32
        )
        attended_list.append(attended_block.astype(jnp.bfloat16))
        log_totals.append(row_max + jnp.log(row_total))
    attended = jnp.concatenate(attended_list, axis=0).reshape(length, heads_local * HD)
    own_start = lax.axis_index("tp") * own_rows
    input_own = layer_input.astype(jnp.float32)
    branch = lax.psum(
        jnp.dot(attended, out_weight, preferred_element_type=jnp.float32).astype(jnp.bfloat16), "tp"
    ).astype(jnp.float32)
    residual = inputs + branch
    normed_second = (residual * rms_scale(residual) * gain_second).astype(jnp.bfloat16)
    resid_own = lax.dynamic_slice_in_dim(residual, own_start, own_rows, 0)
    gate_pre = jnp.dot(normed_second, gate_up_weight[0], preferred_element_type=jnp.float32)
    up_pre = jnp.dot(normed_second, gate_up_weight[1], preferred_element_type=jnp.float32)
    gate_sigmoid = jax.nn.sigmoid(gate_pre)
    activation = (gate_pre * gate_sigmoid * up_pre).astype(jnp.bfloat16)
    layer_output = (
        resid_own
        + lax.psum_scatter(
            jnp.dot(activation, down_weight, preferred_element_type=jnp.float32).astype(
                jnp.bfloat16
            ),
            "tp",
            scatter_dimension=0,
            tiled=True,
        ).astype(jnp.float32)
    ).astype(jnp.bfloat16)
    cot_all = lax.all_gather(cotangent, "tp", axis=0, tiled=True)
    grad_out = (seq_weight * cot_all.astype(jnp.float32)).astype(jnp.bfloat16)
    grad_down = jnp.einsum("tf,td->fd", activation, grad_out, preferred_element_type=jnp.float32)
    grad_act = jnp.einsum("td,fd->tf", grad_out, down_weight, preferred_element_type=jnp.float32)
    grad_gate = (grad_act * up_pre * gate_sigmoid * (1.0 + gate_pre * (1.0 - gate_sigmoid))).astype(
        jnp.bfloat16
    )
    grad_up = (grad_act * gate_pre * gate_sigmoid).astype(jnp.bfloat16)
    grad_gate_up = jnp.stack(
        [
            jnp.einsum("td,tf->df", normed_second, grad_gate, preferred_element_type=jnp.float32),
            jnp.einsum("td,tf->df", normed_second, grad_up, preferred_element_type=jnp.float32),
        ]
    )
    grad_normed_second = lax.psum_scatter(
        (
            jnp.einsum(
                "tf,df->td", grad_gate, gate_up_weight[0], preferred_element_type=jnp.float32
            )
            + jnp.einsum(
                "tf,df->td", grad_up, gate_up_weight[1], preferred_element_type=jnp.float32
            )
        ).astype(jnp.bfloat16),
        "tp",
        scatter_dimension=0,
        tiled=True,
    ).astype(jnp.float32)
    grad_resid_own, gain_second_part = norm_back(resid_own, gain_second, grad_normed_second)
    grad_resid_own = grad_resid_own + seq_weight * cotangent.astype(jnp.float32)
    resid_grad_rows = lax.all_gather(grad_resid_own.astype(jnp.bfloat16), "tp", axis=0, tiled=True)
    grad_out_proj = jnp.einsum(
        "tc,td->cd", attended, resid_grad_rows, preferred_element_type=jnp.float32
    )
    grad_attended = (
        jnp.einsum("td,cd->tc", resid_grad_rows, out_weight, preferred_element_type=jnp.float32)
        .astype(jnp.bfloat16)
        .reshape(length, heads_local, HD)
    )
    grad_keys = jnp.zeros((length, heads_local, HD), jnp.float32)
    grad_values = jnp.zeros((length, heads_local, HD), jnp.float32)
    query_grads = []
    for block_index in range(block_count):
        key_end = (block_index + 1) * block_rows
        query_block, scores = block_scores(block_index)
        soft_scores = jnp.exp(scores - log_totals[block_index])
        grad_block = grad_attended[block_index * block_rows : key_end]
        grad_soft = jnp.einsum(
            "qhd,khd->hqk", grad_block, value_rows[:key_end], preferred_element_type=jnp.float32
        )
        row_delta = jnp.sum(soft_scores * grad_soft, axis=-1, keepdims=True)
        grad_scores = (soft_scores * (grad_soft - row_delta)).astype(jnp.bfloat16)
        query_grads.append(
            score_scale
            * jnp.einsum(
                "hqk,khd->qhd", grad_scores, key_rows[:key_end], preferred_element_type=jnp.float32
            )
        )
        grad_keys = grad_keys.at[:key_end].add(
            score_scale
            * jnp.einsum(
                "hqk,qhd->khd", grad_scores, query_block, preferred_element_type=jnp.float32
            )
        )
        grad_values = grad_values.at[:key_end].add(
            jnp.einsum(
                "hqk,qhd->khd",
                soft_scores.astype(jnp.bfloat16),
                grad_block,
                preferred_element_type=jnp.float32,
            )
        )
    grad_queries = jnp.concatenate(query_grads, axis=0)
    grad_mixture = (
        jnp.stack(
            [
                unrotate(grad_queries, cosine_table, sine_table),
                unrotate(grad_keys, cosine_table, sine_table),
                grad_values,
            ],
            axis=2,
        )
        .astype(jnp.bfloat16)
        .reshape(length, heads_local * 3 * HD)
    )
    grad_qkv = jnp.einsum("td,tc->dc", normed, grad_mixture, preferred_element_type=jnp.float32)
    grad_normed_first = lax.psum_scatter(
        jnp.einsum(
            "tc,dc->td", grad_mixture, qkv_weight, preferred_element_type=jnp.float32
        ).astype(jnp.bfloat16),
        "tp",
        scatter_dimension=0,
        tiled=True,
    ).astype(jnp.float32)
    grad_input_own, gain_first_part = norm_back(input_own, gain_first, grad_normed_first)
    input_grad = grad_resid_own + grad_input_own
    gain_grads = lax.psum(jnp.stack([gain_first_part, gain_second_part]), ("seq", "tp"))
    gain_grad_own = lax.dynamic_slice_in_dim(
        gain_grads, lax.axis_index("seq") * gains_master.shape[1], gains_master.shape[1], 1
    )
    qkv_grad_own, out_grad_own, gate_up_grad_own, down_grad_own = (
        lax.psum_scatter(
            grad_qkv.astype(jnp.bfloat16), "seq", scatter_dimension=0, tiled=True
        ).astype(jnp.float32),
        lax.psum_scatter(
            grad_out_proj.astype(jnp.bfloat16), "seq", scatter_dimension=1, tiled=True
        ).astype(jnp.float32),
        lax.psum_scatter(
            grad_gate_up.astype(jnp.bfloat16), "seq", scatter_dimension=1, tiled=True
        ).astype(jnp.float32),
        lax.psum_scatter(
            grad_down.astype(jnp.bfloat16), "seq", scatter_dimension=1, tiled=True
        ).astype(jnp.float32),
    )
    rate_unit = float(length * seq_size) ** (-0.5)
    qkv_new = apply_update(qkv_master, qkv_grad_own, qkv_moment, qkv_average, rate_qkv * rate_unit)
    out_new = apply_update(out_master, out_grad_own, out_moment, out_average, rate_out * rate_unit)
    gate_up_new = apply_update(
        gate_up_master, gate_up_grad_own, gate_up_moment, gate_up_average, rate_gate_up * rate_unit
    )
    down_new = apply_update(
        down_master, down_grad_own, down_moment, down_average, rate_down * rate_unit
    )
    gains_new = apply_update(
        gains_master, gain_grad_own, gains_moment, gains_average, rate_gains * rate_unit
    )
    return (
        layer_output,
        input_grad,
        qkv_new[0],
        qkv_new[1],
        qkv_new[2],
        qkv_new[3],
        out_new[0],
        out_new[1],
        out_new[2],
        out_new[3],
        gate_up_new[0],
        gate_up_new[1],
        gate_up_new[2],
        gate_up_new[3],
        down_new[0],
        down_new[1],
        down_new[2],
        down_new[3],
        gains_new[0],
        gains_new[1],
        gains_new[2],
        gains_new[3],
    )


AXES = ("y", "c", "h", "l", "x")
RING = ("c", "l", "x")
MESH = pl.DeviceIdType.MESH
ROW = 512
BF = jnp.bfloat16
F32 = jnp.float32
LOG2E = 1.4426950408889634
NT = (((1,), (1,)), ((), ()))
NN = (((1,), (0,)), ((), ()))
TN = (((0,), (0,)), ((), ()))


def ring_plan_fits(mesh):
    return mesh.shape["seq"] == 4 and mesh.shape["tp"] == 8


def device_pairs(target):
    pairs = []
    for index in range(32):
        y, c, h, l, x = (index >> 4) & 1, (index >> 3) & 1, (index >> 2) & 1, (index >> 1) & 1, index & 1
        goal = target(y, c, h, l, x)
        if goal is not None:
            y, c, h, l, x = goal
            pairs.append((index, 16 * y + 8 * c + 4 * h + 2 * l + x))
    return pairs


def move(values, target):
    return lax.ppermute(values, AXES, device_pairs(target))


def flip(values, bits):
    return move(
        values,
        lambda y, c, h, l, x: (
            y ^ ("y" in bits),
            c ^ ("c" in bits),
            h ^ ("h" in bits),
            l ^ ("l" in bits),
            x ^ ("x" in bits),
        ),
    )


def swap_ch(values):
    return move(values, lambda y, c, h, l, x: (y, h, c, l, x))


def rounded(values):
    return values.astype(BF)


def ring_position():
    c, l, x = (lax.axis_index(name) for name in RING)
    partners = ({"x": 1 - x}, {"l": 1 - l}, {"c": 1 - c})
    return 4 * c + 2 * l + x, partners


def enter_ring(partners):
    barrier = pltpu.get_barrier_semaphore()
    for partner in partners:
        pl.semaphore_signal(barrier, inc=1, device_id=partner, device_id_type=MESH)
    pl.semaphore_wait(barrier, len(partners))


def rows_at(block, part=None):
    if part is None:
        return pl.ds(pl.multiple_of(block * ROW, ROW), ROW)
    half = ROW // 2
    return pl.ds(pl.multiple_of(block * ROW + part * half, half), half)


def remote(source, target, sent, received, device):
    return pltpu.make_async_remote_copy(
        src_ref=source,
        dst_ref=target,
        send_sem=sent,
        recv_sem=received,
        device_id=device,
        device_id_type=MESH,
    )


def places():
    y, c, h, l, x = (lax.axis_index(name) for name in AXES)
    return y, c, h, 4 * c + 2 * l + x


def wide_partners():
    y, c, h, _ = places()
    _, (to_x, to_l, to_c) = ring_position()
    mixed = ({**to_x, **to_l}, {**to_x, **to_c}, {**to_l, **to_c}, {**to_x, **to_l, **to_c})
    across = ({"c": 0, "h": 1 - h}, {"c": 1, "h": 1 - h})
    return (to_x, to_l, to_c) + mixed + ({"y": 1 - y},) + across


class Ring:
    def __init__(self, buffer, size, send, recv, lean=False, own=None, cut=None):
        self.buffer, self.size, self.send, self.recv, self.own = buffer, size, send, recv, own
        self.cut = size // 2 if cut is None else cut
        me, (to_x, to_l, to_c) = ring_position()
        self.plan = (
            (me, 0, to_x, me ^ 1),
            (me, 1, to_l, me ^ 2),
            (me, None, to_c, me ^ 4),
            (me, 1, to_x, me ^ 1),
            (me, 0, to_l, me ^ 2),
            (me ^ 1, 0, to_l, me ^ 3),
            (me ^ 2, 1, to_x, me ^ 3),
            (me ^ 1, None, to_c, me ^ 5),
            (me ^ 2, None, to_c, me ^ 6),
            (me ^ 3, None, to_c, me ^ 7),
        )
        if lean:
            self.plan = self.plan[:5] + ((me ^ 2, 0, to_x, me ^ 3),) + self.plan[6:]

    def copy(self, index, block):
        _, part, partner, _ = self.plan[index]
        size = (self.cut, self.size - self.cut, self.size)[2 if part is None else part]
        offset = self.cut if part == 1 else 0
        place = self.buffer.at[pl.ds(pl.multiple_of(block * self.size + offset, 128), size)]
        source = place
        if self.own is not None and index < 5:
            source = self.own.at[pl.ds(offset, size)]
        return remote(source, place, self.send.at[index], self.recv.at[index], partner)

    def start(self, *indices):
        for index in indices:
            self.copy(index, self.plan[index][0]).start()

    def arrived(self, *indices):
        for index in indices:
            self.copy(index, self.plan[index][3]).wait_recv()

    def sent(self):
        for index in range(10):
            self.copy(index, self.plan[index][0]).wait_send()


class Spread:
    def __init__(self, source, target, near, far, keep, stage=None):
        self.source, self.target, self.near, self.far, self.keep = source, target, near, far, keep
        self.stage = stage
        _, self.c, self.h, _ = places()

    def local(self):
        return pltpu.make_async_copy(
            self.source, self.target if self.stage is None else self.stage, self.keep
        )

    def beside(self):
        return remote(self.source, self.target, self.near.at[0], self.near.at[1], {"c": self.h})

    def across(self, core):
        return remote(
            self.source, self.target, self.far.at[2], self.far.at[core], {"c": self.h, "h": 1 - self.h}
        )

    def start(self):
        self.across(self.c).start()

        @pl.when(self.c == self.h)
        def _():
            self.local().start()

        @pl.when(self.c != self.h)
        def _():
            self.beside().start()

    def arrived(self):
        @pl.when(self.c == self.h)
        def _():
            self.local().wait()
            if self.stage is not None:
                copy = pltpu.make_async_copy(self.stage, self.target, self.keep)
                copy.start()
                copy.wait()
            self.beside().wait_recv()

        @pl.when(self.c != self.h)
        def _():
            self.across(0).wait_recv()
            self.across(1).wait_recv()

    def sent(self):
        self.across(self.c).wait_send()

        @pl.when(self.c != self.h)
        def _():
            self.beside().wait_send()


SPREAD_SEMAPHORES = [
    pltpu.SemaphoreType.DMA((4, 2)),
    pltpu.SemaphoreType.DMA((4, 3)),
    pltpu.SemaphoreType.DMA((4,)),
    pltpu.SemaphoreType.DMA((4, 2)),
    pltpu.SemaphoreType.DMA((4, 2)),
]


class First:
    def __init__(self, refs):
        (self.shard, self.grad), (self.whole, self.moved) = refs[:2], refs[2:4]
        self.w, near, far, keep, self.y_send, self.y_recv, self.grad_sems, self.stage = refs[4:]
        self.y, self.c, self.h, _ = places()
        first = (2 * self.y + self.c) * 512
        self.pieces = [
            Spread(
                self.shard.at[pl.ds(k * 256, 256)],
                self.w.at[pl.ds(pl.multiple_of(first + k * 256, 256), 256)],
                near.at[k],
                far.at[k],
                keep.at[k],
            )
            for k in range(2)
        ]

    def over_y(self, k, core, y):
        first = (2 * y + core) * 512 + k * 256
        place = self.w.at[pl.ds(pl.multiple_of(first, 256), 256)]
        return remote(place, place, self.y_send.at[k, core], self.y_recv.at[k, core], {"y": 1 - self.y})

    def grad_load(self):
        return pltpu.make_async_copy(self.grad, self.stage, self.grad_sems.at[2])

    def grad_local(self):
        return pltpu.make_async_copy(self.stage, self.moved, self.grad_sems.at[2])

    def grad_remote(self):
        return remote(
            self.grad, self.moved, self.grad_sems.at[0], self.grad_sems.at[1], {"c": self.h, "h": self.c}
        )

    def run(self, ring):
        for piece in self.pieces:
            piece.start()

        @pl.when(self.c == self.h)
        def _():
            self.grad_load().start()

        for k in range(2):
            self.pieces[k].arrived()
            for core in range(2):
                self.over_y(k, core, self.y).start()
            if k == 0:
                ring.arrived(1)
                ring.start(6)

        @pl.when(self.c == self.h)
        def _():
            self.grad_load().wait()
            self.grad_local().start()

        @pl.when(self.c != self.h)
        def _():
            self.grad_remote().start()

        ring.arrived(4)
        ring.start(5, 8)
        ring.arrived(2, 0, 3)
        ring.start(7)
        for k in range(2):
            for core in range(2):
                self.over_y(k, core, 1 - self.y).wait_recv()
        pltpu.make_async_copy(self.w, self.whole, self.grad_sems.at[3]).start()

    def finish(self):
        for piece in self.pieces:
            piece.sent()
        for k in range(2):
            for core in range(2):
                self.over_y(k, core, self.y).wait_send()
        pltpu.make_async_copy(self.w, self.whole, self.grad_sems.at[3]).wait()

        @pl.when(self.c == self.h)
        def _():
            self.grad_local().wait()

        @pl.when(self.c != self.h)
        def _():
            self.grad_remote().wait_recv()
            self.grad_remote().wait_send()


class Second:
    def __init__(self, refs):
        self.shard, self.whole = refs[:2]
        near, far, keep, self.y_send, self.y_recv, stage = refs[2:]
        self.y, c, _, _ = places()
        columns = pl.ds(pl.multiple_of((2 * self.y + c) * 512, 512), 512)
        self.pieces = [
            Spread(
                self.shard.at[pl.ds(k * 512, 512)],
                self.whole.at[pl.ds(k * 512, 512), columns],
                near.at[k],
                far.at[k],
                keep.at[k],
                stage.at[k],
            )
            for k in range(2)
        ]

    def over_y(self, k, y):
        place = self.whole.at[pl.ds(k * 512, 512), pl.ds(pl.multiple_of(y * 1024, 1024), 1024)]
        return remote(place, place, self.y_send.at[k, 0], self.y_recv.at[k, 0], {"y": 1 - self.y})

    def run(self, ring):
        for piece in self.pieces:
            piece.start()

    def on(self, k):
        self.pieces[k].arrived()
        self.over_y(k, self.y).start()

    def finish(self):
        for k in range(2):
            self.pieces[k].sent()
            self.over_y(k, 1 - self.y).wait_recv()
            self.over_y(k, self.y).wait_send()


def gather_kernel(finish, beside, inputs, outputs, *refs):
    own_ref, refs = refs[0], refs[1:]
    given, refs = refs[:inputs], refs[inputs:]
    full_ref, outs, refs = refs[0], refs[1:4], refs[4:]
    extra_outs, refs = refs[:outputs], refs[outputs:]
    buf, res, send, recv, own_sem, full_sem, out_sem = refs[:7]
    me, _ = ring_position()
    load = pltpu.make_async_copy(own_ref, buf.at[rows_at(me)], own_sem)
    load.start()
    enter_ring(wide_partners())
    load.wait()
    early = beside is First
    ring = Ring(buf, ROW, send, recv, lean=early, cut=256 if early else 128)
    ring.start(0, 1, 2, 3, 4)
    if early:
        more = First(given[2:] + extra_outs + refs[7:])
        w_ref, tables = more.w, given[:2]
    else:
        more = Second(given[1:] + extra_outs + refs[7:])
        w_ref, tables = given[0], ()
    more.run(ring)

    def step_body(step, carry):
        block = me ^ ((step >> 1) | ((step & 1) << 2))
        rows = rows_at(block)
        if not early:

            @pl.when(step == 1)
            def _():
                ring.arrived(2)

            @pl.when(step == 2)
            def _():
                ring.arrived(0)
                ring.start(5)
                ring.arrived(1)
                ring.start(6)
                more.on(0)
                ring.arrived(3)
                ring.start(7)
                more.on(1)
                ring.arrived(4)
                ring.start(8)

        @pl.when(step == 3)
        def _():
            ring.arrived(7)

        @pl.when(step == 5)
        def _():
            ring.arrived(8)

        @pl.when(step == 6)
        def _():
            ring.arrived(5, 6)
            ring.start(9)

        @pl.when(step == 7)
        def _():
            ring.arrived(9)

        pltpu.make_async_copy(buf.at[rows], full_ref.at[rows], full_sem.at[step]).start()
        turn = step & 1

        def out_copy(which, rows):
            return pltpu.make_async_copy(
                res.at[turn, which], outs[which].at[rows], out_sem.at[turn, which]
            )

        @pl.when(step >= 2)
        def _():
            for which in range(3):
                out_copy(which, rows).wait()

        finish(buf, rows, w_ref, tables, res, turn)
        for which in range(3):
            out_copy(which, rows).start()
        return carry

    lax.fori_loop(0, 8, step_body, 0)
    ring.sent()
    more.finish()

    def drain(step, carry):
        rows = rows_at(step)
        pltpu.make_async_copy(buf.at[rows], full_ref.at[rows], full_sem.at[step]).wait()
        return carry

    lax.fori_loop(0, 8, drain, 0)
    for turn in range(2):
        for which in range(3):
            pltpu.make_async_copy(
                res.at[turn, which], outs[which].at[rows_at(0)], out_sem.at[turn, which]
            ).wait()


def feed_forward_finish(buf, rows, w_ref, tables, res, turn):
    def columns(chunk, carry):
        here = pl.multiple_of(chunk * 256, 256)
        block = buf[rows, :]
        g = jnp.dot(block, w_ref[:, pl.ds(here, 256)], preferred_element_type=F32)
        u = jnp.dot(block, w_ref[:, pl.ds(here + 1024, 256)], preferred_element_type=F32)
        res[turn, 0, :, pl.ds(here, 256)] = rounded(g)
        res[turn, 1, :, pl.ds(here, 256)] = rounded(u)
        res[turn, 2, :, pl.ds(here, 256)] = rounded(g * (1.0 / (1.0 + jnp.exp(-g))) * u)
        return carry

    lax.fori_loop(0, 4, columns, 0)


def attention_finish(buf, rows, w_ref, tables, res, turn):
    block = buf[rows, :]
    cs, sn = tables[0][rows, :], tables[1][rows, :]
    for which in range(2):
        m = jnp.dot(block, w_ref[:, which * 256 : which * 256 + 256], preferred_element_type=F32)
        if which == 0:
            m = m * (0.125 * LOG2E)
        m1, m2 = m[:, :128], m[:, 128:]
        res[turn, which, :, 0:128] = rounded(m1 * cs - m2 * sn)
        res[turn, which, :, 128:256] = rounded(m2 * cs + m1 * sn)
    res[turn, 2] = rounded(jnp.dot(block, w_ref[:, 512:768], preferred_element_type=F32))


def gather_product(own, given, anywhere_given, extra_shapes, width, finish, beside, scratch, number):
    anywhere = pl.BlockSpec(memory_space=pl.ANY)
    vmem = pl.BlockSpec(memory_space=pltpu.VMEM)
    length, depth = 8 * ROW, own.shape[1]
    inputs = len(given) + len(anywhere_given)
    return pl.pallas_call(
        lambda *refs: gather_kernel(finish, beside, inputs, len(extra_shapes), *refs),
        in_specs=[anywhere] + [vmem] * len(given) + [anywhere] * len(anywhere_given),
        out_specs=[anywhere] * (4 + len(extra_shapes)),
        out_shape=[jax.ShapeDtypeStruct((length, depth), BF)]
        + [jax.ShapeDtypeStruct((length, width), BF)] * 3
        + [jax.ShapeDtypeStruct(shape, BF) for shape in extra_shapes],
        scratch_shapes=[
            pltpu.VMEM((length, depth), BF),
            pltpu.VMEM((2, 3, ROW, width), BF),
            pltpu.SemaphoreType.DMA((10,)),
            pltpu.SemaphoreType.DMA((10,)),
            pltpu.SemaphoreType.DMA,
            pltpu.SemaphoreType.DMA((8,)),
            pltpu.SemaphoreType.DMA((2, 3)),
        ]
        + scratch,
        compiler_params=pltpu.CompilerParams(
            collective_id=number, has_side_effects=True, vmem_limit_bytes=56 * 2**20
        ),
        cost_estimate=pl.CostEstimate(
            flops=80 * 10**9, bytes_accessed=30 * 2**20, transcendentals=0
        ),
    )(own, *given, *anywhere_given)


def scatter_kernel(dims, cut, kind, *refs):
    beside = 2 if kind == 2 else 0
    if kind == 3:
        grad_ref, gate_ref, up_ref, down_ref, w_ref, out_ref, a_ref = refs[:7]
        refs = refs[7:]
        grad_buf, gate_buf, up_buf, made_sem = refs[11:]
    else:
        a_ref, w_ref, refs = refs[0], refs[1], refs[2:]
        given, refs = refs[:beside], refs[beside:]
        out_ref, refs = refs[0], refs[1:]
        more_outs, refs = refs[: 3 if beside else 0], refs[3 if beside else 0 :]
    abuf, mine, other, sums, ra, rb, near_x, near_l, send, recv, a_sem = refs[:11]
    me, partners = ring_position()
    to_x, to_l, to_c = partners
    order = (7, 3, 5, 6, 1, 2, 4, 0)

    def load(index):
        rows, turn = rows_at(me ^ order[index]), index % 2
        if kind == 3:
            pairs = ((grad_ref, grad_buf), (gate_ref, gate_buf), (up_ref, up_buf))
        else:
            pairs = ((a_ref, abuf),)
        return [
            pltpu.make_async_copy(ref.at[rows], buf.at[turn], a_sem.at[turn, k])
            for k, (ref, buf) in enumerate(pairs)
        ]

    def made(index):
        return pltpu.make_async_copy(
            abuf.at[index % 2], a_ref.at[rows_at(me ^ order[index])], made_sem.at[index % 2]
        )

    def make(index):
        turn = index % 2
        if index >= 2:
            made(index - 2).wait()

        def columns(chunk, carry):
            start = pl.multiple_of(chunk * 256, 256)
            here, there = pl.ds(start, 256), pl.ds(start + 1024, 256)
            d = lax.dot_general(grad_buf[turn], down_ref[here, :], NT, preferred_element_type=F32)
            g = gate_buf[turn, :, here].astype(F32)
            u = up_buf[turn, :, here].astype(F32)
            sigmoid = 1.0 / (1.0 + jnp.exp(-g))
            abuf[turn, :, here] = rounded(d * u * sigmoid * (1.0 + g * (1.0 - sigmoid)))
            abuf[turn, :, there] = rounded(d * g * sigmoid)
            return carry

        lax.fori_loop(0, 4, columns, 0)
        made(index).start()

    for each in load(0):
        each.start()
    enter_ring(wide_partners() if beside else partners)
    if beside:
        tail = WeightTail(given + more_outs + refs[11:])
        tail.begin()

    def copy(index, source, target, partner):
        return pltpu.make_async_remote_copy(
            src_ref=source,
            dst_ref=target,
            send_sem=send.at[index],
            recv_sem=recv.at[index],
            device_id=partner,
            device_id_type=MESH,
        )

    top, bottom = pl.ds(0, cut), pl.ds(cut, ROW - cut)
    turns = {3: 0, 1: 1, 2: 0, 0: 1}
    copies = [copy(slot, mine.at[turns[slot]], other.at[slot], to_c) for slot in range(4)] + [
        copy(4, sums.at[2, top], ra, to_x),
        copy(5, sums.at[2, bottom], rb, to_l),
        copy(6, sums.at[0, top], near_x.at[top], to_x),
        copy(7, sums.at[1, bottom], near_l.at[bottom], to_l),
        copy(8, sums.at[0, bottom], near_x.at[bottom], to_x),
        copy(9, sums.at[1, top], near_l.at[top], to_l),
    ]

    def product(index, store):
        def columns(chunk, carry):
            here = pl.ds(pl.multiple_of(chunk * 256, 256), 256)
            w = w_ref[here, :] if dims == NT else w_ref[:, here]
            store(
                here, lax.dot_general(abuf[index % 2], w, dims, preferred_element_type=F32)
            )
            return carry

        lax.fori_loop(0, 8, columns, 0)

    for index, slot in enumerate(order):
        for each in load(index):
            each.wait()
        if index + 1 < 8:
            for each in load(index + 1):
                each.start()
        if kind == 3:
            make(index)
        if slot >= 4:
            if slot in (6, 4):
                copies[3 if slot == 6 else 1].wait_send()

            def store(here, value, slot=slot):
                mine[turns[slot - 4], :, here] = rounded(value)

            product(index, store)
            copies[slot - 4].start()
        elif slot > 0:
            copies[slot].wait_recv()

            def store(here, value, slot=slot):
                sums[slot - 1, :, here] = rounded(value + other[slot, :, here].astype(F32))

            product(index, store)
            if slot == 3:
                copies[4].start()
                copies[5].start()
            if slot == 1:
                copies[6].start()
            if slot == 2:
                copies[7].start()
                copies[5].wait_recv()
                sums[0, bottom, :] = rounded(
                    sums[0, bottom, :].astype(F32) + rb[...].astype(F32)
                )
                copies[8].start()
                copies[4].wait_recv()
                sums[1, top, :] = rounded(sums[1, top, :].astype(F32) + ra[...].astype(F32))
                copies[9].start()
        else:
            copies[0].wait_recv()

            def store(here, value):
                out_ref[:, here] = value + other[0, :, here].astype(F32)

            product(index, store)
    if beside:
        tail.run()
    for part, first, second in ((top, 6, 9), (bottom, 8, 7)):
        copies[first].wait_recv()
        copies[second].wait_recv()
        out_ref[part, :] = out_ref[part, :] + (
            near_x[part, :].astype(F32) + near_l[part, :].astype(F32)
        )
    for index, each in enumerate(copies):
        if index not in (1, 3):
            each.wait_send()
    if kind == 3:
        made(6).wait()
        made(7).wait()
    if beside:
        tail.end()


class WeightTail:
    def __init__(self, refs):
        self.grad, self.layer, self.totals, self.landing, self.layer_out = refs[:5]
        stage, result, y_sems, z_sems, stage_sems, self.layer_stage, self.layer_sems = refs[5:]
        self.y, self.c, self.h, _ = places()
        self.names = [("Q", 0, 0), ("Q", 1, 0)]
        self.pieces = PieceSums(
            self.names,
            self.piece,
            lambda name: self.landing.at[name[1]],
            lambda name, h: self.totals.at[h],
            y_sems,
            z_sems,
        )
        self.sums = Sums(stage, result, stage_sems)
        for name in self.names:
            self.sums.item(
                0,
                512,
                [self.piece(name, self.y), self.landing.at[name[1]]],
                self.pieces.sends(name),
                [lambda name=name: self.pieces.over_y(name).wait_recv()],
            )

    def piece(self, name, y):
        return self.grad.at[pl.ds(pl.multiple_of((2 * y + name[1]) * 512, 512), 512)]

    def layer_load(self):
        return pltpu.make_async_copy(self.layer, self.layer_stage, self.layer_sems.at[2])

    def layer_local(self):
        return pltpu.make_async_copy(self.layer_stage, self.layer_out, self.layer_sems.at[2])

    def layer_remote(self):
        return remote(
            self.layer, self.layer_out, self.layer_sems.at[0], self.layer_sems.at[1], {"c": self.h, "h": self.c}
        )

    def begin(self):
        for name in self.names:
            self.pieces.over_y(name).start()

        @pl.when(self.c == self.h)
        def _():
            self.layer_load().start()

        @pl.when(self.c != self.h)
        def _():
            self.layer_remote().start()

    def run(self):
        @pl.when(self.c == self.h)
        def _():
            self.layer_load().wait()
            self.layer_local().start()

        for k in range(2):
            self.sums.load(k)
            self.sums.add(k)

    def end(self):
        self.sums.last_sent()
        self.pieces.end()

        @pl.when(self.c == self.h)
        def _():
            self.layer_local().wait()

        @pl.when(self.c != self.h)
        def _():
            self.layer_remote().wait_recv()
            self.layer_remote().wait_send()


def scatter_scratch(depth, width, cut):
    return [
        pltpu.VMEM((2, ROW, depth), BF),
        pltpu.VMEM((2, ROW, width), BF),
        pltpu.VMEM((4, ROW, width), BF),
        pltpu.VMEM((3, ROW, width), BF),
        pltpu.VMEM((cut, width), BF),
        pltpu.VMEM((ROW - cut, width), BF),
        pltpu.VMEM((ROW, width), BF),
        pltpu.VMEM((ROW, width), BF),
        pltpu.SemaphoreType.DMA((10,)),
        pltpu.SemaphoreType.DMA((10,)),
        pltpu.SemaphoreType.DMA((2, 3)),
    ]


def feed_forward_back(grad, gate, up, down_weight, gate_up_weight, number):
    anywhere = pl.BlockSpec(memory_space=pl.ANY)
    vmem = pl.BlockSpec(memory_space=pltpu.VMEM)
    return pl.pallas_call(
        lambda *refs: scatter_kernel(NT, ROW // 2, 3, *refs),
        in_specs=[anywhere] * 3 + [vmem] * 2,
        out_specs=[vmem, anywhere],
        out_shape=[
            jax.ShapeDtypeStruct((ROW, 2048), F32),
            jax.ShapeDtypeStruct((8 * ROW, 2048), BF),
        ],
        scratch_shapes=scatter_scratch(2048, 2048, ROW // 2)
        + [
            pltpu.VMEM((2, ROW, 2048), BF),
            pltpu.VMEM((2, ROW, 1024), BF),
            pltpu.VMEM((2, ROW, 1024), BF),
            pltpu.SemaphoreType.DMA((2,)),
        ],
        compiler_params=pltpu.CompilerParams(
            collective_id=number, has_side_effects=True, vmem_limit_bytes=62 * 2**20
        ),
        cost_estimate=pl.CostEstimate(
            flops=80 * 10**9, bytes_accessed=60 * 2**20, transcendentals=0
        ),
    )(grad, gate, up, down_weight, gate_up_weight)


def product_scatter(a, weight, dims, number, *more):
    anywhere = pl.BlockSpec(memory_space=pl.ANY)
    vmem = pl.BlockSpec(memory_space=pltpu.VMEM)
    depth = a.shape[1]
    width = weight.shape[0] if dims == NT else weight.shape[1]
    cut = 448 if more else 256
    return pl.pallas_call(
        lambda *refs: scatter_kernel(dims, cut, len(more), *refs),
        in_specs=[anywhere, vmem] + [anywhere] * len(more),
        out_specs=[vmem] + [anywhere] * (3 if more else 0),
        out_shape=[jax.ShapeDtypeStruct((ROW, width), F32)]
        + [
            jax.ShapeDtypeStruct((2, 512, 768), BF),
            jax.ShapeDtypeStruct((2, 512, 768), BF),
            jax.ShapeDtypeStruct((ROW, 2048), BF),
        ]
        * bool(more),
        scratch_shapes=scatter_scratch(depth, width, cut)
        + [
            pltpu.VMEM((2, 2, 512, 768), BF),
            pltpu.VMEM((2, 512, 768), BF),
            pltpu.SemaphoreType.DMA((2, 2)),
            pltpu.SemaphoreType.DMA((3, 2)),
            pltpu.SemaphoreType.DMA((2, 5)),
            pltpu.VMEM((ROW, 2048), BF),
            pltpu.SemaphoreType.DMA((3,)),
        ]
        * bool(more),
        compiler_params=pltpu.CompilerParams(
            collective_id=number, has_side_effects=True, vmem_limit_bytes=58 * 2**20
        ),
        cost_estimate=pl.CostEstimate(
            flops=80 * 10**9, bytes_accessed=30 * 2**20, transcendentals=0
        ),
    )(a, weight, *more)


def column_order():
    column = lax.broadcasted_iota(jnp.int32, (768, 768), 1)
    row = lax.broadcasted_iota(jnp.int32, (768, 768), 0)
    part, within = column // 256, column % 256
    turned = ((within % 128) // 32) * 192 + part * 64 + (within // 128) * 32 + within % 32
    plain = (within // 64) * 192 + 128 + within % 64
    return (row == jnp.where(part == 2, plain, turned)).astype(BF)


def head_lanes_turned(head):
    lane = lax.broadcasted_iota(jnp.int32, (1, 256), 1)
    return (lane % 128) // 32 == head


def head_lanes_plain(head):
    lane = lax.broadcasted_iota(jnp.int32, (1, 256), 1)
    return lane // 64 == head


def picked_block(step, blocks):
    block = jnp.int32(blocks[0])
    for index in range(1, len(blocks)):
        block = jnp.where(step == index, blocks[index], block)
    return block


def mark(*values):
    return sum(value[(0,) * value.ndim].astype(F32) for value in values) * 0.0


def after(values, zero):
    return values + zero.astype(values.dtype)


def held(values, zero):
    if zero is None:
        return values
    return after(lax.optimization_barrier(values), zero)


class Beside:
    def __init__(self, refs):
        self.out_shard, self.gate_up_shard, self.grad_own = refs[:3]
        self.out_full, self.gate_up, self.grad_full, self.rows_own = refs[3:7]
        (
            near,
            far,
            keep,
            self.y_send,
            self.y_recv,
            out_near,
            out_far,
            out_keep,
            self.out_y,
            grad_send,
            grad_recv,
            out_send,
            out_recv,
            self.row_send,
            self.row_recv,
            self.own_sem,
            stage,
            out_stage,
            self.grad_stage,
        ) = refs[7:]
        self.y, self.c, self.h, self.me = places()
        _, _, _, l, x = (lax.axis_index(name) for name in AXES)
        s = 2 * self.y + self.c
        self.pieces = [
            Spread(
                self.gate_up_shard.at[pl.ds(k * 128, 128)],
                self.gate_up.at[pl.ds(pl.multiple_of(s * 512 + k * 128, 128), 128)],
                near.at[k],
                far.at[k],
                keep.at[k],
                stage.at[k],
            )
            for k in range(4)
        ]
        heads = 4 * self.h + 2 * l + x
        self.out_piece = Spread(
            self.out_shard,
            self.out_full.at[
                pl.ds(pl.multiple_of(heads * 256, 256), 256), pl.ds(pl.multiple_of(s * 512, 512), 512)
            ],
            out_near,
            out_far,
            out_keep,
            out_stage,
        )
        self.grad_ring = Ring(self.grad_full, ROW, grad_send, grad_recv, lean=True, own=self.grad_stage)
        self.out_ring = Ring(self.out_full, 256, out_send, out_recv)

    def over_y(self, k, core, y):
        first = (2 * y + core) * 512 + k * 128
        place = self.gate_up.at[pl.ds(pl.multiple_of(first, 128), 128)]
        return remote(place, place, self.y_send.at[k, core], self.y_recv.at[k, core], {"y": 1 - self.y})

    def out_over_y(self, y):
        place = self.out_full.at[
            pl.ds(pl.multiple_of(self.me * 256, 256), 256), pl.ds(pl.multiple_of(y * 1024, 1024), 1024)
        ]
        return remote(place, place, self.out_y.at[0], self.out_y.at[1], {"y": 1 - self.y})

    def piece_over_y(self, k):
        self.pieces[k].arrived()
        for core in range(2):
            self.over_y(k, core, self.y).start()

    def own_out(self):
        return pltpu.make_async_copy(
            self.grad_stage, self.grad_full.at[rows_at(self.me)], self.own_sem.at[0]
        )

    def begin(self):
        own = pltpu.make_async_copy(self.grad_own, self.grad_stage, self.own_sem.at[0])
        own.start()
        enter_ring(wide_partners())
        self.out_piece.start()
        own.wait()
        self.grad_ring.start(0, 1, 2, 3, 4)
        self.own_out().start()

    def at(self, step):
        def when(number, *actions):
            @pl.when(step == number)
            def _():
                for action in actions:
                    action()

        def out_on():
            self.out_piece.arrived()
            self.out_over_y(self.y).start()
            self.pieces[0].start()

        def out_ring_on():
            self.out_over_y(1 - self.y).wait_recv()
            self.out_ring.start(0, 1, 2, 3, 4)
            self.pieces[1].start()

        def grad_one():
            self.grad_ring.arrived(1)
            self.grad_ring.start(6)

        def grad_two():
            self.grad_ring.arrived(4)
            self.grad_ring.start(5, 8)
            self.grad_ring.arrived(0, 3)
            self.grad_ring.start(7)

        def out_one():
            self.out_ring.arrived(0)
            self.out_ring.start(5)
            self.out_ring.arrived(1)
            self.out_ring.start(6)

        def out_two():
            self.out_ring.arrived(3)
            self.out_ring.start(7)
            self.out_ring.arrived(4)
            self.out_ring.start(8)

        when(0, self.begin)
        when(3, out_on)
        when(6, out_ring_on)
        when(9, grad_one, lambda: self.piece_over_y(0), self.pieces[2].start)
        when(12, grad_two)
        when(14, lambda: self.piece_over_y(1), self.pieces[3].start)
        when(17, out_one)
        when(19, lambda: self.piece_over_y(2))
        when(24, out_two)
        when(28, lambda: self.piece_over_y(3))

    def row_local(self, block, o_all):
        columns = pl.ds(pl.multiple_of(self.me * 256, 256), 256)
        return pltpu.make_async_copy(
            o_all.at[rows_at(block)], self.rows_own.at[:, columns], self.own_sem.at[1]
        )

    def row_remote(self, block, o_all, sender):
        columns = pl.ds(pl.multiple_of(sender * 256, 256), 256)
        return remote(
            o_all.at[rows_at(block)],
            self.rows_own.at[:, columns],
            self.row_send.at[block],
            self.row_recv.at[sender],
            {"c": block >> 2, "l": (block >> 1) & 1, "x": block & 1},
        )

    def send_rows(self, block, o_all):
        @pl.when(block == self.me)
        def _():
            self.row_local(block, o_all).start()

        @pl.when(block != self.me)
        def _():
            self.row_remote(block, o_all, self.me).start()

    def end(self, o_all):
        for ring in (self.out_ring, self.grad_ring):
            ring.arrived(5, 6)
            ring.start(9)
        self.own_out().wait()
        self.out_piece.sent()
        self.out_over_y(self.y).wait_send()
        for k in range(4):
            self.pieces[k].sent()
            for core in range(2):
                self.over_y(k, core, self.y).wait_send()
                self.over_y(k, core, 1 - self.y).wait_recv()
        for ring in (self.grad_ring, self.out_ring):
            ring.arrived(2, 7, 8, 9)
            ring.sent()

        def each(block, carry):
            @pl.when(block == self.me)
            def _():
                self.row_local(block, o_all).wait()

            @pl.when(block != self.me)
            def _():
                self.row_remote(block, o_all, self.me).wait_send()
                self.row_remote(block, o_all, block).wait_recv()

            return carry

        lax.fori_loop(0, 8, each, 0)


def attend_kernel(q_ref, k_ref, v_ref, out_shard, gate_up_shard, grad_own, o_ref, l_ref, *refs):
    beside = Beside((out_shard, gate_up_shard, grad_own) + refs[:4] + refs[8:])
    s_scr, m_scr, acc_scr, o_all = refs[4:8]
    head = pl.program_id(1)
    step = pl.program_id(0) * 4 + head
    block = 7 - pl.program_id(0)
    beside.at(step)
    row = lax.broadcasted_iota(jnp.int32, (ROW, ROW), 0)
    col = lax.broadcasted_iota(jnp.int32, (ROW, ROW), 1)

    def lane_max(s):
        return jnp.maximum(
            jnp.maximum(s[:, :128], s[:, 128:256]), jnp.maximum(s[:, 256:384], s[:, 384:])
        )

    def lane_sum(s):
        return (s[:, :128] + s[:, 128:256]) + (s[:, 256:384] + s[:, 384:])

    def keys_at(key_block):
        return pl.ds(pl.multiple_of(key_block * ROW, ROW), ROW)

    q = q_ref[...]
    qh = jnp.where(head_lanes_turned(head), q, jnp.zeros_like(q))

    def scores(key_block):
        return lax.dot_general(qh, k_ref[keys_at(key_block), :], NT, preferred_element_type=F32)

    s = jnp.where(col <= row, scores(block), masked_score)
    s_scr[block] = s
    m_scr[...] = lane_max(s)

    def first_pass(key_block, carry):
        s = scores(key_block)
        s_scr[key_block] = s
        m_scr[...] = jnp.maximum(m_scr[...], lane_max(s))
        return carry

    lax.fori_loop(0, block, first_pass, 0)
    top = jnp.max(m_scr[...], axis=1, keepdims=True)
    m_scr[...] = jnp.zeros_like(m_scr)
    acc_scr[...] = jnp.zeros_like(acc_scr)

    def second_pass(key_block, carry):
        e = jnp.exp2(s_scr[key_block] - top)
        m_scr[...] += lane_sum(e)
        acc_scr[...] += lax.dot_general(
            e.astype(BF), v_ref[keys_at(key_block), :], NN, preferred_element_type=F32
        )
        return carry

    lax.fori_loop(0, block + 1, second_pass, 0)
    total = jnp.sum(m_scr[...], axis=1, keepdims=True)
    part = rounded(acc_scr[...] * (1.0 / total))
    rows = rows_at(block)

    @pl.when(head == 0)
    def _():
        o_all[rows, :] = part

    @pl.when(head > 0)
    def _():
        o_all[rows, :] = jnp.where(head_lanes_plain(head), part, o_all[rows, :])

    level = jnp.transpose(jnp.broadcast_to(top + jnp.log2(total), (ROW, 128)))[0:4, :]
    row4 = lax.broadcasted_iota(jnp.int32, (4, ROW), 0)
    l_ref[0] = jnp.where(row4 == head, level, l_ref[0])

    @pl.when(head == 3)
    def _():
        o_ref[...] = o_all[rows, :]
        beside.send_rows(block, o_all)

    @pl.when(step == 31)
    def _():
        beside.end(o_all)


def attend(q, k, v, out_shard, gate_up_shard, grad_own):
    length = q.shape[0]
    blocks = length // ROW
    whole = pl.BlockSpec((length, 256), lambda i, head: (0, 0))
    anywhere = pl.BlockSpec(memory_space=pl.ANY)
    dma = pltpu.SemaphoreType.DMA
    return pl.pallas_call(
        attend_kernel,
        grid=(blocks, 4),
        in_specs=[pl.BlockSpec((ROW, 256), lambda i, head: (7 - i, 0)), whole, whole] + [anywhere] * 3,
        out_specs=[
            pl.BlockSpec((ROW, 256), lambda i, head: (7 - i, 0)),
            pl.BlockSpec((1, 4, ROW), lambda i, head: (7 - i, 0, 0)),
        ]
        + [anywhere] * 4,
        out_shape=[
            jax.ShapeDtypeStruct((length, 256), BF),
            jax.ShapeDtypeStruct((blocks, 4, ROW), F32),
            jax.ShapeDtypeStruct((2048, 2048), BF),
            jax.ShapeDtypeStruct((2048, 2048), BF),
            jax.ShapeDtypeStruct((length, 2048), BF),
            jax.ShapeDtypeStruct((ROW, 2048), BF),
        ],
        scratch_shapes=[
            pltpu.VMEM((blocks, ROW, ROW), F32),
            pltpu.VMEM((ROW, 128), F32),
            pltpu.VMEM((ROW, 256), F32),
            pltpu.VMEM((length, 256), BF),
        ]
        + SPREAD_SEMAPHORES
        + [dma((2,)), dma((3,)), dma, dma((2,))]
        + [dma((10,))] * 4
        + [dma((8,)), dma((8,)), dma((2,))]
        + [pltpu.VMEM((4, 128, 2048), BF), pltpu.VMEM((256, 512), BF), pltpu.VMEM((ROW, 2048), BF)],
        compiler_params=pltpu.CompilerParams(
            collective_id=6, has_side_effects=True, vmem_limit_bytes=48 * 2**20
        ),
        cost_estimate=pl.CostEstimate(
            flops=14 * 10**9 * blocks, bytes_accessed=10 * 2**20, transcendentals=0
        ),
    )(q, k, v, out_shard, gate_up_shard, grad_own)


KEYS = 256


class Sums:
    def __init__(self, stage, result, stage_sems):
        self.stage, self.result, self.stage_sems = stage, result, stage_sems
        self.depth = result.shape[0]
        self.items = []
        self.early = ()

    def item(self, due, rows, terms, sends, waits=(), extra=None, then=None):
        self.items.append((due, rows, terms, sends, waits, extra, then))

    def loads(self, k):
        _, rows, terms, _, _, extra, _ = self.items[k]
        turn = k % 2
        copies = [
            pltpu.make_async_copy(
                term, self.stage.at[turn, index, pl.ds(0, rows)], self.stage_sems.at[turn, index]
            )
            for index, term in enumerate(terms)
        ]
        if extra is not None:
            copies.append(pltpu.make_async_copy(extra[0], extra[1], self.stage_sems.at[turn, 4]))
        return copies

    def load(self, k):
        for wait in self.items[k][4]:
            wait()
        for copy in self.loads(k):
            copy.start()

    def add(self, k):
        _, rows, terms, sends, _, extra, then = self.items[k]
        turn = k % 2
        for copy in self.loads(k):
            copy.wait()
        if k >= self.depth and k - self.depth not in self.early:
            self.sent(k - self.depth)
        target = self.result.at[k % self.depth]
        size = rows // 8

        def chunk(index, carry):
            here = pl.ds(pl.multiple_of(index * size, size), size)
            total = self.stage[turn, 0, here, :].astype(F32)
            for term in range(1, len(terms)):
                total += self.stage[turn, term, here, :].astype(F32)
            if extra is not None:
                total += extra[1][here, :]
            target[here, :] = rounded(total)
            return carry

        lax.fori_loop(0, 8, chunk, 0)
        for here, away, local in sends(self.result.at[k % self.depth, pl.ds(0, rows)]):
            self.either(here, away, local, "start")
        if then is not None:
            then()

    def either(self, here, away, local, method):
        if local is None:
            getattr(away(), method)()
            return
        if away is None:
            getattr(local(), "wait" if method == "wait_send" else method)()
            return

        @pl.when(here)
        def _():
            getattr(local(), "wait" if method == "wait_send" else method)()

        @pl.when(jnp.logical_not(here))
        def _():
            getattr(away(), method)()

    def sent(self, k):
        _, rows, _, sends, _, _, _ = self.items[k]
        for here, away, local in sends(self.result.at[k % self.depth, pl.ds(0, rows)]):
            self.either(here, away, local, "wait_send")

    def poll(self, unit):
        for k, item in enumerate(self.items):

            @pl.when(unit == item[0])
            def _(k=k):
                self.load(k)

            @pl.when(unit == item[0] + 1)
            def _(k=k):
                self.add(k)

    def last_sent(self):
        for k in range(max(len(self.items) - self.depth, 0), len(self.items)):
            if k not in self.early:
                self.sent(k)


def half_columns(half):
    return pl.ds(half * 1024, 1024)


class RingSum:
    def __init__(self, parts, size, core_land, far_land, core_sems, far_sems, lean):
        self.lean = lean
        self.parts, self.size, self.core_land, self.far_land = parts, size, core_land, far_land
        self.core_sems, self.far_sems = core_sems, far_sems
        self.me, (self.to_x, self.to_l, self.to_c) = ring_position()

    def block(self, slot):
        return pl.ds(pl.multiple_of((self.me ^ slot) * self.size, self.size), self.size)

    def core(self, slot):
        return remote(
            self.parts.at[self.block(slot | 4)],
            self.core_land.at[slot],
            self.core_sems.at[0, slot],
            self.core_sems.at[1, slot],
            self.to_c,
        )

    def begin(self):
        for slot in (3, 1, 2, 0):
            self.core(slot).start()

    def far(self, index, source):
        device = self.to_x if index in ((0, 1, 2, 3) if self.lean else (0, 2, 4)) else self.to_l
        return remote(
            source, self.far_land.at[index], self.far_sems.at[0, index], self.far_sems.at[1, index], device
        )

    def landed(self, index):
        return lambda: self.far(index, self.far_land.at[index]).wait_recv()

    def terms(self, slot, half):
        return [
            self.parts.at[self.block(slot), half_columns(half)],
            self.core_land.at[slot, :, half_columns(half)],
        ]

    def work(self, due, last_sends, extra):
        if self.lean:
            plan = ((3, 0), (3, 1), (1, 0), (1, 1), (2, 0, 0), (2, 1, 1), (0, 0, 2, 4), (0, 1, 3, 5))
        else:
            plan = ((3, 0), (3, 1), (1, 0), (2, 1), (1, 1, 1), (2, 0, 0), (0, 0, 2, 5), (0, 1, 4, 3))
        first = {}
        for index in sorted(range(8), key=lambda index: due[index]):
            first.setdefault(plan[index][0], index)
        items = []
        for index, (slot, half, *landings) in enumerate(plan):
            waits = [self.landed(landing) for landing in landings]
            if first[slot] == index:
                waits.append(lambda slot=slot: self.core(slot).wait_recv())
            if index < 6:
                sends = lambda source, index=index: [(None, lambda: self.far(index, source), None)]
            else:
                sends = last_sends(half)
            terms = self.terms(slot, half) + [self.far_land.at[landing] for landing in landings]
            items.append((due[index], self.size, terms, sends, waits, extra(half) if index >= 6 else None))
        return items

    def end(self):
        for slot in range(4):
            self.core(slot).wait_send()


class PieceSums:
    def __init__(self, names, piece, landing, sums_at, y_sems, z_sems):
        self.names, self.piece, self.landing, self.sums_at = names, piece, landing, sums_at
        self.y_sems, self.z_sems = y_sems, z_sems
        self.y, self.c, self.h, _ = places()

    def core_of(self, name):
        return name[1]

    def over_y(self, name):
        index = self.names.index(name)
        return remote(
            self.piece(name, 1 - self.y),
            self.landing(name),
            self.y_sems.at[0, index],
            self.y_sems.at[1, index],
            {"y": 1 - self.y},
        )

    def group(self, name):
        groups = []
        for each in self.names:
            key = (each[0], each[2])
            if key not in groups:
                groups.append(key)
        return groups.index((name[0], name[2])), groups

    def over_z(self, name, h, source):
        index = self.names.index(name)
        target = self.sums_at(name, h)
        return (
            lambda: remote(
                source,
                target,
                self.z_sems.at[0, index],
                self.z_sems.at[1 + h, self.group(name)[0]],
                {"c": self.core_of(name), "h": self.c},
            ),
            lambda: pltpu.make_async_copy(source, target, self.z_sems.at[0, index]),
        )

    def sends(self, name):
        here = jnp.logical_and(self.core_of(name) == self.c, self.h == self.c)
        return lambda source: [(here, *self.over_z(name, self.h, source))]

    def end(self):
        for name in self.names:
            self.over_y(name).wait_send()
        self.owned()

    def owned(self):
        seen = []
        for name in self.names:
            group, _ = self.group(name)
            if group in seen:
                continue
            seen.append(group)
            for h in range(2):
                here = jnp.logical_and(h == self.h, self.c == self.h)

                @pl.when(jnp.logical_not(here))
                def _(name=name, h=h):
                    self.over_z(name, h, self.sums_at(name, h))[0]().wait_recv()


class BesideBack:
    def __init__(self, refs):
        self.heads_own, self.parts, self.gate_up, self.down, self.out, self.residual, self.cos, self.sin = refs[:8]
        (
            self.gate_up_sums,
            self.down_sums,
            self.out_sums,
            self.layer,
            core_land,
            far_land,
            self.y_land,
            out_core_land,
            out_far_land,
            self.out_own,
            self.out_y_land,
        ) = refs[8:19]
        (
            self.do,
            self.cs,
            self.sn,
            stage,
            result,
            self.rest,
            self.row_send,
            self.row_recv,
            core_sems,
            far_sems,
            out_core_sems,
            out_far_sems,
            self.layer_sems,
            y_sems,
            z_sems,
            self.out_sems,
            out_y_sems,
            out_z_sems,
            stage_sems,
            self.own_sem,
        ) = refs[19:]
        self.y, self.c, self.h, self.me = places()
        self.sums = Sums(stage, result, stage_sems)
        self.layer_ring = RingSum(self.parts, ROW, core_land, far_land, core_sems, far_sems, True)
        self.out_ring = RingSum(
            self.out, 256, out_core_land, out_far_land, out_core_sems, out_far_sems, False
        )
        names = [("D", 0, 0), ("D", 1, 0), ("G", 0, 0), ("G", 0, 1), ("G", 1, 0), ("G", 1, 1)]
        self.pieces = PieceSums(names, self.piece, lambda name: self.y_land.at[names.index(name)], self.sums_at, y_sems, z_sems)
        self.names = names
        out_names = [("O", 0, 0), ("O", 1, 0)]
        self.out_pieces = PieceSums(out_names, None, None, self.sums_at, out_y_sems, out_z_sems)
        work = self.layer_ring.work((22, 35, 48, 61, 36, 56, 62, 70), self.layer_sends, self.residual_half)
        work += self.out_ring.work((1, 2, 8, 14, 15, 25, 37, 26), self.out_sends, lambda half: None)
        for name, due in zip(names, (3, 12, 24, 38, 47, 58)):
            terms = [self.piece(name, self.y), self.y_land.at[names.index(name)]]
            work.append((due, ROW, terms, self.pieces.sends(name), [self.arrived(name)], None))
        work.append((64, 256, [self.out_own, self.out_y_land], self.out_owners, [self.out_landed], None))
        work.sort(key=lambda item: item[0])
        for item in work:
            self.sums.item(*item)
        last = [item[0] for item in work].index(64)
        depth = self.sums.depth
        self.sums.early = [k for k, item in enumerate(work) if item[0] in (37, 26) and k + depth >= last]

    def arrived(self, name):
        def wait():
            self.pieces.over_y(name).wait_recv()
            place = self.names.index(name) + 2
            if place < 6:
                self.pieces.over_y(self.names[place]).start()

        return wait

    def out_landed(self):
        for k in self.sums.early:
            self.sums.sent(k)
        remote(
            self.out_own, self.out_y_land, self.out_sems.at[0], self.out_sems.at[2], {"y": 1 - self.y}
        ).wait_recv()

    def out_owners(self, source):
        sends = []
        for name in self.out_pieces.names:
            sends += self.out_pieces.sends(name)(source.at[:, pl.ds(name[1] * 512, 512)])
        return sends

    def residual_half(self, half):
        return (self.residual.at[:, half_columns(half)], self.rest)

    def layer_sends(self, half):
        def sends(source):
            return [
                (
                    None,
                    None,
                    lambda: pltpu.make_async_copy(
                        source, self.layer.at[:, half_columns(half)], self.layer_sems.at[half]
                    ),
                )
            ]

        return sends

    def out_sends(self, half):
        def sends(source):
            return [
                (
                    self.y == half,
                    lambda: remote(
                        source, self.out_y_land, self.out_sems.at[half], self.out_sems.at[2], {"y": 1 - self.y}
                    ),
                    lambda: pltpu.make_async_copy(source, self.out_own, self.out_sems.at[half]),
                )
            ]

        return sends

    def piece(self, name, y):
        kind, core, half = name
        rows = pl.ds(pl.multiple_of((2 * y + core) * 512, 512), 512)
        if kind == "G":
            return self.gate_up.at[rows, half_columns(half)]
        return self.down.at[rows]

    def sums_at(self, name, h):
        kind, _, half = name
        if kind == "G":
            return self.gate_up_sums.at[h, :, half_columns(half)]
        return self.down_sums.at[h] if kind == "D" else self.out_sums.at[h]

    def tables(self):
        return (
            pltpu.make_async_copy(self.cos, self.cs, self.own_sem.at[0]),
            pltpu.make_async_copy(self.sin, self.sn, self.own_sem.at[1]),
        )

    def row_local(self):
        columns = pl.ds(pl.multiple_of(self.me * 256, 256), 256)
        return pltpu.make_async_copy(
            self.heads_own.at[:, columns], self.do.at[rows_at(self.me)], self.own_sem.at[2]
        )

    def row_remote(self, block, sender):
        columns = pl.ds(pl.multiple_of(block * 256, 256), 256)
        return remote(
            self.heads_own.at[:, columns],
            self.do.at[rows_at(sender)],
            self.row_send.at[block],
            self.row_recv.at[sender],
            {"c": block >> 2, "l": (block >> 1) & 1, "x": block & 1},
        )

    def begin(self):
        for copy in self.tables():
            copy.start()
        self.row_local().start()
        enter_ring(wide_partners())

        def send(index, carry):
            block = 7 - index

            @pl.when(block != self.me)
            def _():
                self.row_remote(block, self.me).start()

            return carry

        lax.fori_loop(0, 8, send, 0)
        self.layer_ring.begin()
        self.out_ring.begin()
        for name in self.names[:2]:
            self.pieces.over_y(name).start()
        for copy in self.tables():
            copy.wait()

    def rows_there(self, block):
        @pl.when(block == self.me)
        def _():
            self.row_local().wait()

        @pl.when(block != self.me)
        def _():
            self.row_remote(block, block).wait_recv()

    def poll(self, unit):
        self.sums.poll(unit)

    def end(self):
        def each(block, carry):
            @pl.when(block != self.me)
            def _():
                self.row_remote(block, self.me).wait_send()

            return carry

        lax.fori_loop(0, 8, each, 0)
        self.sums.last_sent()
        self.layer_ring.end()
        self.out_ring.end()
        self.pieces.end()
        self.out_pieces.owned()


def attend_back_kernel(q_ref, k_ref, v_ref, o_ref, l_ref, *refs):
    given, (dkv_ref, dq_out), outs = refs[:8], refs[8:10], refs[10:21]
    qm, dom, delta, dq, dk, dv, km, pt, dst = refs[21:30]
    beside = BesideBack(given + outs + refs[30:])
    heads = 4
    i, sub = pl.program_id(0), pl.program_id(1)
    block = 7 - i
    blocks = 8
    unit = i * (i + 1) + sub * (i + 1)
    rows_here = rows_at(block)

    @pl.when(jnp.logical_and(i == 0, sub == 0))
    def _():
        beside.begin()

    @pl.when(sub == 0)
    def _():
        beside.rows_there(block)
        q = q_ref[...]
        do = beside.do[rows_here, :]
        for head in range(heads):
            part = slice(head * ROW, (head + 1) * ROW)
            qm[block, part, :] = jnp.where(head_lanes_turned(head), q, jnp.zeros_like(q))
            dom[block, part, :] = jnp.where(head_lanes_plain(head), do, jnp.zeros_like(do))
        product = do.astype(F32) * o_ref[...].astype(F32)
        high = rounded(product)
        low = rounded(product - high.astype(F32))
        head_row = lax.broadcasted_iota(jnp.int32, (8, 256), 0)
        lane = lax.broadcasted_iota(jnp.int32, (8, 256), 1)
        pick = jnp.where(lane // 64 == head_row, 1.0, 0.0).astype(BF)
        sums = lax.dot_general(pick, high, NT, preferred_element_type=F32)
        sums += lax.dot_general(pick, low, NT, preferred_element_type=F32)
        delta[block] = sums[:heads, :]
        dq[rows_here, :] = jnp.zeros((ROW, 256), F32)

    beside.poll(unit)
    key_row = lax.broadcasted_iota(jnp.int32, (KEYS, ROW), 0)
    query_col = lax.broadcasted_iota(jnp.int32, (KEYS, ROW), 1)
    inner = pl.multiple_of(sub * KEYS, KEYS)
    k = k_ref[pl.ds(inner, KEYS), :]
    v = v_ref[pl.ds(inner, KEYS), :]
    for head in range(heads):
        km[head] = jnp.where(head_lanes_turned(head), k, jnp.zeros_like(k))
    dk[...] = jnp.zeros_like(dk)
    dv[...] = jnp.zeros_like(dv)

    def query_part(place, diagonal):
        rows = rows_at(place)
        for head in range(heads):
            part = slice(head * ROW, (head + 1) * ROW)
            st = lax.dot_general(k, qm[place, part, :], NT, preferred_element_type=F32)
            dp = lax.dot_general(v, dom[place, part, :], NT, preferred_element_type=F32)
            p = jnp.exp2(st - l_ref[place, head : head + 1, :])
            if diagonal:
                p = jnp.where(key_row + inner <= query_col, p, 0.0)
            ds = p * (dp - delta[place, head : head + 1, :])
            pt[:, part] = p.astype(BF)
            dst[:, part] = ds.astype(BF)
        dv[...] += lax.dot_general(pt[...], dom[place], NN, preferred_element_type=F32)
        dk[...] += lax.dot_general(dst[...], qm[place], NN, preferred_element_type=F32)
        total = lax.dot_general(dst[:, 0:ROW], km[0], TN, preferred_element_type=F32)
        for head in range(1, heads):
            part = slice(head * ROW, (head + 1) * ROW)
            total += lax.dot_general(dst[:, part], km[head], TN, preferred_element_type=F32)
        dq[rows, :] += total

    query_part(block, True)

    def later(query_block, carry):
        beside.poll(unit + query_block - block)
        query_part(query_block, False)
        return carry

    lax.fori_loop(block + 1, blocks, later, 0)
    table = pl.ds(pl.multiple_of(block * ROW + inner, KEYS), KEYS)
    cs, sn = beside.cs[table, :], beside.sn[table, :]
    d = dk[...] * (1.0 / LOG2E)
    d1, d2 = d[:, :128], d[:, 128:]
    dkv_ref[pl.ds(inner, KEYS), 0:128] = rounded(d1 * cs + d2 * sn)
    dkv_ref[pl.ds(inner, KEYS), 128:256] = rounded(d2 * cs - d1 * sn)
    dkv_ref[pl.ds(inner, KEYS), 256:512] = rounded(dv[...])

    @pl.when(jnp.logical_and(i == 7, sub == 1))
    def _():
        def finish(place, carry):
            rows = rows_at(place)
            cs, sn = beside.cs[rows, :], beside.sn[rows, :]
            d = dq[rows, :] * 0.125
            d1, d2 = d[:, :128], d[:, 128:]
            beside.do[rows, 0:128] = rounded(d1 * cs + d2 * sn)
            beside.do[rows, 128:256] = rounded(d2 * cs - d1 * sn)
            return carry

        lax.fori_loop(0, blocks, finish, 0)
        copy = pltpu.make_async_copy(beside.do, dq_out, beside.own_sem.at[4])
        copy.start()
        copy.wait()
        beside.end()


def attend_back(q, k, v, o, level, heads_own, parts, gate_up, down, out, residual, cos, sin):
    length = q.shape[0]
    blocks = length // ROW
    dma = pltpu.SemaphoreType.DMA
    anywhere = pl.BlockSpec(memory_space=pl.ANY)

    def key_spec(width):
        return pl.BlockSpec((ROW, width), lambda i, sub: (7 - i, 0))

    shapes = [
        (2, 512, 2048),
        (2, 512, 1024),
        (2, 256, 512),
        (ROW, 2048),
        (4, ROW, 2048),
        (6, ROW, 1024),
        (6, 512, 1024),
        (4, 256, 2048),
        (6, 256, 1024),
        (256, 1024),
        (256, 1024),
    ]
    return pl.pallas_call(
        attend_back_kernel,
        grid=(blocks, 2),
        in_specs=[key_spec(256)] * 4
        + [pl.BlockSpec((blocks, 4, ROW), lambda i, sub: (0, 0, 0))]
        + [anywhere] * 8,
        out_specs=[key_spec(512)] + [anywhere] * (1 + len(shapes)),
        out_shape=[jax.ShapeDtypeStruct((length, 512), BF), jax.ShapeDtypeStruct((length, 256), BF)]
        + [jax.ShapeDtypeStruct(shape, BF) for shape in shapes],
        scratch_shapes=[
            pltpu.VMEM((blocks, 4 * ROW, 256), BF),
            pltpu.VMEM((blocks, 4 * ROW, 256), BF),
            pltpu.VMEM((blocks, 4, ROW), F32),
            pltpu.VMEM((length, 256), F32),
            pltpu.VMEM((KEYS, 256), F32),
            pltpu.VMEM((KEYS, 256), F32),
            pltpu.VMEM((4, KEYS, 256), BF),
            pltpu.VMEM((KEYS, 4 * ROW), BF),
            pltpu.VMEM((KEYS, 4 * ROW), BF),
            pltpu.VMEM((length, 256), BF),
            pltpu.VMEM((length, 128), F32),
            pltpu.VMEM((length, 128), F32),
            pltpu.VMEM((2, 4, ROW, 1024), BF),
            pltpu.VMEM((8, ROW, 1024), BF),
            pltpu.VMEM((ROW, 1024), F32),
            dma((8,)),
            dma((8,)),
            dma((2, 4)),
            dma((2, 6)),
            dma((2, 4)),
            dma((2, 6)),
            dma((2,)),
            dma((2, 6)),
            dma((3, 6)),
            dma((3,)),
            dma((2, 2)),
            dma((3, 2)),
            dma((2, 5)),
            dma((5,)),
        ],
        compiler_params=pltpu.CompilerParams(
            collective_id=7, has_side_effects=True, vmem_limit_bytes=60 * 2**20
        ),
        cost_estimate=pl.CostEstimate(
            flops=19 * 10**9 * blocks, bytes_accessed=20 * 2**20, transcendentals=0
        ),
    )(q, k, v, o, level, heads_own, parts, gate_up, down, out, residual, cos, sin)


def ring_shards(
    layer_input,
    cotangent,
    counts,
    positions,
    qkv_master,
    qkv_moment,
    qkv_average,
    out_master,
    out_moment,
    out_average,
    gate_up_master,
    gate_up_moment,
    gate_up_average,
    down_master,
    down_moment,
    down_average,
    gains_master,
    gains_moment,
    gains_average,
):
    y, c, h, l, x = (lax.axis_index(name) for name in AXES)
    own = 4 * c + 2 * l + x
    plain_y, plain_c, straight = y == 0, c == 0, c == h

    def both_y(mine, other, axis):
        return jnp.where(
            plain_y,
            jnp.concatenate([mine, other], axis=axis),
            jnp.concatenate([other, mine], axis=axis),
        )

    def both_cores(mine, other):
        return jnp.where(plain_c, mine, other), jnp.where(plain_c, other, mine)

    turn = column_order()
    rows_in = swap_ch(layer_input).astype(F32)
    gains_here = gains_master.astype(BF)
    gains_near = jnp.concatenate(both_cores(gains_here, flip(gains_here, "c")), axis=1)
    gains_all = both_y(gains_near, flip(gains_near, "y"), 1).astype(F32)
    gain_first, gain_second = gains_all[0], gains_all[1]
    qkv_shard = jnp.dot(qkv_master.astype(BF), turn, preferred_element_type=F32).astype(BF)
    scale_first = rms_scale(rows_in)
    normed_own = (rows_in * scale_first * gain_first).astype(BF)
    frequency = rope_theta ** (
        -((jnp.arange(128, dtype=jnp.int32) % 32).astype(F32) * 2.0) / HD
    )
    positions_here = jnp.where(straight, positions, flip(positions, "c"))
    angles = positions_here.astype(F32)[:, None] * frequency[None, :]
    cosine, sine = jnp.cos(angles), jnp.sin(angles)
    count_here = counts.astype(F32)
    count_total = count_here + flip(count_here, "c")
    count_total = count_total + flip(count_total, "y")
    grad_here = (4.0 * count_here[0] / count_total[0] * cotangent.astype(F32)).astype(BF)
    normed, queries, keys, values, qkv_weight, grad_own = gather_product(
        normed_own,
        (cosine, sine),
        (qkv_shard, grad_here),
        ((2048, 768), (ROW, 2048)),
        256,
        attention_finish,
        First,
        [pltpu.VMEM((2048, 768), BF)]
        + SPREAD_SEMAPHORES
        + [pltpu.SemaphoreType.DMA((4,)), pltpu.VMEM((ROW, 2048), BF)],
        1,
    )
    gate_up_shard = jnp.concatenate([gate_up_master[0], gate_up_master[1]], axis=1).astype(BF)
    attended, level, out_weight, gate_up_weight, grad_out, attended_own = attend(
        queries, keys, values, out_master.astype(BF), gate_up_shard, grad_own
    )
    grad_rows = grad_own.astype(F32)
    residual = rows_in + jnp.dot(attended_own, out_weight, preferred_element_type=F32)
    scale_second = rms_scale(residual)
    normed_second, gate, up, activation, down_weight = gather_product(
        (residual * scale_second * gain_second).astype(BF),
        (gate_up_weight,),
        (down_master.astype(BF),),
        ((1024, 2048),),
        1024,
        feed_forward_finish,
        Second,
        SPREAD_SEMAPHORES + [pltpu.VMEM((2, 512, 512), BF)],
        2,
    )

    grad_normed_second, grad_gate_up = feed_forward_back(
        grad_out, gate, up, down_weight, gate_up_weight, 3
    )
    gate_up_grad = lax.dot_general(
        normed_second, grad_gate_up, TN, preferred_element_type=F32
    ).astype(BF)
    down_grad = lax.dot_general(grad_out, activation, TN, preferred_element_type=F32).astype(BF)
    layer_parts = jnp.dot(activation, down_weight, preferred_element_type=F32).astype(BF)

    def norm_grad(values, scale, gain, grad):
        scaled = grad * gain
        back = scale * (
            scaled - values * scale * scale * jnp.mean(scaled * values, axis=-1, keepdims=True)
        )
        return back, jnp.sum(grad * values * scale, axis=0)

    residual_grad, gain_second_part = norm_grad(
        residual, scale_second, gain_second, grad_normed_second
    )
    residual_grad = residual_grad + grad_rows
    residual_low = residual_grad.astype(BF)
    grad_heads = lax.dot_general(residual_low, out_weight, NT, preferred_element_type=F32).astype(BF)
    out_grad = lax.dot_general(attended_own, residual_low, TN, preferred_element_type=F32).astype(BF)
    grad_kv, grad_q, gate_up_sums, down_sums, out_sums, layer_own, *_ = attend_back(
        queries, keys, values, attended, level, grad_heads, layer_parts, gate_up_grad, down_grad, out_grad, residual, cosine, sine
    )
    gate_up_grad_own = gate_up_sums[0].astype(F32) + gate_up_sums[1].astype(F32)
    unit = jnp.eye(512, dtype=BF)
    down_grad_own = lax.dot_general(
        down_sums.reshape(1024, 1024), jnp.concatenate([unit, unit]), TN, preferred_element_type=F32
    )
    out_grad_own = out_sums[0].astype(F32) + out_sums[1].astype(F32)

    grad_mixture = jnp.concatenate([grad_q, grad_kv], axis=1)
    qkv_grad = lax.dot_general(normed, grad_mixture, TN, preferred_element_type=F32).astype(BF)
    qkv_grad = lax.dot_general(qkv_grad, turn, NT, preferred_element_type=F32).astype(BF)
    grad_normed_first, qkv_sums, _, layer_output = product_scatter(
        grad_mixture, qkv_weight, NT, 5, qkv_grad, layer_own
    )
    qkv_grad_own = qkv_sums[0].astype(F32) + qkv_sums[1].astype(F32)

    input_back, gain_first_part = norm_grad(rows_in, scale_first, gain_first, grad_normed_first)
    input_grad = swap_ch((residual_grad + input_back).astype(BF)).astype(F32)

    gain_grads = jnp.stack([gain_first_part, gain_second_part])
    for bit in "xlchy":
        gain_grads = gain_grads + flip(gain_grads, bit)
    gain_grad_own = lax.dynamic_slice_in_dim(gain_grads, (2 * y + c) * 512, 512, 1)

    rate_unit = float(4 * 8 * ROW) ** (-0.5)
    qkv_new = apply_update(qkv_master, qkv_grad_own, qkv_moment, qkv_average, rate_qkv * rate_unit)
    out_new = apply_update(out_master, out_grad_own, out_moment, out_average, rate_out * rate_unit)
    gate_up_grad_own = jnp.stack([gate_up_grad_own[:, :1024], gate_up_grad_own[:, 1024:]])
    gate_up_new = apply_update(
        gate_up_master, gate_up_grad_own, gate_up_moment, gate_up_average, rate_gate_up * rate_unit
    )
    down_new = apply_update(
        down_master, down_grad_own, down_moment, down_average, rate_down * rate_unit
    )
    gains_new = apply_update(
        gains_master, gain_grad_own, gains_moment, gains_average, rate_gains * rate_unit
    )
    return (layer_output, input_grad) + qkv_new + out_new + gate_up_new + down_new + gains_new


def solution(mesh):
    in_specs = (
        P(("seq", "tp"), None),
        P(("seq", "tp"), None),
        P("seq"),
        P("seq"),
        P("seq", "tp"),
        P("seq", "tp"),
        P("seq", "tp"),
        P("tp", "seq"),
        P("tp", "seq"),
        P("tp", "seq"),
        P(None, "seq", "tp"),
        P(None, "seq", "tp"),
        P(None, "seq", "tp"),
        P("tp", "seq"),
        P("tp", "seq"),
        P("tp", "seq"),
        P(None, "seq"),
        P(None, "seq"),
        P(None, "seq"),
    )
    out_specs = (
        P(("seq", "tp"), None),
        P(("seq", "tp"), None),
        P("seq", "tp"),
        P("seq", "tp"),
        P("seq", "tp"),
        P("seq", "tp"),
        P("tp", "seq"),
        P("tp", "seq"),
        P("tp", "seq"),
        P("tp", "seq"),
        P(None, "seq", "tp"),
        P(None, "seq", "tp"),
        P(None, "seq", "tp"),
        P(None, "seq", "tp"),
        P("tp", "seq"),
        P("tp", "seq"),
        P("tp", "seq"),
        P("tp", "seq"),
        P(None, "seq"),
        P(None, "seq"),
        P(None, "seq"),
        P(None, "seq"),
    )
    if ring_plan_fits(mesh):
        fine = jax.sharding.Mesh(mesh.devices.reshape(2, 2, 2, 2, 2), AXES)
        names = {"seq": ("y", "c"), "tp": ("h", "l", "x")}

        def finer(spec):
            parts = []
            for entry in spec:
                entry = (entry,) if isinstance(entry, str) else (entry or ())
                parts.append(sum((names[name] for name in entry), ()) or None)
            return P(*parts)

        return jax.shard_map(
            ring_shards,
            mesh=fine,
            in_specs=tuple(finer(spec) for spec in in_specs),
            out_specs=tuple(finer(spec) for spec in out_specs),
            check_vma=False,
        )
    return jax.shard_map(shards, mesh=mesh, in_specs=in_specs, out_specs=out_specs, check_vma=False)
```
